32 devices in a mesh: blk: 8 (over y, x, core), head: 4 (over z).
Axes of the slice: x: 2, y: 2, z: 4, core: 2. Of those that a mesh axis runs over, the one named last changes fastest.
Arguments:
- tokens: bfloat16 [4096, 768], P(('blk', 'head')), may hold values from -6 to 6
- w_qkv: bfloat16 [768, 2304], P('blk', 'head'), may hold values from -0.21875 to 0.21875
- w_out: bfloat16 [768, 768], P('head', 'blk'), may hold values from -0.875 to 0.875
- w_gate_up: bfloat16 [2, 768, 3072], P(None, 'blk', 'head'), may hold values from -0.21875 to 0.21875
- w_down: bfloat16 [3072, 768], P('head', 'blk'), may hold values from -0.109375 to 0.109375
- norm_params: bfloat16 [768, 4], P('blk', 'head'), may hold values from 0.25 to 1.75
- alibi_slope: float32 [12], replicated, may hold values from 0.00012207031 to 0.001953125
- lengths: int32 [8], replicated, may hold values from 1 to 2048, 4096 in all
- placement: int32 [4096], replicated, may hold values from 0 to 4095, as said below
- out_grad: bfloat16 [4096, 768], P(('blk', 'head')), may hold values from -6 to 6
Outputs:
- activations: bfloat16 [4096, 768], P(('blk', 'head'))
- input_grad: float32 [4096, 768], P(('blk', 'head'))
- grad_qkv: float32 [768, 2304], P('blk', 'head')
- grad_out: float32 [768, 768], P('head', 'blk')
- grad_gate_up: float32 [2, 768, 3072], P(None, 'blk', 'head')
- grad_down: float32 [3072, 768], P('head', 'blk')
- grad_norm: float32 [768, 4], P('blk', 'head')
The draws below stay inside these ranges and needn't reach their ends.
Inputs may be any that keep to these rules, and one draw needn't show every extreme that they name: `placement`: A permutation of the positions: the row at slot s of a device's 128 rows holds a position from s * 32 to (s + 1) * 32 - 1, and each such run of positions has exactly one on every device.
All inputs are finite; a program needn't handle non-finite values.
Results may differ from the reference program's by a relative error of at most 0.023.
Values may be sent and summed in bfloat16 or wider, within the bound.
A program may use at most 128 MiB of HBM per device.

```python
import math
import jax
import jax.numpy as jnp
import numpy as np
from jax import lax

D = 768
HEADS = 12
HEAD_DIM = 64
FF = 3072
TOK_DEV = 128
SEQS = 8
TOKENS = 4096
LONGEST = 2048


def draw_placement(key, part):
    devices_n = TOKENS // TOK_DEV
    slot_keys = jax.random.split(jax.random.fold_in(key, 21), TOK_DEV)
    shuffle_table = jax.vmap(lambda one_key: jax.random.permutation(one_key, devices_n))(slot_keys)
    slot_index = jnp.arange(TOK_DEV, dtype=jnp.int32)[:, None]
    positions = slot_index * devices_n + shuffle_table.astype(jnp.int32)
    return positions.T.reshape(TOKENS).astype(jnp.int32)


def steps_of(key, extent, pieces, smallest, high):
    gain, own = 1.0, jax.random.fold_in(key, 6)
    for position, blocks in pieces:
        steps = jnp.exp(jax.random.uniform(jax.random.fold_in(own, position), (blocks,), jnp.float32, smallest / len(pieces), high / len(pieces)))
        gain = gain * jnp.repeat(steps, extent[position] // blocks).reshape([-1 if axis == position else 1 for axis in range(len(extent))])
    return gain


def split_up(number_of, total, most, lean):
    weights = [(1 << 20) // math.isqrt(standing ** lean) + 1 for standing in range(2, number_of + 1)]
    surplus, counts = total - most - (number_of - 1), [1] * (number_of - 1)
    while surplus > 0:
        candidates = [i for i in range(number_of - 1) if counts[i] < most]
        mass, remaining = sum([weights[i] for i in candidates]), surplus
        for i in candidates:
            more = min(most - counts[i], max(1, remaining * weights[i] // mass), surplus)
            counts[i] = counts[i] + more
            surplus = surplus - more
    return np.array([most] + counts)


def ragged_sizes(stream_key, count, total, limit, skew):
    if count == 2:
        one = jax.random.randint(stream_key, (), max(1, total - limit), min(limit, total - 1) + 1)
        return jnp.stack([one, total - one])
    sizes = jnp.asarray(split_up(count, total, limit, skew), jnp.int32)
    couples = (count - 1) // 2
    donor, taker = sizes[1:1 + 2 * couples:2], sizes[2:2 + 2 * couples:2]
    room = jnp.minimum(donor - 1, limit - taker)
    moved = jax.random.randint(jax.random.fold_in(stream_key, 1), (couples,), 0, 1 << 20) % (room + 1)
    sizes = sizes.at[1:1 + 2 * couples:2].set(donor - moved).at[2:2 + 2 * couples:2].set(taker + moved)
    return sizes[jax.random.permutation(jax.random.fold_in(stream_key, 2), count)]


def noise(rng, shape, deviation, reach, cuts=(), kind=jnp.bfloat16):
    drawn = deviation * jax.random.normal(rng, shape, jnp.float32)
    if cuts:
        drawn = drawn * steps_of(rng, shape, cuts, -0.22, 0.18)
    return jnp.clip(drawn, -reach, reach).astype(kind)


def setup_inputs(seed: int = 0) -> dict:
    arg_keys = jax.random.split(jax.random.key(seed), 11)
    tokens = noise(arg_keys[0], (TOKENS, D), 1.0, 6.0, ((0, 32),))
    w_qkv = noise(arg_keys[1], (D, 3 * D), D ** -0.5, 0.21875, ((0, 8), (1, 4)))
    w_out = noise(arg_keys[2], (D, D), (D // 16) ** -0.5, 0.875, ((0, 4), (1, 8)))
    w_gate_up = noise(arg_keys[3], (2, D, FF), D ** -0.5, 0.21875, ((1, 8), (2, 4)))
    w_down = noise(arg_keys[4], (FF, D), FF ** -0.5, 0.109375, ((0, 4), (1, 8)))
    norm_params = jnp.clip(1.0 + 0.15 * jax.random.normal(arg_keys[5], (D, 4), jnp.float32), 0.25, 1.75).astype(jnp.bfloat16)
    alibi_slope = jnp.clip(jnp.exp(jax.random.uniform(arg_keys[6], (HEADS,), jnp.float32, math.log(0.00012207031), math.log(0.001953125))), 0.00012207031, 0.001953125)
    lengths = ragged_sizes(arg_keys[7], SEQS, TOKENS, LONGEST, 2).astype(jnp.int32)
    placement = draw_placement(jax.random.fold_in(arg_keys[10], 71), 0)
    out_grad = noise(arg_keys[9], (TOKENS, D), 1.0, 6.0, ((0, 32),))
    return dict(tokens=tokens, w_qkv=w_qkv, w_out=w_out, w_gate_up=w_gate_up, w_down=w_down, norm_params=norm_params, alibi_slope=alibi_slope, lengths=lengths, placement=placement, out_grad=out_grad)


@jax.custom_vjp
def low(v):
    return lax.optimization_barrier(v.astype(jnp.bfloat16)).astype(jnp.float32)

@jax.custom_vjp
def low_back(v):
    return v

def low_keep(v):
    return (low(v), None)

def low_pass(kept, grad):
    return (grad,)

def back_keep(v):
    return (v, None)

def back_low(kept, grad):
    return (low(grad),)
low.defvjp(low_keep, low_pass)
low_back.defvjp(back_keep, back_low)

def layer_norm(residual, norm_gain, norm_shift):
    center = residual - lax.optimization_barrier(jnp.mean(residual, axis=-1, keepdims=True))
    spread = lax.optimization_barrier(jnp.mean(center * center, axis=-1, keepdims=True))
    return center * lax.rsqrt(spread + 1e-05) * norm_gain + norm_shift

def dense_hi(left, right):
    return jnp.dot(left, right, precision=lax.Precision.HIGHEST, preferred_element_type=jnp.float32)

def attention(queries, key_rows, values, slopes, seq_ids, positions):
    row_count = queries.shape[0]
    block_rows = min(512, row_count)
    qk_scale = HEAD_DIM ** (-0.5)

    def per_block(block_in):
        q_blk, first_row = block_in
        q_pos = lax.dynamic_slice_in_dim(positions, first_row, block_rows)
        q_seq = lax.dynamic_slice_in_dim(seq_ids, first_row, block_rows)
        scores = jnp.einsum('qhd,khd->hqk', q_blk, key_rows, precision=lax.Precision.HIGHEST) * qk_scale
        distance = jnp.abs(q_pos[:, None] - positions[None, :]).astype(jnp.float32)
        scores = low_back(scores - slopes[:, None, None] * distance[None])
        same_seq = (q_seq[:, None] == seq_ids[None, :])[None]
        masked = jnp.where(same_seq, scores, -1e+30)
        row_top = lax.optimization_barrier(jnp.max(masked, axis=2, keepdims=True))
        expo = jnp.where(same_seq, jnp.exp(masked - row_top), 0.0)
        prob_tile = low(expo / lax.optimization_barrier(jnp.sum(expo, axis=2, keepdims=True)))
        return jnp.einsum('hqk,khd->qhd', prob_tile, values, precision=lax.Precision.HIGHEST)
    starts = block_rows * jnp.arange(row_count // block_rows, dtype=jnp.int32)
    blocked = queries.reshape(row_count // block_rows, block_rows, HEADS, HEAD_DIM)
    attended = lax.map(jax.checkpoint(per_block), (blocked, starts))
    return attended.reshape(row_count, HEADS, HEAD_DIM)

def reference(tokens, w_qkv, w_out, w_gate_up, w_down, norm_params, alibi_slope, lengths, placement, out_grad):
    row_count = tokens.shape[0]
    positions = placement.astype(jnp.int32)
    seq_ends = jnp.cumsum(lengths).astype(jnp.int32)
    seq_ids = lax.optimization_barrier(jnp.sum((positions[:, None] >= seq_ends[None, :]).astype(jnp.int32), axis=1)).astype(jnp.int32)

    def forward(inputs, qkv_weight, out_weight, gu_weight, down_weight, norms):
        qkv = low_back(low(dense_hi(inputs, qkv_weight))).reshape(row_count, HEADS, 3, HEAD_DIM)
        mixed = attention(qkv[:, :, 0], qkv[:, :, 1], qkv[:, :, 2], alibi_slope, seq_ids, positions)
        mixed = low_back(low(mixed.reshape(row_count, D)))
        attn_out = low_back(dense_hi(mixed, out_weight))
        hidden = layer_norm(inputs + attn_out, norms[:, 0], norms[:, 1])
        hidden_low = low(hidden)
        gate = low_back(dense_hi(hidden_low, gu_weight[0]))
        upward = low_back(dense_hi(hidden_low, gu_weight[1]))
        gated = low(jax.nn.gelu(gate, approximate=False) * upward)
        branch = low_back(dense_hi(gated, down_weight))
        return layer_norm(hidden + branch, norms[:, 2], norms[:, 3])
    floats = (tokens.astype(jnp.float32), w_qkv.astype(jnp.float32), w_out.astype(jnp.float32), w_gate_up.astype(jnp.float32), w_down.astype(jnp.float32), norm_params.astype(jnp.float32))
    result, backward = jax.vjp(forward, *floats)
    grads = backward(out_grad.astype(jnp.float32))
    return (result.astype(jnp.bfloat16), grads[0], grads[1], grads[2], grads[3], grads[4], grads[5])
```

```python
import jax
import jax.numpy as jnp
from jax import lax
from jax.sharding import PartitionSpec as P

HEADS = 12
HEAD_DIM = 64


masked_score = -1e30


def layer_norm(residual, norm_gain, norm_shift):
    center = residual - jnp.mean(residual, axis=-1, keepdims=True)
    spread = jnp.mean(center * center, axis=-1, keepdims=True)
    return center * lax.rsqrt(spread + 1e-05) * norm_gain + norm_shift


def geglu(gate, upward):
    return jax.nn.gelu(gate, approximate=False) * upward


def dot_back(grad_rows, weight):
    return lax.dot_general(
        grad_rows, weight, (((1,), (1,)), ((), ())), preferred_element_type=jnp.float32
    )


def weight_grad(left, right):
    return lax.dot_general(
        left, right, (((0,), (0,)), ((), ())), preferred_element_type=jnp.float32
    )


def seq_of(positions, seq_ends):
    return jnp.sum((positions[:, None] >= seq_ends[None, :]).astype(jnp.int32), axis=1)


def prefix_sums(lengths):
    count = lengths.shape[0]
    upto = jnp.arange(count)[None, :] <= jnp.arange(count)[:, None]
    return jnp.sum(jnp.where(upto, lengths[None, :], 0), axis=1)


def biased_scores(queries, key_rows, q_pos, k_pos, q_seq, k_seq, slopes, qk_scale):
    scores = (
        jnp.einsum("qhd,khd->hqk", queries, key_rows, preferred_element_type=jnp.float32) * qk_scale
    )
    distance = jnp.abs(q_pos[:, None] - k_pos[None, :]).astype(jnp.float32)
    scores = scores - slopes[:, None, None] * distance[None]
    same_seq = (q_seq[:, None] == k_seq[None, :])[None]
    return (scores, same_seq)


def shards(
    tokens, w_qkv, w_out, w_gate_up, w_down, norm_params, alibi_slope, lengths, placement, out_grad
):
    heads_n = lax.axis_size("head")
    head_idx = lax.axis_index("head")
    blk_idx = lax.axis_index("blk")
    tok_rows = tokens.shape[0]
    per_dev = HEADS // heads_n
    group_rows = heads_n * tok_rows
    qk_scale = HEAD_DIM ** (-0.5)
    group_tokens, norm_cols = (
        lax.all_gather(tokens, "head", axis=0, tiled=True),
        lax.all_gather(norm_params, "head", axis=1, tiled=True),
    )
    f_qkv, f_out, f_gu, f_down, f_norm = (
        lax.all_gather(w_qkv, "blk", axis=0, tiled=True),
        lax.all_gather(w_out, "blk", axis=1, tiled=True),
        lax.all_gather(w_gate_up, "blk", axis=1, tiled=True),
        lax.all_gather(w_down, "blk", axis=1, tiled=True),
        lax.all_gather(norm_cols, "blk", axis=0, tiled=True),
    )
    grouped = jnp.dot(group_tokens, f_qkv, preferred_element_type=jnp.float32).astype(jnp.bfloat16)
    grouped = grouped.reshape(group_rows, per_dev, 3, HEAD_DIM)
    norms = f_norm.astype(jnp.float32)
    queries = grouped[:, :, 0]
    key_rows = grouped[:, :, 1]
    values = grouped[:, :, 2]
    seq_ends = prefix_sums(lengths)
    q_pos = lax.dynamic_slice_in_dim(placement, blk_idx * group_rows, group_rows)
    q_seq = seq_of(q_pos, seq_ends)
    slopes = lax.dynamic_slice_in_dim(alibi_slope, head_idx * per_dev, per_dev)

    def split_rows(shard_part):
        block_count = shard_part[0].shape[0] // group_rows
        pieces = tuple(
            (arr.reshape((block_count, group_rows) + arr.shape[1:]) for arr in shard_part)
        )
        starts = group_rows * jnp.arange(block_count, dtype=jnp.int32)
        return pieces + (starts,)

    start_state = (
        jnp.full((per_dev, group_rows), masked_score, jnp.float32),
        jnp.zeros((per_dev, group_rows), jnp.float32),
        jnp.zeros((group_rows, per_dev, HEAD_DIM), jnp.float32),
    )
    running = start_state

    def forward_per_block(state, block_in):
        k_blk, v_blk, k_first = block_in
        row_best, row_total, out_sum = state
        k_pos = lax.dynamic_slice_in_dim(placement, k_first, group_rows)
        scores, same_seq = biased_scores(
            queries, k_blk, q_pos, k_pos, q_seq, seq_of(k_pos, seq_ends), slopes, qk_scale
        )
        row_top = jnp.max(jnp.where(same_seq, scores, masked_score), axis=2)
        new_best = jnp.maximum(row_best, row_top)
        factor = jnp.exp(row_best - new_best)
        prob_tile = jnp.where(same_seq, jnp.exp(scores - new_best[:, :, None]), 0.0)
        row_total = row_total * factor + jnp.sum(prob_tile, axis=2)
        out_sum = out_sum * factor.T[:, :, None] + jnp.einsum(
            "hqk,khd->qhd",
            prob_tile.astype(jnp.bfloat16),
            v_blk,
            preferred_element_type=jnp.float32,
        )
        return ((new_best, row_total, out_sum), None)

    running, _ = lax.scan(
        forward_per_block,
        running,
        split_rows(
            (
                lax.all_gather(key_rows, "blk", axis=0, tiled=True),
                lax.all_gather(values, "blk", axis=0, tiled=True),
            )
        ),
    )
    row_best, row_total, out_sum = running
    attended = (out_sum / row_total.T[:, :, None]).astype(jnp.bfloat16)
    log_total = row_best + jnp.log(row_total)
    mixed = attended.reshape(group_rows, per_dev * HEAD_DIM)
    attn_out = lax.psum_scatter(
        jnp.dot(mixed, f_out, preferred_element_type=jnp.float32).astype(jnp.bfloat16),
        "head",
        scatter_dimension=0,
        tiled=True,
    ).astype(jnp.float32)
    resid_one = tokens.astype(jnp.float32) + attn_out
    hidden, norm_one_back = jax.vjp(layer_norm, resid_one, norms[:, 0], norms[:, 1])
    hidden_low = hidden.astype(jnp.bfloat16)
    ffn_rows = lax.all_gather(hidden_low, "head", axis=0, tiled=True)
    gate = jnp.dot(ffn_rows, f_gu[0], preferred_element_type=jnp.float32)
    upward = jnp.dot(ffn_rows, f_gu[1], preferred_element_type=jnp.float32)
    gated, geglu_back = jax.vjp(geglu, gate, upward)
    gated_low = gated.astype(jnp.bfloat16)
    branch_part = jnp.dot(gated_low, f_down, preferred_element_type=jnp.float32)
    branch = lax.psum_scatter(
        branch_part.astype(jnp.bfloat16), "head", scatter_dimension=0, tiled=True
    ).astype(jnp.float32)
    result, norm_two_back = jax.vjp(layer_norm, hidden + branch, norms[:, 2], norms[:, 3])
    d_two, d_gain_two, d_shift_two = norm_two_back(out_grad.astype(jnp.float32))
    d_branch = d_two.astype(jnp.bfloat16)
    branch_rows = lax.all_gather(d_branch, "head", axis=0, tiled=True)
    g_down = weight_grad(gated_low, branch_rows)
    d_gate, d_up = geglu_back(dot_back(branch_rows, f_down))
    d_gate_low = d_gate.astype(jnp.bfloat16)
    d_up_low = d_up.astype(jnp.bfloat16)
    g_gate_up = jnp.stack([weight_grad(ffn_rows, d_gate_low), weight_grad(ffn_rows, d_up_low)])
    hidden_part = dot_back(d_gate_low, f_gu[0]) + dot_back(d_up_low, f_gu[1])
    d_hidden = d_two + lax.psum_scatter(
        hidden_part.astype(jnp.bfloat16), "head", scatter_dimension=0, tiled=True
    ).astype(jnp.float32)
    d_one, d_gain_one, d_shift_one = norm_one_back(d_hidden)
    d_attn = d_one.astype(jnp.bfloat16)
    attn_rows = lax.all_gather(d_attn, "head", axis=0, tiled=True)
    g_out = weight_grad(mixed, attn_rows)
    d_heads = dot_back(attn_rows, f_out).astype(jnp.bfloat16).reshape(group_rows, per_dev, HEAD_DIM)
    delta = jnp.sum(d_heads.astype(jnp.float32) * attended.astype(jnp.float32), axis=2).T
    zero_grad = jnp.zeros((group_rows, per_dev, HEAD_DIM), jnp.float32)
    grad_q = zero_grad

    def query_per_block(running, block_in):
        k_blk, v_blk, k_first = block_in
        k_pos = lax.dynamic_slice_in_dim(placement, k_first, group_rows)
        scores, same_seq = biased_scores(
            queries, k_blk, q_pos, k_pos, q_seq, seq_of(k_pos, seq_ends), slopes, qk_scale
        )
        prob_tile = jnp.where(same_seq, jnp.exp(scores - log_total[:, :, None]), 0.0)
        d_prob = jnp.einsum("qhd,khd->hqk", d_heads, v_blk, preferred_element_type=jnp.float32)
        d_score = (prob_tile * (d_prob - delta[:, :, None])).astype(jnp.bfloat16)
        running = (
            running
            + jnp.einsum("hqk,khd->qhd", d_score, k_blk, preferred_element_type=jnp.float32)
            * qk_scale
        )
        return (running, None)

    grad_q, _ = lax.scan(
        query_per_block,
        grad_q,
        split_rows(
            (
                lax.all_gather(key_rows, "blk", axis=0, tiled=True),
                lax.all_gather(values, "blk", axis=0, tiled=True),
            )
        ),
    )
    stats_lse, stats_delta = (
        lax.all_gather(log_total, "blk", axis=1, tiled=True),
        lax.all_gather(delta, "blk", axis=1, tiled=True),
    )
    running = (zero_grad, zero_grad)

    def key_per_block(state, block_in):
        q_blk, do_blk, q_first = block_in
        grad_k, grad_v = state
        other_pos = lax.dynamic_slice_in_dim(placement, q_first, group_rows)
        lse_blk = lax.dynamic_slice_in_dim(stats_lse, q_first, group_rows, 1)
        delta_blk = lax.dynamic_slice_in_dim(stats_delta, q_first, group_rows, 1)
        scores, same_seq = biased_scores(
            q_blk, key_rows, other_pos, q_pos, seq_of(other_pos, seq_ends), q_seq, slopes, qk_scale
        )
        prob_tile = jnp.where(same_seq, jnp.exp(scores - lse_blk[:, :, None]), 0.0)
        grad_v = grad_v + jnp.einsum(
            "hqk,qhd->khd",
            prob_tile.astype(jnp.bfloat16),
            do_blk,
            preferred_element_type=jnp.float32,
        )
        d_prob = jnp.einsum("qhd,khd->hqk", do_blk, values, preferred_element_type=jnp.float32)
        d_score = (prob_tile * (d_prob - delta_blk[:, :, None])).astype(jnp.bfloat16)
        grad_k = (
            grad_k
            + jnp.einsum("hqk,qhd->khd", d_score, q_blk, preferred_element_type=jnp.float32)
            * qk_scale
        )
        return ((grad_k, grad_v), None)

    running, _ = lax.scan(
        key_per_block,
        running,
        split_rows(
            (
                lax.all_gather(queries, "blk", axis=0, tiled=True),
                lax.all_gather(d_heads, "blk", axis=0, tiled=True),
            )
        ),
    )
    grad_k, grad_v = running
    d_grouped = jnp.stack([grad_q, grad_k, grad_v], axis=2).astype(jnp.bfloat16)
    g_norm = jnp.stack([d_gain_one, d_shift_one, d_gain_two, d_shift_two], axis=1)
    d_qkv = d_grouped.reshape(group_rows, per_dev * 3 * HEAD_DIM)
    g_qkv = weight_grad(group_tokens, d_qkv)
    input_sum, norm_share = (
        lax.psum_scatter(
            dot_back(d_qkv, f_qkv).astype(jnp.bfloat16), "head", scatter_dimension=0, tiled=True
        ).astype(jnp.float32),
        lax.psum_scatter(
            g_norm.astype(jnp.bfloat16), "head", scatter_dimension=1, tiled=True
        ).astype(jnp.float32),
    )
    input_grad = d_one + input_sum
    s_qkv, s_out, s_gu, s_down, s_norm = (
        lax.psum_scatter(g_qkv, "blk", scatter_dimension=0, tiled=True),
        lax.psum_scatter(g_out, "blk", scatter_dimension=1, tiled=True),
        lax.psum_scatter(g_gate_up, "blk", scatter_dimension=1, tiled=True),
        lax.psum_scatter(g_down, "blk", scatter_dimension=1, tiled=True),
        lax.psum_scatter(norm_share, "blk", scatter_dimension=0, tiled=True),
    )
    return (result.astype(jnp.bfloat16), input_grad, s_qkv, s_out, s_gu, s_down, s_norm)


def solution(mesh):
    placed = (
        P(("blk", "head"), None),
        P("blk", "head"),
        P("head", "blk"),
        P(None, "blk", "head"),
        P("head", "blk"),
        P("blk", "head"),
        P(),
        P(),
        P(),
        P(("blk", "head"), None),
    )
    return jax.shard_map(
        shards,
        mesh=mesh,
        in_specs=placed,
        out_specs=(
            P(("blk", "head"), None),
            P(("blk", "head"), None),
            P("blk", "head"),
            P("head", "blk"),
            P(None, "blk", "head"),
            P("head", "blk"),
            P("blk", "head"),
        ),
        check_vma=False,
    )
```

```python
import jax
import jax.numpy as jnp
from jax import lax
from jax.experimental import pallas as pl
from jax.experimental.pallas import tpu as pltpu
from jax.sharding import PartitionSpec as P

HEADS = 12
HEAD_DIM = 64


masked_score = -1e30


def layer_norm(residual, norm_gain, norm_shift):
    center = residual - jnp.mean(residual, axis=-1, keepdims=True)
    spread = jnp.mean(center * center, axis=-1, keepdims=True)
    return center * lax.rsqrt(spread + 1e-05) * norm_gain + norm_shift


def geglu(gate, upward):
    return jax.nn.gelu(gate, approximate=False) * upward


def dot_back(grad_rows, weight):
    return lax.dot_general(
        grad_rows, weight, (((1,), (1,)), ((), ())), preferred_element_type=jnp.float32
    )


def weight_grad(left, right):
    return lax.dot_general(
        left, right, (((0,), (0,)), ((), ())), preferred_element_type=jnp.float32
    )


def seq_of(positions, seq_ends):
    return jnp.sum((positions[:, None] >= seq_ends[None, :]).astype(jnp.int32), axis=1)


def prefix_sums(lengths):
    count = lengths.shape[0]
    upto = jnp.arange(count)[None, :] <= jnp.arange(count)[:, None]
    return jnp.sum(jnp.where(upto, lengths[None, :], 0), axis=1)


def biased_scores(queries, key_rows, q_pos, k_pos, q_seq, k_seq, slopes, qk_scale):
    scores = (
        jnp.einsum("qhd,khd->hqk", queries, key_rows, preferred_element_type=jnp.float32) * qk_scale
    )
    distance = jnp.abs(q_pos[:, None] - k_pos[None, :]).astype(jnp.float32)
    scores = scores - slopes[:, None, None] * distance[None]
    same_seq = (q_seq[:, None] == k_seq[None, :])[None]
    return (scores, same_seq)


def shards(
    tokens, w_qkv, w_out, w_gate_up, w_down, norm_params, alibi_slope, lengths, placement, out_grad
):
    heads_n = lax.axis_size("head")
    head_idx = lax.axis_index("head")
    blk_idx = lax.axis_index("blk")
    tok_rows = tokens.shape[0]
    per_dev = HEADS // heads_n
    group_rows = heads_n * tok_rows
    qk_scale = HEAD_DIM ** (-0.5)
    group_tokens, norm_cols = (
        lax.all_gather(tokens, "head", axis=0, tiled=True),
        lax.all_gather(norm_params, "head", axis=1, tiled=True),
    )
    f_qkv, f_out, f_gu, f_down, f_norm = (
        lax.all_gather(w_qkv, "blk", axis=0, tiled=True),
        lax.all_gather(w_out, "blk", axis=1, tiled=True),
        lax.all_gather(w_gate_up, "blk", axis=1, tiled=True),
        lax.all_gather(w_down, "blk", axis=1, tiled=True),
        lax.all_gather(norm_cols, "blk", axis=0, tiled=True),
    )
    grouped = jnp.dot(group_tokens, f_qkv, preferred_element_type=jnp.float32).astype(jnp.bfloat16)
    grouped = grouped.reshape(group_rows, per_dev, 3, HEAD_DIM)
    norms = f_norm.astype(jnp.float32)
    queries = grouped[:, :, 0]
    key_rows = grouped[:, :, 1]
    values = grouped[:, :, 2]
    seq_ends = prefix_sums(lengths)
    q_pos = lax.dynamic_slice_in_dim(placement, blk_idx * group_rows, group_rows)
    q_seq = seq_of(q_pos, seq_ends)
    slopes = lax.dynamic_slice_in_dim(alibi_slope, head_idx * per_dev, per_dev)

    def split_rows(shard_part):
        block_count = shard_part[0].shape[0] // group_rows
        pieces = tuple(
            (arr.reshape((block_count, group_rows) + arr.shape[1:]) for arr in shard_part)
        )
        starts = group_rows * jnp.arange(block_count, dtype=jnp.int32)
        return pieces + (starts,)

    start_state = (
        jnp.full((per_dev, group_rows), masked_score, jnp.float32),
        jnp.zeros((per_dev, group_rows), jnp.float32),
        jnp.zeros((group_rows, per_dev, HEAD_DIM), jnp.float32),
    )
    running = start_state

    def forward_per_block(state, block_in):
        k_blk, v_blk, k_first = block_in
        row_best, row_total, out_sum = state
        k_pos = lax.dynamic_slice_in_dim(placement, k_first, group_rows)
        scores, same_seq = biased_scores(
            queries, k_blk, q_pos, k_pos, q_seq, seq_of(k_pos, seq_ends), slopes, qk_scale
        )
        row_top = jnp.max(jnp.where(same_seq, scores, masked_score), axis=2)
        new_best = jnp.maximum(row_best, row_top)
        factor = jnp.exp(row_best - new_best)
        prob_tile = jnp.where(same_seq, jnp.exp(scores - new_best[:, :, None]), 0.0)
        row_total = row_total * factor + jnp.sum(prob_tile, axis=2)
        out_sum = out_sum * factor.T[:, :, None] + jnp.einsum(
            "hqk,khd->qhd",
            prob_tile.astype(jnp.bfloat16),
            v_blk,
            preferred_element_type=jnp.float32,
        )
        return ((new_best, row_total, out_sum), None)

    running, _ = lax.scan(
        forward_per_block,
        running,
        split_rows(
            (
                lax.all_gather(key_rows, "blk", axis=0, tiled=True),
                lax.all_gather(values, "blk", axis=0, tiled=True),
            )
        ),
    )
    row_best, row_total, out_sum = running
    attended = (out_sum / row_total.T[:, :, None]).astype(jnp.bfloat16)
    log_total = row_best + jnp.log(row_total)
    mixed = attended.reshape(group_rows, per_dev * HEAD_DIM)
    attn_out = lax.psum_scatter(
        jnp.dot(mixed, f_out, preferred_element_type=jnp.float32).astype(jnp.bfloat16),
        "head",
        scatter_dimension=0,
        tiled=True,
    ).astype(jnp.float32)
    resid_one = tokens.astype(jnp.float32) + attn_out
    hidden, norm_one_back = jax.vjp(layer_norm, resid_one, norms[:, 0], norms[:, 1])
    hidden_low = hidden.astype(jnp.bfloat16)
    ffn_rows = lax.all_gather(hidden_low, "head", axis=0, tiled=True)
    gate = jnp.dot(ffn_rows, f_gu[0], preferred_element_type=jnp.float32)
    upward = jnp.dot(ffn_rows, f_gu[1], preferred_element_type=jnp.float32)
    gated, geglu_back = jax.vjp(geglu, gate, upward)
    gated_low = gated.astype(jnp.bfloat16)
    branch_part = jnp.dot(gated_low, f_down, preferred_element_type=jnp.float32)
    branch = lax.psum_scatter(
        branch_part.astype(jnp.bfloat16), "head", scatter_dimension=0, tiled=True
    ).astype(jnp.float32)
    result, norm_two_back = jax.vjp(layer_norm, hidden + branch, norms[:, 2], norms[:, 3])
    d_two, d_gain_two, d_shift_two = norm_two_back(out_grad.astype(jnp.float32))
    d_branch = d_two.astype(jnp.bfloat16)
    branch_rows = lax.all_gather(d_branch, "head", axis=0, tiled=True)
    g_down = weight_grad(gated_low, branch_rows)
    d_gate, d_up = geglu_back(dot_back(branch_rows, f_down))
    d_gate_low = d_gate.astype(jnp.bfloat16)
    d_up_low = d_up.astype(jnp.bfloat16)
    g_gate_up = jnp.stack([weight_grad(ffn_rows, d_gate_low), weight_grad(ffn_rows, d_up_low)])
    hidden_part = dot_back(d_gate_low, f_gu[0]) + dot_back(d_up_low, f_gu[1])
    d_hidden = d_two + lax.psum_scatter(
        hidden_part.astype(jnp.bfloat16), "head", scatter_dimension=0, tiled=True
    ).astype(jnp.float32)
    d_one, d_gain_one, d_shift_one = norm_one_back(d_hidden)
    d_attn = d_one.astype(jnp.bfloat16)
    attn_rows = lax.all_gather(d_attn, "head", axis=0, tiled=True)
    g_out = weight_grad(mixed, attn_rows)
    d_heads = dot_back(attn_rows, f_out).astype(jnp.bfloat16).reshape(group_rows, per_dev, HEAD_DIM)
    delta = jnp.sum(d_heads.astype(jnp.float32) * attended.astype(jnp.float32), axis=2).T
    zero_grad = jnp.zeros((group_rows, per_dev, HEAD_DIM), jnp.float32)
    grad_q = zero_grad

    def query_per_block(running, block_in):
        k_blk, v_blk, k_first = block_in
        k_pos = lax.dynamic_slice_in_dim(placement, k_first, group_rows)
        scores, same_seq = biased_scores(
            queries, k_blk, q_pos, k_pos, q_seq, seq_of(k_pos, seq_ends), slopes, qk_scale
        )
        prob_tile = jnp.where(same_seq, jnp.exp(scores - log_total[:, :, None]), 0.0)
        d_prob = jnp.einsum("qhd,khd->hqk", d_heads, v_blk, preferred_element_type=jnp.float32)
        d_score = (prob_tile * (d_prob - delta[:, :, None])).astype(jnp.bfloat16)
        running = (
            running
            + jnp.einsum("hqk,khd->qhd", d_score, k_blk, preferred_element_type=jnp.float32)
            * qk_scale
        )
        return (running, None)

    grad_q, _ = lax.scan(
        query_per_block,
        grad_q,
        split_rows(
            (
                lax.all_gather(key_rows, "blk", axis=0, tiled=True),
                lax.all_gather(values, "blk", axis=0, tiled=True),
            )
        ),
    )
    stats_lse, stats_delta = (
        lax.all_gather(log_total, "blk", axis=1, tiled=True),
        lax.all_gather(delta, "blk", axis=1, tiled=True),
    )
    running = (zero_grad, zero_grad)

    def key_per_block(state, block_in):
        q_blk, do_blk, q_first = block_in
        grad_k, grad_v = state
        other_pos = lax.dynamic_slice_in_dim(placement, q_first, group_rows)
        lse_blk = lax.dynamic_slice_in_dim(stats_lse, q_first, group_rows, 1)
        delta_blk = lax.dynamic_slice_in_dim(stats_delta, q_first, group_rows, 1)
        scores, same_seq = biased_scores(
            q_blk, key_rows, other_pos, q_pos, seq_of(other_pos, seq_ends), q_seq, slopes, qk_scale
        )
        prob_tile = jnp.where(same_seq, jnp.exp(scores - lse_blk[:, :, None]), 0.0)
        grad_v = grad_v + jnp.einsum(
            "hqk,qhd->khd",
            prob_tile.astype(jnp.bfloat16),
            do_blk,
            preferred_element_type=jnp.float32,
        )
        d_prob = jnp.einsum("qhd,khd->hqk", do_blk, values, preferred_element_type=jnp.float32)
        d_score = (prob_tile * (d_prob - delta_blk[:, :, None])).astype(jnp.bfloat16)
        grad_k = (
            grad_k
            + jnp.einsum("hqk,qhd->khd", d_score, q_blk, preferred_element_type=jnp.float32)
            * qk_scale
        )
        return ((grad_k, grad_v), None)

    running, _ = lax.scan(
        key_per_block,
        running,
        split_rows(
            (
                lax.all_gather(queries, "blk", axis=0, tiled=True),
                lax.all_gather(d_heads, "blk", axis=0, tiled=True),
            )
        ),
    )
    grad_k, grad_v = running
    d_grouped = jnp.stack([grad_q, grad_k, grad_v], axis=2).astype(jnp.bfloat16)
    g_norm = jnp.stack([d_gain_one, d_shift_one, d_gain_two, d_shift_two], axis=1)
    d_qkv = d_grouped.reshape(group_rows, per_dev * 3 * HEAD_DIM)
    g_qkv = weight_grad(group_tokens, d_qkv)
    input_sum, norm_share = (
        lax.psum_scatter(
            dot_back(d_qkv, f_qkv).astype(jnp.bfloat16), "head", scatter_dimension=0, tiled=True
        ).astype(jnp.float32),
        lax.psum_scatter(
            g_norm.astype(jnp.bfloat16), "head", scatter_dimension=1, tiled=True
        ).astype(jnp.float32),
    )
    input_grad = d_one + input_sum
    s_qkv, s_out, s_gu, s_down, s_norm = (
        lax.psum_scatter(g_qkv, "blk", scatter_dimension=0, tiled=True),
        lax.psum_scatter(g_out, "blk", scatter_dimension=1, tiled=True),
        lax.psum_scatter(g_gate_up, "blk", scatter_dimension=1, tiled=True),
        lax.psum_scatter(g_down, "blk", scatter_dimension=1, tiled=True),
        lax.psum_scatter(norm_share, "blk", scatter_dimension=0, tiled=True),
    )
    return (result.astype(jnp.bfloat16), input_grad, s_qkv, s_out, s_gu, s_down, s_norm)


Q_SLOTS = 32
K_SLOTS = 16
SEQ_STEP = 65536.0
FAR = 32768.0
LANE_OF = (0, 64, 192)


def by_head(rows, lanes):
    lane = lax.broadcasted_iota(jnp.int32, rows.shape, 1)
    parts = [jnp.where((lane >= first) & (lane < first + HEAD_DIM), rows, 0.0) for first in lanes]
    return jnp.concatenate(parts, axis=0).astype(jnp.bfloat16)


def key_tiles(kv_ref, j):
    rows = kv_ref.shape[0] * K_SLOTS
    blk = kv_ref[:, pl.ds(pl.multiple_of(j * K_SLOTS, K_SLOTS), K_SLOTS), :]
    return blk.reshape(rows, blk.shape[2])


def attend(span_ref, slope_ref, q_ref, kv_ref, kcode_ref, qcode_ref, out_ref, lse_ref, vt_ref):
    devs, slots, _ = kv_ref.shape
    rows = devs * K_SLOTS
    q_rows = q_ref.shape[0] * Q_SLOTS

    def turn(j, _):
        kv = key_tiles(kv_ref, j)[:, 128:384]
        vt_ref[j] = kv.astype(jnp.float32).T.astype(jnp.bfloat16)
        return 0

    lax.fori_loop(0, slots // K_SLOTS, turn, 0)

    def chunk(i, _):
        first = pl.multiple_of(i * Q_SLOTS, Q_SLOTS)
        q = q_ref[:, pl.ds(first, Q_SLOTS), :].reshape(q_rows, 192).astype(jnp.float32)
        q = jnp.concatenate([q, jnp.zeros((q_rows, 64), jnp.float32)], axis=1)
        qbd = by_head(q, (0, 64, 128))
        qcode = qcode_ref[i]

        def block(j, state):
            kv = key_tiles(kv_ref, j)
            keys = jnp.concatenate([kv[:, 0:128], kv[:, 256:384]], axis=1)
            s_all = lax.dot_general(keys, qbd, (((1,), (1,)), ((), ())), preferred_element_type=jnp.float32)
            dist = jnp.abs(kcode_ref[pl.ds(pl.multiple_of(j * rows, rows), rows), :] - qcode)
            keep = dist < FAR
            fresh = []
            for h in range(3):
                best, total, acc = state[h]
                s = jnp.where(keep, s_all[:, 128 * h : 128 * h + 128] - slope_ref[h] * dist, masked_score)
                top = jnp.maximum(best, jnp.max(s, axis=0, keepdims=True))
                factor = jnp.exp(best - top)
                p = jnp.exp(s - top)
                total = total * factor + jnp.sum(p, axis=0, keepdims=True)
                vt = vt_ref[j, LANE_OF[h] : LANE_OF[h] + 64, :]
                acc = acc * factor + jnp.dot(vt, p.astype(jnp.bfloat16), preferred_element_type=jnp.float32)
                fresh.append((top, total, acc))
            return tuple(fresh)

        start = tuple(
            (
                jnp.full((1, q_rows), masked_score, jnp.float32),
                jnp.zeros((1, q_rows), jnp.float32),
                jnp.zeros((64, q_rows), jnp.float32),
            )
            for _ in range(3)
        )
        done = lax.fori_loop(span_ref[i, 0], span_ref[i, 1], block, start)
        outs = [acc / total for _, total, acc in done]
        full = jnp.concatenate([outs[0], outs[1], jnp.zeros((64, q_rows), jnp.float32), outs[2]], axis=0)
        out_ref[:, pl.ds(first, Q_SLOTS), :] = full.T.astype(jnp.bfloat16).reshape(-1, Q_SLOTS, 256)
        for h in range(3):
            lse_ref[i, h : h + 1, :] = done[h][0] + jnp.log(done[h][1])
        return 0

    lax.fori_loop(0, slots // Q_SLOTS, chunk, 0)


def attend_back(span_ref, slope_ref, q_ref, kv_ref, kcode_ref, qcode_ref, out_ref, do_ref, lse_ref,
                dq_ref, dkv_ref, kt_ref, sum_ref):
    devs, slots, _ = kv_ref.shape
    rows = devs * K_SLOTS
    q_rows = q_ref.shape[0] * Q_SLOTS
    scale = HEAD_DIM ** (-0.5)

    def turn(j, _):
        kv = key_tiles(kv_ref, j)
        keys = jnp.concatenate([kv[:, 0:128], kv[:, 256:384]], axis=1)
        kt_ref[j] = keys.astype(jnp.float32).T.astype(jnp.bfloat16)
        sum_ref[j] = jnp.zeros((rows, 384), jnp.float32)
        return 0

    lax.fori_loop(0, slots // K_SLOTS, turn, 0)

    def chunk(i, _):
        first = pl.multiple_of(i * Q_SLOTS, Q_SLOTS)
        q = q_ref[:, pl.ds(first, Q_SLOTS), :].reshape(q_rows, 192).astype(jnp.float32)
        q = jnp.concatenate([q, jnp.zeros((q_rows, 64), jnp.float32)], axis=1)
        qbd = by_head(q, (0, 64, 128))
        do = do_ref[:, pl.ds(first, Q_SLOTS), :].reshape(q_rows, 256).astype(jnp.float32)
        out = out_ref[:, pl.ds(first, Q_SLOTS), :].reshape(q_rows, 256).astype(jnp.float32)
        dobd = by_head(do, LANE_OF)
        prod = (do * out).T
        delta = [jnp.sum(prod[f : f + 64, :], axis=0, keepdims=True) for f in LANE_OF]
        qcode = qcode_ref[i]

        def block(j, state):
            kv = key_tiles(kv_ref, j)
            keys = jnp.concatenate([kv[:, 0:128], kv[:, 256:384]], axis=1)
            vals = kv[:, 128:384]
            s_all = lax.dot_general(keys, qbd, (((1,), (1,)), ((), ())), preferred_element_type=jnp.float32)
            dp_all = lax.dot_general(vals, dobd, (((1,), (1,)), ((), ())), preferred_element_type=jnp.float32)
            dist = jnp.abs(kcode_ref[pl.ds(pl.multiple_of(j * rows, rows), rows), :] - qcode)
            keep = dist < FAR
            ps, dss, fresh = [], [], []
            for h in range(3):
                s = s_all[:, 128 * h : 128 * h + 128] - slope_ref[h] * dist - lse_ref[i, h : h + 1, :]
                p = jnp.exp(jnp.where(keep, s, masked_score))
                ds = (p * (dp_all[:, 128 * h : 128 * h + 128] - delta[h])).astype(jnp.bfloat16)
                ps.append(p.astype(jnp.bfloat16))
                dss.append(ds)
                kt = kt_ref[j, 64 * h : 64 * h + 64, :]
                fresh.append(state[h] + jnp.dot(kt, ds, preferred_element_type=jnp.float32))
            dv = jnp.dot(jnp.concatenate(ps, axis=1), dobd, preferred_element_type=jnp.float32)
            dk = jnp.dot(jnp.concatenate(dss, axis=1), qbd, preferred_element_type=jnp.float32)
            sum_ref[j, :, 0:128] += dk[:, 0:128]
            sum_ref[j, :, 128:256] += dv[:, 0:128]
            sum_ref[j, :, 256:384] += dk[:, 128:256] + dv[:, 128:256]
            return tuple(fresh)

        start = tuple(jnp.zeros((64, q_rows), jnp.float32) for _ in range(3))
        done = lax.fori_loop(span_ref[i, 0], span_ref[i, 1], block, start)
        full = jnp.concatenate(done + (jnp.zeros((64, q_rows), jnp.float32),), axis=0) * scale
        dq_ref[:, pl.ds(first, Q_SLOTS), :] = full.T[:, 0:192].astype(jnp.bfloat16).reshape(-1, Q_SLOTS, 192)
        return 0

    lax.fori_loop(0, slots // Q_SLOTS, chunk, 0)

    def leave(j, _):
        dkv_ref[:, pl.ds(pl.multiple_of(j * K_SLOTS, K_SLOTS), K_SLOTS), :] = (
            sum_ref[j].astype(jnp.bfloat16).reshape(devs, K_SLOTS, 384)
        )
        return 0

    lax.fori_loop(0, slots // K_SLOTS, leave, 0)


VM = pl.BlockSpec(memory_space=pltpu.VMEM)
SM = pl.BlockSpec(memory_space=pltpu.SMEM)


def run_attend(span, slopes, q, kv, kcode, qcode):
    heads_n, slots, _ = q.shape
    devs = kv.shape[0]
    return pl.pallas_call(
        attend,
        out_shape=(
            jax.ShapeDtypeStruct((heads_n, slots, 256), jnp.bfloat16),
            jax.ShapeDtypeStruct((slots // Q_SLOTS, 8, heads_n * Q_SLOTS), jnp.float32),
        ),
        in_specs=[SM, SM, VM, VM, VM, VM],
        out_specs=(VM, VM),
        scratch_shapes=[pltpu.VMEM((slots // K_SLOTS, 256, devs * K_SLOTS), jnp.bfloat16)],
        compiler_params=pltpu.CompilerParams(vmem_limit_bytes=40 << 20),
        name="attend",
    )(span, slopes, q, kv, kcode, qcode)


def run_attend_back(span, slopes, q, kv, kcode, qcode, out, do, lse):
    heads_n, slots, _ = q.shape
    devs = kv.shape[0]
    return pl.pallas_call(
        attend_back,
        out_shape=(
            jax.ShapeDtypeStruct((heads_n, slots, 192), jnp.bfloat16),
            jax.ShapeDtypeStruct((devs, slots, 384), jnp.bfloat16),
        ),
        in_specs=[SM, SM, VM, VM, VM, VM, VM, VM, VM],
        out_specs=(VM, VM),
        scratch_shapes=[
            pltpu.VMEM((slots // K_SLOTS, 256, devs * K_SLOTS), jnp.bfloat16),
            pltpu.VMEM((slots // K_SLOTS, devs * K_SLOTS, 384), jnp.float32),
        ],
        compiler_params=pltpu.CompilerParams(vmem_limit_bytes=48 << 20),
        name="attend_back",
    )(span, slopes, q, kv, kcode, qcode, out, do, lse)


def key_spans(seq_starts, seq_ends, chunk_positions, block_positions, chunks):
    first = chunk_positions * jnp.arange(chunks, dtype=jnp.int32)
    last = first + chunk_positions - 1
    lo_seq = jnp.sum((first[:, None] >= seq_ends[None, :]).astype(jnp.int32), axis=1)
    hi_seq = jnp.sum((last[:, None] >= seq_ends[None, :]).astype(jnp.int32), axis=1)
    seqs = jnp.arange(seq_ends.shape[0], dtype=jnp.int32)[None, :]
    lo = jnp.sum(jnp.where(seqs == lo_seq[:, None], seq_starts[None, :], 0), axis=1)
    hi = jnp.sum(jnp.where(seqs == hi_seq[:, None], seq_ends[None, :], 0), axis=1)
    return jnp.stack([lo // block_positions, (hi + block_positions - 1) // block_positions], axis=1)


def to_cols(w):
    p = [[w[:, (h * 3 + c) * 64 : (h * 3 + c) * 64 + 64] for c in range(3)] for h in range(3)]
    return jnp.concatenate(
        [p[0][1], p[1][1], p[0][2], p[1][2], p[2][1], p[2][2], p[0][0], p[1][0], p[2][0]], axis=1
    )


def from_cols(g):
    piece = [g[:, 64 * i : 64 * i + 64] for i in range(9)]
    order = (6, 0, 2, 7, 1, 3, 8, 4, 5)
    return jnp.concatenate([piece[i] for i in order], axis=1)


def pad_heads(rows):
    return jnp.concatenate([rows[:128], jnp.zeros((64, rows.shape[1]), rows.dtype), rows[128:]], axis=0)


def fast_shards(
    tokens, w_qkv, w_out, w_gate_up, w_down, norm_params, alibi_slope, lengths, placement, out_grad
):
    heads_n = lax.axis_size("head")
    blk_n = lax.axis_size("blk")
    head_idx = lax.axis_index("head")
    blk_idx = lax.axis_index("blk")
    tok_rows, width = tokens.shape
    per_dev = HEADS // heads_n
    group_rows = heads_n * tok_rows
    devs = heads_n * blk_n
    share = w_qkv.shape[0]
    bf16 = jnp.bfloat16

    attn_w = lax.all_gather(jnp.concatenate([to_cols(w_qkv), w_out.T], axis=1), "blk", axis=0, tiled=True)
    ffn_w = lax.all_gather(
        jnp.concatenate([w_gate_up, w_down.T[None]], axis=0), "blk", axis=1, tiled=True
    )
    norms = lax.all_gather(norm_params.reshape(share), ("blk", "head"), axis=0, tiled=False)
    norms = norms.reshape(blk_n, heads_n, share).transpose(1, 0, 2).reshape(heads_n, width).astype(jnp.float32)
    group_tokens = lax.all_gather(tokens, "head", axis=0, tiled=True)
    w_in = attn_w[:, :576]
    out_t = attn_w[:, 576:]
    w_gate, w_up, down_t = ffn_w[0], ffn_w[1], ffn_w[2]

    kvq = jnp.dot(group_tokens, w_in, preferred_element_type=jnp.float32).astype(bf16)
    kv = lax.all_gather(kvq[:, :384], "blk", axis=0, tiled=True).reshape(devs, tok_rows, 384)
    q = (kvq[:, 384:] * bf16(HEAD_DIM ** (-0.5))).reshape(heads_n, tok_rows, 192)

    seq_ends = prefix_sums(lengths)
    code = placement.astype(jnp.float32) + SEQ_STEP * seq_of(placement, seq_ends).astype(jnp.float32)
    k_blocks = tok_rows // K_SLOTS
    q_chunks = tok_rows // Q_SLOTS
    kcode = code.reshape(devs, k_blocks, K_SLOTS).transpose(1, 0, 2).reshape(-1, 1)
    kcode = jnp.broadcast_to(kcode, (kcode.shape[0], 128))
    qcode = lax.dynamic_slice_in_dim(code, blk_idx * group_rows, group_rows)
    qcode = qcode.reshape(heads_n, q_chunks, Q_SLOTS).transpose(1, 0, 2).reshape(q_chunks, 1, heads_n * Q_SLOTS)
    slopes = lax.dynamic_slice_in_dim(alibi_slope, head_idx * per_dev, per_dev)
    span = key_spans(seq_ends - lengths, seq_ends, Q_SLOTS * devs, K_SLOTS * devs, q_chunks)

    mixed, lse = run_attend(span, slopes, q, kv, kcode, qcode)
    mixed_rows = mixed.reshape(group_rows, 256)
    out_pad = pad_heads(out_t.T)
    attn_out = lax.psum_scatter(
        jnp.dot(mixed_rows, out_pad, preferred_element_type=jnp.float32).astype(bf16),
        "head", scatter_dimension=0, tiled=True,
    ).astype(jnp.float32)
    resid_one = tokens.astype(jnp.float32) + attn_out
    hidden, norm_one_back = jax.vjp(layer_norm, resid_one, norms[0], norms[1])
    ffn_rows = lax.all_gather(hidden.astype(bf16), "head", axis=0, tiled=True)
    gate = jnp.dot(ffn_rows, w_gate, preferred_element_type=jnp.float32)
    upward = jnp.dot(ffn_rows, w_up, preferred_element_type=jnp.float32)
    gated, geglu_back = jax.vjp(geglu, gate, upward)
    gated_low = gated.astype(bf16)
    branch = lax.psum_scatter(
        dot_back(gated_low, down_t).astype(bf16), "head", scatter_dimension=0, tiled=True
    ).astype(jnp.float32)
    result, norm_two_back = jax.vjp(layer_norm, hidden + branch, norms[2], norms[3])
    d_two, d_gain_two, d_shift_two = norm_two_back(out_grad.astype(jnp.float32))
    branch_rows = lax.all_gather(d_two.astype(bf16), "head", axis=0, tiled=True)
    d_gate, d_up = geglu_back(jnp.dot(branch_rows, down_t, preferred_element_type=jnp.float32))
    d_gate_low = d_gate.astype(bf16)
    d_up_low = d_up.astype(bf16)
    hidden_part = dot_back(d_gate_low, w_gate) + dot_back(d_up_low, w_up)
    d_hidden = d_two + lax.psum_scatter(
        hidden_part.astype(bf16), "head", scatter_dimension=0, tiled=True
    ).astype(jnp.float32)
    g_ffn = jnp.stack(
        [weight_grad(ffn_rows, d_gate_low), weight_grad(ffn_rows, d_up_low), weight_grad(branch_rows, gated_low)]
    ).astype(bf16)
    s_ffn = lax.psum_scatter(g_ffn, "blk", scatter_dimension=1, tiled=True).astype(jnp.float32)
    d_one, d_gain_one, d_shift_one = norm_one_back(d_hidden)
    attn_rows = lax.all_gather(d_one.astype(bf16), "head", axis=0, tiled=True)
    d_heads = dot_back(attn_rows, out_pad).astype(bf16)
    d_q, dkv = run_attend_back(
        span, slopes, q, kv, kcode, qcode, mixed, d_heads.reshape(heads_n, tok_rows, 256), lse
    )
    d_kv = lax.psum_scatter(dkv.reshape(devs * tok_rows, 384), "blk", scatter_dimension=0, tiled=True)
    d_kvq = jnp.concatenate([d_kv, d_q.reshape(group_rows, 192)], axis=1)
    input_grad = d_one + lax.psum_scatter(
        dot_back(d_kvq, w_in).astype(bf16), "head", scatter_dimension=0, tiled=True
    ).astype(jnp.float32)
    g_out_t = weight_grad(attn_rows, mixed_rows)
    g_attn = jnp.concatenate(
        [weight_grad(group_tokens, d_kvq), g_out_t[:, :128], g_out_t[:, 192:]], axis=1
    ).astype(bf16)
    s_attn = lax.psum_scatter(g_attn, "blk", scatter_dimension=0, tiled=True).astype(jnp.float32)
    g_norm = jnp.stack([d_gain_one, d_shift_one, d_gain_two, d_shift_two], axis=0)
    g_norm = g_norm.reshape(heads_n, blk_n, share).transpose(1, 0, 2).reshape(devs, share)
    s_norm = lax.psum_scatter(g_norm, ("blk", "head"), scatter_dimension=0, tiled=True)
    return (
        result.astype(bf16),
        input_grad,
        from_cols(s_attn[:, :576]),
        s_attn[:, 576:].T,
        s_ffn[:2],
        s_ffn[2].T,
        s_norm.reshape(share, 1),
    )


def solution(mesh):
    placed = (
        P(("blk", "head"), None),
        P("blk", "head"),
        P("head", "blk"),
        P(None, "blk", "head"),
        P("head", "blk"),
        P("blk", "head"),
        P(),
        P(),
        P(),
        P(("blk", "head"), None),
    )
    small = mesh.shape["blk"] == 8 and mesh.shape["head"] == 4
    return jax.shard_map(
        fast_shards if small else shards,
        mesh=mesh,
        in_specs=placed,
        out_specs=(
            P(("blk", "head"), None),
            P(("blk", "head"), None),
            P("blk", "head"),
            P("head", "blk"),
            P(None, "blk", "head"),
            P("head", "blk"),
            P("blk", "head"),
        ),
        check_vma=False,
    )
```

```python
import jax
import jax.numpy as jnp
from jax import lax
from jax.experimental import pallas as pl
from jax.experimental.pallas import tpu as pltpu
from jax.sharding import PartitionSpec as P

HEADS = 12
HEAD_DIM = 64


masked_score = -1e30


def layer_norm(residual, norm_gain, norm_shift):
    center = residual - jnp.mean(residual, axis=-1, keepdims=True)
    spread = jnp.mean(center * center, axis=-1, keepdims=True)
    return center * lax.rsqrt(spread + 1e-05) * norm_gain + norm_shift


def geglu(gate, upward):
    return jax.nn.gelu(gate, approximate=False) * upward


def dot_back(grad_rows, weight):
    return lax.dot_general(
        grad_rows, weight, (((1,), (1,)), ((), ())), preferred_element_type=jnp.float32
    )


def weight_grad(left, right):
    return lax.dot_general(
        left, right, (((0,), (0,)), ((), ())), preferred_element_type=jnp.float32
    )


def seq_of(positions, seq_ends):
    return jnp.sum((positions[:, None] >= seq_ends[None, :]).astype(jnp.int32), axis=1)


def prefix_sums(lengths):
    count = lengths.shape[0]
    upto = jnp.arange(count)[None, :] <= jnp.arange(count)[:, None]
    return jnp.sum(jnp.where(upto, lengths[None, :], 0), axis=1)


def biased_scores(queries, key_rows, q_pos, k_pos, q_seq, k_seq, slopes, qk_scale):
    scores = (
        jnp.einsum("qhd,khd->hqk", queries, key_rows, preferred_element_type=jnp.float32) * qk_scale
    )
    distance = jnp.abs(q_pos[:, None] - k_pos[None, :]).astype(jnp.float32)
    scores = scores - slopes[:, None, None] * distance[None]
    same_seq = (q_seq[:, None] == k_seq[None, :])[None]
    return (scores, same_seq)


def shards(
    tokens, w_qkv, w_out, w_gate_up, w_down, norm_params, alibi_slope, lengths, placement, out_grad
):
    heads_n = lax.axis_size("head")
    head_idx = lax.axis_index("head")
    blk_idx = lax.axis_index("blk")
    tok_rows = tokens.shape[0]
    per_dev = HEADS // heads_n
    group_rows = heads_n * tok_rows
    qk_scale = HEAD_DIM ** (-0.5)
    group_tokens, norm_cols = (
        lax.all_gather(tokens, "head", axis=0, tiled=True),
        lax.all_gather(norm_params, "head", axis=1, tiled=True),
    )
    f_qkv, f_out, f_gu, f_down, f_norm = (
        lax.all_gather(w_qkv, "blk", axis=0, tiled=True),
        lax.all_gather(w_out, "blk", axis=1, tiled=True),
        lax.all_gather(w_gate_up, "blk", axis=1, tiled=True),
        lax.all_gather(w_down, "blk", axis=1, tiled=True),
        lax.all_gather(norm_cols, "blk", axis=0, tiled=True),
    )
    grouped = jnp.dot(group_tokens, f_qkv, preferred_element_type=jnp.float32).astype(jnp.bfloat16)
    grouped = grouped.reshape(group_rows, per_dev, 3, HEAD_DIM)
    norms = f_norm.astype(jnp.float32)
    queries = grouped[:, :, 0]
    key_rows = grouped[:, :, 1]
    values = grouped[:, :, 2]
    seq_ends = prefix_sums(lengths)
    q_pos = lax.dynamic_slice_in_dim(placement, blk_idx * group_rows, group_rows)
    q_seq = seq_of(q_pos, seq_ends)
    slopes = lax.dynamic_slice_in_dim(alibi_slope, head_idx * per_dev, per_dev)

    def split_rows(shard_part):
        block_count = shard_part[0].shape[0] // group_rows
        pieces = tuple(
            (arr.reshape((block_count, group_rows) + arr.shape[1:]) for arr in shard_part)
        )
        starts = group_rows * jnp.arange(block_count, dtype=jnp.int32)
        return pieces + (starts,)

    start_state = (
        jnp.full((per_dev, group_rows), masked_score, jnp.float32),
        jnp.zeros((per_dev, group_rows), jnp.float32),
        jnp.zeros((group_rows, per_dev, HEAD_DIM), jnp.float32),
    )
    running = start_state

    def forward_per_block(state, block_in):
        k_blk, v_blk, k_first = block_in
        row_best, row_total, out_sum = state
        k_pos = lax.dynamic_slice_in_dim(placement, k_first, group_rows)
        scores, same_seq = biased_scores(
            queries, k_blk, q_pos, k_pos, q_seq, seq_of(k_pos, seq_ends), slopes, qk_scale
        )
        row_top = jnp.max(jnp.where(same_seq, scores, masked_score), axis=2)
        new_best = jnp.maximum(row_best, row_top)
        factor = jnp.exp(row_best - new_best)
        prob_tile = jnp.where(same_seq, jnp.exp(scores - new_best[:, :, None]), 0.0)
        row_total = row_total * factor + jnp.sum(prob_tile, axis=2)
        out_sum = out_sum * factor.T[:, :, None] + jnp.einsum(
            "hqk,khd->qhd",
            prob_tile.astype(jnp.bfloat16),
            v_blk,
            preferred_element_type=jnp.float32,
        )
        return ((new_best, row_total, out_sum), None)

    running, _ = lax.scan(
        forward_per_block,
        running,
        split_rows(
            (
                lax.all_gather(key_rows, "blk", axis=0, tiled=True),
                lax.all_gather(values, "blk", axis=0, tiled=True),
            )
        ),
    )
    row_best, row_total, out_sum = running
    attended = (out_sum / row_total.T[:, :, None]).astype(jnp.bfloat16)
    log_total = row_best + jnp.log(row_total)
    mixed = attended.reshape(group_rows, per_dev * HEAD_DIM)
    attn_out = lax.psum_scatter(
        jnp.dot(mixed, f_out, preferred_element_type=jnp.float32).astype(jnp.bfloat16),
        "head",
        scatter_dimension=0,
        tiled=True,
    ).astype(jnp.float32)
    resid_one = tokens.astype(jnp.float32) + attn_out
    hidden, norm_one_back = jax.vjp(layer_norm, resid_one, norms[:, 0], norms[:, 1])
    hidden_low = hidden.astype(jnp.bfloat16)
    ffn_rows = lax.all_gather(hidden_low, "head", axis=0, tiled=True)
    gate = jnp.dot(ffn_rows, f_gu[0], preferred_element_type=jnp.float32)
    upward = jnp.dot(ffn_rows, f_gu[1], preferred_element_type=jnp.float32)
    gated, geglu_back = jax.vjp(geglu, gate, upward)
    gated_low = gated.astype(jnp.bfloat16)
    branch_part = jnp.dot(gated_low, f_down, preferred_element_type=jnp.float32)
    branch = lax.psum_scatter(
        branch_part.astype(jnp.bfloat16), "head", scatter_dimension=0, tiled=True
    ).astype(jnp.float32)
    result, norm_two_back = jax.vjp(layer_norm, hidden + branch, norms[:, 2], norms[:, 3])
    d_two, d_gain_two, d_shift_two = norm_two_back(out_grad.astype(jnp.float32))
    d_branch = d_two.astype(jnp.bfloat16)
    branch_rows = lax.all_gather(d_branch, "head", axis=0, tiled=True)
    g_down = weight_grad(gated_low, branch_rows)
    d_gate, d_up = geglu_back(dot_back(branch_rows, f_down))
    d_gate_low = d_gate.astype(jnp.bfloat16)
    d_up_low = d_up.astype(jnp.bfloat16)
    g_gate_up = jnp.stack([weight_grad(ffn_rows, d_gate_low), weight_grad(ffn_rows, d_up_low)])
    hidden_part = dot_back(d_gate_low, f_gu[0]) + dot_back(d_up_low, f_gu[1])
    d_hidden = d_two + lax.psum_scatter(
        hidden_part.astype(jnp.bfloat16), "head", scatter_dimension=0, tiled=True
    ).astype(jnp.float32)
    d_one, d_gain_one, d_shift_one = norm_one_back(d_hidden)
    d_attn = d_one.astype(jnp.bfloat16)
    attn_rows = lax.all_gather(d_attn, "head", axis=0, tiled=True)
    g_out = weight_grad(mixed, attn_rows)
    d_heads = dot_back(attn_rows, f_out).astype(jnp.bfloat16).reshape(group_rows, per_dev, HEAD_DIM)
    delta = jnp.sum(d_heads.astype(jnp.float32) * attended.astype(jnp.float32), axis=2).T
    zero_grad = jnp.zeros((group_rows, per_dev, HEAD_DIM), jnp.float32)
    grad_q = zero_grad

    def query_per_block(running, block_in):
        k_blk, v_blk, k_first = block_in
        k_pos = lax.dynamic_slice_in_dim(placement, k_first, group_rows)
        scores, same_seq = biased_scores(
            queries, k_blk, q_pos, k_pos, q_seq, seq_of(k_pos, seq_ends), slopes, qk_scale
        )
        prob_tile = jnp.where(same_seq, jnp.exp(scores - log_total[:, :, None]), 0.0)
        d_prob = jnp.einsum("qhd,khd->hqk", d_heads, v_blk, preferred_element_type=jnp.float32)
        d_score = (prob_tile * (d_prob - delta[:, :, None])).astype(jnp.bfloat16)
        running = (
            running
            + jnp.einsum("hqk,khd->qhd", d_score, k_blk, preferred_element_type=jnp.float32)
            * qk_scale
        )
        return (running, None)

    grad_q, _ = lax.scan(
        query_per_block,
        grad_q,
        split_rows(
            (
                lax.all_gather(key_rows, "blk", axis=0, tiled=True),
                lax.all_gather(values, "blk", axis=0, tiled=True),
            )
        ),
    )
    stats_lse, stats_delta = (
        lax.all_gather(log_total, "blk", axis=1, tiled=True),
        lax.all_gather(delta, "blk", axis=1, tiled=True),
    )
    running = (zero_grad, zero_grad)

    def key_per_block(state, block_in):
        q_blk, do_blk, q_first = block_in
        grad_k, grad_v = state
        other_pos = lax.dynamic_slice_in_dim(placement, q_first, group_rows)
        lse_blk = lax.dynamic_slice_in_dim(stats_lse, q_first, group_rows, 1)
        delta_blk = lax.dynamic_slice_in_dim(stats_delta, q_first, group_rows, 1)
        scores, same_seq = biased_scores(
            q_blk, key_rows, other_pos, q_pos, seq_of(other_pos, seq_ends), q_seq, slopes, qk_scale
        )
        prob_tile = jnp.where(same_seq, jnp.exp(scores - lse_blk[:, :, None]), 0.0)
        grad_v = grad_v + jnp.einsum(
            "hqk,qhd->khd",
            prob_tile.astype(jnp.bfloat16),
            do_blk,
            preferred_element_type=jnp.float32,
        )
        d_prob = jnp.einsum("qhd,khd->hqk", do_blk, values, preferred_element_type=jnp.float32)
        d_score = (prob_tile * (d_prob - delta_blk[:, :, None])).astype(jnp.bfloat16)
        grad_k = (
            grad_k
            + jnp.einsum("hqk,qhd->khd", d_score, q_blk, preferred_element_type=jnp.float32)
            * qk_scale
        )
        return ((grad_k, grad_v), None)

    running, _ = lax.scan(
        key_per_block,
        running,
        split_rows(
            (
                lax.all_gather(queries, "blk", axis=0, tiled=True),
                lax.all_gather(d_heads, "blk", axis=0, tiled=True),
            )
        ),
    )
    grad_k, grad_v = running
    d_grouped = jnp.stack([grad_q, grad_k, grad_v], axis=2).astype(jnp.bfloat16)
    g_norm = jnp.stack([d_gain_one, d_shift_one, d_gain_two, d_shift_two], axis=1)
    d_qkv = d_grouped.reshape(group_rows, per_dev * 3 * HEAD_DIM)
    g_qkv = weight_grad(group_tokens, d_qkv)
    input_sum, norm_share = (
        lax.psum_scatter(
            dot_back(d_qkv, f_qkv).astype(jnp.bfloat16), "head", scatter_dimension=0, tiled=True
        ).astype(jnp.float32),
        lax.psum_scatter(
            g_norm.astype(jnp.bfloat16), "head", scatter_dimension=1, tiled=True
        ).astype(jnp.float32),
    )
    input_grad = d_one + input_sum
    s_qkv, s_out, s_gu, s_down, s_norm = (
        lax.psum_scatter(g_qkv, "blk", scatter_dimension=0, tiled=True),
        lax.psum_scatter(g_out, "blk", scatter_dimension=1, tiled=True),
        lax.psum_scatter(g_gate_up, "blk", scatter_dimension=1, tiled=True),
        lax.psum_scatter(g_down, "blk", scatter_dimension=1, tiled=True),
        lax.psum_scatter(norm_share, "blk", scatter_dimension=0, tiled=True),
    )
    return (result.astype(jnp.bfloat16), input_grad, s_qkv, s_out, s_gu, s_down, s_norm)


Q_SLOTS = 32
K_SLOTS = 16
SEQ_STEP = 65536.0
FAR = 32768.0
LANE_OF = (0, 64, 192)


def by_head(rows, lanes):
    lane = lax.broadcasted_iota(jnp.int32, rows.shape, 1)
    parts = [jnp.where((lane >= first) & (lane < first + HEAD_DIM), rows, 0.0) for first in lanes]
    return jnp.concatenate(parts, axis=0).astype(jnp.bfloat16)


def key_tiles(kv_ref, j):
    rows = kv_ref.shape[0] * K_SLOTS
    blk = kv_ref[:, pl.ds(pl.multiple_of(j * K_SLOTS, K_SLOTS), K_SLOTS), :]
    return blk.reshape(rows, blk.shape[2])


def attend(span_ref, slope_ref, q_ref, kv_ref, kcode_ref, qcode_ref, out_ref, lse_ref, vt_ref):
    devs, slots, _ = kv_ref.shape
    rows = devs * K_SLOTS
    q_rows = q_ref.shape[0] * Q_SLOTS

    def turn(j, _):
        kv = key_tiles(kv_ref, j)[:, 128:384]
        vt_ref[j] = kv.astype(jnp.float32).T.astype(jnp.bfloat16)
        return 0

    lax.fori_loop(0, slots // K_SLOTS, turn, 0)

    def chunk(i, _):
        first = pl.multiple_of(i * Q_SLOTS, Q_SLOTS)
        q = q_ref[:, pl.ds(first, Q_SLOTS), :].reshape(q_rows, 256).astype(jnp.float32)
        qbd = by_head(q, (0, 64, 128))
        qcode = qcode_ref[i]

        def block(j, state):
            kv = key_tiles(kv_ref, j)
            keys = jnp.concatenate([kv[:, 0:128], kv[:, 256:384]], axis=1)
            s_all = lax.dot_general(keys, qbd, (((1,), (1,)), ((), ())), preferred_element_type=jnp.float32)
            dist = jnp.abs(kcode_ref[pl.ds(pl.multiple_of(j * rows, rows), rows), :] - qcode)
            keep = dist < FAR
            fresh = []
            for h in range(3):
                best, total, acc = state[h]
                s = jnp.where(keep, s_all[:, 128 * h : 128 * h + 128] - slope_ref[h] * dist, masked_score)
                top = jnp.maximum(best, jnp.max(s, axis=0, keepdims=True))
                factor = jnp.exp(best - top)
                p = jnp.exp(s - top)
                total = total * factor + jnp.sum(p, axis=0, keepdims=True)
                vt = vt_ref[j, LANE_OF[h] : LANE_OF[h] + 64, :]
                acc = acc * factor + jnp.dot(vt, p.astype(jnp.bfloat16), preferred_element_type=jnp.float32)
                fresh.append((top, total, acc))
            return tuple(fresh)

        start = tuple(
            (
                jnp.full((1, q_rows), masked_score, jnp.float32),
                jnp.zeros((1, q_rows), jnp.float32),
                jnp.zeros((64, q_rows), jnp.float32),
            )
            for _ in range(3)
        )
        done = lax.fori_loop(span_ref[i, 0], span_ref[i, 1], block, start)
        outs = [acc / total for _, total, acc in done]
        full = jnp.concatenate([outs[0], outs[1], jnp.zeros((64, q_rows), jnp.float32), outs[2]], axis=0)
        out_ref[:, pl.ds(first, Q_SLOTS), :] = full.T.astype(jnp.bfloat16).reshape(-1, Q_SLOTS, 256)
        for h in range(3):
            lse_ref[i, h : h + 1, :] = done[h][0] + jnp.log(done[h][1])
        return 0

    lax.fori_loop(0, slots // Q_SLOTS, chunk, 0)


def attend_back(span_ref, slope_ref, q_ref, kv_ref, kcode_ref, qcode_ref, out_ref, do_ref, lse_ref,
                dq_ref, dkv_ref, kt_ref, sum_ref):
    devs, slots, _ = kv_ref.shape
    rows = devs * K_SLOTS
    q_rows = q_ref.shape[0] * Q_SLOTS
    scale = HEAD_DIM ** (-0.5)

    def turn(j, _):
        kv = key_tiles(kv_ref, j)
        keys = jnp.concatenate([kv[:, 0:128], kv[:, 256:384]], axis=1)
        kt_ref[j] = keys.astype(jnp.float32).T.astype(jnp.bfloat16)
        sum_ref[j] = jnp.zeros((rows, 384), jnp.float32)
        return 0

    lax.fori_loop(0, slots // K_SLOTS, turn, 0)

    def chunk(i, _):
        first = pl.multiple_of(i * Q_SLOTS, Q_SLOTS)
        q = q_ref[:, pl.ds(first, Q_SLOTS), :].reshape(q_rows, 256).astype(jnp.float32)
        qbd = by_head(q, (0, 64, 128))
        do = do_ref[:, pl.ds(first, Q_SLOTS), :].reshape(q_rows, 256).astype(jnp.float32)
        out = out_ref[:, pl.ds(first, Q_SLOTS), :].reshape(q_rows, 256).astype(jnp.float32)
        dobd = by_head(do, LANE_OF)
        prod = (do * out).T
        delta = [jnp.sum(prod[f : f + 64, :], axis=0, keepdims=True) for f in LANE_OF]
        qcode = qcode_ref[i]

        def block(j, state):
            kv = key_tiles(kv_ref, j)
            keys = jnp.concatenate([kv[:, 0:128], kv[:, 256:384]], axis=1)
            vals = kv[:, 128:384]
            s_all = lax.dot_general(keys, qbd, (((1,), (1,)), ((), ())), preferred_element_type=jnp.float32)
            dp_all = lax.dot_general(vals, dobd, (((1,), (1,)), ((), ())), preferred_element_type=jnp.float32)
            dist = jnp.abs(kcode_ref[pl.ds(pl.multiple_of(j * rows, rows), rows), :] - qcode)
            keep = dist < FAR
            ps, dss, fresh = [], [], []
            for h in range(3):
                s = s_all[:, 128 * h : 128 * h + 128] - slope_ref[h] * dist - lse_ref[i, h : h + 1, :]
                p = jnp.exp(jnp.where(keep, s, masked_score))
                ds = (p * (dp_all[:, 128 * h : 128 * h + 128] - delta[h])).astype(jnp.bfloat16)
                ps.append(p.astype(jnp.bfloat16))
                dss.append(ds)
                kt = kt_ref[j, 64 * h : 64 * h + 64, :]
                fresh.append(state[h] + jnp.dot(kt, ds, preferred_element_type=jnp.float32))
            dv = jnp.dot(jnp.concatenate(ps, axis=1), dobd, preferred_element_type=jnp.float32)
            dk = jnp.dot(jnp.concatenate(dss, axis=1), qbd, preferred_element_type=jnp.float32)
            sum_ref[j, :, 0:128] += dk[:, 0:128]
            sum_ref[j, :, 128:256] += dv[:, 0:128]
            sum_ref[j, :, 256:384] += dk[:, 128:256] + dv[:, 128:256]
            return tuple(fresh)

        start = tuple(jnp.zeros((64, q_rows), jnp.float32) for _ in range(3))
        done = lax.fori_loop(span_ref[i, 0], span_ref[i, 1], block, start)
        full = jnp.concatenate(done + (jnp.zeros((64, q_rows), jnp.float32),), axis=0) * scale
        dq_ref[:, pl.ds(first, Q_SLOTS), :] = full.T.astype(jnp.bfloat16).reshape(-1, Q_SLOTS, 256)
        return 0

    lax.fori_loop(0, slots // Q_SLOTS, chunk, 0)

    def leave(j, _):
        dkv_ref[:, pl.ds(pl.multiple_of(j * K_SLOTS, K_SLOTS), K_SLOTS), :] = (
            sum_ref[j].astype(jnp.bfloat16).reshape(devs, K_SLOTS, 384)
        )
        return 0

    lax.fori_loop(0, slots // K_SLOTS, leave, 0)


VM = pl.BlockSpec(memory_space=pltpu.VMEM)
SM = pl.BlockSpec(memory_space=pltpu.SMEM)


def run_attend(span, slopes, q, kv, kcode, qcode):
    heads_n, slots, _ = q.shape
    devs = kv.shape[0]
    return pl.pallas_call(
        attend,
        out_shape=(
            jax.ShapeDtypeStruct((heads_n, slots, 256), jnp.bfloat16),
            jax.ShapeDtypeStruct((slots // Q_SLOTS, 8, heads_n * Q_SLOTS), jnp.float32),
        ),
        in_specs=[SM, SM, VM, VM, VM, VM],
        out_specs=(VM, VM),
        scratch_shapes=[pltpu.VMEM((slots // K_SLOTS, 256, devs * K_SLOTS), jnp.bfloat16)],
        compiler_params=pltpu.CompilerParams(vmem_limit_bytes=40 << 20),
        name="attend",
    )(span, slopes, q, kv, kcode, qcode)


def run_attend_back(span, slopes, q, kv, kcode, qcode, out, do, lse):
    heads_n, slots, _ = q.shape
    devs = kv.shape[0]
    return pl.pallas_call(
        attend_back,
        out_shape=(
            jax.ShapeDtypeStruct((heads_n, slots, 256), jnp.bfloat16),
            jax.ShapeDtypeStruct((devs, slots, 384), jnp.bfloat16),
        ),
        in_specs=[SM, SM, VM, VM, VM, VM, VM, VM, VM],
        out_specs=(VM, VM),
        scratch_shapes=[
            pltpu.VMEM((slots // K_SLOTS, 256, devs * K_SLOTS), jnp.bfloat16),
            pltpu.VMEM((slots // K_SLOTS, devs * K_SLOTS, 384), jnp.float32),
        ],
        compiler_params=pltpu.CompilerParams(vmem_limit_bytes=48 << 20),
        name="attend_back",
    )(span, slopes, q, kv, kcode, qcode, out, do, lse)


def key_spans(seq_starts, seq_ends, chunk_positions, block_positions, chunks):
    first = chunk_positions * jnp.arange(chunks, dtype=jnp.int32)
    last = first + chunk_positions - 1
    lo_seq = jnp.sum((first[:, None] >= seq_ends[None, :]).astype(jnp.int32), axis=1)
    hi_seq = jnp.sum((last[:, None] >= seq_ends[None, :]).astype(jnp.int32), axis=1)
    seqs = jnp.arange(seq_ends.shape[0], dtype=jnp.int32)[None, :]
    lo = jnp.sum(jnp.where(seqs == lo_seq[:, None], seq_starts[None, :], 0), axis=1)
    hi = jnp.sum(jnp.where(seqs == hi_seq[:, None], seq_ends[None, :], 0), axis=1)
    return jnp.stack([lo // block_positions, (hi + block_positions - 1) // block_positions], axis=1)


MESH = pl.DeviceIdType.MESH


def dot_tn(left, right):
    return lax.dot_general(left, right, (((0,), (0,)), ((), ())), preferred_element_type=jnp.float32)


def dot_nt(left, right):
    return lax.dot_general(left, right, (((1,), (1,)), ((), ())), preferred_element_type=jnp.float32)


def greet(peers):
    barrier = pltpu.get_barrier_semaphore()
    for peer in peers:
        pl.semaphore_signal(barrier, inc=1, device_id=peer, device_id_type=MESH)
    pl.semaphore_wait(barrier, len(peers))


def remote(src, dst, sems, i, peer):
    return pltpu.make_async_remote_copy(
        src_ref=src, dst_ref=dst, send_sem=sems.at[0, i], recv_sem=sems.at[1, i],
        device_id=peer, device_id_type=MESH,
    )


def finish(
    dkv_ref, dq_ref, tok_ref, w_ref, datt_ref, mixed_ref, done_ref, gffn_ref, gn_ref,
    dx_ref, sattn_ref, sffn_ref, snorm_ref,
    kv_sib, kv_sum, kv_in, ffn_sib, ffn_sum, ffn_in, gat, gat_sib, gat_sum, gat_in,
    part, part_in, att, dkvq, nz_in, nrow, np_in, sems,
):
    b = lax.axis_index("blk")
    z = lax.axis_index("head")
    chip, core = b // 2, b % 2
    sib = (chip * 2 + 1 - core, z)
    flat = [((chip ^ r) * 2 + core, z) for r in (1, 2, 3)]
    line = [(b, z ^ r) for r in (1, 2, 3)]
    greet([sib] + flat + line)
    f32, bf16 = jnp.float32, jnp.bfloat16
    started = []

    def go(src, dst, i, peer):
        copy = remote(src, dst, sems, i, peer)
        copy.start()
        started.append(copy)
        return copy

    kv_c = [go(dkv_ref.at[(chip ^ r) * 2 + 1 - core], kv_sib.at[r], r, sib) for r in (3, 1, 2, 0)]
    att_c = [go(datt_ref, att.at[r], 4 + r, line[r - 1]) for r in (3, 2, 1)]
    nz_c = [go(gn_ref.at[pl.ds((z ^ r) * 8, 8)], nz_in.at[r - 1], 8 + r, line[r - 1]) for r in (1, 2, 3)]
    kv_out = []
    for k, r in enumerate((3, 1, 2, 0)):
        kv_c[k].wait_recv()
        both = dkv_ref[(chip ^ r) * 2 + core].astype(f32) + kv_sib[r].astype(f32)
        kv_sum[r] = both.astype(bf16)
        if r:
            kv_out.append(go(kv_sum.at[r], kv_in.at[r - 1], 12 + r, flat[r - 1]))
    ffn_c = [
        go(gffn_ref.at[:, pl.ds(pl.multiple_of(((chip ^ r) * 2 + 1 - core) * 96, 96), 96)], ffn_sib.at[r], 16 + r, sib)
        for r in (3, 1, 2, 0)
    ]
    ffn_out = []
    for k, r in enumerate((3, 1, 2, 0)):
        ffn_c[k].wait_recv()
        mine = gffn_ref[:, pl.ds(pl.multiple_of(((chip ^ r) * 2 + core) * 96, 96), 96), :].astype(f32)
        ffn_sum[r] = (mine + ffn_sib[r].astype(f32)).astype(bf16)
        if r:
            ffn_out.append(go(ffn_sum.at[r], ffn_in.at[r - 1], 20 + r, flat[r - 1]))
    for c in nz_c:
        c.wait_recv()
    nrow[0] = gn_ref[pl.ds(z * 8, 8)] + nz_in[0] + nz_in[1] + nz_in[2]
    np_c = [go(nrow.at[0], np_in.at[r], 24 + r, flat[r - 1]) for r in (1, 2, 3)]
    for c in kv_out:
        c.wait_recv()
    dkvq[:, 0:384] = (
        kv_sum[0].astype(f32) + kv_in[0].astype(f32) + kv_in[1].astype(f32) + kv_in[2].astype(f32)
    ).astype(bf16)
    dkvq[:, 384:640] = dq_ref[...]
    dx_c = []
    for r in (3, 2, 1, 0):
        rows = pl.ds(pl.multiple_of((z ^ r) * 128, 128), 128)
        got = dkvq[rows, :]
        term = dot_nt(got[:, 0:512], w_ref[:, 0:512]) + dot_nt(got[:, 512:640], w_ref[:, 640:768])
        if r:
            part[r - 1] = term.astype(bf16)
            dx_c.append(go(part.at[r - 1], part_in.at[r - 1], 28 + r, line[r - 1]))
        else:
            dx_ref[...] = done_ref[...] + term
    for c in att_c:
        c.wait_recv()
    att[0] = datt_ref[...]
    gat[:, 0:512] = dot_tn(tok_ref[...], dkvq[:, 0:512]).astype(bf16)
    last = dot_tn(tok_ref[...], dkvq[:, 512:640])
    outs = jnp.zeros((768, 256), f32)
    for r in range(4):
        outs = outs + dot_tn(att[r], mixed_ref[pl.ds(pl.multiple_of((z ^ r) * 128, 128), 128), :])
    gat[:, 512:640] = outs[:, 0:128].astype(bf16)
    gat[:, 640:768] = (outs[:, 128:256] + last).astype(bf16)
    gat_c = [
        go(gat.at[pl.ds(pl.multiple_of(((chip ^ r) * 2 + 1 - core) * 96, 96), 96)], gat_sib.at[r], 32 + r, sib)
        for r in (3, 1, 2, 0)
    ]
    gat_out = []
    for k, r in enumerate((3, 1, 2, 0)):
        gat_c[k].wait_recv()
        mine = gat[pl.ds(pl.multiple_of(((chip ^ r) * 2 + core) * 96, 96), 96), :].astype(f32)
        gat_sum[r] = (mine + gat_sib[r].astype(f32)).astype(bf16)
        if r:
            gat_out.append(go(gat_sum.at[r], gat_in.at[r - 1], 36 + r, flat[r - 1]))
    for c in np_c:
        c.wait_recv()
    nrow[1] = nrow[0] + np_in[1] + np_in[2] + np_in[3]
    half = go(nrow.at[1], np_in.at[0], 24, sib)
    for c in ffn_out:
        c.wait_recv()
    for t in range(3):
        sffn_ref[t] = (
            ffn_sum[0, t].astype(f32) + ffn_in[0, t].astype(f32) + ffn_in[1, t].astype(f32) + ffn_in[2, t].astype(f32)
        )
    for c in dx_c:
        c.wait_recv()
    dx_ref[...] += part_in[0].astype(f32) + part_in[1].astype(f32) + part_in[2].astype(f32)
    half.wait_recv()
    snorm_ref[...] = nrow[1] + np_in[0]
    for c in gat_out:
        c.wait_recv()
    sattn_ref[...] = (
        gat_sum[0].astype(f32) + gat_in[0].astype(f32) + gat_in[1].astype(f32) + gat_in[2].astype(f32)
    )
    for c in started:
        c.wait_send()


def run_finish(dkv, dq, toks, w, datt, mixed, done, gffn, gn):
    f32, bf16 = jnp.float32, jnp.bfloat16
    V = pltpu.VMEM
    return pl.pallas_call(
        finish,
        out_shape=(
            jax.ShapeDtypeStruct((128, 768), f32),
            jax.ShapeDtypeStruct((96, 768), f32),
            jax.ShapeDtypeStruct((3, 96, 768), f32),
            jax.ShapeDtypeStruct((8, 768), f32),
        ),
        in_specs=[VM] * 9,
        out_specs=(VM,) * 4,
        scratch_shapes=[
            V((4, 512, 384), bf16), V((4, 512, 384), bf16), V((3, 512, 384), bf16),
            V((4, 3, 96, 768), bf16), V((4, 3, 96, 768), bf16), V((3, 3, 96, 768), bf16),
            V((768, 768), bf16), V((4, 96, 768), bf16), V((4, 96, 768), bf16), V((3, 96, 768), bf16),
            V((3, 128, 768), bf16), V((3, 128, 768), bf16), V((4, 128, 768), bf16), V((512, 640), bf16),
            V((3, 8, 768), f32), V((2, 8, 768), f32), V((4, 8, 768), f32),
            pltpu.SemaphoreType.DMA((2, 40)),
        ],
        compiler_params=pltpu.CompilerParams(
            collective_id=5, has_side_effects=True, vmem_limit_bytes=56 << 20
        ),
        name="finish",
    )(dkv, dq, toks, w, datt, mixed, done, gffn, gn)


PACK = (1, 4, 2, 5, 7, 8, 0, 3)


def packed(w_qkv, w_out):
    piece = [w_qkv[:, 64 * i : 64 * i + 64] for i in range(9)]
    out = w_out.T
    return jnp.concatenate([piece[i] for i in PACK] + [out[:, :128], piece[6], out[:, 128:]], axis=1)


def unpacked(g):
    piece = [g[:, 64 * i : 64 * i + 64] for i in range(12)]
    qkv = jnp.concatenate([piece[i] for i in (6, 0, 2, 7, 1, 3, 10, 4, 5)], axis=1)
    return qkv, jnp.concatenate([piece[8], piece[9], piece[11]], axis=1).T


def fast_shards(
    tokens, w_qkv, w_out, w_gate_up, w_down, norm_params, alibi_slope, lengths, placement, out_grad
):
    heads_n = lax.axis_size("head")
    blk_n = lax.axis_size("blk")
    head_idx = lax.axis_index("head")
    blk_idx = lax.axis_index("blk")
    tok_rows, width = tokens.shape
    per_dev = HEADS // heads_n
    group_rows = heads_n * tok_rows
    devs = heads_n * blk_n
    share = w_qkv.shape[0]
    bf16 = jnp.bfloat16

    attn_w = lax.all_gather(packed(w_qkv, w_out), "blk", axis=0, tiled=True)
    ffn_w = lax.all_gather(
        jnp.concatenate([w_gate_up, w_down.T[None]], axis=0), "blk", axis=1, tiled=True
    )
    norms = lax.all_gather(norm_params.reshape(share), ("blk", "head"), axis=0, tiled=False)
    norms = norms.reshape(blk_n, heads_n, share).transpose(1, 0, 2).reshape(heads_n, width).astype(jnp.float32)
    group_tokens = lax.all_gather(tokens, "head", axis=0, tiled=True)
    out_pad = attn_w[:, 512:]
    w_gate, w_up, down_t = ffn_w[0], ffn_w[1], ffn_w[2]

    kvq = jnp.dot(group_tokens, attn_w, preferred_element_type=jnp.float32).astype(bf16)
    kv = lax.all_gather(kvq[:, :384], "blk", axis=0, tiled=True).reshape(devs, tok_rows, 384)
    q = jnp.concatenate([kvq[:, 384:512], kvq[:, 640:]], axis=1) * bf16(HEAD_DIM ** (-0.5))
    q = q.reshape(heads_n, tok_rows, 256)

    seq_ends = prefix_sums(lengths)
    code = placement.astype(jnp.float32) + SEQ_STEP * seq_of(placement, seq_ends).astype(jnp.float32)
    k_blocks = tok_rows // K_SLOTS
    q_chunks = tok_rows // Q_SLOTS
    kcode = code.reshape(devs, k_blocks, K_SLOTS).transpose(1, 0, 2).reshape(-1, 1)
    kcode = jnp.broadcast_to(kcode, (kcode.shape[0], 128))
    qcode = lax.dynamic_slice_in_dim(code, blk_idx * group_rows, group_rows)
    qcode = qcode.reshape(heads_n, q_chunks, Q_SLOTS).transpose(1, 0, 2).reshape(q_chunks, 1, heads_n * Q_SLOTS)
    slopes = lax.dynamic_slice_in_dim(alibi_slope, head_idx * per_dev, per_dev)
    span = key_spans(seq_ends - lengths, seq_ends, Q_SLOTS * devs, K_SLOTS * devs, q_chunks)

    mixed, lse = run_attend(span, slopes, q, kv, kcode, qcode)
    mixed_rows = mixed.reshape(group_rows, 256)
    attn_out = lax.psum_scatter(
        dot_back(mixed_rows, out_pad).astype(bf16),
        "head", scatter_dimension=0, tiled=True,
    ).astype(jnp.float32)
    resid_one = tokens.astype(jnp.float32) + attn_out
    hidden, norm_one_back = jax.vjp(layer_norm, resid_one, norms[0], norms[1])
    ffn_rows = lax.all_gather(hidden.astype(bf16), "head", axis=0, tiled=True)
    gate = jnp.dot(ffn_rows, w_gate, preferred_element_type=jnp.float32)
    upward = jnp.dot(ffn_rows, w_up, preferred_element_type=jnp.float32)
    gated, geglu_back = jax.vjp(geglu, gate, upward)
    gated_low = gated.astype(bf16)
    branch = lax.psum_scatter(
        dot_back(gated_low, down_t).astype(bf16), "head", scatter_dimension=0, tiled=True
    ).astype(jnp.float32)
    result, norm_two_back = jax.vjp(layer_norm, hidden + branch, norms[2], norms[3])
    d_two, d_gain_two, d_shift_two = norm_two_back(out_grad.astype(jnp.float32))
    branch_rows = lax.all_gather(d_two.astype(bf16), "head", axis=0, tiled=True)
    d_gate, d_up = geglu_back(jnp.dot(branch_rows, down_t, preferred_element_type=jnp.float32))
    d_gate_low = d_gate.astype(bf16)
    d_up_low = d_up.astype(bf16)
    hidden_part = dot_back(d_gate_low, w_gate) + dot_back(d_up_low, w_up)
    d_hidden = d_two + lax.psum_scatter(
        hidden_part.astype(bf16), "head", scatter_dimension=0, tiled=True
    ).astype(jnp.float32)
    g_ffn = jnp.stack(
        [weight_grad(ffn_rows, d_gate_low), weight_grad(ffn_rows, d_up_low), weight_grad(branch_rows, gated_low)]
    ).astype(bf16)
    d_one, d_gain_one, d_shift_one = norm_one_back(d_hidden)
    attn_rows = lax.all_gather(d_one.astype(bf16), "head", axis=0, tiled=True)
    d_heads = jnp.dot(attn_rows, out_pad, preferred_element_type=jnp.float32).astype(bf16)
    d_q, dkv = run_attend_back(
        span, slopes, q, kv, kcode, qcode, mixed, d_heads.reshape(heads_n, tok_rows, 256), lse
    )
    g_norm = jnp.stack([d_gain_one, d_shift_one, d_gain_two, d_shift_two], axis=0)
    g_norm = jnp.pad(g_norm[:, None, :], ((0, 0), (0, 7), (0, 0))).reshape(8 * heads_n, width)
    input_grad, s_attn, s_ffn, s_norm = run_finish(
        dkv.reshape(blk_n, group_rows, 384), d_q.reshape(group_rows, 256), group_tokens, attn_w,
        d_one.astype(bf16), mixed_rows, d_one, g_ffn, g_norm,
    )
    s_qkv, s_out = unpacked(s_attn)
    return (
        result.astype(bf16),
        input_grad,
        s_qkv,
        s_out,
        s_ffn[:2],
        s_ffn[2].T,
        lax.dynamic_slice(s_norm, (0, blk_idx * share), (1, share)).reshape(share, 1),
    )


def solution(mesh):
    placed = (
        P(("blk", "head"), None),
        P("blk", "head"),
        P("head", "blk"),
        P(None, "blk", "head"),
        P("head", "blk"),
        P("blk", "head"),
        P(),
        P(),
        P(),
        P(("blk", "head"), None),
    )
    small = mesh.shape["blk"] == 8 and mesh.shape["head"] == 4
    return jax.shard_map(
        fast_shards if small else shards,
        mesh=mesh,
        in_specs=placed,
        out_specs=(
            P(("blk", "head"), None),
            P(("blk", "head"), None),
            P("blk", "head"),
            P("head", "blk"),
            P(None, "blk", "head"),
            P("head", "blk"),
            P("blk", "head"),
        ),
        check_vma=False,
    )
```

```python
import jax
import jax.numpy as jnp
from jax import lax
from jax.experimental import pallas as pl
from jax.experimental.pallas import tpu as pltpu
from jax.sharding import PartitionSpec as P

HEADS = 12
HEAD_DIM = 64


masked_score = -1e30


def layer_norm(residual, norm_gain, norm_shift):
    center = residual - jnp.mean(residual, axis=-1, keepdims=True)
    spread = jnp.mean(center * center, axis=-1, keepdims=True)
    return center * lax.rsqrt(spread + 1e-05) * norm_gain + norm_shift


def geglu(gate, upward):
    return jax.nn.gelu(gate, approximate=False) * upward


def dot_back(grad_rows, weight):
    return lax.dot_general(
        grad_rows, weight, (((1,), (1,)), ((), ())), preferred_element_type=jnp.float32
    )


def weight_grad(left, right):
    return lax.dot_general(
        left, right, (((0,), (0,)), ((), ())), preferred_element_type=jnp.float32
    )


def seq_of(positions, seq_ends):
    return jnp.sum((positions[:, None] >= seq_ends[None, :]).astype(jnp.int32), axis=1)


def prefix_sums(lengths):
    count = lengths.shape[0]
    upto = jnp.arange(count)[None, :] <= jnp.arange(count)[:, None]
    return jnp.sum(jnp.where(upto, lengths[None, :], 0), axis=1)


def biased_scores(queries, key_rows, q_pos, k_pos, q_seq, k_seq, slopes, qk_scale):
    scores = (
        jnp.einsum("qhd,khd->hqk", queries, key_rows, preferred_element_type=jnp.float32) * qk_scale
    )
    distance = jnp.abs(q_pos[:, None] - k_pos[None, :]).astype(jnp.float32)
    scores = scores - slopes[:, None, None] * distance[None]
    same_seq = (q_seq[:, None] == k_seq[None, :])[None]
    return (scores, same_seq)


def shards(
    tokens, w_qkv, w_out, w_gate_up, w_down, norm_params, alibi_slope, lengths, placement, out_grad
):
    heads_n = lax.axis_size("head")
    head_idx = lax.axis_index("head")
    blk_idx = lax.axis_index("blk")
    tok_rows = tokens.shape[0]
    per_dev = HEADS // heads_n
    group_rows = heads_n * tok_rows
    qk_scale = HEAD_DIM ** (-0.5)
    group_tokens, norm_cols = (
        lax.all_gather(tokens, "head", axis=0, tiled=True),
        lax.all_gather(norm_params, "head", axis=1, tiled=True),
    )
    f_qkv, f_out, f_gu, f_down, f_norm = (
        lax.all_gather(w_qkv, "blk", axis=0, tiled=True),
        lax.all_gather(w_out, "blk", axis=1, tiled=True),
        lax.all_gather(w_gate_up, "blk", axis=1, tiled=True),
        lax.all_gather(w_down, "blk", axis=1, tiled=True),
        lax.all_gather(norm_cols, "blk", axis=0, tiled=True),
    )
    grouped = jnp.dot(group_tokens, f_qkv, preferred_element_type=jnp.float32).astype(jnp.bfloat16)
    grouped = grouped.reshape(group_rows, per_dev, 3, HEAD_DIM)
    norms = f_norm.astype(jnp.float32)
    queries = grouped[:, :, 0]
    key_rows = grouped[:, :, 1]
    values = grouped[:, :, 2]
    seq_ends = prefix_sums(lengths)
    q_pos = lax.dynamic_slice_in_dim(placement, blk_idx * group_rows, group_rows)
    q_seq = seq_of(q_pos, seq_ends)
    slopes = lax.dynamic_slice_in_dim(alibi_slope, head_idx * per_dev, per_dev)

    def split_rows(shard_part):
        block_count = shard_part[0].shape[0] // group_rows
        pieces = tuple(
            (arr.reshape((block_count, group_rows) + arr.shape[1:]) for arr in shard_part)
        )
        starts = group_rows * jnp.arange(block_count, dtype=jnp.int32)
        return pieces + (starts,)

    start_state = (
        jnp.full((per_dev, group_rows), masked_score, jnp.float32),
        jnp.zeros((per_dev, group_rows), jnp.float32),
        jnp.zeros((group_rows, per_dev, HEAD_DIM), jnp.float32),
    )
    running = start_state

    def forward_per_block(state, block_in):
        k_blk, v_blk, k_first = block_in
        row_best, row_total, out_sum = state
        k_pos = lax.dynamic_slice_in_dim(placement, k_first, group_rows)
        scores, same_seq = biased_scores(
            queries, k_blk, q_pos, k_pos, q_seq, seq_of(k_pos, seq_ends), slopes, qk_scale
        )
        row_top = jnp.max(jnp.where(same_seq, scores, masked_score), axis=2)
        new_best = jnp.maximum(row_best, row_top)
        factor = jnp.exp(row_best - new_best)
        prob_tile = jnp.where(same_seq, jnp.exp(scores - new_best[:, :, None]), 0.0)
        row_total = row_total * factor + jnp.sum(prob_tile, axis=2)
        out_sum = out_sum * factor.T[:, :, None] + jnp.einsum(
            "hqk,khd->qhd",
            prob_tile.astype(jnp.bfloat16),
            v_blk,
            preferred_element_type=jnp.float32,
        )
        return ((new_best, row_total, out_sum), None)

    running, _ = lax.scan(
        forward_per_block,
        running,
        split_rows(
            (
                lax.all_gather(key_rows, "blk", axis=0, tiled=True),
                lax.all_gather(values, "blk", axis=0, tiled=True),
            )
        ),
    )
    row_best, row_total, out_sum = running
    attended = (out_sum / row_total.T[:, :, None]).astype(jnp.bfloat16)
    log_total = row_best + jnp.log(row_total)
    mixed = attended.reshape(group_rows, per_dev * HEAD_DIM)
    attn_out = lax.psum_scatter(
        jnp.dot(mixed, f_out, preferred_element_type=jnp.float32).astype(jnp.bfloat16),
        "head",
        scatter_dimension=0,
        tiled=True,
    ).astype(jnp.float32)
    resid_one = tokens.astype(jnp.float32) + attn_out
    hidden, norm_one_back = jax.vjp(layer_norm, resid_one, norms[:, 0], norms[:, 1])
    hidden_low = hidden.astype(jnp.bfloat16)
    ffn_rows = lax.all_gather(hidden_low, "head", axis=0, tiled=True)
    gate = jnp.dot(ffn_rows, f_gu[0], preferred_element_type=jnp.float32)
    upward = jnp.dot(ffn_rows, f_gu[1], preferred_element_type=jnp.float32)
    gated, geglu_back = jax.vjp(geglu, gate, upward)
    gated_low = gated.astype(jnp.bfloat16)
    branch_part = jnp.dot(gated_low, f_down, preferred_element_type=jnp.float32)
    branch = lax.psum_scatter(
        branch_part.astype(jnp.bfloat16), "head", scatter_dimension=0, tiled=True
    ).astype(jnp.float32)
    result, norm_two_back = jax.vjp(layer_norm, hidden + branch, norms[:, 2], norms[:, 3])
    d_two, d_gain_two, d_shift_two = norm_two_back(out_grad.astype(jnp.float32))
    d_branch = d_two.astype(jnp.bfloat16)
    branch_rows = lax.all_gather(d_branch, "head", axis=0, tiled=True)
    g_down = weight_grad(gated_low, branch_rows)
    d_gate, d_up = geglu_back(dot_back(branch_rows, f_down))
    d_gate_low = d_gate.astype(jnp.bfloat16)
    d_up_low = d_up.astype(jnp.bfloat16)
    g_gate_up = jnp.stack([weight_grad(ffn_rows, d_gate_low), weight_grad(ffn_rows, d_up_low)])
    hidden_part = dot_back(d_gate_low, f_gu[0]) + dot_back(d_up_low, f_gu[1])
    d_hidden = d_two + lax.psum_scatter(
        hidden_part.astype(jnp.bfloat16), "head", scatter_dimension=0, tiled=True
    ).astype(jnp.float32)
    d_one, d_gain_one, d_shift_one = norm_one_back(d_hidden)
    d_attn = d_one.astype(jnp.bfloat16)
    attn_rows = lax.all_gather(d_attn, "head", axis=0, tiled=True)
    g_out = weight_grad(mixed, attn_rows)
    d_heads = dot_back(attn_rows, f_out).astype(jnp.bfloat16).reshape(group_rows, per_dev, HEAD_DIM)
    delta = jnp.sum(d_heads.astype(jnp.float32) * attended.astype(jnp.float32), axis=2).T
    zero_grad = jnp.zeros((group_rows, per_dev, HEAD_DIM), jnp.float32)
    grad_q = zero_grad

    def query_per_block(running, block_in):
        k_blk, v_blk, k_first = block_in
        k_pos = lax.dynamic_slice_in_dim(placement, k_first, group_rows)
        scores, same_seq = biased_scores(
            queries, k_blk, q_pos, k_pos, q_seq, seq_of(k_pos, seq_ends), slopes, qk_scale
        )
        prob_tile = jnp.where(same_seq, jnp.exp(scores - log_total[:, :, None]), 0.0)
        d_prob = jnp.einsum("qhd,khd->hqk", d_heads, v_blk, preferred_element_type=jnp.float32)
        d_score = (prob_tile * (d_prob - delta[:, :, None])).astype(jnp.bfloat16)
        running = (
            running
            + jnp.einsum("hqk,khd->qhd", d_score, k_blk, preferred_element_type=jnp.float32)
            * qk_scale
        )
        return (running, None)

    grad_q, _ = lax.scan(
        query_per_block,
        grad_q,
        split_rows(
            (
                lax.all_gather(key_rows, "blk", axis=0, tiled=True),
                lax.all_gather(values, "blk", axis=0, tiled=True),
            )
        ),
    )
    stats_lse, stats_delta = (
        lax.all_gather(log_total, "blk", axis=1, tiled=True),
        lax.all_gather(delta, "blk", axis=1, tiled=True),
    )
    running = (zero_grad, zero_grad)

    def key_per_block(state, block_in):
        q_blk, do_blk, q_first = block_in
        grad_k, grad_v = state
        other_pos = lax.dynamic_slice_in_dim(placement, q_first, group_rows)
        lse_blk = lax.dynamic_slice_in_dim(stats_lse, q_first, group_rows, 1)
        delta_blk = lax.dynamic_slice_in_dim(stats_delta, q_first, group_rows, 1)
        scores, same_seq = biased_scores(
            q_blk, key_rows, other_pos, q_pos, seq_of(other_pos, seq_ends), q_seq, slopes, qk_scale
        )
        prob_tile = jnp.where(same_seq, jnp.exp(scores - lse_blk[:, :, None]), 0.0)
        grad_v = grad_v + jnp.einsum(
            "hqk,qhd->khd",
            prob_tile.astype(jnp.bfloat16),
            do_blk,
            preferred_element_type=jnp.float32,
        )
        d_prob = jnp.einsum("qhd,khd->hqk", do_blk, values, preferred_element_type=jnp.float32)
        d_score = (prob_tile * (d_prob - delta_blk[:, :, None])).astype(jnp.bfloat16)
        grad_k = (
            grad_k
            + jnp.einsum("hqk,qhd->khd", d_score, q_blk, preferred_element_type=jnp.float32)
            * qk_scale
        )
        return ((grad_k, grad_v), None)

    running, _ = lax.scan(
        key_per_block,
        running,
        split_rows(
            (
                lax.all_gather(queries, "blk", axis=0, tiled=True),
                lax.all_gather(d_heads, "blk", axis=0, tiled=True),
            )
        ),
    )
    grad_k, grad_v = running
    d_grouped = jnp.stack([grad_q, grad_k, grad_v], axis=2).astype(jnp.bfloat16)
    g_norm = jnp.stack([d_gain_one, d_shift_one, d_gain_two, d_shift_two], axis=1)
    d_qkv = d_grouped.reshape(group_rows, per_dev * 3 * HEAD_DIM)
    g_qkv = weight_grad(group_tokens, d_qkv)
    input_sum, norm_share = (
        lax.psum_scatter(
            dot_back(d_qkv, f_qkv).astype(jnp.bfloat16), "head", scatter_dimension=0, tiled=True
        ).astype(jnp.float32),
        lax.psum_scatter(
            g_norm.astype(jnp.bfloat16), "head", scatter_dimension=1, tiled=True
        ).astype(jnp.float32),
    )
    input_grad = d_one + input_sum
    s_qkv, s_out, s_gu, s_down, s_norm = (
        lax.psum_scatter(g_qkv, "blk", scatter_dimension=0, tiled=True),
        lax.psum_scatter(g_out, "blk", scatter_dimension=1, tiled=True),
        lax.psum_scatter(g_gate_up, "blk", scatter_dimension=1, tiled=True),
        lax.psum_scatter(g_down, "blk", scatter_dimension=1, tiled=True),
        lax.psum_scatter(norm_share, "blk", scatter_dimension=0, tiled=True),
    )
    return (result.astype(jnp.bfloat16), input_grad, s_qkv, s_out, s_gu, s_down, s_norm)


Q_SLOTS = 32
K_SLOTS = 16
SEQ_STEP = 65536.0
FAR = 32768.0
LANE_OF = (0, 64, 192)


def by_head(rows, lanes):
    lane = lax.broadcasted_iota(jnp.int32, rows.shape, 1)
    parts = [jnp.where((lane >= first) & (lane < first + HEAD_DIM), rows, 0.0) for first in lanes]
    return jnp.concatenate(parts, axis=0).astype(jnp.bfloat16)


def key_tiles(kv_ref, j):
    rows = kv_ref.shape[0] * K_SLOTS
    blk = kv_ref[:, pl.ds(pl.multiple_of(j * K_SLOTS, K_SLOTS), K_SLOTS), :]
    return blk.reshape(rows, blk.shape[2])


def attend(span_ref, slope_ref, q_ref, kv_ref, kcode_ref, qcode_ref, out_ref, lse_ref, vt_ref):
    devs, slots, _ = kv_ref.shape
    rows = devs * K_SLOTS
    q_rows = q_ref.shape[0] * Q_SLOTS

    def turn(j, _):
        kv = key_tiles(kv_ref, j)[:, 128:384]
        vt_ref[j] = kv.astype(jnp.float32).T.astype(jnp.bfloat16)
        return 0

    lax.fori_loop(0, slots // K_SLOTS, turn, 0)

    def chunk(i, _):
        first = pl.multiple_of(i * Q_SLOTS, Q_SLOTS)
        q = q_ref[:, pl.ds(first, Q_SLOTS), :].reshape(q_rows, 256).astype(jnp.float32)
        qbd = by_head(q, (0, 64, 128))
        qcode = qcode_ref[i]

        def block(j, state):
            kv = key_tiles(kv_ref, j)
            keys = jnp.concatenate([kv[:, 0:128], kv[:, 256:384]], axis=1)
            s_all = lax.dot_general(keys, qbd, (((1,), (1,)), ((), ())), preferred_element_type=jnp.float32)
            dist = jnp.abs(kcode_ref[pl.ds(pl.multiple_of(j * rows, rows), rows), :] - qcode)
            keep = dist < FAR
            fresh = []
            for h in range(3):
                best, total, acc = state[h]
                s = jnp.where(keep, s_all[:, 128 * h : 128 * h + 128] - slope_ref[h] * dist, masked_score)
                top = jnp.maximum(best, jnp.max(s, axis=0, keepdims=True))
                factor = jnp.exp(best - top)
                p = jnp.exp(s - top)
                total = total * factor + jnp.sum(p, axis=0, keepdims=True)
                vt = vt_ref[j, LANE_OF[h] : LANE_OF[h] + 64, :]
                acc = acc * factor + jnp.dot(vt, p.astype(jnp.bfloat16), preferred_element_type=jnp.float32)
                fresh.append((top, total, acc))
            return tuple(fresh)

        start = tuple(
            (
                jnp.full((1, q_rows), masked_score, jnp.float32),
                jnp.zeros((1, q_rows), jnp.float32),
                jnp.zeros((64, q_rows), jnp.float32),
            )
            for _ in range(3)
        )
        done = lax.fori_loop(span_ref[i, 0], span_ref[i, 1], block, start)
        outs = [acc / total for _, total, acc in done]
        full = jnp.concatenate([outs[0], outs[1], jnp.zeros((64, q_rows), jnp.float32), outs[2]], axis=0)
        out_ref[:, pl.ds(first, Q_SLOTS), :] = full.T.astype(jnp.bfloat16).reshape(-1, Q_SLOTS, 256)
        for h in range(3):
            lse_ref[i, h : h + 1, :] = done[h][0] + jnp.log(done[h][1])
        return 0

    lax.fori_loop(0, slots // Q_SLOTS, chunk, 0)


def attend_back(span_ref, slope_ref, q_ref, kv_ref, kcode_ref, qcode_ref, out_ref, do_ref, lse_ref,
                dq_ref, dkv_ref, kt_ref, sum_ref):
    devs, slots, _ = kv_ref.shape
    rows = devs * K_SLOTS
    q_rows = q_ref.shape[0] * Q_SLOTS
    scale = HEAD_DIM ** (-0.5)

    def turn(j, _):
        kv = key_tiles(kv_ref, j)
        keys = jnp.concatenate([kv[:, 0:128], kv[:, 256:384]], axis=1)
        kt_ref[j] = keys.astype(jnp.float32).T.astype(jnp.bfloat16)
        sum_ref[j] = jnp.zeros((rows, 384), jnp.float32)
        return 0

    lax.fori_loop(0, slots // K_SLOTS, turn, 0)

    def chunk(i, _):
        first = pl.multiple_of(i * Q_SLOTS, Q_SLOTS)
        q = q_ref[:, pl.ds(first, Q_SLOTS), :].reshape(q_rows, 256).astype(jnp.float32)
        qbd = by_head(q, (0, 64, 128))
        do = do_ref[:, pl.ds(first, Q_SLOTS), :].reshape(q_rows, 256).astype(jnp.float32)
        out = out_ref[:, pl.ds(first, Q_SLOTS), :].reshape(q_rows, 256).astype(jnp.float32)
        dobd = by_head(do, LANE_OF)
        prod = (do * out).T
        delta = [jnp.sum(prod[f : f + 64, :], axis=0, keepdims=True) for f in LANE_OF]
        qcode = qcode_ref[i]

        def block(j, state):
            kv = key_tiles(kv_ref, j)
            keys = jnp.concatenate([kv[:, 0:128], kv[:, 256:384]], axis=1)
            vals = kv[:, 128:384]
            s_all = lax.dot_general(keys, qbd, (((1,), (1,)), ((), ())), preferred_element_type=jnp.float32)
            dp_all = lax.dot_general(vals, dobd, (((1,), (1,)), ((), ())), preferred_element_type=jnp.float32)
            dist = jnp.abs(kcode_ref[pl.ds(pl.multiple_of(j * rows, rows), rows), :] - qcode)
            keep = dist < FAR
            ps, dss, fresh = [], [], []
            for h in range(3):
                s = s_all[:, 128 * h : 128 * h + 128] - slope_ref[h] * dist - lse_ref[i, h : h + 1, :]
                p = jnp.exp(jnp.where(keep, s, masked_score))
                ds = (p * (dp_all[:, 128 * h : 128 * h + 128] - delta[h])).astype(jnp.bfloat16)
                ps.append(p.astype(jnp.bfloat16))
                dss.append(ds)
                kt = kt_ref[j, 64 * h : 64 * h + 64, :]
                fresh.append(state[h] + jnp.dot(kt, ds, preferred_element_type=jnp.float32))
            dv = jnp.dot(jnp.concatenate(ps, axis=1), dobd, preferred_element_type=jnp.float32)
            dk = jnp.dot(jnp.concatenate(dss, axis=1), qbd, preferred_element_type=jnp.float32)
            sum_ref[j, :, 0:128] += dk[:, 0:128]
            sum_ref[j, :, 128:256] += dv[:, 0:128]
            sum_ref[j, :, 256:384] += dk[:, 128:256] + dv[:, 128:256]
            return tuple(fresh)

        start = tuple(jnp.zeros((64, q_rows), jnp.float32) for _ in range(3))
        done = lax.fori_loop(span_ref[i, 0], span_ref[i, 1], block, start)
        full = jnp.concatenate(done + (jnp.zeros((64, q_rows), jnp.float32),), axis=0) * scale
        dq_ref[:, pl.ds(first, Q_SLOTS), :] = full.T.astype(jnp.bfloat16).reshape(-1, Q_SLOTS, 256)
        return 0

    lax.fori_loop(0, slots // Q_SLOTS, chunk, 0)

    def leave(j, _):
        dkv_ref[:, pl.ds(pl.multiple_of(j * K_SLOTS, K_SLOTS), K_SLOTS), :] = (
            sum_ref[j].astype(jnp.bfloat16).reshape(devs, K_SLOTS, 384)
        )
        return 0

    lax.fori_loop(0, slots // K_SLOTS, leave, 0)


VM = pl.BlockSpec(memory_space=pltpu.VMEM)
SM = pl.BlockSpec(memory_space=pltpu.SMEM)


def run_attend(span, slopes, q, kv, kcode, qcode):
    heads_n, slots, _ = q.shape
    devs = kv.shape[0]
    return pl.pallas_call(
        attend,
        out_shape=(
            jax.ShapeDtypeStruct((heads_n, slots, 256), jnp.bfloat16),
            jax.ShapeDtypeStruct((slots // Q_SLOTS, 8, heads_n * Q_SLOTS), jnp.float32),
        ),
        in_specs=[SM, SM, VM, VM, VM, VM],
        out_specs=(VM, VM),
        scratch_shapes=[pltpu.VMEM((slots // K_SLOTS, 256, devs * K_SLOTS), jnp.bfloat16)],
        compiler_params=pltpu.CompilerParams(vmem_limit_bytes=40 << 20),
        name="attend",
    )(span, slopes, q, kv, kcode, qcode)


def run_attend_back(span, slopes, q, kv, kcode, qcode, out, do, lse):
    heads_n, slots, _ = q.shape
    devs = kv.shape[0]
    return pl.pallas_call(
        attend_back,
        out_shape=(
            jax.ShapeDtypeStruct((heads_n, slots, 256), jnp.bfloat16),
            jax.ShapeDtypeStruct((devs, slots, 384), jnp.bfloat16),
        ),
        in_specs=[SM, SM, VM, VM, VM, VM, VM, VM, VM],
        out_specs=(VM, VM),
        scratch_shapes=[
            pltpu.VMEM((slots // K_SLOTS, 256, devs * K_SLOTS), jnp.bfloat16),
            pltpu.VMEM((slots // K_SLOTS, devs * K_SLOTS, 384), jnp.float32),
        ],
        compiler_params=pltpu.CompilerParams(vmem_limit_bytes=48 << 20),
        name="attend_back",
    )(span, slopes, q, kv, kcode, qcode, out, do, lse)


def key_spans(seq_starts, seq_ends, chunk_positions, block_positions, chunks):
    first = chunk_positions * jnp.arange(chunks, dtype=jnp.int32)
    last = first + chunk_positions - 1
    lo_seq = jnp.sum((first[:, None] >= seq_ends[None, :]).astype(jnp.int32), axis=1)
    hi_seq = jnp.sum((last[:, None] >= seq_ends[None, :]).astype(jnp.int32), axis=1)
    seqs = jnp.arange(seq_ends.shape[0], dtype=jnp.int32)[None, :]
    lo = jnp.sum(jnp.where(seqs == lo_seq[:, None], seq_starts[None, :], 0), axis=1)
    hi = jnp.sum(jnp.where(seqs == hi_seq[:, None], seq_ends[None, :], 0), axis=1)
    return jnp.stack([lo // block_positions, (hi + block_positions - 1) // block_positions], axis=1)


MESH = pl.DeviceIdType.MESH


def dot_tn(left, right):
    return lax.dot_general(left, right, (((0,), (0,)), ((), ())), preferred_element_type=jnp.float32)


def dot_nt(left, right):
    return lax.dot_general(left, right, (((1,), (1,)), ((), ())), preferred_element_type=jnp.float32)


def greet(peers):
    barrier = pltpu.get_barrier_semaphore()
    for peer in peers:
        pl.semaphore_signal(barrier, inc=1, device_id=peer, device_id_type=MESH)
    pl.semaphore_wait(barrier, len(peers))


def remote(src, dst, sems, i, peer):
    return pltpu.make_async_remote_copy(
        src_ref=src, dst_ref=dst, send_sem=sems.at[0, i], recv_sem=sems.at[1, i],
        device_id=peer, device_id_type=MESH,
    )


def finish(
    dkv_ref, dq_ref, tok_ref, w_ref, datt_ref, mixed_ref, done_ref, gn_ref,
    dx_ref, sattn_ref, snorm_ref,
    kv_sib, kv_sum, kv_in, gat, gat_sib, gat_sum, gat_in,
    part, part_in, att, dkvq, nz_in, nrow, np_in, sems,
):
    b = lax.axis_index("blk")
    z = lax.axis_index("head")
    chip, core = b // 2, b % 2
    sib = (chip * 2 + 1 - core, z)
    flat = [((chip ^ r) * 2 + core, z) for r in (1, 2, 3)]
    line = [(b, z ^ r) for r in (1, 2, 3)]
    greet([sib] + flat + line)
    f32, bf16 = jnp.float32, jnp.bfloat16
    started = []

    def go(src, dst, i, peer):
        copy = remote(src, dst, sems, i, peer)
        copy.start()
        started.append(copy)
        return copy

    kv_c = [go(dkv_ref.at[(chip ^ r) * 2 + 1 - core], kv_sib.at[r], r, sib) for r in (3, 1, 2, 0)]
    att_c = [go(datt_ref, att.at[r], 4 + r, line[r - 1]) for r in (3, 2, 1)]
    nz_c = [go(gn_ref.at[pl.ds((z ^ r) * 8, 8)], nz_in.at[r - 1], 8 + r, line[r - 1]) for r in (1, 2, 3)]
    kv_out = []
    for k, r in enumerate((3, 1, 2, 0)):
        kv_c[k].wait_recv()
        both = dkv_ref[(chip ^ r) * 2 + core].astype(f32) + kv_sib[r].astype(f32)
        kv_sum[r] = both.astype(bf16)
        if r:
            kv_out.append(go(kv_sum.at[r], kv_in.at[r - 1], 12 + r, flat[r - 1]))
    for c in nz_c:
        c.wait_recv()
    nrow[0] = gn_ref[pl.ds(z * 8, 8)] + nz_in[0] + nz_in[1] + nz_in[2]
    np_c = [go(nrow.at[0], np_in.at[r], 24 + r, flat[r - 1]) for r in (1, 2, 3)]
    for c in kv_out:
        c.wait_recv()
    dkvq[:, 0:384] = (
        kv_sum[0].astype(f32) + kv_in[0].astype(f32) + kv_in[1].astype(f32) + kv_in[2].astype(f32)
    ).astype(bf16)
    dkvq[:, 384:640] = dq_ref[...]
    dx_c = []
    for r in (3, 2, 1, 0):
        rows = pl.ds(pl.multiple_of((z ^ r) * 128, 128), 128)
        got = dkvq[rows, :]
        term = dot_nt(got, w_ref[...])
        if r:
            part[r - 1] = term.astype(bf16)
            dx_c.append(go(part.at[r - 1], part_in.at[r - 1], 28 + r, line[r - 1]))
        else:
            dx_ref[...] = done_ref[...] + term
    for c in att_c:
        c.wait_recv()
    att[0] = datt_ref[...]
    gat[:, 0:512] = dot_tn(tok_ref[...], dkvq[:, 0:512]).astype(bf16)
    last = dot_tn(tok_ref[...], dkvq[:, 512:640])
    outs = jnp.zeros((768, 256), f32)
    for r in range(4):
        outs = outs + dot_tn(att[r], mixed_ref[pl.ds(pl.multiple_of((z ^ r) * 128, 128), 128), :])
    gat[:, 512:640] = outs[:, 0:128].astype(bf16)
    gat[:, 640:768] = (outs[:, 128:256] + last).astype(bf16)
    gat_c = [
        go(gat.at[pl.ds(pl.multiple_of(((chip ^ r) * 2 + 1 - core) * 96, 96), 96)], gat_sib.at[r], 32 + r, sib)
        for r in (3, 1, 2, 0)
    ]
    gat_out = []
    for k, r in enumerate((3, 1, 2, 0)):
        gat_c[k].wait_recv()
        mine = gat[pl.ds(pl.multiple_of(((chip ^ r) * 2 + core) * 96, 96), 96), :].astype(f32)
        gat_sum[r] = (mine + gat_sib[r].astype(f32)).astype(bf16)
        if r:
            gat_out.append(go(gat_sum.at[r], gat_in.at[r - 1], 36 + r, flat[r - 1]))
    for c in np_c:
        c.wait_recv()
    nrow[1] = nrow[0] + np_in[1] + np_in[2] + np_in[3]
    half = go(nrow.at[1], np_in.at[0], 24, sib)
    for c in dx_c:
        c.wait_recv()
    dx_ref[...] += part_in[0].astype(f32) + part_in[1].astype(f32) + part_in[2].astype(f32)
    half.wait_recv()
    snorm_ref[...] = nrow[1] + np_in[0]
    for c in gat_out:
        c.wait_recv()
    sattn_ref[...] = (
        gat_sum[0].astype(f32) + gat_in[0].astype(f32) + gat_in[1].astype(f32) + gat_in[2].astype(f32)
    )
    for c in started:
        c.wait_send()


def run_finish(dkv, dq, toks, w, datt, mixed, done, gn):
    f32, bf16 = jnp.float32, jnp.bfloat16
    V = pltpu.VMEM
    return pl.pallas_call(
        finish,
        out_shape=(
            jax.ShapeDtypeStruct((128, 768), f32),
            jax.ShapeDtypeStruct((96, 768), f32),
            jax.ShapeDtypeStruct((8, 768), f32),
        ),
        in_specs=[VM] * 8,
        out_specs=(VM,) * 3,
        scratch_shapes=[
            V((4, 512, 384), bf16), V((4, 512, 384), bf16), V((3, 512, 384), bf16),
            V((768, 768), bf16), V((4, 96, 768), bf16), V((4, 96, 768), bf16), V((3, 96, 768), bf16),
            V((3, 128, 768), bf16), V((3, 128, 768), bf16), V((4, 128, 768), bf16), V((512, 640), bf16),
            V((3, 8, 768), f32), V((2, 8, 768), f32), V((4, 8, 768), f32),
            pltpu.SemaphoreType.DMA((2, 40)),
        ],
        compiler_params=pltpu.CompilerParams(
            collective_id=5, has_side_effects=True, vmem_limit_bytes=32 << 20
        ),
        name="finish",
    )(dkv, dq, toks, w, datt, mixed, done, gn)


def collect(
    tok_ref, wa_ref, wo_ref, nrm_ref,
    gt, wat, q_ref, kv, wout, nr,
    sems, lsem,
):
    b = lax.axis_index("blk")
    z = lax.axis_index("head")
    chip, core = b // 2, b % 2
    sib = (chip * 2 + 1 - core, z)
    near = [(chip ^ r) * 2 + core for r in (0, 1, 2, 3)]
    flat = [(n, z) for n in near]
    line = [(b, z ^ r) for r in (0, 1, 2, 3)]
    greet([sib] + flat[1:] + line[1:])
    f32, bf16 = jnp.float32, jnp.bfloat16
    started = []
    count = [0]

    def go(src, dst, peer):
        assert count[0] < sems.shape[1]
        copy = remote(src, dst, sems, count[0], peer)
        count[0] += 1
        copy.start()
        started.append(copy)
        return copy

    own = [
        pltpu.make_async_copy(tok_ref, gt.at[z], lsem.at[0]),
        pltpu.make_async_copy(wa_ref, wat.at[b], lsem.at[1]),
        pltpu.make_async_copy(wo_ref, wout.at[z, b], lsem.at[2]),
        pltpu.make_async_copy(nrm_ref, nr.at[b, z], lsem.at[3]),
    ]
    for c in own:
        c.start()
    wo_z = [go(wo_ref, wout.at[z, b], line[r]) for r in (3, 2, 1)]
    nr_z = [go(nrm_ref, nr.at[b, z], line[r]) for r in (3, 2, 1)]
    wa_p = [go(wa_ref, wat.at[b], flat[r]) for r in (3, 1, 2)]
    tok_z = {r: go(tok_ref, gt.at[z], line[r]) for r in (3, 2, 1)}
    wa_s = [go(wa_ref, wat.at[b], sib)]
    passed = []
    for c in own:
        c.wait()
    for c in wo_z + nr_z:
        c.wait_recv()
    for k, r in enumerate((3, 1, 2)):
        wa_p[k].wait_recv()
        wa_s.append(go(wat.at[near[r]], wat.at[near[r]], sib))
    wo_p = [go(wout.at[:, b], wout.at[:, b], flat[r]) for r in (3, 1, 2)]
    passed.append(go(wout.at[:, b], wout.at[:, b], sib))
    nr_p = [go(nr.at[b], nr.at[b], flat[r]) for r in (3, 1, 2)]
    passed.append(go(nr.at[b], nr.at[b], sib))
    for c in wa_s:
        c.wait_recv()
    kv_p = []
    for r in (0, 1, 2, 3):
        if r:
            tok_z[r].wait_recv()
        j = z ^ r
        rows = jnp.dot(gt[j], wat[...].reshape(768, 640), preferred_element_type=f32)
        kv[b * 4 + j] = rows[:, 0:384].astype(bf16)
        kv_p.append([go(kv.at[b * 4 + j], kv.at[b * 4 + j], flat[s]) for s in (3, 1, 2)])
        passed.append(go(kv.at[b * 4 + j], kv.at[b * 4 + j], sib))
        q_ref[j] = rows[:, 384:640].astype(bf16) * bf16(HEAD_DIM ** (-0.5))
    for k, r in enumerate((3, 1, 2)):
        wo_p[k].wait_recv()
        nr_p[k].wait_recv()
        n = near[r]
        passed.append(go(wout.at[:, n], wout.at[:, n], sib))
        passed.append(go(nr.at[n], nr.at[n], sib))
    for step, r in enumerate((0, 1, 2, 3)):
        j = z ^ r
        for k, s in enumerate((3, 1, 2)):
            kv_p[step][k].wait_recv()
            n = near[s] * 4 + j
            passed.append(go(kv.at[n], kv.at[n], sib))
    for c in passed:
        c.wait_recv()
    for c in started:
        c.wait_send()


def run_collect(tok, wa, wo, nrm):
    f32, bf16 = jnp.float32, jnp.bfloat16
    S = jax.ShapeDtypeStruct
    return pl.pallas_call(
        collect,
        out_shape=(
            S((4, 128, 768), bf16), S((8, 96, 640), bf16), S((4, 128, 256), bf16), S((32, 128, 384), bf16),
            S((4, 8, 96, 256), bf16), S((8, 4, 8, 128), f32),
        ),
        in_specs=[VM] * 4,
        out_specs=(VM,) * 6,
        scratch_shapes=[pltpu.SemaphoreType.DMA((2, 64)), pltpu.SemaphoreType.DMA((4,))],
        compiler_params=pltpu.CompilerParams(
            collective_id=1, has_side_effects=True, vmem_limit_bytes=16 << 20
        ),
        name="collect",
    )(tok, wa, wo, nrm)


def moments(rows):
    center = rows - jnp.mean(rows, axis=-1, keepdims=True)
    spread = lax.rsqrt(jnp.mean(center * center, axis=-1, keepdims=True) + 1e-05)
    return center * spread, spread


def norm_back(grad, gain, unit, spread):
    scaled = grad * gain
    return spread * (
        scaled - jnp.mean(scaled, axis=-1, keepdims=True) - unit * jnp.mean(scaled * unit, axis=-1, keepdims=True)
    )


def middle(
    mixed_ref, tok_ref, og_ref, norm_ref, wout_ref, wf_ref,
    act_ref, done_ref, datt_ref, dheads, sffn_ref, gn_ref,
    mix_in, wffn, rows_in, drow_in, gelu_a, gelu_b, gated, dgate, dup,
    part, part_in, part2, part2_in, gff, ffn_sib, ffn_sum, ffn_in, hid, unit_one, held, head_out, sems, lsem,
):
    b = lax.axis_index("blk")
    z = lax.axis_index("head")
    chip, core = b // 2, b % 2
    sib = (chip * 2 + 1 - core, z)
    near = [(chip ^ r) * 2 + core for r in (0, 1, 2, 3)]
    flat = [(n, z) for n in near]
    line = [(b, z ^ r) for r in (0, 1, 2, 3)]
    greet([sib] + flat[1:] + line[1:])
    f32, bf16 = jnp.float32, jnp.bfloat16
    started = []
    count = [0]

    def go(src, dst, peer):
        assert count[0] < sems.shape[1]
        copy = remote(src, dst, sems, count[0], peer)
        count[0] += 1
        copy.start()
        started.append(copy)
        return copy

    own = [
        pltpu.make_async_copy(mixed_ref.at[z], mix_in.at[z], lsem.at[0]),
        pltpu.make_async_copy(wf_ref, wffn.at[:, b], lsem.at[1]),
    ]
    for c in own:
        c.start()
    mix_c = [go(mixed_ref.at[z ^ r], mix_in.at[z], line[r]) for r in (3, 2, 1)]
    wf_p = [[go(wf_ref.at[t], wffn.at[t, b], flat[r]) for r in (3, 1, 2)] for t in range(3)]
    wf_s = [go(wf_ref, wffn.at[:, b], sib)]
    for c in own:
        c.wait()
    for c in mix_c:
        c.wait_recv()
    attn = dot_nt(mix_in[0], wout_ref[0])
    for j in (1, 2, 3):
        attn = attn + dot_nt(mix_in[j], wout_ref[j])
    unit, spread = moments(tok_ref[...].astype(f32) + attn)
    hidden = unit * norm_ref[0:1, :] + norm_ref[1:2, :]
    unit_one[...] = unit
    hid[...] = hidden
    rows_in[z] = hidden.astype(bf16)
    row_c = {r: go(rows_in.at[z], rows_in.at[z], line[r]) for r in (3, 2, 1)}
    for t in range(3):
        for k, r in enumerate((3, 1, 2)):
            wf_p[t][k].wait_recv()
            wf_s.append(go(wffn.at[t, near[r]], wffn.at[t, near[r]], sib))
    for c in wf_s:
        c.wait_recv()

    def weight(t):
        return wffn[t].reshape(768, 768)

    part_c = []
    for r in (0, 1, 2, 3):
        if r:
            row_c[r].wait_recv()
        rows = rows_in[z ^ r]
        gate = jnp.dot(rows, weight(0), preferred_element_type=f32)
        up = jnp.dot(rows, weight(1), preferred_element_type=f32)
        half = 0.5 + 0.5 * lax.erf(gate * (0.5**0.5))
        value = gate * half
        slope = half + gate * jnp.exp(-0.5 * gate * gate) * 0.3989422804014327
        gelu_a[r] = slope * up
        gelu_b[r] = value
        low = (value * up).astype(bf16)
        gated[r] = low
        term = dot_nt(low, weight(2))
        if r:
            part[r - 1] = term.astype(bf16)
            part_c.append(go(part.at[r - 1], part_in.at[r - 1], line[r]))
        else:
            held[...] = term
    for c in part_c:
        c.wait_recv()
    branch = held[...] + part_in[0].astype(f32) + part_in[1].astype(f32) + part_in[2].astype(f32)
    unit_two, spread_two = moments(hid[...] + branch)
    act_ref[...] = (unit_two * norm_ref[2:3, :] + norm_ref[3:4, :]).astype(bf16)
    grad = og_ref[...].astype(f32)
    d_two = norm_back(grad, norm_ref[2:3, :], unit_two, spread_two)
    drow_in[0] = d_two.astype(bf16)
    drow_c = {r: go(drow_in.at[0], drow_in.at[r], line[r]) for r in (3, 2, 1)}
    gn_ref[...] = jnp.zeros((32, 768), f32)
    gn_ref[16:17, :] = jnp.sum(grad * unit_two, axis=0, keepdims=True)
    gn_ref[24:25, :] = jnp.sum(grad, axis=0, keepdims=True)
    part2_c = []
    for r in (0, 1, 2, 3):
        if r:
            drow_c[r].wait_recv()
        d_gated = jnp.dot(drow_in[r], weight(2), preferred_element_type=f32)
        dg = (d_gated * gelu_a[r]).astype(bf16)
        du = (d_gated * gelu_b[r]).astype(bf16)
        dgate[r] = dg
        dup[r] = du
        term = dot_nt(dg, weight(0)) + dot_nt(du, weight(1))
        if r:
            part2[r - 1] = term.astype(bf16)
            part2_c.append(go(part2.at[r - 1], part2_in.at[r - 1], line[r]))
        else:
            held[...] = d_two + term
    sib_c = []
    for t in (2, 0, 1):
        total = jnp.zeros((768, 768), f32)
        for r in range(4):
            if t == 2:
                total = total + dot_tn(drow_in[r], gated[r])
            else:
                total = total + dot_tn(rows_in[z ^ r], (dgate, dup)[t][r])
        gff[t] = total.astype(bf16).reshape(4, 2, 96, 768)
        sib_c.append(go(gff.at[t, :, 1 - core], ffn_sib.at[t], sib))
    ffn_c = []
    for k, t in enumerate((2, 0, 1)):
        sib_c[k].wait_recv()
        for r in (3, 1, 2, 0):
            ffn_sum[t, r] = (gff[t, chip ^ r, core].astype(f32) + ffn_sib[t, chip ^ r].astype(f32)).astype(bf16)
            if r:
                ffn_c.append(go(ffn_sum.at[t, r], ffn_in.at[t, r - 1], flat[r]))
    for c in part2_c:
        c.wait_recv()
    d_hidden = held[...] + part2_in[0].astype(f32) + part2_in[1].astype(f32) + part2_in[2].astype(f32)
    unit = unit_one[...]
    d_one = norm_back(d_hidden, norm_ref[0:1, :], unit, spread)
    gn_ref[0:1, :] = jnp.sum(d_hidden * unit, axis=0, keepdims=True)
    gn_ref[8:9, :] = jnp.sum(d_hidden, axis=0, keepdims=True)
    done_ref[...] = d_one
    low_one = d_one.astype(bf16)
    datt_ref[...] = low_one
    head_c = []
    for r in (3, 2, 1, 0):
        term = jnp.dot(low_one, wout_ref[z ^ r], preferred_element_type=f32).astype(bf16)
        if r:
            head_out[r - 1] = term
            head_c.append(go(head_out.at[r - 1], dheads.at[z], line[r]))
        else:
            dheads[z] = term
    for c in ffn_c:
        c.wait_recv()
    for t in range(3):
        sffn_ref[t] = (
            ffn_sum[t, 0].astype(f32) + ffn_in[t, 0].astype(f32) + ffn_in[t, 1].astype(f32) + ffn_in[t, 2].astype(f32)
        )
    for c in head_c:
        c.wait_recv()
    for c in started:
        c.wait_send()


def run_middle(mixed, tok, og, norms, wout, wf):
    f32, bf16 = jnp.float32, jnp.bfloat16
    S = jax.ShapeDtypeStruct
    V = pltpu.VMEM
    return pl.pallas_call(
        middle,
        out_shape=(
            S((128, 768), bf16), S((128, 768), f32), S((128, 768), bf16), S((4, 128, 256), bf16),
            S((3, 96, 768), f32), S((32, 768), f32),
        ),
        in_specs=[VM] * 6,
        out_specs=(VM,) * 6,
        scratch_shapes=[
            V((4, 128, 256), bf16), V((3, 8, 96, 768), bf16), V((4, 128, 768), bf16), V((4, 128, 768), bf16),
            V((4, 128, 768), f32), V((4, 128, 768), f32), V((4, 128, 768), bf16), V((4, 128, 768), bf16),
            V((4, 128, 768), bf16),
            V((3, 128, 768), bf16), V((3, 128, 768), bf16), V((3, 128, 768), bf16), V((3, 128, 768), bf16),
            V((3, 4, 2, 96, 768), bf16), V((3, 4, 96, 768), bf16), V((3, 4, 96, 768), bf16), V((3, 3, 96, 768), bf16),
            V((128, 768), f32), V((128, 768), f32), V((128, 768), f32), V((3, 128, 256), bf16),
            pltpu.SemaphoreType.DMA((2, 56)), pltpu.SemaphoreType.DMA((2,)),
        ],
        compiler_params=pltpu.CompilerParams(
            collective_id=3, has_side_effects=True, vmem_limit_bytes=48 << 20
        ),
        name="middle",
    )(mixed, tok, og, norms, wout, wf)


PACK = (1, 4, 2, 5, 7, 8, 0, 3)


def packed(w_qkv, w_out):
    piece = [w_qkv[:, 64 * i : 64 * i + 64] for i in range(9)]
    out = w_out.T
    return jnp.concatenate([piece[i] for i in PACK] + [piece[6], out[:, 128:]], axis=1)


def unpacked(g):
    piece = [g[:, 64 * i : 64 * i + 64] for i in range(12)]
    qkv = jnp.concatenate([piece[i] for i in (6, 0, 2, 7, 1, 3, 10, 4, 5)], axis=1)
    return qkv, jnp.concatenate([piece[8], piece[9], piece[11]], axis=1).T


def fast_shards(
    tokens, w_qkv, w_out, w_gate_up, w_down, norm_params, alibi_slope, lengths, placement, out_grad
):
    heads_n = lax.axis_size("head")
    blk_n = lax.axis_size("blk")
    head_idx = lax.axis_index("head")
    blk_idx = lax.axis_index("blk")
    tok_rows, width = tokens.shape
    per_dev = HEADS // heads_n
    group_rows = heads_n * tok_rows
    devs = heads_n * blk_n
    share = w_qkv.shape[0]
    bf16 = jnp.bfloat16

    wo = w_out.T
    wo = jnp.concatenate([wo[:, :128], jnp.zeros((share, 64), bf16), wo[:, 128:]], axis=1)
    nrm = jnp.pad(norm_params.astype(jnp.float32).reshape(1, share), ((0, 7), (0, 128 - share)))
    group_tokens, attn_w, q, kv, wout, nr = run_collect(tokens, packed(w_qkv, w_out), wo, nrm)
    group_tokens = group_tokens.reshape(group_rows, width)
    attn_w = attn_w.reshape(width, 640)
    norms = nr[:, :, 0, :share].transpose(1, 0, 2).reshape(heads_n, width)
    norms = jnp.pad(norms, ((0, 4), (0, 0)))

    seq_ends = prefix_sums(lengths)
    code = placement.astype(jnp.float32) + SEQ_STEP * seq_of(placement, seq_ends).astype(jnp.float32)
    k_blocks = tok_rows // K_SLOTS
    q_chunks = tok_rows // Q_SLOTS
    kcode = code.reshape(devs, k_blocks, K_SLOTS).transpose(1, 0, 2).reshape(-1, 1)
    kcode = jnp.broadcast_to(kcode, (kcode.shape[0], 128))
    qcode = lax.dynamic_slice_in_dim(code, blk_idx * group_rows, group_rows)
    qcode = qcode.reshape(heads_n, q_chunks, Q_SLOTS).transpose(1, 0, 2).reshape(q_chunks, 1, heads_n * Q_SLOTS)
    slopes = lax.dynamic_slice_in_dim(alibi_slope, head_idx * per_dev, per_dev)
    span = key_spans(seq_ends - lengths, seq_ends, Q_SLOTS * devs, K_SLOTS * devs, q_chunks)

    mixed, lse = run_attend(span, slopes, q, kv, kcode, qcode)
    wf = jnp.concatenate([w_gate_up, w_down.T[None]], axis=0)
    result, d_one, d_attn, d_heads, s_ffn, g_norm = run_middle(
        mixed, tokens, out_grad, norms, wout.reshape(heads_n, width, 256), wf
    )
    d_q, dkv = run_attend_back(span, slopes, q, kv, kcode, qcode, mixed, d_heads, lse)
    input_grad, s_attn, s_norm = run_finish(
        dkv.reshape(blk_n, group_rows, 384), d_q.reshape(group_rows, 256), group_tokens, attn_w,
        d_attn, mixed.reshape(group_rows, 256), d_one, g_norm,
    )
    s_qkv, s_out = unpacked(s_attn)
    return (
        result,
        input_grad,
        s_qkv,
        s_out,
        s_ffn[:2],
        s_ffn[2].T,
        lax.dynamic_slice(s_norm, (0, blk_idx * share), (1, share)).reshape(share, 1),
    )


def solution(mesh):
    placed = (
        P(("blk", "head"), None),
        P("blk", "head"),
        P("head", "blk"),
        P(None, "blk", "head"),
        P("head", "blk"),
        P("blk", "head"),
        P(),
        P(),
        P(),
        P(("blk", "head"), None),
    )
    small = mesh.shape["blk"] == 8 and mesh.shape["head"] == 4
    return jax.shard_map(
        fast_shards if small else shards,
        mesh=mesh,
        in_specs=placed,
        out_specs=(
            P(("blk", "head"), None),
            P(("blk", "head"), None),
            P("blk", "head"),
            P("head", "blk"),
            P(None, "blk", "head"),
            P("head", "blk"),
            P("blk", "head"),
        ),
        check_vma=False,
    )
```

```python
import jax
import jax.numpy as jnp
from jax import lax
from jax.experimental import pallas as pl
from jax.experimental.pallas import tpu as pltpu
from jax.sharding import PartitionSpec as P

HEADS = 12
HEAD_DIM = 64


masked_score = -1e30


def layer_norm(residual, norm_gain, norm_shift):
    center = residual - jnp.mean(residual, axis=-1, keepdims=True)
    spread = jnp.mean(center * center, axis=-1, keepdims=True)
    return center * lax.rsqrt(spread + 1e-05) * norm_gain + norm_shift


def geglu(gate, upward):
    return jax.nn.gelu(gate, approximate=False) * upward


def dot_back(grad_rows, weight):
    return lax.dot_general(
        grad_rows, weight, (((1,), (1,)), ((), ())), preferred_element_type=jnp.float32
    )


def weight_grad(left, right):
    return lax.dot_general(
        left, right, (((0,), (0,)), ((), ())), preferred_element_type=jnp.float32
    )


def seq_of(positions, seq_ends):
    return jnp.sum((positions[:, None] >= seq_ends[None, :]).astype(jnp.int32), axis=1)


def prefix_sums(lengths):
    count = lengths.shape[0]
    upto = jnp.arange(count)[None, :] <= jnp.arange(count)[:, None]
    return jnp.sum(jnp.where(upto, lengths[None, :], 0), axis=1)


def biased_scores(queries, key_rows, q_pos, k_pos, q_seq, k_seq, slopes, qk_scale):
    scores = (
        jnp.einsum("qhd,khd->hqk", queries, key_rows, preferred_element_type=jnp.float32) * qk_scale
    )
    distance = jnp.abs(q_pos[:, None] - k_pos[None, :]).astype(jnp.float32)
    scores = scores - slopes[:, None, None] * distance[None]
    same_seq = (q_seq[:, None] == k_seq[None, :])[None]
    return (scores, same_seq)


def shards(
    tokens, w_qkv, w_out, w_gate_up, w_down, norm_params, alibi_slope, lengths, placement, out_grad
):
    heads_n = lax.axis_size("head")
    head_idx = lax.axis_index("head")
    blk_idx = lax.axis_index("blk")
    tok_rows = tokens.shape[0]
    per_dev = HEADS // heads_n
    group_rows = heads_n * tok_rows
    qk_scale = HEAD_DIM ** (-0.5)
    group_tokens, norm_cols = (
        lax.all_gather(tokens, "head", axis=0, tiled=True),
        lax.all_gather(norm_params, "head", axis=1, tiled=True),
    )
    f_qkv, f_out, f_gu, f_down, f_norm = (
        lax.all_gather(w_qkv, "blk", axis=0, tiled=True),
        lax.all_gather(w_out, "blk", axis=1, tiled=True),
        lax.all_gather(w_gate_up, "blk", axis=1, tiled=True),
        lax.all_gather(w_down, "blk", axis=1, tiled=True),
        lax.all_gather(norm_cols, "blk", axis=0, tiled=True),
    )
    grouped = jnp.dot(group_tokens, f_qkv, preferred_element_type=jnp.float32).astype(jnp.bfloat16)
    grouped = grouped.reshape(group_rows, per_dev, 3, HEAD_DIM)
    norms = f_norm.astype(jnp.float32)
    queries = grouped[:, :, 0]
    key_rows = grouped[:, :, 1]
    values = grouped[:, :, 2]
    seq_ends = prefix_sums(lengths)
    q_pos = lax.dynamic_slice_in_dim(placement, blk_idx * group_rows, group_rows)
    q_seq = seq_of(q_pos, seq_ends)
    slopes = lax.dynamic_slice_in_dim(alibi_slope, head_idx * per_dev, per_dev)

    def split_rows(shard_part):
        block_count = shard_part[0].shape[0] // group_rows
        pieces = tuple(
            (arr.reshape((block_count, group_rows) + arr.shape[1:]) for arr in shard_part)
        )
        starts = group_rows * jnp.arange(block_count, dtype=jnp.int32)
        return pieces + (starts,)

    start_state = (
        jnp.full((per_dev, group_rows), masked_score, jnp.float32),
        jnp.zeros((per_dev, group_rows), jnp.float32),
        jnp.zeros((group_rows, per_dev, HEAD_DIM), jnp.float32),
    )
    running = start_state

    def forward_per_block(state, block_in):
        k_blk, v_blk, k_first = block_in
        row_best, row_total, out_sum = state
        k_pos = lax.dynamic_slice_in_dim(placement, k_first, group_rows)
        scores, same_seq = biased_scores(
            queries, k_blk, q_pos, k_pos, q_seq, seq_of(k_pos, seq_ends), slopes, qk_scale
        )
        row_top = jnp.max(jnp.where(same_seq, scores, masked_score), axis=2)
        new_best = jnp.maximum(row_best, row_top)
        factor = jnp.exp(row_best - new_best)
        prob_tile = jnp.where(same_seq, jnp.exp(scores - new_best[:, :, None]), 0.0)
        row_total = row_total * factor + jnp.sum(prob_tile, axis=2)
        out_sum = out_sum * factor.T[:, :, None] + jnp.einsum(
            "hqk,khd->qhd",
            prob_tile.astype(jnp.bfloat16),
            v_blk,
            preferred_element_type=jnp.float32,
        )
        return ((new_best, row_total, out_sum), None)

    running, _ = lax.scan(
        forward_per_block,
        running,
        split_rows(
            (
                lax.all_gather(key_rows, "blk", axis=0, tiled=True),
                lax.all_gather(values, "blk", axis=0, tiled=True),
            )
        ),
    )
    row_best, row_total, out_sum = running
    attended = (out_sum / row_total.T[:, :, None]).astype(jnp.bfloat16)
    log_total = row_best + jnp.log(row_total)
    mixed = attended.reshape(group_rows, per_dev * HEAD_DIM)
    attn_out = lax.psum_scatter(
        jnp.dot(mixed, f_out, preferred_element_type=jnp.float32).astype(jnp.bfloat16),
        "head",
        scatter_dimension=0,
        tiled=True,
    ).astype(jnp.float32)
    resid_one = tokens.astype(jnp.float32) + attn_out
    hidden, norm_one_back = jax.vjp(layer_norm, resid_one, norms[:, 0], norms[:, 1])
    hidden_low = hidden.astype(jnp.bfloat16)
    ffn_rows = lax.all_gather(hidden_low, "head", axis=0, tiled=True)
    gate = jnp.dot(ffn_rows, f_gu[0], preferred_element_type=jnp.float32)
    upward = jnp.dot(ffn_rows, f_gu[1], preferred_element_type=jnp.float32)
    gated, geglu_back = jax.vjp(geglu, gate, upward)
    gated_low = gated.astype(jnp.bfloat16)
    branch_part = jnp.dot(gated_low, f_down, preferred_element_type=jnp.float32)
    branch = lax.psum_scatter(
        branch_part.astype(jnp.bfloat16), "head", scatter_dimension=0, tiled=True
    ).astype(jnp.float32)
    result, norm_two_back = jax.vjp(layer_norm, hidden + branch, norms[:, 2], norms[:, 3])
    d_two, d_gain_two, d_shift_two = norm_two_back(out_grad.astype(jnp.float32))
    d_branch = d_two.astype(jnp.bfloat16)
    branch_rows = lax.all_gather(d_branch, "head", axis=0, tiled=True)
    g_down = weight_grad(gated_low, branch_rows)
    d_gate, d_up = geglu_back(dot_back(branch_rows, f_down))
    d_gate_low = d_gate.astype(jnp.bfloat16)
    d_up_low = d_up.astype(jnp.bfloat16)
    g_gate_up = jnp.stack([weight_grad(ffn_rows, d_gate_low), weight_grad(ffn_rows, d_up_low)])
    hidden_part = dot_back(d_gate_low, f_gu[0]) + dot_back(d_up_low, f_gu[1])
    d_hidden = d_two + lax.psum_scatter(
        hidden_part.astype(jnp.bfloat16), "head", scatter_dimension=0, tiled=True
    ).astype(jnp.float32)
    d_one, d_gain_one, d_shift_one = norm_one_back(d_hidden)
    d_attn = d_one.astype(jnp.bfloat16)
    attn_rows = lax.all_gather(d_attn, "head", axis=0, tiled=True)
    g_out = weight_grad(mixed, attn_rows)
    d_heads = dot_back(attn_rows, f_out).astype(jnp.bfloat16).reshape(group_rows, per_dev, HEAD_DIM)
    delta = jnp.sum(d_heads.astype(jnp.float32) * attended.astype(jnp.float32), axis=2).T
    zero_grad = jnp.zeros((group_rows, per_dev, HEAD_DIM), jnp.float32)
    grad_q = zero_grad

    def query_per_block(running, block_in):
        k_blk, v_blk, k_first = block_in
        k_pos = lax.dynamic_slice_in_dim(placement, k_first, group_rows)
        scores, same_seq = biased_scores(
            queries, k_blk, q_pos, k_pos, q_seq, seq_of(k_pos, seq_ends), slopes, qk_scale
        )
        prob_tile = jnp.where(same_seq, jnp.exp(scores - log_total[:, :, None]), 0.0)
        d_prob = jnp.einsum("qhd,khd->hqk", d_heads, v_blk, preferred_element_type=jnp.float32)
        d_score = (prob_tile * (d_prob - delta[:, :, None])).astype(jnp.bfloat16)
        running = (
            running
            + jnp.einsum("hqk,khd->qhd", d_score, k_blk, preferred_element_type=jnp.float32)
            * qk_scale
        )
        return (running, None)

    grad_q, _ = lax.scan(
        query_per_block,
        grad_q,
        split_rows(
            (
                lax.all_gather(key_rows, "blk", axis=0, tiled=True),
                lax.all_gather(values, "blk", axis=0, tiled=True),
            )
        ),
    )
    stats_lse, stats_delta = (
        lax.all_gather(log_total, "blk", axis=1, tiled=True),
        lax.all_gather(delta, "blk", axis=1, tiled=True),
    )
    running = (zero_grad, zero_grad)

    def key_per_block(state, block_in):
        q_blk, do_blk, q_first = block_in
        grad_k, grad_v = state
        other_pos = lax.dynamic_slice_in_dim(placement, q_first, group_rows)
        lse_blk = lax.dynamic_slice_in_dim(stats_lse, q_first, group_rows, 1)
        delta_blk = lax.dynamic_slice_in_dim(stats_delta, q_first, group_rows, 1)
        scores, same_seq = biased_scores(
            q_blk, key_rows, other_pos, q_pos, seq_of(other_pos, seq_ends), q_seq, slopes, qk_scale
        )
        prob_tile = jnp.where(same_seq, jnp.exp(scores - lse_blk[:, :, None]), 0.0)
        grad_v = grad_v + jnp.einsum(
            "hqk,qhd->khd",
            prob_tile.astype(jnp.bfloat16),
            do_blk,
            preferred_element_type=jnp.float32,
        )
        d_prob = jnp.einsum("qhd,khd->hqk", do_blk, values, preferred_element_type=jnp.float32)
        d_score = (prob_tile * (d_prob - delta_blk[:, :, None])).astype(jnp.bfloat16)
        grad_k = (
            grad_k
            + jnp.einsum("hqk,qhd->khd", d_score, q_blk, preferred_element_type=jnp.float32)
            * qk_scale
        )
        return ((grad_k, grad_v), None)

    running, _ = lax.scan(
        key_per_block,
        running,
        split_rows(
            (
                lax.all_gather(queries, "blk", axis=0, tiled=True),
                lax.all_gather(d_heads, "blk", axis=0, tiled=True),
            )
        ),
    )
    grad_k, grad_v = running
    d_grouped = jnp.stack([grad_q, grad_k, grad_v], axis=2).astype(jnp.bfloat16)
    g_norm = jnp.stack([d_gain_one, d_shift_one, d_gain_two, d_shift_two], axis=1)
    d_qkv = d_grouped.reshape(group_rows, per_dev * 3 * HEAD_DIM)
    g_qkv = weight_grad(group_tokens, d_qkv)
    input_sum, norm_share = (
        lax.psum_scatter(
            dot_back(d_qkv, f_qkv).astype(jnp.bfloat16), "head", scatter_dimension=0, tiled=True
        ).astype(jnp.float32),
        lax.psum_scatter(
            g_norm.astype(jnp.bfloat16), "head", scatter_dimension=1, tiled=True
        ).astype(jnp.float32),
    )
    input_grad = d_one + input_sum
    s_qkv, s_out, s_gu, s_down, s_norm = (
        lax.psum_scatter(g_qkv, "blk", scatter_dimension=0, tiled=True),
        lax.psum_scatter(g_out, "blk", scatter_dimension=1, tiled=True),
        lax.psum_scatter(g_gate_up, "blk", scatter_dimension=1, tiled=True),
        lax.psum_scatter(g_down, "blk", scatter_dimension=1, tiled=True),
        lax.psum_scatter(norm_share, "blk", scatter_dimension=0, tiled=True),
    )
    return (result.astype(jnp.bfloat16), input_grad, s_qkv, s_out, s_gu, s_down, s_norm)


Q_SLOTS = 32
K_SLOTS = 16
SEQ_STEP = 65536.0
FAR = 32768.0
LANE_OF = (0, 64, 192)


def by_head(rows, lanes):
    lane = lax.broadcasted_iota(jnp.int32, rows.shape, 1)
    parts = [jnp.where((lane >= first) & (lane < first + HEAD_DIM), rows, 0.0) for first in lanes]
    return jnp.concatenate(parts, axis=0).astype(jnp.bfloat16)


def key_tiles(kv_ref, j):
    rows = kv_ref.shape[0] * K_SLOTS
    blk = kv_ref[:, pl.ds(pl.multiple_of(j * K_SLOTS, K_SLOTS), K_SLOTS), :]
    return blk.reshape(rows, blk.shape[2])


def key_span(len_ref, i, devs):
    first = i * (Q_SLOTS * devs)
    last = first + Q_SLOTS * devs - 1
    end, low, high = 0, 0, 0
    for k in range(8):
        start = end
        end = end + len_ref[k]
        low = jnp.where((first >= start) & (first < end), start, low)
        high = jnp.where((last >= start) & (last < end), end, high)
    step = K_SLOTS * devs
    return low // step, (high + step - 1) // step


def attend(len_ref, slope_ref, q_ref, kv_ref, kcode_ref, qcode_ref, out_ref, lse_ref, vt_ref):
    z = lax.axis_index("head")
    devs, slots, _ = kv_ref.shape
    rows = devs * K_SLOTS
    q_rows = q_ref.shape[0] * Q_SLOTS

    def turn(j, _):
        kv = key_tiles(kv_ref, j)[:, 128:384]
        vt_ref[j] = kv.T
        return 0

    lax.fori_loop(0, slots // K_SLOTS, turn, 0)

    def chunk(i, _):
        first = pl.multiple_of(i * Q_SLOTS, Q_SLOTS)
        q = q_ref[:, pl.ds(first, Q_SLOTS), :].reshape(q_rows, 256).astype(jnp.float32)
        qbd = by_head(q, (0, 64, 128))
        qcode = qcode_ref[i, 0:1, :]
        lo, hi = key_span(len_ref, i, devs)

        def block(j, state):
            kv = key_tiles(kv_ref, j)
            keys = jnp.concatenate([kv[:, 0:128], kv[:, 256:384]], axis=1)
            s_all = lax.dot_general(keys, qbd, (((1,), (1,)), ((), ())), preferred_element_type=jnp.float32)
            dist = jnp.abs(key_tiles(kcode_ref, j) - qcode)
            keep = dist < FAR
            fresh = []
            for h in range(3):
                best, total, acc = state[h]
                s = jnp.where(keep, s_all[:, 128 * h : 128 * h + 128] - slope_ref[3 * z + h] * dist, masked_score)
                top = jnp.maximum(best, jnp.max(s, axis=0, keepdims=True))
                factor = jnp.exp(best - top)
                p = jnp.exp(s - top)
                total = total * factor + jnp.sum(p, axis=0, keepdims=True)
                vt = vt_ref[j, LANE_OF[h] : LANE_OF[h] + 64, :]
                acc = acc * factor + jnp.dot(vt, p.astype(jnp.bfloat16), preferred_element_type=jnp.float32)
                fresh.append((top, total, acc))
            return tuple(fresh)

        start = tuple(
            (
                jnp.full((1, q_rows), masked_score, jnp.float32),
                jnp.zeros((1, q_rows), jnp.float32),
                jnp.zeros((64, q_rows), jnp.float32),
            )
            for _ in range(3)
        )
        done = lax.fori_loop(lo, hi, block, start)
        outs = [acc / total for _, total, acc in done]
        full = jnp.concatenate([outs[0], outs[1], jnp.zeros((64, q_rows), jnp.float32), outs[2]], axis=0)
        out_ref[:, pl.ds(first, Q_SLOTS), :] = full.T.astype(jnp.bfloat16).reshape(-1, Q_SLOTS, 256)
        for h in range(3):
            lse_ref[i, h : h + 1, :] = done[h][0] + jnp.log(done[h][1])
        return 0

    lax.fori_loop(0, slots // Q_SLOTS, chunk, 0)


def attend_back(len_ref, slope_ref, q_ref, kv_ref, kcode_ref, qcode_ref, out_ref, do_ref, lse_ref, act_any, sdown_any,
                dq_ref, dkv_ref, act_out, sdown_out, kt_ref, sum_ref, sem):
    z = lax.axis_index("head")
    devs, slots, _ = kv_ref.shape
    rows = devs * K_SLOTS
    q_rows = q_ref.shape[0] * Q_SLOTS
    scale = HEAD_DIM ** (-0.5)
    along = [
        pltpu.make_async_copy(act_any, act_out, sem.at[0]),
        pltpu.make_async_copy(sdown_any, sdown_out, sem.at[1]),
    ]
    for c in along:
        c.start()

    def turn(j, _):
        kv = key_tiles(kv_ref, j)
        keys = jnp.concatenate([kv[:, 0:128], kv[:, 256:384]], axis=1)
        kt_ref[j] = keys.T
        sum_ref[j] = jnp.zeros((rows, 384), jnp.float32)
        return 0

    lax.fori_loop(0, slots // K_SLOTS, turn, 0)

    def chunk(i, _):
        first = pl.multiple_of(i * Q_SLOTS, Q_SLOTS)
        q = q_ref[:, pl.ds(first, Q_SLOTS), :].reshape(q_rows, 256).astype(jnp.float32)
        qbd = by_head(q, (0, 64, 128))
        do = do_ref[:, pl.ds(first, Q_SLOTS), :].reshape(q_rows, 256).astype(jnp.float32)
        out = out_ref[:, pl.ds(first, Q_SLOTS), :].reshape(q_rows, 256).astype(jnp.float32)
        dobd = by_head(do, LANE_OF)
        prod = (do * out).T
        delta = [jnp.sum(prod[f : f + 64, :], axis=0, keepdims=True) for f in LANE_OF]
        qcode = qcode_ref[i, 0:1, :]
        lo, hi = key_span(len_ref, i, devs)

        def block(j, state):
            kv = key_tiles(kv_ref, j)
            keys = jnp.concatenate([kv[:, 0:128], kv[:, 256:384]], axis=1)
            vals = kv[:, 128:384]
            s_all = lax.dot_general(keys, qbd, (((1,), (1,)), ((), ())), preferred_element_type=jnp.float32)
            dp_all = lax.dot_general(vals, dobd, (((1,), (1,)), ((), ())), preferred_element_type=jnp.float32)
            dist = jnp.abs(key_tiles(kcode_ref, j) - qcode)
            keep = dist < FAR
            ps, dss, fresh = [], [], []
            for h in range(3):
                s = s_all[:, 128 * h : 128 * h + 128] - slope_ref[3 * z + h] * dist - lse_ref[i, h : h + 1, :]
                p = jnp.exp(jnp.where(keep, s, masked_score))
                ds = (p * (dp_all[:, 128 * h : 128 * h + 128] - delta[h])).astype(jnp.bfloat16)
                ps.append(p.astype(jnp.bfloat16))
                dss.append(ds)
                kt = kt_ref[j, 64 * h : 64 * h + 64, :]
                fresh.append(state[h] + jnp.dot(kt, ds, preferred_element_type=jnp.float32))
            dv = jnp.dot(jnp.concatenate(ps, axis=1), dobd, preferred_element_type=jnp.float32)
            dk = jnp.dot(jnp.concatenate(dss, axis=1), qbd, preferred_element_type=jnp.float32)
            sum_ref[j, :, 0:128] += dk[:, 0:128]
            sum_ref[j, :, 128:256] += dv[:, 0:128]
            sum_ref[j, :, 256:384] += dk[:, 128:256] + dv[:, 128:256]
            return tuple(fresh)

        start = tuple(jnp.zeros((64, q_rows), jnp.float32) for _ in range(3))
        done = lax.fori_loop(lo, hi, block, start)
        full = jnp.concatenate(done + (jnp.zeros((64, q_rows), jnp.float32),), axis=0) * scale
        dq_ref[:, pl.ds(first, Q_SLOTS), :] = full.T.astype(jnp.bfloat16).reshape(-1, Q_SLOTS, 256)
        return 0

    lax.fori_loop(0, slots // Q_SLOTS, chunk, 0)

    def leave(j, _):
        dkv_ref[:, pl.ds(pl.multiple_of(j * K_SLOTS, K_SLOTS), K_SLOTS), :] = (
            sum_ref[j].astype(jnp.bfloat16).reshape(devs, K_SLOTS, 384)
        )
        return 0

    lax.fori_loop(0, slots // K_SLOTS, leave, 0)
    for c in along:
        c.wait()


VM = pl.BlockSpec(memory_space=pltpu.VMEM)
SM = pl.BlockSpec(memory_space=pltpu.SMEM)
ANY = pl.BlockSpec(memory_space=pl.ANY)
HBM = pl.BlockSpec(memory_space=pltpu.MemorySpace.HBM)


def run_attend(lengths, slopes, q, kv, kcode, qcode):
    heads_n, slots, _ = q.shape
    devs = kv.shape[0]
    return pl.pallas_call(
        attend,
        out_shape=(
            jax.ShapeDtypeStruct((heads_n, slots, 256), jnp.bfloat16),
            jax.ShapeDtypeStruct((slots // Q_SLOTS, 8, heads_n * Q_SLOTS), jnp.float32),
        ),
        in_specs=[SM, SM, VM, VM, VM, VM],
        out_specs=(VM, VM),
        scratch_shapes=[pltpu.VMEM((slots // K_SLOTS, 256, devs * K_SLOTS), jnp.bfloat16)],
        compiler_params=pltpu.CompilerParams(vmem_limit_bytes=16 << 20),
        name="attend",
    )(lengths, slopes, q, kv, kcode, qcode)


def run_attend_back(lengths, slopes, q, kv, kcode, qcode, out, do, lse, act, s_down):
    heads_n, slots, _ = q.shape
    devs = kv.shape[0]
    return pl.pallas_call(
        attend_back,
        out_shape=(
            jax.ShapeDtypeStruct((heads_n, slots, 256), jnp.bfloat16),
            jax.ShapeDtypeStruct((devs, slots, 384), jnp.bfloat16),
            jax.ShapeDtypeStruct(act.shape, act.dtype),
            jax.ShapeDtypeStruct(s_down.shape, s_down.dtype),
        ),
        in_specs=[SM, SM, VM, VM, VM, VM, VM, VM, VM, ANY, ANY],
        out_specs=(VM, VM, ANY, ANY),
        scratch_shapes=[
            pltpu.VMEM((slots // K_SLOTS, 256, devs * K_SLOTS), jnp.bfloat16),
            pltpu.VMEM((slots // K_SLOTS, devs * K_SLOTS, 384), jnp.float32),
            pltpu.SemaphoreType.DMA((2,)),
        ],
        compiler_params=pltpu.CompilerParams(vmem_limit_bytes=26 << 20),
        name="attend_back",
    )(lengths, slopes, q, kv, kcode, qcode, out, do, lse, act, s_down)


MESH = pl.DeviceIdType.MESH


def dot_tn(left, right):
    return lax.dot_general(left, right, (((0,), (0,)), ((), ())), preferred_element_type=jnp.float32)


def dot_nt(left, right):
    return lax.dot_general(left, right, (((1,), (1,)), ((), ())), preferred_element_type=jnp.float32)


def greet(peers):
    barrier = pltpu.get_barrier_semaphore()
    for peer in peers:
        pl.semaphore_signal(barrier, inc=1, device_id=peer, device_id_type=MESH)
    pl.semaphore_wait(barrier, len(peers))


class Sender:
    def __init__(self, sems):
        self.sems = sems
        self.used = 0
        self.left = []

    def __call__(self, src, dst, peer, only=None, arrive=None):
        i = self.used
        self.used += 1
        assert i < self.sems.shape[1]
        copy = pltpu.make_async_remote_copy(
            src_ref=src, dst_ref=dst, send_sem=self.sems.at[0, i],
            recv_sem=self.sems.at[1, i] if arrive is None else arrive,
            device_id=peer, device_id_type=MESH,
        )
        copy.arrive = self.sems.at[1, i]
        self.left.append((copy, only))
        if only is None:
            copy.start()
        else:
            pl.when(only)(copy.start)
        return copy

    def finish(self):
        for copy, only in self.left:
            if only is None:
                copy.wait_send()
            else:
                pl.when(only)(copy.wait_send)


class Spread:
    def __init__(self, go, mid, slot, z, line):
        self.go, self.mid, self.slot, self.z, self.line = go, mid, slot, z, line
        self.two = go(slot(z), slot(z), line[2])
        self.three = go(slot(z), slot(z), line[3], only=mid)
        self.one = go(slot(z), slot(z), line[1])

    def pass_on(self):
        self.two.wait_recv()
        far = self.slot(self.z ^ 2)
        self.go(far, far, self.line[1], only=self.mid, arrive=self.three.arrive)


def finish(
    dkv_ref, dq_ref, tok_ref, w_ref, datt_ref, mixed_ref, done_ref, gn_ref, up_ref,
    dx_ref, sqkv_ref, sout_ref, snorm_ref, sup_ref,
    up_in, kv_sib, kv_sum, kv_in, g_one, g_two, g_sib, g_sum, g_in,
    part, part_in, att, dkvq, nz_in, nrow, np_in, relay, sems,
):
    b = lax.axis_index("blk")
    z = lax.axis_index("head")
    chip, core = b // 2, b % 2
    sib = (chip * 2 + 1 - core, z)
    flat = [((chip ^ r) * 2 + core, z) for r in (0, 1, 2, 3)]
    line = [(b, z ^ r) for r in (0, 1, 2, 3)]
    greet([sib] + flat[1:] + line[1:])
    f32, bf16 = jnp.float32, jnp.bfloat16
    go = Sender(sems)
    mid = (z == 1) | (z == 2)
    ends = (z == 0) | (z == 3)

    def member(r):
        return pl.ds(pl.multiple_of((z ^ r) * 128, 128), 128)

    kv_c = {
        (q, r): go(dkv_ref.at[(chip ^ r) * 2 + 1 - core, member(q)], kv_sib.at[q, r], sib)
        for q in (3, 2, 1, 0) for r in (3, 1, 2, 0)
    }
    att[z] = datt_ref[...]
    att_c = Spread(go, mid, lambda j: att.at[j], z, line)
    nz_c = [go(gn_ref.at[pl.ds((z ^ r) * 8, 8)], nz_in.at[r - 1], line[r]) for r in (1, 2, 3)]
    kv_out = {}
    for q in (3, 2, 1, 0):
        for r in (3, 1, 2, 0):
            kv_c[q, r].wait_recv()
            both = dkv_ref[(chip ^ r) * 2 + core, member(q), :].astype(f32) + kv_sib[q, r].astype(f32)
            kv_sum[q, r] = both.astype(bf16)
            if r:
                kv_out[q, r] = go(kv_sum.at[q, r], kv_in.at[q, r - 1], flat[r])
    dkvq[:, 384:640] = dq_ref[...]

    @pl.when(ends)
    def _():
        relay[...] = jnp.zeros((128, 768), bf16)
        part_in[2] = jnp.zeros((128, 768), bf16)

    up_c = [go(up_ref.at[r], up_in.at[r - 1], flat[r]) for r in (3, 1, 2)]

    def send_half(part_i, grads):
        return [
            go(grads.at[pl.ds(pl.multiple_of(((chip ^ r) * 2 + 1 - core) * 96, 96), 96)], g_sib.at[part_i, r], sib)
            for r in (3, 1, 2, 0)
        ]

    def send_sum(part_i, grads, copies):
        out = []
        for k, r in enumerate((3, 1, 2, 0)):
            copies[k].wait_recv()
            mine = grads[pl.ds(pl.multiple_of(((chip ^ r) * 2 + core) * 96, 96), 96), :].astype(f32)
            g_sum[part_i, r] = (mine + g_sib[part_i, r].astype(f32)).astype(bf16)
            if r:
                out.append(go(g_sum.at[part_i, r], g_in.at[part_i, r - 1], flat[r]))
        return out

    def settle(part_i, copies):
        for c in copies:
            c.wait_recv()
        return (
            g_sum[part_i, 0].astype(f32) + g_in[part_i, 0].astype(f32)
            + g_in[part_i, 1].astype(f32) + g_in[part_i, 2].astype(f32)
        )

    att_c.pass_on()
    for c in nz_c:
        c.wait_recv()
    nrow[0] = gn_ref[pl.ds(z * 8, 8)] + nz_in[0] + nz_in[1] + nz_in[2]
    np_c = [go(nrow.at[0], np_in.at[r], flat[r]) for r in (1, 2, 3)]
    last = dot_tn(tok_ref[...], dq_ref[...])
    g_one[:, 0:128] = last[:, 0:128].astype(bf16)
    dx_c = []
    for q in (3, 2, 1, 0):
        for r in (1, 2, 3):
            kv_out[q, r].wait_recv()
        dkvq[member(q), 0:384] = (
            kv_sum[q, 0].astype(f32) + kv_in[q, 0].astype(f32) + kv_in[q, 1].astype(f32) + kv_in[q, 2].astype(f32)
        ).astype(bf16)
        term = dot_nt(dkvq[member(q), :], w_ref[...])
        if q == 3:
            part[2] = term.astype(bf16)
            passed = go(part.at[2], relay, line[1], only=ends)
            dx_three = go(part.at[2], part_in.at[2], line[3], only=mid)
        elif q == 2:
            far = term
        elif q == 1:
            part[0] = term.astype(bf16)
            dx_c.append(go(part.at[0], part_in.at[0], line[1]))
            pl.when(mid)(passed.wait_recv)
            part[1] = (far + relay[...].astype(f32)).astype(bf16)
            dx_c.append(go(part.at[1], part_in.at[1], line[2]))
        else:
            dx_ref[...] = done_ref[...] + term
    g_two[...] = dot_tn(tok_ref[...], dkvq[:, 0:384]).astype(bf16)
    two_c = send_half(1, g_two)
    att_c.one.wait_recv()
    att_c.three.wait_recv()
    outs = dot_tn(att[...].reshape(512, 768), mixed_ref[...])
    g_one[:, 128:256] = outs[:, 0:128].astype(bf16)
    g_one[:, 256:384] = (outs[:, 128:256] + last[:, 128:256]).astype(bf16)
    one_c = send_half(0, g_one)
    two_out = send_sum(1, g_two, two_c)
    one_out = send_sum(0, g_one, one_c)
    for c in np_c:
        c.wait_recv()
    nrow[1] = nrow[0] + np_in[1] + np_in[2] + np_in[3]
    half = go(nrow.at[1], np_in.at[0], sib)
    half.wait_recv()
    full = nrow[1] + np_in[0]
    snorm_ref[...] = pltpu.roll(full, lax.rem(768 - 96 * b, 768), 1)[:, 0:128]
    for c in up_c:
        c.wait_recv()
    sup_ref[...] = up_ref[0].astype(f32) + up_in[0].astype(f32) + up_in[1].astype(f32) + up_in[2].astype(f32)
    two = settle(1, two_out)
    one = settle(0, one_out)
    piece = [two[:, 64 * i : 64 * i + 64] for i in range(6)]
    piece += [one[:, 0:64], one[:, 64:128], one[:, 256:320]]
    for k, i in enumerate((6, 0, 2, 7, 1, 3, 8, 4, 5)):
        sqkv_ref[:, 64 * k : 64 * k + 64] = piece[i]
    turned = jnp.concatenate([one[:, 128:384], jnp.zeros((32, 256), f32)], axis=0).T
    sout_ref[0:128, :] = turned[0:128, 0:96]
    sout_ref[128:192, :] = turned[192:256, 0:96]
    for c in dx_c:
        c.wait_recv()
    pl.when(mid)(dx_three.wait_recv)
    dx_ref[...] += part_in[0].astype(f32) + part_in[1].astype(f32) + part_in[2].astype(f32)
    go.finish()


def run_finish(dkv, dq, toks, w, datt, mixed, done, gn, up):
    f32, bf16 = jnp.float32, jnp.bfloat16
    V = pltpu.VMEM
    return pl.pallas_call(
        finish,
        out_shape=(
            jax.ShapeDtypeStruct((128, 768), f32),
            jax.ShapeDtypeStruct((96, 576), f32),
            jax.ShapeDtypeStruct((192, 96), f32),
            jax.ShapeDtypeStruct((8, 128), f32),
            jax.ShapeDtypeStruct((96, 768), f32),
        ),
        in_specs=[VM] * 9,
        out_specs=(VM,) * 5,
        scratch_shapes=[
            V((3, 96, 768), bf16),
            V((4, 4, 128, 384), bf16), V((4, 4, 128, 384), bf16), V((4, 3, 128, 384), bf16),
            V((768, 384), bf16), V((768, 384), bf16),
            V((2, 4, 96, 384), bf16), V((2, 4, 96, 384), bf16), V((2, 3, 96, 384), bf16),
            V((3, 128, 768), bf16), V((3, 128, 768), bf16), V((4, 128, 768), bf16), V((512, 640), bf16),
            V((3, 8, 768), f32), V((2, 8, 768), f32), V((4, 8, 768), f32), V((128, 768), bf16),
            pltpu.SemaphoreType.DMA((2, 72)),
        ],
        compiler_params=pltpu.CompilerParams(
            collective_id=5, has_side_effects=True, vmem_limit_bytes=28 << 20
        ),
        name="finish",
    )(dkv, dq, toks, w, datt, mixed, done, gn, up)


def collect(
    len_any, tok_any, wq_any, wout_any, nrm_any, pos_any,
    gt, wat, q_ref, kv, wout, norm_out, kcode, qcode,
    wa_ref, wo_ref, nr, code_ref, wq_ref, wout_ref, nrm_row, pos_ref, nrm_ref, len_ref, sems, lsem,
):
    b = lax.axis_index("blk")
    z = lax.axis_index("head")
    chip, core = b // 2, b % 2
    sib = (chip * 2 + 1 - core, z)
    near = [(chip ^ r) * 2 + core for r in (0, 1, 2, 3)]
    flat = [(n, z) for n in near]
    line = [(b, z ^ r) for r in (0, 1, 2, 3)]
    f32, bf16 = jnp.float32, jnp.bfloat16
    fetch = [
        pltpu.make_async_copy(wq_any, wq_ref, lsem.at[0]),
        pltpu.make_async_copy(wout_any, wout_ref, lsem.at[1]),
        pltpu.make_async_copy(nrm_any, nrm_row, lsem.at[2]),
        pltpu.make_async_copy(pos_any, pos_ref, lsem.at[3]),
        pltpu.make_async_copy(tok_any, gt.at[z], lsem.at[4]),
        pltpu.make_async_copy(len_any, len_ref, lsem.at[5]),
    ]
    for c in fetch:
        c.start()
    for c in fetch:
        c.wait()
    go = Sender(sems)
    mid = (z == 1) | (z == 2)
    ends = (z == 0) | (z == 3)

    wq = wq_ref[...].astype(f32)
    wo = wout_ref[...].astype(f32)
    wo = jnp.concatenate([wo[0:128], jnp.zeros((64, 96), f32), wo[128:192]], axis=0)
    wo = jnp.concatenate([wo, jnp.zeros((256, 32), f32)], axis=1).T[0:96]
    wo_ref[...] = wo.astype(bf16)
    piece = [wq[:, 64 * i : 64 * i + 64] for i in range(9)] + [wo[:, 192:256]]
    for k in range(5):
        tile = jnp.concatenate([piece[PACK[2 * k]], piece[PACK[2 * k + 1]]], axis=1)
        wa_ref[:, 128 * k : 128 * k + 128] = tile.astype(bf16)
    wat[b] = wa_ref[...]
    wout[z, b] = wo_ref[...]
    nrm_ref[...] = jnp.zeros((8, 128), f32)
    nrm_ref[0:1, 0:96] = nrm_row[...].astype(f32)
    nr[b, z] = nrm_ref[...]
    greet([sib] + flat[1:] + line[1:])
    wo_z = [go(wo_ref, wout.at[z, b], line[r]) for r in (3, 2, 1)]
    nr_z = [go(nrm_ref, nr.at[b, z], line[r]) for r in (3, 2, 1)]
    wa_p = [go(wa_ref, wat.at[b], flat[r]) for r in (3, 1, 2)]
    tok_z = Spread(go, mid, lambda j: gt.at[j], z, line)
    wa_s = [go(wa_ref, wat.at[b], sib)]
    passed = []
    pos = pos_ref[...]
    seq = jnp.zeros(pos.shape, f32)
    end = 0
    for k in range(8):
        end = end + len_ref[k]
        seq = seq + jnp.where(pos >= end, 1.0, 0.0)
    code_ref[...] = pos.astype(f32) + SEQ_STEP * seq

    def spread_code(d, _):
        kcode[d] = jnp.broadcast_to(code_ref[pl.ds(d, 1), :], (128, 128)).T
        return 0

    lax.fori_loop(0, 32, spread_code, 0)
    own_code = [code_ref[pl.ds(b * 4 + j, 1), :] for j in range(4)]
    for i in range(4):
        qcode[i, 0:1, :] = jnp.concatenate([c[:, 32 * i : 32 * i + 32] for c in own_code], axis=1)
    for c in wo_z + nr_z:
        c.wait_recv()
    for k, r in enumerate((3, 1, 2)):
        wa_p[k].wait_recv()
        wa_s.append(go(wat.at[near[r]], wat.at[near[r]], sib))
    wo_p = [go(wout.at[:, b], wout.at[:, b], flat[r]) for r in (3, 1, 2)]
    passed.append(go(wout.at[:, b], wout.at[:, b], sib))
    nr_p = [go(nr.at[b], nr.at[b], flat[r]) for r in (3, 1, 2)]
    passed.append(go(nr.at[b], nr.at[b], sib))
    for c in wa_s:
        c.wait_recv()
    kv_p = []
    for r in (0, 2, 1, 3):
        if r == 2:
            tok_z.pass_on()
        elif r:
            (tok_z.one if r == 1 else tok_z.three).wait_recv()
        j = z ^ r
        rows = jnp.dot(gt[j], wat[...].reshape(768, 640), preferred_element_type=f32)
        kv[b * 4 + j] = rows[:, 0:384].astype(bf16)
        kv_p.append([go(kv.at[b * 4 + j], kv.at[b * 4 + j], flat[s]) for s in (3, 1, 2)])
        passed.append(go(kv.at[b * 4 + j], kv.at[b * 4 + j], sib))
        q_ref[j] = rows[:, 384:640].astype(bf16) * bf16(HEAD_DIM ** (-0.5))
    for k, r in enumerate((3, 1, 2)):
        wo_p[k].wait_recv()
        nr_p[k].wait_recv()
        n = near[r]
        passed.append(go(wout.at[:, n], wout.at[:, n], sib))
        passed.append(go(nr.at[n], nr.at[n], sib))
    for step, r in enumerate((0, 2, 1, 3)):
        j = z ^ r
        for k, s in enumerate((3, 1, 2)):
            kv_p[step][k].wait_recv()
            n = near[s] * 4 + j
            passed.append(go(kv.at[n], kv.at[n], sib))
    for c in passed:
        c.wait_recv()
    total = jnp.zeros((8, 768), f32)
    for n in range(8):
        rows = jnp.concatenate([nr[n, j, 0:1, :] for j in range(4)] + [jnp.zeros((4, 128), f32)], axis=0)
        total = total + pltpu.roll(jnp.concatenate([rows, jnp.zeros((8, 640), f32)], axis=1), 96 * n, 1)
    norm_out[...] = total
    go.finish()


def run_collect(lengths, tok, wq, wo, nrm, pos):
    f32, bf16 = jnp.float32, jnp.bfloat16
    S = jax.ShapeDtypeStruct
    V = pltpu.VMEM
    return pl.pallas_call(
        collect,
        out_shape=(
            S((4, 128, 768), bf16), S((8, 96, 640), bf16), S((4, 128, 256), bf16), S((32, 128, 384), bf16),
            S((4, 8, 96, 256), bf16), S((8, 768), f32), S((32, 128, 128), f32), S((4, 8, 128), f32),
        ),
        in_specs=[HBM] * 6,
        out_specs=(VM,) * 8,
        scratch_shapes=[
            V((96, 640), bf16), V((96, 256), bf16), V((8, 4, 8, 128), f32), V((32, 128), f32),
            V((96, 576), bf16), V((192, 96), bf16), V((1, 96), bf16), V((32, 128), jnp.int32), V((8, 128), f32),
            pltpu.SMEM((8,), jnp.int32), pltpu.SemaphoreType.DMA((2, 64)), pltpu.SemaphoreType.DMA((6,)),
        ],
        compiler_params=pltpu.CompilerParams(
            collective_id=1, has_side_effects=True, vmem_limit_bytes=20 << 20
        ),
        name="collect",
    )(lengths, tok, wq, wo, nrm, pos)


def moments(rows):
    center = rows - jnp.mean(rows, axis=-1, keepdims=True)
    spread = lax.rsqrt(jnp.mean(center * center, axis=-1, keepdims=True) + 1e-05)
    return center * spread, spread


def norm_back(grad, gain, unit, spread):
    scaled = grad * gain
    return spread * (
        scaled - jnp.mean(scaled, axis=-1, keepdims=True) - unit * jnp.mean(scaled * unit, axis=-1, keepdims=True)
    )


def middle(
    mixed_ref, tok_any, og_any, norm_ref, wout_ref, gu_any, down_any,
    act_ref, done_ref, datt_ref, dheads, sgate_ref, sdown_ref, up_ref, gn_ref,
    mix_in, wffn, rows_in, drow_in, gelu_a, gelu_b, gated, dgate, dup,
    part, part_in, part2, part2_in, gff, ffn_sib, ffn_sum, ffn_in, hid, unit_one, held, held_two, head_out,
    wf_ref, tok_ref, og_ref, part_relay, part2_relay, sems, lsem,
):
    b = lax.axis_index("blk")
    z = lax.axis_index("head")
    chip, core = b // 2, b % 2
    sib = (chip * 2 + 1 - core, z)
    near = [(chip ^ r) * 2 + core for r in (0, 1, 2, 3)]
    flat = [(n, z) for n in near]
    line = [(b, z ^ r) for r in (0, 1, 2, 3)]
    f32, bf16 = jnp.float32, jnp.bfloat16
    own = [
        pltpu.make_async_copy(gu_any, wf_ref.at[0:2], lsem.at[0]),
        pltpu.make_async_copy(down_any, wf_ref.at[2], lsem.at[1]),
        pltpu.make_async_copy(tok_any, tok_ref, lsem.at[2]),
        pltpu.make_async_copy(og_any, og_ref, lsem.at[3]),
    ]
    for c in own:
        c.start()
    greet([sib] + flat[1:] + line[1:])
    go = Sender(sems)
    mid = (z == 1) | (z == 2)
    ends = (z == 0) | (z == 3)

    HALF = 64

    @pl.when(ends)
    def _():
        for h in range(2):
            part_in[h, 2] = jnp.zeros((HALF, 768), bf16)
            part2_in[h, 2] = jnp.zeros((HALF, 768), bf16)

    def scatter(out, arrived, relay, terms, h):
        passed = go(out.at[h, z ^ 3], relay.at[h], line[1], only=ends)
        three = go(out.at[h, z ^ 3], arrived.at[h, 2], line[3], only=mid)
        one = go(out.at[h, z ^ 1], arrived.at[h, 0], line[1])

        @pl.when(mid)
        def _():
            passed.wait_recv()
            out[h, z ^ 2] = (terms[h, z ^ 2] + relay[h].astype(f32)).astype(bf16)

        two = go(out.at[h, z ^ 2], arrived.at[h, 1], line[2])
        return one, two, three

    def gathered(copies):
        copies[0].wait_recv()
        copies[1].wait_recv()
        pl.when(mid)(copies[2].wait_recv)

    mix_c = []
    for h in range(2):
        rows = pl.ds(HALF * h, HALF)
        mix_c.append([go(mixed_ref.at[z ^ r, rows], mix_in.at[h, z], line[r]) for r in (3, 2, 1)])
    for c in own:
        c.wait()
    mine = pltpu.make_async_copy(wf_ref, wffn.at[:, b], lsem.at[0])
    mine.start()
    wf_p = [[go(wf_ref.at[t], wffn.at[t, b], flat[r]) for r in (3, 1, 2)] for t in range(3)]
    wf_s = [go(wf_ref, wffn.at[:, b], sib)]
    mine.wait()

    spreads = []
    row_c = []
    for h in range(2):
        rows = pl.ds(HALF * h, HALF)
        mix_in[h, z] = mixed_ref[z, rows, :]
        for c in mix_c[h]:
            c.wait_recv()
        attn = dot_nt(mix_in[h, 0], wout_ref[0])
        for j in (1, 2, 3):
            attn = attn + dot_nt(mix_in[h, j], wout_ref[j])
        unit, spread = moments(tok_ref[rows, :].astype(f32) + attn)
        hidden = unit * norm_ref[0:1, :] + norm_ref[1:2, :]
        unit_one[h] = unit
        spreads.append(spread)
        hid[h] = hidden
        rows_in[h, z] = hidden.astype(bf16)
        row_c.append(Spread(go, mid, lambda j, h=h: rows_in.at[h, j], z, line))
    row_c[0].pass_on()
    row_c[1].pass_on()
    for t in range(3):
        for k, r in enumerate((3, 1, 2)):
            wf_p[t][k].wait_recv()
            wf_s.append(go(wffn.at[t, near[r]], wffn.at[t, near[r]], sib))
    for c in wf_s:
        c.wait_recv()

    def weight(t):
        return wffn[t].reshape(768, 768)

    part_c = []
    for h in range(2):
        row_c[h].one.wait_recv()
        row_c[h].three.wait_recv()
        rows = rows_in[h].reshape(4 * HALF, 768)
        gate = jnp.dot(rows, weight(0), preferred_element_type=f32)
        up = jnp.dot(rows, weight(1), preferred_element_type=f32)
        half = 0.5 + 0.5 * lax.erf(gate * (0.5**0.5))
        value = gate * half
        slope = half + gate * jnp.exp(-0.5 * gate * gate) * 0.3989422804014327
        gelu_a[h] = slope * up
        gelu_b[h] = value
        low = (value * up).astype(bf16)
        gated[h] = low
        term = dot_nt(low, weight(2)).reshape(4, HALF, 768)
        held[h] = term
        part[h] = term.astype(bf16)
        part_c.append(scatter(part, part_in, part_relay, held, h))
    gains = []
    drow_c = []
    for h in range(2):
        rows = pl.ds(HALF * h, HALF)
        gathered(part_c[h])
        branch = held[h, z] + part_in[h, 0].astype(f32) + part_in[h, 1].astype(f32) + part_in[h, 2].astype(f32)
        unit_two, spread_two = moments(hid[h] + branch)
        grad = og_ref[rows, :].astype(f32)
        d_two = norm_back(grad, norm_ref[2:3, :], unit_two, spread_two)
        hid[h] = d_two
        drow_in[h, z] = d_two.astype(bf16)
        drow_c.append(Spread(go, mid, lambda j, h=h: drow_in.at[h, j], z, line))
        act_ref[rows, :] = (unit_two * norm_ref[2:3, :] + norm_ref[3:4, :]).astype(bf16)
        gains.append((jnp.sum(grad * unit_two, axis=0, keepdims=True), jnp.sum(grad, axis=0, keepdims=True)))
    gn_ref[...] = jnp.zeros((32, 768), f32)
    gn_ref[16:17, :] = gains[0][0] + gains[1][0]
    gn_ref[24:25, :] = gains[0][1] + gains[1][1]
    part2_c = []
    for h in range(2):
        drow_c[h].pass_on()
        drow_c[h].one.wait_recv()
        drow_c[h].three.wait_recv()
        d_gated = jnp.dot(drow_in[h].reshape(4 * HALF, 768), weight(2), preferred_element_type=f32)
        dg = (d_gated * gelu_a[h]).astype(bf16)
        du = (d_gated * gelu_b[h]).astype(bf16)
        dgate[h] = dg
        dup[h] = du
        term = (dot_nt(dg, weight(0)) + dot_nt(du, weight(1))).reshape(4, HALF, 768)
        held_two[h] = term
        part2[h] = term.astype(bf16)
        part2_c.append(scatter(part2, part2_in, part2_relay, held_two, h))
    sib_c = []
    acts = rows_in[...].reshape(512, 768)
    for t in (2, 0, 1):
        if t == 2:
            total = dot_tn(drow_in[...].reshape(512, 768), gated[...].reshape(512, 768))
        else:
            total = dot_tn(acts, (dgate, dup)[t][...].reshape(512, 768))
        gff[t] = total.astype(bf16).reshape(4, 2, 96, 768)
        sib_c.append(go(gff.at[t, :, 1 - core], ffn_sib.at[t], sib))
    ffn_c = []
    for k, t in enumerate((2, 0, 1)):
        sib_c[k].wait_recv()
        for r in (3, 1, 2, 0):
            both = (gff[t, chip ^ r, core].astype(f32) + ffn_sib[t, chip ^ r].astype(f32)).astype(bf16)
            if t == 1:
                up_ref[r] = both
                continue
            ffn_sum[t, r] = both
            if r:
                ffn_c.append(go(ffn_sum.at[t, r], ffn_in.at[t, r - 1], flat[r]))
    gains = []
    head_c = []
    for h in range(2):
        rows = pl.ds(HALF * h, HALF)
        gathered(part2_c[h])
        d_hidden = (
            hid[h] + held_two[h, z]
            + part2_in[h, 0].astype(f32) + part2_in[h, 1].astype(f32) + part2_in[h, 2].astype(f32)
        )
        unit = unit_one[h]
        d_one = norm_back(d_hidden, norm_ref[0:1, :], unit, spreads[h])
        low_one = d_one.astype(bf16)
        for r in (3, 2, 1, 0):
            term = jnp.dot(low_one, wout_ref[z ^ r], preferred_element_type=f32).astype(bf16)
            if r:
                head_out[h, r - 1] = term
                head_c.append(go(head_out.at[h, r - 1], dheads.at[z, rows], line[r]))
            else:
                dheads[z, rows, :] = term
        done_ref[rows, :] = d_one
        datt_ref[rows, :] = low_one
        gains.append((jnp.sum(d_hidden * unit, axis=0, keepdims=True), jnp.sum(d_hidden, axis=0, keepdims=True)))
    gn_ref[0:1, :] = gains[0][0] + gains[1][0]
    gn_ref[8:9, :] = gains[0][1] + gains[1][1]
    for c in ffn_c:
        c.wait_recv()
    for t, ref in ((2, sdown_ref), (0, sgate_ref)):
        ref[...] = (
            ffn_sum[t, 0].astype(f32) + ffn_in[t, 0].astype(f32) + ffn_in[t, 1].astype(f32) + ffn_in[t, 2].astype(f32)
        )
    for c in head_c:
        c.wait_recv()
    go.finish()


def run_middle(mixed, tok, og, norms, wout, gu, down):
    f32, bf16 = jnp.float32, jnp.bfloat16
    S = jax.ShapeDtypeStruct
    V = pltpu.VMEM
    halves = (2, 256, 768)
    return pl.pallas_call(
        middle,
        out_shape=(
            S((128, 768), bf16), S((128, 768), f32), S((128, 768), bf16), S((4, 128, 256), bf16),
            S((96, 768), f32), S((96, 768), f32), S((4, 96, 768), bf16), S((32, 768), f32),
        ),
        in_specs=[VM, HBM, HBM, VM, VM, HBM, HBM],
        out_specs=(VM,) * 8,
        scratch_shapes=[
            V((2, 4, 64, 256), bf16), V((3, 8, 96, 768), bf16), V((2, 4, 64, 768), bf16), V((2, 4, 64, 768), bf16),
            V(halves, f32), V(halves, f32), V(halves, bf16), V(halves, bf16), V(halves, bf16),
            V((2, 4, 64, 768), bf16), V((2, 3, 64, 768), bf16), V((2, 4, 64, 768), bf16), V((2, 3, 64, 768), bf16),
            V((3, 4, 2, 96, 768), bf16), V((3, 4, 96, 768), bf16), V((3, 4, 96, 768), bf16), V((3, 3, 96, 768), bf16),
            V((2, 64, 768), f32), V((2, 64, 768), f32), V((2, 4, 64, 768), f32), V((2, 4, 64, 768), f32),
            V((2, 3, 64, 256), bf16),
            V((3, 96, 768), bf16), V((128, 768), bf16), V((128, 768), bf16), V((2, 64, 768), bf16), V((2, 64, 768), bf16),
            pltpu.SemaphoreType.DMA((2, 84)), pltpu.SemaphoreType.DMA((4,)),
        ],
        compiler_params=pltpu.CompilerParams(
            collective_id=3, has_side_effects=True, vmem_limit_bytes=36 << 20
        ),
        name="middle",
    )(mixed, tok, og, norms, wout, gu, down)


def deliver(*refs):
    dx, sgate, sup, sqkv, sout = refs[:5]
    o_dx, o_gu, o_qkv, o_out, sem = refs[5:]
    pairs = ((dx, o_dx), (sgate, o_gu.at[0]), (sup, o_gu.at[1]), (sqkv, o_qkv), (sout, o_out))
    copies = [pltpu.make_async_copy(s, d, sem.at[i]) for i, (s, d) in enumerate(pairs)]
    for c in copies:
        c.start()
    for c in copies:
        c.wait()


def run_deliver(*arrays):
    f32 = jnp.float32
    S = jax.ShapeDtypeStruct
    return pl.pallas_call(
        deliver,
        out_shape=(S((128, 768), f32), S((2, 96, 768), f32), S((96, 576), f32), S((192, 96), f32)),
        in_specs=[ANY] * 5,
        out_specs=(ANY,) * 4,
        scratch_shapes=[pltpu.SemaphoreType.DMA((5,))],
        compiler_params=pltpu.CompilerParams(vmem_limit_bytes=1 << 20),
        name="deliver",
    )(*arrays)


PACK = (1, 4, 2, 5, 7, 8, 0, 3, 6, 9)


def fast_shards(
    tokens, w_qkv, w_out, w_gate_up, w_down, norm_params, alibi_slope, lengths, placement, out_grad
):
    heads_n = lax.axis_size("head")
    blk_n = lax.axis_size("blk")
    head_idx = lax.axis_index("head")
    blk_idx = lax.axis_index("blk")
    tok_rows, width = tokens.shape
    per_dev = HEADS // heads_n
    group_rows = heads_n * tok_rows
    devs = heads_n * blk_n
    share = w_qkv.shape[0]
    bf16 = jnp.bfloat16

    group_tokens, attn_w, q, kv, wout, norms, kcode, qcode = run_collect(
        lengths, tokens, w_qkv, w_out, norm_params.reshape(1, share), placement.reshape(devs, tok_rows)
    )
    mixed, lse = run_attend(lengths, alibi_slope, q, kv, kcode, qcode)
    act, d_one, d_attn, d_heads, s_gate, s_down, up_sum, g_norm = run_middle(
        mixed, tokens, out_grad, norms, wout.reshape(heads_n, width, 256), w_gate_up, w_down.T
    )
    d_q, dkv, result, s_down = run_attend_back(
        lengths, alibi_slope, q, kv, kcode, qcode, mixed, d_heads, lse, act, s_down
    )
    input_grad, s_qkv, s_out, s_norm, s_up = run_finish(
        dkv.reshape(blk_n, group_rows, 384), d_q.reshape(group_rows, 256),
        group_tokens.reshape(group_rows, width), attn_w.reshape(width, 640),
        d_attn, mixed.reshape(group_rows, 256), d_one, g_norm, up_sum,
    )
    input_grad, s_gu, s_qkv, s_out = run_deliver(input_grad, s_gate, s_up, s_qkv, s_out)
    return (
        result,
        input_grad,
        s_qkv,
        s_out,
        s_gu,
        s_down.T,
        s_norm[0, :share].reshape(share, 1),
    )


def solution(mesh):
    placed = (
        P(("blk", "head"), None),
        P("blk", "head"),
        P("head", "blk"),
        P(None, "blk", "head"),
        P("head", "blk"),
        P("blk", "head"),
        P(),
        P(),
        P(),
        P(("blk", "head"), None),
    )
    small = mesh.shape["blk"] == 8 and mesh.shape["head"] == 4
    return jax.shard_map(
        fast_shards if small else shards,
        mesh=mesh,
        in_specs=placed,
        out_specs=(
            P(("blk", "head"), None),
            P(("blk", "head"), None),
            P("blk", "head"),
            P("head", "blk"),
            P(None, "blk", "head"),
            P("head", "blk"),
            P("blk", "head"),
        ),
        check_vma=False,
    )
```

```python
import jax
import jax.numpy as jnp
from jax import lax
from jax.experimental import pallas as pl
from jax.experimental.pallas import tpu as pltpu
from jax.sharding import PartitionSpec as P

HEADS = 12
HEAD_DIM = 64


masked_score = -1e30


def layer_norm(residual, norm_gain, norm_shift):
    center = residual - jnp.mean(residual, axis=-1, keepdims=True)
    spread = jnp.mean(center * center, axis=-1, keepdims=True)
    return center * lax.rsqrt(spread + 1e-05) * norm_gain + norm_shift


def geglu(gate, upward):
    return jax.nn.gelu(gate, approximate=False) * upward


def dot_back(grad_rows, weight):
    return lax.dot_general(
        grad_rows, weight, (((1,), (1,)), ((), ())), preferred_element_type=jnp.float32
    )


def weight_grad(left, right):
    return lax.dot_general(
        left, right, (((0,), (0,)), ((), ())), preferred_element_type=jnp.float32
    )


def seq_of(positions, seq_ends):
    return jnp.sum((positions[:, None] >= seq_ends[None, :]).astype(jnp.int32), axis=1)


def prefix_sums(lengths):
    count = lengths.shape[0]
    upto = jnp.arange(count)[None, :] <= jnp.arange(count)[:, None]
    return jnp.sum(jnp.where(upto, lengths[None, :], 0), axis=1)


def biased_scores(queries, key_rows, q_pos, k_pos, q_seq, k_seq, slopes, qk_scale):
    scores = (
        jnp.einsum("qhd,khd->hqk", queries, key_rows, preferred_element_type=jnp.float32) * qk_scale
    )
    distance = jnp.abs(q_pos[:, None] - k_pos[None, :]).astype(jnp.float32)
    scores = scores - slopes[:, None, None] * distance[None]
    same_seq = (q_seq[:, None] == k_seq[None, :])[None]
    return (scores, same_seq)


def shards(
    tokens, w_qkv, w_out, w_gate_up, w_down, norm_params, alibi_slope, lengths, placement, out_grad
):
    heads_n = lax.axis_size("head")
    head_idx = lax.axis_index("head")
    blk_idx = lax.axis_index("blk")
    tok_rows = tokens.shape[0]
    per_dev = HEADS // heads_n
    group_rows = heads_n * tok_rows
    qk_scale = HEAD_DIM ** (-0.5)
    group_tokens, norm_cols = (
        lax.all_gather(tokens, "head", axis=0, tiled=True),
        lax.all_gather(norm_params, "head", axis=1, tiled=True),
    )
    f_qkv, f_out, f_gu, f_down, f_norm = (
        lax.all_gather(w_qkv, "blk", axis=0, tiled=True),
        lax.all_gather(w_out, "blk", axis=1, tiled=True),
        lax.all_gather(w_gate_up, "blk", axis=1, tiled=True),
        lax.all_gather(w_down, "blk", axis=1, tiled=True),
        lax.all_gather(norm_cols, "blk", axis=0, tiled=True),
    )
    grouped = jnp.dot(group_tokens, f_qkv, preferred_element_type=jnp.float32).astype(jnp.bfloat16)
    grouped = grouped.reshape(group_rows, per_dev, 3, HEAD_DIM)
    norms = f_norm.astype(jnp.float32)
    queries = grouped[:, :, 0]
    key_rows = grouped[:, :, 1]
    values = grouped[:, :, 2]
    seq_ends = prefix_sums(lengths)
    q_pos = lax.dynamic_slice_in_dim(placement, blk_idx * group_rows, group_rows)
    q_seq = seq_of(q_pos, seq_ends)
    slopes = lax.dynamic_slice_in_dim(alibi_slope, head_idx * per_dev, per_dev)

    def split_rows(shard_part):
        block_count = shard_part[0].shape[0] // group_rows
        pieces = tuple(
            (arr.reshape((block_count, group_rows) + arr.shape[1:]) for arr in shard_part)
        )
        starts = group_rows * jnp.arange(block_count, dtype=jnp.int32)
        return pieces + (starts,)

    start_state = (
        jnp.full((per_dev, group_rows), masked_score, jnp.float32),
        jnp.zeros((per_dev, group_rows), jnp.float32),
        jnp.zeros((group_rows, per_dev, HEAD_DIM), jnp.float32),
    )
    running = start_state

    def forward_per_block(state, block_in):
        k_blk, v_blk, k_first = block_in
        row_best, row_total, out_sum = state
        k_pos = lax.dynamic_slice_in_dim(placement, k_first, group_rows)
        scores, same_seq = biased_scores(
            queries, k_blk, q_pos, k_pos, q_seq, seq_of(k_pos, seq_ends), slopes, qk_scale
        )
        row_top = jnp.max(jnp.where(same_seq, scores, masked_score), axis=2)
        new_best = jnp.maximum(row_best, row_top)
        factor = jnp.exp(row_best - new_best)
        prob_tile = jnp.where(same_seq, jnp.exp(scores - new_best[:, :, None]), 0.0)
        row_total = row_total * factor + jnp.sum(prob_tile, axis=2)
        out_sum = out_sum * factor.T[:, :, None] + jnp.einsum(
            "hqk,khd->qhd",
            prob_tile.astype(jnp.bfloat16),
            v_blk,
            preferred_element_type=jnp.float32,
        )
        return ((new_best, row_total, out_sum), None)

    running, _ = lax.scan(
        forward_per_block,
        running,
        split_rows(
            (
                lax.all_gather(key_rows, "blk", axis=0, tiled=True),
                lax.all_gather(values, "blk", axis=0, tiled=True),
            )
        ),
    )
    row_best, row_total, out_sum = running
    attended = (out_sum / row_total.T[:, :, None]).astype(jnp.bfloat16)
    log_total = row_best + jnp.log(row_total)
    mixed = attended.reshape(group_rows, per_dev * HEAD_DIM)
    attn_out = lax.psum_scatter(
        jnp.dot(mixed, f_out, preferred_element_type=jnp.float32).astype(jnp.bfloat16),
        "head",
        scatter_dimension=0,
        tiled=True,
    ).astype(jnp.float32)
    resid_one = tokens.astype(jnp.float32) + attn_out
    hidden, norm_one_back = jax.vjp(layer_norm, resid_one, norms[:, 0], norms[:, 1])
    hidden_low = hidden.astype(jnp.bfloat16)
    ffn_rows = lax.all_gather(hidden_low, "head", axis=0, tiled=True)
    gate = jnp.dot(ffn_rows, f_gu[0], preferred_element_type=jnp.float32)
    upward = jnp.dot(ffn_rows, f_gu[1], preferred_element_type=jnp.float32)
    gated, geglu_back = jax.vjp(geglu, gate, upward)
    gated_low = gated.astype(jnp.bfloat16)
    branch_part = jnp.dot(gated_low, f_down, preferred_element_type=jnp.float32)
    branch = lax.psum_scatter(
        branch_part.astype(jnp.bfloat16), "head", scatter_dimension=0, tiled=True
    ).astype(jnp.float32)
    result, norm_two_back = jax.vjp(layer_norm, hidden + branch, norms[:, 2], norms[:, 3])
    d_two, d_gain_two, d_shift_two = norm_two_back(out_grad.astype(jnp.float32))
    d_branch = d_two.astype(jnp.bfloat16)
    branch_rows = lax.all_gather(d_branch, "head", axis=0, tiled=True)
    g_down = weight_grad(gated_low, branch_rows)
    d_gate, d_up = geglu_back(dot_back(branch_rows, f_down))
    d_gate_low = d_gate.astype(jnp.bfloat16)
    d_up_low = d_up.astype(jnp.bfloat16)
    g_gate_up = jnp.stack([weight_grad(ffn_rows, d_gate_low), weight_grad(ffn_rows, d_up_low)])
    hidden_part = dot_back(d_gate_low, f_gu[0]) + dot_back(d_up_low, f_gu[1])
    d_hidden = d_two + lax.psum_scatter(
        hidden_part.astype(jnp.bfloat16), "head", scatter_dimension=0, tiled=True
    ).astype(jnp.float32)
    d_one, d_gain_one, d_shift_one = norm_one_back(d_hidden)
    d_attn = d_one.astype(jnp.bfloat16)
    attn_rows = lax.all_gather(d_attn, "head", axis=0, tiled=True)
    g_out = weight_grad(mixed, attn_rows)
    d_heads = dot_back(attn_rows, f_out).astype(jnp.bfloat16).reshape(group_rows, per_dev, HEAD_DIM)
    delta = jnp.sum(d_heads.astype(jnp.float32) * attended.astype(jnp.float32), axis=2).T
    zero_grad = jnp.zeros((group_rows, per_dev, HEAD_DIM), jnp.float32)
    grad_q = zero_grad

    def query_per_block(running, block_in):
        k_blk, v_blk, k_first = block_in
        k_pos = lax.dynamic_slice_in_dim(placement, k_first, group_rows)
        scores, same_seq = biased_scores(
            queries, k_blk, q_pos, k_pos, q_seq, seq_of(k_pos, seq_ends), slopes, qk_scale
        )
        prob_tile = jnp.where(same_seq, jnp.exp(scores - log_total[:, :, None]), 0.0)
        d_prob = jnp.einsum("qhd,khd->hqk", d_heads, v_blk, preferred_element_type=jnp.float32)
        d_score = (prob_tile * (d_prob - delta[:, :, None])).astype(jnp.bfloat16)
        running = (
            running
            + jnp.einsum("hqk,khd->qhd", d_score, k_blk, preferred_element_type=jnp.float32)
            * qk_scale
        )
        return (running, None)

    grad_q, _ = lax.scan(
        query_per_block,
        grad_q,
        split_rows(
            (
                lax.all_gather(key_rows, "blk", axis=0, tiled=True),
                lax.all_gather(values, "blk", axis=0, tiled=True),
            )
        ),
    )
    stats_lse, stats_delta = (
        lax.all_gather(log_total, "blk", axis=1, tiled=True),
        lax.all_gather(delta, "blk", axis=1, tiled=True),
    )
    running = (zero_grad, zero_grad)

    def key_per_block(state, block_in):
        q_blk, do_blk, q_first = block_in
        grad_k, grad_v = state
        other_pos = lax.dynamic_slice_in_dim(placement, q_first, group_rows)
        lse_blk = lax.dynamic_slice_in_dim(stats_lse, q_first, group_rows, 1)
        delta_blk = lax.dynamic_slice_in_dim(stats_delta, q_first, group_rows, 1)
        scores, same_seq = biased_scores(
            q_blk, key_rows, other_pos, q_pos, seq_of(other_pos, seq_ends), q_seq, slopes, qk_scale
        )
        prob_tile = jnp.where(same_seq, jnp.exp(scores - lse_blk[:, :, None]), 0.0)
        grad_v = grad_v + jnp.einsum(
            "hqk,qhd->khd",
            prob_tile.astype(jnp.bfloat16),
            do_blk,
            preferred_element_type=jnp.float32,
        )
        d_prob = jnp.einsum("qhd,khd->hqk", do_blk, values, preferred_element_type=jnp.float32)
        d_score = (prob_tile * (d_prob - delta_blk[:, :, None])).astype(jnp.bfloat16)
        grad_k = (
            grad_k
            + jnp.einsum("hqk,qhd->khd", d_score, q_blk, preferred_element_type=jnp.float32)
            * qk_scale
        )
        return ((grad_k, grad_v), None)

    running, _ = lax.scan(
        key_per_block,
        running,
        split_rows(
            (
                lax.all_gather(queries, "blk", axis=0, tiled=True),
                lax.all_gather(d_heads, "blk", axis=0, tiled=True),
            )
        ),
    )
    grad_k, grad_v = running
    d_grouped = jnp.stack([grad_q, grad_k, grad_v], axis=2).astype(jnp.bfloat16)
    g_norm = jnp.stack([d_gain_one, d_shift_one, d_gain_two, d_shift_two], axis=1)
    d_qkv = d_grouped.reshape(group_rows, per_dev * 3 * HEAD_DIM)
    g_qkv = weight_grad(group_tokens, d_qkv)
    input_sum, norm_share = (
        lax.psum_scatter(
            dot_back(d_qkv, f_qkv).astype(jnp.bfloat16), "head", scatter_dimension=0, tiled=True
        ).astype(jnp.float32),
        lax.psum_scatter(
            g_norm.astype(jnp.bfloat16), "head", scatter_dimension=1, tiled=True
        ).astype(jnp.float32),
    )
    input_grad = d_one + input_sum
    s_qkv, s_out, s_gu, s_down, s_norm = (
        lax.psum_scatter(g_qkv, "blk", scatter_dimension=0, tiled=True),
        lax.psum_scatter(g_out, "blk", scatter_dimension=1, tiled=True),
        lax.psum_scatter(g_gate_up, "blk", scatter_dimension=1, tiled=True),
        lax.psum_scatter(g_down, "blk", scatter_dimension=1, tiled=True),
        lax.psum_scatter(norm_share, "blk", scatter_dimension=0, tiled=True),
    )
    return (result.astype(jnp.bfloat16), input_grad, s_qkv, s_out, s_gu, s_down, s_norm)


Q_SLOTS = 32
K_SLOTS = 16
SEQ_STEP = 65536.0
FAR = 32768.0
LANE_OF = (0, 64, 192)


def by_head(rows, lanes):
    lane = lax.broadcasted_iota(jnp.int32, rows.shape, 1)
    parts = [jnp.where((lane >= first) & (lane < first + HEAD_DIM), rows, 0.0) for first in lanes]
    return jnp.concatenate(parts, axis=0).astype(jnp.bfloat16)


def by_head_turned(rows, lanes):
    turned = rows.T
    lane = lax.broadcasted_iota(jnp.int32, turned.shape, 0)
    parts = [jnp.where((lane >= first) & (lane < first + HEAD_DIM), turned, 0.0) for first in lanes]
    return jnp.concatenate(parts, axis=1).astype(jnp.bfloat16)


def key_tiles(kv_ref, j):
    rows = kv_ref.shape[0] * K_SLOTS
    blk = kv_ref[:, pl.ds(pl.multiple_of(j * K_SLOTS, K_SLOTS), K_SLOTS), :]
    return blk.reshape(rows, blk.shape[2])


def key_span(len_ref, i, devs):
    first = i * (Q_SLOTS * devs)
    last = first + Q_SLOTS * devs - 1
    end, low, high = 0, 0, 0
    for k in range(8):
        start = end
        end = end + len_ref[k]
        low = jnp.where((first >= start) & (first < end), start, low)
        high = jnp.where((last >= start) & (last < end), end, high)
    step = K_SLOTS * devs
    return low // step, (high + step - 1) // step


def attend(len_any, slope_any, q_ref, kv_ref, kcode_ref, qcode_ref, out_ref, lse_ref, vt_ref, len_ref, slope_ref, few):
    z = lax.axis_index("head")
    scalars = [
        pltpu.make_async_copy(len_any, len_ref, few.at[0]),
        pltpu.make_async_copy(slope_any, slope_ref, few.at[1]),
    ]
    for c in scalars:
        c.start()
    devs, slots, _ = kv_ref.shape
    rows = devs * K_SLOTS
    q_rows = q_ref.shape[0] * Q_SLOTS

    def turn(j, _):
        kv = key_tiles(kv_ref, j)[:, 128:384]
        vt_ref[j] = kv.T
        return 0

    lax.fori_loop(0, slots // K_SLOTS, turn, 0)
    for c in scalars:
        c.wait()

    def chunk(i, _):
        first = pl.multiple_of(i * Q_SLOTS, Q_SLOTS)
        q = q_ref[:, pl.ds(first, Q_SLOTS), :].reshape(q_rows, 256).astype(jnp.float32)
        qbt = by_head_turned(q, (0, 64, 128))
        qcode = qcode_ref[i, 0:1, :]
        lo, hi = key_span(len_ref, i, devs)

        def block(j, state):
            kv = key_tiles(kv_ref, j)
            keys = jnp.concatenate([kv[:, 0:128], kv[:, 256:384]], axis=1)
            s_all = jnp.dot(keys, qbt, preferred_element_type=jnp.float32)
            dist = jnp.abs(key_tiles(kcode_ref, j) - qcode)
            keep = dist < FAR
            fresh, ps = [], []
            for h in range(3):
                best, total, acc = state[h]
                s = jnp.where(keep, s_all[:, 128 * h : 128 * h + 128] - slope_ref[3 * z + h] * dist, masked_score)
                top = jnp.maximum(best, jnp.max(s, axis=0, keepdims=True))
                factor = jnp.exp(best - top)
                p = jnp.exp(s - top)
                total = total * factor + jnp.sum(p, axis=0, keepdims=True)
                ps.append(p.astype(jnp.bfloat16))
                fresh.append((top, total, acc * factor))
            both = jnp.dot(vt_ref[j, 0:128, :], jnp.concatenate(ps[0:2], axis=1), preferred_element_type=jnp.float32)
            last = jnp.dot(vt_ref[j, 192:256, :], ps[2], preferred_element_type=jnp.float32)
            new = (both[0:64, 0:128], both[64:128, 128:256], last)
            fresh = [(top, total, acc + term) for (top, total, acc), term in zip(fresh, new)]
            return tuple(fresh)

        start = tuple(
            (
                jnp.full((1, q_rows), masked_score, jnp.float32),
                jnp.zeros((1, q_rows), jnp.float32),
                jnp.zeros((64, q_rows), jnp.float32),
            )
            for _ in range(3)
        )
        done = lax.fori_loop(lo, hi, block, start)
        outs = [acc / total for _, total, acc in done]
        full = jnp.concatenate([outs[0], outs[1], jnp.zeros((64, q_rows), jnp.float32), outs[2]], axis=0)
        out_ref[:, pl.ds(first, Q_SLOTS), :] = full.T.astype(jnp.bfloat16).reshape(-1, Q_SLOTS, 256)
        for h in range(3):
            lse_ref[i, h : h + 1, :] = done[h][0] + jnp.log(done[h][1])
        return 0

    lax.fori_loop(0, slots // Q_SLOTS, chunk, 0)


def attend_back(len_any, slope_any, q_ref, kv_ref, kcode_ref, qcode_ref, out_ref, do_ref, lse_ref, act_any, sdown_any,
                dq_ref, dkv_ref, act_out, sdown_out, kt_ref, sum_ref, sem, len_ref, slope_ref, few):
    z = lax.axis_index("head")
    scalars = [
        pltpu.make_async_copy(len_any, len_ref, few.at[0]),
        pltpu.make_async_copy(slope_any, slope_ref, few.at[1]),
    ]
    for c in scalars:
        c.start()
    devs, slots, _ = kv_ref.shape
    rows = devs * K_SLOTS
    q_rows = q_ref.shape[0] * Q_SLOTS
    scale = HEAD_DIM ** (-0.5)
    along = [
        pltpu.make_async_copy(act_any, act_out, sem.at[0]),
        pltpu.make_async_copy(sdown_any, sdown_out, sem.at[1]),
    ]
    for c in along:
        c.start()

    def turn(j, _):
        kv = key_tiles(kv_ref, j)
        keys = jnp.concatenate([kv[:, 0:128], kv[:, 256:384]], axis=1)
        kt_ref[j] = keys.T
        sum_ref[j] = jnp.zeros((rows, 384), jnp.float32)
        return 0

    lax.fori_loop(0, slots // K_SLOTS, turn, 0)
    for c in scalars:
        c.wait()

    def chunk(i, _):
        first = pl.multiple_of(i * Q_SLOTS, Q_SLOTS)
        q = q_ref[:, pl.ds(first, Q_SLOTS), :].reshape(q_rows, 256).astype(jnp.float32)
        qbd = by_head(q, (0, 64, 128))
        qbt = by_head_turned(q, (0, 64, 128))
        do = do_ref[:, pl.ds(first, Q_SLOTS), :].reshape(q_rows, 256).astype(jnp.float32)
        out = out_ref[:, pl.ds(first, Q_SLOTS), :].reshape(q_rows, 256).astype(jnp.float32)
        dobd = by_head(do, LANE_OF)
        dobt = by_head_turned(do, LANE_OF)
        prod = (do * out).T
        delta = [jnp.sum(prod[f : f + 64, :], axis=0, keepdims=True) for f in LANE_OF]
        qcode = qcode_ref[i, 0:1, :]
        lo, hi = key_span(len_ref, i, devs)

        def block(j, state):
            kv = key_tiles(kv_ref, j)
            keys = jnp.concatenate([kv[:, 0:128], kv[:, 256:384]], axis=1)
            vals = kv[:, 128:384]
            s_all = jnp.dot(keys, qbt, preferred_element_type=jnp.float32)
            dp_all = jnp.dot(vals, dobt, preferred_element_type=jnp.float32)
            dist = jnp.abs(key_tiles(kcode_ref, j) - qcode)
            keep = dist < FAR
            ps, dss, fresh = [], [], []
            for h in range(3):
                s = s_all[:, 128 * h : 128 * h + 128] - slope_ref[3 * z + h] * dist - lse_ref[i, h : h + 1, :]
                p = jnp.exp(jnp.where(keep, s, masked_score))
                ds = (p * (dp_all[:, 128 * h : 128 * h + 128] - delta[h])).astype(jnp.bfloat16)
                ps.append(p.astype(jnp.bfloat16))
                dss.append(ds)
            both = jnp.dot(kt_ref[j, 0:128, :], jnp.concatenate(dss[0:2], axis=1), preferred_element_type=jnp.float32)
            last = jnp.dot(kt_ref[j, 128:192, :], dss[2], preferred_element_type=jnp.float32)
            fresh = [state[0] + both[0:64, 0:128], state[1] + both[64:128, 128:256], state[2] + last]
            dv = jnp.dot(jnp.concatenate(ps, axis=1), dobd, preferred_element_type=jnp.float32)
            dk = jnp.dot(jnp.concatenate(dss, axis=1), qbd, preferred_element_type=jnp.float32)
            sum_ref[j, :, 0:128] += dk[:, 0:128]
            sum_ref[j, :, 128:256] += dv[:, 0:128]
            sum_ref[j, :, 256:384] += dk[:, 128:256] + dv[:, 128:256]
            return tuple(fresh)

        start = tuple(jnp.zeros((64, q_rows), jnp.float32) for _ in range(3))
        done = lax.fori_loop(lo, hi, block, start)
        full = jnp.concatenate(done + (jnp.zeros((64, q_rows), jnp.float32),), axis=0) * scale
        dq_ref[:, pl.ds(first, Q_SLOTS), :] = full.T.astype(jnp.bfloat16).reshape(-1, Q_SLOTS, 256)
        return 0

    lax.fori_loop(0, slots // Q_SLOTS, chunk, 0)

    def leave(j, _):
        dkv_ref[:, pl.ds(pl.multiple_of(j * K_SLOTS, K_SLOTS), K_SLOTS), :] = (
            sum_ref[j].astype(jnp.bfloat16).reshape(devs, K_SLOTS, 384)
        )
        return 0

    lax.fori_loop(0, slots // K_SLOTS, leave, 0)
    for c in along:
        c.wait()


VM = pl.BlockSpec(memory_space=pltpu.VMEM)
SM = pl.BlockSpec(memory_space=pltpu.SMEM)
ANY = pl.BlockSpec(memory_space=pl.ANY)
HBM = pl.BlockSpec(memory_space=pltpu.MemorySpace.HBM)


def run_attend(lengths, slopes, q, kv, kcode, qcode):
    heads_n, slots, _ = q.shape
    devs = kv.shape[0]
    return pl.pallas_call(
        attend,
        out_shape=(
            jax.ShapeDtypeStruct((heads_n, slots, 256), jnp.bfloat16),
            jax.ShapeDtypeStruct((slots // Q_SLOTS, 8, heads_n * Q_SLOTS), jnp.float32),
        ),
        in_specs=[HBM, HBM, VM, VM, VM, VM],
        out_specs=(VM, VM),
        scratch_shapes=[
            pltpu.VMEM((slots // K_SLOTS, 256, devs * K_SLOTS), jnp.bfloat16),
            pltpu.SMEM((8,), jnp.int32),
            pltpu.SMEM((HEADS,), jnp.float32),
            pltpu.SemaphoreType.DMA((2,)),
        ],
        compiler_params=pltpu.CompilerParams(vmem_limit_bytes=16 << 20),
        name="attend",
    )(lengths, slopes, q, kv, kcode, qcode)


def run_attend_back(lengths, slopes, q, kv, kcode, qcode, out, do, lse, act, s_down):
    heads_n, slots, _ = q.shape
    devs = kv.shape[0]
    return pl.pallas_call(
        attend_back,
        out_shape=(
            jax.ShapeDtypeStruct((heads_n, slots, 256), jnp.bfloat16),
            jax.ShapeDtypeStruct((devs, slots, 384), jnp.bfloat16),
            jax.ShapeDtypeStruct(act.shape, act.dtype),
            jax.ShapeDtypeStruct(s_down.shape, s_down.dtype),
        ),
        in_specs=[HBM, HBM, VM, VM, VM, VM, VM, VM, VM, ANY, ANY],
        out_specs=(VM, VM, ANY, ANY),
        scratch_shapes=[
            pltpu.VMEM((slots // K_SLOTS, 256, devs * K_SLOTS), jnp.bfloat16),
            pltpu.VMEM((slots // K_SLOTS, devs * K_SLOTS, 384), jnp.float32),
            pltpu.SemaphoreType.DMA((2,)),
            pltpu.SMEM((8,), jnp.int32),
            pltpu.SMEM((HEADS,), jnp.float32),
            pltpu.SemaphoreType.DMA((2,)),
        ],
        compiler_params=pltpu.CompilerParams(vmem_limit_bytes=26 << 20),
        name="attend_back",
    )(lengths, slopes, q, kv, kcode, qcode, out, do, lse, act, s_down)


MESH = pl.DeviceIdType.MESH


def dot_tn(left, right):
    return lax.dot_general(left, right, (((0,), (0,)), ((), ())), preferred_element_type=jnp.float32)


def dot_nt(left, right):
    return lax.dot_general(left, right, (((1,), (1,)), ((), ())), preferred_element_type=jnp.float32)


def greet(peers):
    barrier = pltpu.get_barrier_semaphore()
    for peer in peers:
        pl.semaphore_signal(barrier, inc=1, device_id=peer, device_id_type=MESH)
    pl.semaphore_wait(barrier, len(peers))


class Sender:
    def __init__(self, sems):
        self.sems = sems
        self.used = 0
        self.left = []

    def make(self, src, dst, peer, arrive=None):
        i = self.used
        self.used += 1
        assert i < self.sems.shape[1]
        copy = pltpu.make_async_remote_copy(
            src_ref=src, dst_ref=dst, send_sem=self.sems.at[0, i],
            recv_sem=self.sems.at[1, i] if arrive is None else arrive,
            device_id=peer, device_id_type=MESH,
        )
        copy.arrive = self.sems.at[1, i]
        return copy

    def start(self, copy, only=None):
        self.left.append((copy, only))
        if only is None:
            copy.start()
        else:
            pl.when(only)(copy.start)
        return copy

    def __call__(self, src, dst, peer, only=None, arrive=None):
        return self.start(self.make(src, dst, peer, arrive), only)

    def sent(self, copy):
        [(_, only)] = [item for item in self.left if item[0] is copy]
        self.left = [item for item in self.left if item[0] is not copy]
        if only is None:
            copy.wait_send()
        else:
            pl.when(only)(copy.wait_send)

    def finish(self):
        for copy, only in self.left:
            if only is None:
                copy.wait_send()
            else:
                pl.when(only)(copy.wait_send)


class Plane:
    def __init__(self, go, core, slot, me, near, flat, sib):
        self.go, self.core, self.slot, self.near, self.flat, self.sib = go, core, slot, near, flat, sib
        self.one = go(slot(me), slot(me), flat[1])
        self.two = go(slot(me), slot(me), flat[2])
        self.three = go.make(slot(me), slot(me), flat[3])
        self.handed = [self.hand(me)]

    def hand(self, n):
        return self.go(self.slot(n), self.slot(n), self.sib)

    def pass_on(self):
        for copy, r, turn in ((self.one, 1, 0), (self.two, 2, 1)):
            copy.wait_recv()
            block = self.slot(self.near[r])
            self.go(block, block, self.flat[3 - r], only=self.core == turn, arrive=self.three.arrive)
            self.handed.append(self.hand(self.near[r]))

    def last(self):
        self.three.wait_recv()
        self.handed.append(self.hand(self.near[3]))

    def whole(self):
        for copy in self.handed:
            copy.wait_recv()


class Spread:
    def __init__(self, go, mid, slot, z, line):
        self.go, self.mid, self.slot, self.z, self.line = go, mid, slot, z, line
        self.two = go(slot(z), slot(z), line[2])
        self.three = go.make(slot(z), slot(z), line[3])
        self.one = go.make(slot(z), slot(z), line[1])

    def rest(self):
        self.go.start(self.three, only=self.mid)
        self.go.start(self.one)

    def pass_on(self):
        self.two.wait_recv()
        far = self.slot(self.z ^ 2)
        self.go(far, far, self.line[1], only=self.mid, arrive=self.three.arrive)

    def wait(self):
        self.one.wait_recv()
        self.three.wait_recv()


def finish(
    dkv_ref, dq_ref, tok_ref, w_ref, datt_ref, mixed_ref, done_ref, gn_ref, up_ref,
    dx_ref, sqkv_ref, sout_ref, snorm_ref, sup_ref,
    up_in, kv_sib, kv_sum, kv_in, g_one, g_two, g_sib, g_sum, g_in,
    part, part_in, att, dkvq, nz_in, nrow, np_in, relay, sems,
):
    b = lax.axis_index("blk")
    z = lax.axis_index("head")
    chip, core = b // 2, b % 2
    sib = (chip * 2 + 1 - core, z)
    flat = [((chip ^ r) * 2 + core, z) for r in (0, 1, 2, 3)]
    line = [(b, z ^ r) for r in (0, 1, 2, 3)]
    greet([sib] + flat[1:] + line[1:])
    f32, bf16 = jnp.float32, jnp.bfloat16
    go = Sender(sems)
    mid = (z == 1) | (z == 2)
    ends = (z == 0) | (z == 3)

    def member(r):
        return pl.ds(pl.multiple_of((z ^ r) * 128, 128), 128)

    kv_c = {
        (q, r): go(dkv_ref.at[(chip ^ r) * 2 + 1 - core, member(q)], kv_sib.at[q, r], sib)
        for q in (3, 2, 1, 0) for r in (3, 1, 2, 0)
    }
    att[z] = datt_ref[...]
    att_c = Spread(go, mid, lambda j: att.at[j], z, line)
    att_c.rest()
    nz_c = [go(gn_ref.at[pl.ds((z ^ r) * 8, 8)], nz_in.at[r - 1], line[r]) for r in (1, 2, 3)]
    kv_out = {}
    for q in (3, 2, 1, 0):
        for r in (3, 1, 2, 0):
            kv_c[q, r].wait_recv()
            both = dkv_ref[(chip ^ r) * 2 + core, member(q), :].astype(f32) + kv_sib[q, r].astype(f32)
            kv_sum[q, r] = both.astype(bf16)
            if r:
                kv_out[q, r] = go(kv_sum.at[q, r], kv_in.at[q, r - 1], flat[r])
    dkvq[:, 384:640] = dq_ref[...]

    @pl.when(ends)
    def _():
        relay[...] = jnp.zeros((128, 768), bf16)
        part_in[2] = jnp.zeros((128, 768), bf16)

    up_c = [go(up_ref.at[r], up_in.at[r - 1], flat[r]) for r in (3, 1, 2)]

    def send_half(part_i, grads):
        return [
            go(grads.at[pl.ds(pl.multiple_of(((chip ^ r) * 2 + 1 - core) * 96, 96), 96)], g_sib.at[part_i, r], sib)
            for r in (3, 1, 2, 0)
        ]

    def send_sum(part_i, grads, copies):
        out = []
        for k, r in enumerate((3, 1, 2, 0)):
            copies[k].wait_recv()
            mine = grads[pl.ds(pl.multiple_of(((chip ^ r) * 2 + core) * 96, 96), 96), :].astype(f32)
            g_sum[part_i, r] = (mine + g_sib[part_i, r].astype(f32)).astype(bf16)
            if r:
                out.append(go(g_sum.at[part_i, r], g_in.at[part_i, r - 1], flat[r]))
        return out

    def settle(part_i, copies):
        for c in copies:
            c.wait_recv()
        return (
            g_sum[part_i, 0].astype(f32) + g_in[part_i, 0].astype(f32)
            + g_in[part_i, 1].astype(f32) + g_in[part_i, 2].astype(f32)
        )

    att_c.pass_on()
    for c in nz_c:
        c.wait_recv()
    nrow[0] = gn_ref[pl.ds(z * 8, 8)] + nz_in[0] + nz_in[1] + nz_in[2]
    np_c = [go(nrow.at[0], np_in.at[r], flat[r]) for r in (1, 2, 3)]
    last = dot_tn(tok_ref[...], dq_ref[...])
    g_one[:, 0:128] = last[:, 0:128].astype(bf16)
    dx_c = []
    for q in (3, 2, 1, 0):
        for r in (1, 2, 3):
            kv_out[q, r].wait_recv()
        dkvq[member(q), 0:384] = (
            kv_sum[q, 0].astype(f32) + kv_in[q, 0].astype(f32) + kv_in[q, 1].astype(f32) + kv_in[q, 2].astype(f32)
        ).astype(bf16)
        term = dot_nt(dkvq[member(q), :], w_ref[...])
        if q == 3:
            part[2] = term.astype(bf16)
            passed = go(part.at[2], relay, line[1], only=ends)
            dx_three = go(part.at[2], part_in.at[2], line[3], only=mid)
        elif q == 2:
            far = term
        elif q == 1:
            part[0] = term.astype(bf16)
            dx_c.append(go(part.at[0], part_in.at[0], line[1]))
            pl.when(mid)(passed.wait_recv)
            part[1] = (far + relay[...].astype(f32)).astype(bf16)
            dx_c.append(go(part.at[1], part_in.at[1], line[2]))
        else:
            dx_ref[...] = done_ref[...] + term
    g_two[...] = dot_tn(tok_ref[...], dkvq[:, 0:384]).astype(bf16)
    two_c = send_half(1, g_two)
    att_c.one.wait_recv()
    att_c.three.wait_recv()
    outs = dot_tn(att[...].reshape(512, 768), mixed_ref[...])
    g_one[:, 128:256] = outs[:, 0:128].astype(bf16)
    g_one[:, 256:384] = (outs[:, 128:256] + last[:, 128:256]).astype(bf16)
    one_c = send_half(0, g_one)
    two_out = send_sum(1, g_two, two_c)
    one_out = send_sum(0, g_one, one_c)
    for c in np_c:
        c.wait_recv()
    nrow[1] = nrow[0] + np_in[1] + np_in[2] + np_in[3]
    half = go(nrow.at[1], np_in.at[0], sib)
    half.wait_recv()
    full = nrow[1] + np_in[0]
    snorm_ref[...] = pltpu.roll(full, lax.rem(768 - 96 * b, 768), 1)[:, 0:128]
    for c in up_c:
        c.wait_recv()
    sup_ref[...] = up_ref[0].astype(f32) + up_in[0].astype(f32) + up_in[1].astype(f32) + up_in[2].astype(f32)
    two = settle(1, two_out)
    one = settle(0, one_out)
    piece = [two[:, 64 * i : 64 * i + 64] for i in range(6)]
    piece += [one[:, 0:64], one[:, 64:128], one[:, 256:320]]
    for k, i in enumerate((6, 0, 2, 7, 1, 3, 8, 4, 5)):
        sqkv_ref[:, 64 * k : 64 * k + 64] = piece[i]
    turned = jnp.concatenate([one[:, 128:384], jnp.zeros((32, 256), f32)], axis=0).T
    sout_ref[0:128, :] = turned[0:128, 0:96]
    sout_ref[128:192, :] = turned[192:256, 0:96]
    for c in dx_c:
        c.wait_recv()
    pl.when(mid)(dx_three.wait_recv)
    dx_ref[...] += part_in[0].astype(f32) + part_in[1].astype(f32) + part_in[2].astype(f32)
    go.finish()


def run_finish(dkv, dq, toks, w, datt, mixed, done, gn, up):
    f32, bf16 = jnp.float32, jnp.bfloat16
    V = pltpu.VMEM
    return pl.pallas_call(
        finish,
        out_shape=(
            jax.ShapeDtypeStruct((128, 768), f32),
            jax.ShapeDtypeStruct((96, 576), f32),
            jax.ShapeDtypeStruct((192, 96), f32),
            jax.ShapeDtypeStruct((8, 128), f32),
            jax.ShapeDtypeStruct((96, 768), f32),
        ),
        in_specs=[VM] * 9,
        out_specs=(VM,) * 5,
        scratch_shapes=[
            V((3, 96, 768), bf16),
            V((4, 4, 128, 384), bf16), V((4, 4, 128, 384), bf16), V((4, 3, 128, 384), bf16),
            V((768, 384), bf16), V((768, 384), bf16),
            V((2, 4, 96, 384), bf16), V((2, 4, 96, 384), bf16), V((2, 3, 96, 384), bf16),
            V((3, 128, 768), bf16), V((3, 128, 768), bf16), V((4, 128, 768), bf16), V((512, 640), bf16),
            V((3, 8, 768), f32), V((2, 8, 768), f32), V((4, 8, 768), f32), V((128, 768), bf16),
            pltpu.SemaphoreType.DMA((2, 72)),
        ],
        compiler_params=pltpu.CompilerParams(
            collective_id=5, has_side_effects=True, vmem_limit_bytes=28 << 20
        ),
        name="finish",
    )(dkv, dq, toks, w, datt, mixed, done, gn, up)


def collect(
    len_any, tok_any, wq_any, wout_any, nrm_any, pos_any,
    gt, wat, q_ref, kv, wout, norm_out, kcode, qcode,
    wa_ref, wo_ref, nr, code_ref, wq_ref, wout_ref, nrm_row, pos_ref, nrm_ref, len_ref, sems, lsem,
):
    b = lax.axis_index("blk")
    z = lax.axis_index("head")
    chip, core = b // 2, b % 2
    sib = (chip * 2 + 1 - core, z)
    near = [(chip ^ r) * 2 + core for r in (0, 1, 2, 3)]
    flat = [(n, z) for n in near]
    line = [(b, z ^ r) for r in (0, 1, 2, 3)]
    f32, bf16 = jnp.float32, jnp.bfloat16
    fetch = [
        pltpu.make_async_copy(wq_any, wq_ref, lsem.at[0]),
        pltpu.make_async_copy(wout_any, wout_ref, lsem.at[1]),
        pltpu.make_async_copy(nrm_any, nrm_row, lsem.at[2]),
        pltpu.make_async_copy(pos_any, pos_ref, lsem.at[3]),
        pltpu.make_async_copy(tok_any, gt.at[z], lsem.at[4]),
        pltpu.make_async_copy(len_any, len_ref, lsem.at[5]),
    ]
    for c in fetch:
        c.start()
    for c in fetch:
        c.wait()
    go = Sender(sems)
    mid = (z == 1) | (z == 2)
    ends = (z == 0) | (z == 3)

    wq = wq_ref[...].astype(f32)
    wo = wout_ref[...].astype(f32)
    wo = jnp.concatenate([wo[0:128], jnp.zeros((64, 96), f32), wo[128:192]], axis=0)
    wo = jnp.concatenate([wo, jnp.zeros((256, 32), f32)], axis=1).T[0:96]
    wo_ref[...] = wo.astype(bf16)
    piece = [wq[:, 64 * i : 64 * i + 64] for i in range(9)] + [wo[:, 192:256]]
    for k in range(5):
        tile = jnp.concatenate([piece[PACK[2 * k]], piece[PACK[2 * k + 1]]], axis=1)
        wa_ref[:, 128 * k : 128 * k + 128] = tile.astype(bf16)
    wat[b] = wa_ref[...]
    wout[z] = wo_ref[...]
    nrm_ref[...] = jnp.zeros((8, 128), f32)
    nrm_ref[0:1, 0:96] = nrm_row[...].astype(f32)
    nr[b, z] = nrm_ref[...]
    greet([sib] + flat[1:] + line[1:])
    tok_z = [Spread(go, mid, lambda j, h=h: gt.at[j, pl.ds(64 * h, 64)], z, line) for h in range(2)]
    wa_p = [go(wa_ref, wat.at[b], flat[r]) for r in (3, 1, 2)]
    wa_s = [go(wa_ref, wat.at[b], sib)]
    pos = pos_ref[...]
    seq = jnp.zeros(pos.shape, f32)
    end = 0
    for k in range(8):
        end = end + len_ref[k]
        seq = seq + jnp.where(pos >= end, 1.0, 0.0)
    code_ref[...] = pos.astype(f32) + SEQ_STEP * seq

    def spread_code(d, _):
        kcode[d] = jnp.broadcast_to(code_ref[pl.ds(d, 1), :], (128, 128)).T
        return 0

    lax.fori_loop(0, 32, spread_code, 0)
    own_code = [code_ref[pl.ds(b * 4 + j, 1), :] for j in range(4)]
    for i in range(4):
        qcode[i, 0:1, :] = jnp.concatenate([c[:, 32 * i : 32 * i + 32] for c in own_code], axis=1)
    go.sent(tok_z[0].two)
    tok_z[0].rest()
    tok_z[0].pass_on()
    go.sent(tok_z[1].two)
    tok_z[1].rest()
    wo_z = [go(wo_ref, wout.at[z], line[r]) for r in (3, 2, 1)]
    nr_z = [go(nrm_ref, nr.at[b, z], line[r]) for r in (3, 2, 1)]
    for k, r in enumerate((3, 1, 2)):
        wa_p[k].wait_recv()
        wa_s.append(go(wat.at[near[r]], wat.at[near[r]], sib))
    tok_z[1].pass_on()
    for c in wa_s:
        c.wait_recv()
    kv_p = []
    for r in (0, 2, 1, 3):
        for s in tok_z:
            if r in (1, 3):
                (s.one if r == 1 else s.three).wait_recv()
        j = z ^ r
        rows = jnp.dot(gt[j], wat[...].reshape(768, 640), preferred_element_type=f32)
        kv[b * 4 + j] = rows[:, 0:384].astype(bf16)
        kv_p.append(Plane(go, core, lambda n, j=j: kv.at[n * 4 + j], b, near, flat, sib))
        q_ref[j] = rows[:, 384:640].astype(bf16) * bf16(HEAD_DIM ** (-0.5))
        if r:
            kv_p[-2].pass_on()
        if r == 1:
            for c in wo_z + nr_z:
                c.wait_recv()
            nr_p = [go(nr.at[b], nr.at[b], flat[r]) for r in (3, 1, 2)]
            passed = [go(nr.at[b], nr.at[b], sib)]
    for k, r in enumerate((3, 1, 2)):
        nr_p[k].wait_recv()
        passed.append(go(nr.at[near[r]], nr.at[near[r]], sib))
    kv_p[3].pass_on()
    for p in kv_p:
        p.last()
    for p in kv_p:
        p.whole()
    for c in passed:
        c.wait_recv()
    total = jnp.zeros((8, 768), f32)
    for n in range(8):
        rows = jnp.concatenate([nr[n, j, 0:1, :] for j in range(4)] + [jnp.zeros((4, 128), f32)], axis=0)
        total = total + pltpu.roll(jnp.concatenate([rows, jnp.zeros((8, 640), f32)], axis=1), 96 * n, 1)
    norm_out[...] = total
    go.finish()


def run_collect(lengths, tok, wq, wo, nrm, pos):
    f32, bf16 = jnp.float32, jnp.bfloat16
    S = jax.ShapeDtypeStruct
    V = pltpu.VMEM
    return pl.pallas_call(
        collect,
        out_shape=(
            S((4, 128, 768), bf16), S((8, 96, 640), bf16), S((4, 128, 256), bf16), S((32, 128, 384), bf16),
            S((4, 96, 256), bf16), S((8, 768), f32), S((32, 128, 128), f32), S((4, 8, 128), f32),
        ),
        in_specs=[HBM] * 6,
        out_specs=(VM,) * 8,
        scratch_shapes=[
            V((96, 640), bf16), V((96, 256), bf16), V((8, 4, 8, 128), f32), V((32, 128), f32),
            V((96, 576), bf16), V((192, 96), bf16), V((1, 96), bf16), V((32, 128), jnp.int32), V((8, 128), f32),
            pltpu.SMEM((8,), jnp.int32), pltpu.SemaphoreType.DMA((2, 80)), pltpu.SemaphoreType.DMA((6,)),
        ],
        compiler_params=pltpu.CompilerParams(
            collective_id=1, has_side_effects=True, vmem_limit_bytes=20 << 20
        ),
        name="collect",
    )(lengths, tok, wq, wo, nrm, pos)


def moments(rows):
    center = rows - jnp.mean(rows, axis=-1, keepdims=True)
    spread = lax.rsqrt(jnp.mean(center * center, axis=-1, keepdims=True) + 1e-05)
    return center * spread, spread


def norm_back(grad, gain, unit, spread):
    scaled = grad * gain
    return spread * (
        scaled - jnp.mean(scaled, axis=-1, keepdims=True) - unit * jnp.mean(scaled * unit, axis=-1, keepdims=True)
    )


def middle(
    mixed_ref, tok_any, og_any, norm_ref, wo_0, wo_1, wo_2, wo_3, gu_any, down_any,
    act_ref, done_ref, datt_ref, dheads, sgate_ref, sdown_ref, up_ref, gn_ref,
    mix_in, wffn, rows_in, drow_in, gelu_a, gelu_b, gated, dgate, dup,
    part, part_in, part2, part2_in, gff, ffn_sib, ffn_sum, ffn_in, hid, unit_one, held, held_two, head_out,
    wf_ref, tok_ref, og_ref, wout, part_relay, part2_relay, sems, lsem,
):
    b = lax.axis_index("blk")
    z = lax.axis_index("head")
    chip, core = b // 2, b % 2
    sib = (chip * 2 + 1 - core, z)
    near = [(chip ^ r) * 2 + core for r in (0, 1, 2, 3)]
    flat = [(n, z) for n in near]
    line = [(b, z ^ r) for r in (0, 1, 2, 3)]
    f32, bf16 = jnp.float32, jnp.bfloat16
    own = [
        pltpu.make_async_copy(gu_any, wf_ref.at[0:2], lsem.at[0]),
        pltpu.make_async_copy(down_any, wf_ref.at[2], lsem.at[1]),
        pltpu.make_async_copy(tok_any, tok_ref, lsem.at[2]),
        pltpu.make_async_copy(og_any, og_ref, lsem.at[3]),
    ]
    for c in own:
        c.start()
    greet([sib] + flat[1:] + line[1:])
    go = Sender(sems)
    mid = (z == 1) | (z == 2)
    ends = (z == 0) | (z == 3)

    HALF = 64

    def scatter(out, arrived, relay, terms, h):
        return [go(out.at[h, z ^ r], arrived.at[h, r - 1], line[r]) for r in (3, 2, 1)]

    def gathered(copies):
        for c in copies:
            c.wait_recv()

    wo_s = []
    for r, ref in enumerate((wo_0, wo_1, wo_2, wo_3)):
        wo_s.append(go(ref, wout.at[:, near[r]], sib))
        wout[:, near[r]] = ref[...]
    mix_c = []
    for h in range(2):
        rows = pl.ds(HALF * h, HALF)
        mix_c.append([go(mixed_ref.at[z ^ r, rows], mix_in.at[h, z], line[r]) for r in (3, 2, 1)])
    for c in own:
        c.wait()
    mine = pltpu.make_async_copy(wf_ref, wffn.at[:, b], lsem.at[0])
    mine.start()
    mine.wait()
    wf_p = [Plane(go, core, lambda n, t=t: wffn.at[t, n], b, near, flat, sib) for t in range(3)]

    for c in wo_s:
        c.wait_recv()

    def out_weight(j):
        return wout[j].reshape(768, 256)

    spreads = []
    row_c = []
    for h in range(2):
        rows = pl.ds(HALF * h, HALF)
        mix_in[h, z] = mixed_ref[z, rows, :]
        for c in mix_c[h]:
            c.wait_recv()
        attn = dot_nt(mix_in[h, 0], out_weight(0))
        for j in (1, 2, 3):
            attn = attn + dot_nt(mix_in[h, j], out_weight(j))
        unit, spread = moments(tok_ref[rows, :].astype(f32) + attn)
        hidden = unit * norm_ref[0:1, :] + norm_ref[1:2, :]
        unit_one[h] = unit
        spreads.append(spread)
        hid[h] = hidden
        rows_in[h, z] = hidden.astype(bf16)
        row_c.append(Spread(go, mid, lambda j, h=h: rows_in.at[h, j], z, line))
        if h == 1:
            row_c[0].rest()
        wf_p[h].pass_on()
    row_c[0].pass_on()
    row_c[1].rest()
    wf_p[2].pass_on()
    row_c[1].pass_on()
    for p in wf_p:
        p.last()
    wf_p[0].whole()
    wf_p[1].whole()

    def weight(t):
        return wffn[t].reshape(768, 768)

    part_c = []
    for h in range(2):
        row_c[h].wait()
        rows = rows_in[h].reshape(4 * HALF, 768)
        gate = jnp.dot(rows, weight(0), preferred_element_type=f32)
        up = jnp.dot(rows, weight(1), preferred_element_type=f32)
        half = 0.5 + 0.5 * lax.erf(gate * (0.5**0.5))
        value = gate * half
        slope = half + gate * jnp.exp(-0.5 * gate * gate) * 0.3989422804014327
        gelu_a[h] = slope * up
        gelu_b[h] = value
        low = (value * up).astype(bf16)
        gated[h] = low
        if h == 0:
            wf_p[2].whole()
        term = dot_nt(low, weight(2)).reshape(4, HALF, 768)
        held[h] = term
        part[h] = term.astype(bf16)
        part_c.append(scatter(part, part_in, part_relay, held, h))
    gains = []
    drow_c = []
    for h in range(2):
        rows = pl.ds(HALF * h, HALF)
        gathered(part_c[h])
        branch = held[h, z] + part_in[h, 0].astype(f32) + part_in[h, 1].astype(f32) + part_in[h, 2].astype(f32)
        unit_two, spread_two = moments(hid[h] + branch)
        grad = og_ref[rows, :].astype(f32)
        d_two = norm_back(grad, norm_ref[2:3, :], unit_two, spread_two)
        hid[h] = d_two
        drow_in[h, z] = d_two.astype(bf16)
        drow_c.append(Spread(go, mid, lambda j, h=h: drow_in.at[h, j], z, line))
        act_ref[rows, :] = (unit_two * norm_ref[2:3, :] + norm_ref[3:4, :]).astype(bf16)
        gains.append((jnp.sum(grad * unit_two, axis=0, keepdims=True), jnp.sum(grad, axis=0, keepdims=True)))
        drow_c[h].rest()
    gn_ref[...] = jnp.zeros((32, 768), f32)
    gn_ref[16:17, :] = gains[0][0] + gains[1][0]
    gn_ref[24:25, :] = gains[0][1] + gains[1][1]
    part2_c = []
    for h in range(2):
        drow_c[h].pass_on()
        drow_c[h].wait()
        d_gated = jnp.dot(drow_in[h].reshape(4 * HALF, 768), weight(2), preferred_element_type=f32)
        dg = (d_gated * gelu_a[h]).astype(bf16)
        du = (d_gated * gelu_b[h]).astype(bf16)
        dgate[h] = dg
        dup[h] = du
        term = (dot_nt(dg, weight(0)) + dot_nt(du, weight(1))).reshape(4, HALF, 768)
        held_two[h] = term
        part2[h] = term.astype(bf16)
        part2_c.append(scatter(part2, part2_in, part2_relay, held_two, h))
    sib_c = []
    acts = rows_in[...].reshape(512, 768)
    for t in (2, 0, 1):
        if t == 2:
            total = dot_tn(drow_in[...].reshape(512, 768), gated[...].reshape(512, 768))
        else:
            total = dot_tn(acts, (dgate, dup)[t][...].reshape(512, 768))
        gff[t] = total.astype(bf16).reshape(4, 2, 96, 768)
        sib_c.append(go(gff.at[t, :, 1 - core], ffn_sib.at[t], sib))
    ffn_c = []
    for k, t in enumerate((2, 0, 1)):
        sib_c[k].wait_recv()
        for r in (3, 1, 2, 0):
            both = (gff[t, chip ^ r, core].astype(f32) + ffn_sib[t, chip ^ r].astype(f32)).astype(bf16)
            if t == 1:
                up_ref[r] = both
                continue
            ffn_sum[t, r] = both
            if r:
                ffn_c.append(go(ffn_sum.at[t, r], ffn_in.at[t, r - 1], flat[r]))
    gains = []
    head_c = []
    for h in range(2):
        rows = pl.ds(HALF * h, HALF)
        gathered(part2_c[h])
        d_hidden = (
            hid[h] + held_two[h, z]
            + part2_in[h, 0].astype(f32) + part2_in[h, 1].astype(f32) + part2_in[h, 2].astype(f32)
        )
        unit = unit_one[h]
        d_one = norm_back(d_hidden, norm_ref[0:1, :], unit, spreads[h])
        low_one = d_one.astype(bf16)
        for r in (3, 2, 1, 0):
            term = jnp.dot(low_one, out_weight(z ^ r), preferred_element_type=f32).astype(bf16)
            if r:
                head_out[h, r - 1] = term
                head_c.append(go(head_out.at[h, r - 1], dheads.at[z, rows], line[r]))
            else:
                dheads[z, rows, :] = term
        done_ref[rows, :] = d_one
        datt_ref[rows, :] = low_one
        gains.append((jnp.sum(d_hidden * unit, axis=0, keepdims=True), jnp.sum(d_hidden, axis=0, keepdims=True)))
    gn_ref[0:1, :] = gains[0][0] + gains[1][0]
    gn_ref[8:9, :] = gains[0][1] + gains[1][1]
    for c in ffn_c:
        c.wait_recv()
    for t, ref in ((2, sdown_ref), (0, sgate_ref)):
        ref[...] = (
            ffn_sum[t, 0].astype(f32) + ffn_in[t, 0].astype(f32) + ffn_in[t, 1].astype(f32) + ffn_in[t, 2].astype(f32)
        )
    for c in head_c:
        c.wait_recv()
    go.finish()


def run_middle(mixed, tok, og, norms, wo, gu, down):
    f32, bf16 = jnp.float32, jnp.bfloat16
    S = jax.ShapeDtypeStruct
    V = pltpu.VMEM
    halves = (2, 256, 768)
    return pl.pallas_call(
        middle,
        out_shape=(
            S((128, 768), bf16), S((128, 768), f32), S((128, 768), bf16), S((4, 128, 256), bf16),
            S((96, 768), f32), S((96, 768), f32), S((4, 96, 768), bf16), S((32, 768), f32),
        ),
        in_specs=[VM, HBM, HBM, VM, VM, VM, VM, VM, HBM, HBM],
        out_specs=(VM,) * 8,
        scratch_shapes=[
            V((2, 4, 64, 256), bf16), V((3, 8, 96, 768), bf16), V((2, 4, 64, 768), bf16), V((2, 4, 64, 768), bf16),
            V(halves, f32), V(halves, f32), V(halves, bf16), V(halves, bf16), V(halves, bf16),
            V((2, 4, 64, 768), bf16), V((2, 3, 64, 768), bf16), V((2, 4, 64, 768), bf16), V((2, 3, 64, 768), bf16),
            V((3, 4, 2, 96, 768), bf16), V((3, 4, 96, 768), bf16), V((3, 4, 96, 768), bf16), V((3, 3, 96, 768), bf16),
            V((2, 64, 768), f32), V((2, 64, 768), f32), V((2, 4, 64, 768), f32), V((2, 4, 64, 768), f32),
            V((2, 3, 64, 256), bf16),
            V((3, 96, 768), bf16), V((128, 768), bf16), V((128, 768), bf16), V((4, 8, 96, 256), bf16), V((2, 64, 768), bf16), V((2, 64, 768), bf16),
            pltpu.SemaphoreType.DMA((2, 108)), pltpu.SemaphoreType.DMA((4,)),
        ],
        compiler_params=pltpu.CompilerParams(
            collective_id=3, has_side_effects=True, vmem_limit_bytes=36 << 20
        ),
        name="middle",
    )(mixed, tok, og, norms, *wo, gu, down)


def deliver(*refs):
    dx, sgate, sup, sqkv, sout = refs[:5]
    o_dx, o_gu, o_qkv, o_out, sem = refs[5:]
    pairs = ((dx, o_dx), (sgate, o_gu.at[0]), (sup, o_gu.at[1]), (sqkv, o_qkv), (sout, o_out))
    copies = [pltpu.make_async_copy(s, d, sem.at[i]) for i, (s, d) in enumerate(pairs)]
    for c in copies:
        c.start()
    for c in copies:
        c.wait()


def run_deliver(*arrays):
    f32 = jnp.float32
    S = jax.ShapeDtypeStruct
    return pl.pallas_call(
        deliver,
        out_shape=(S((128, 768), f32), S((2, 96, 768), f32), S((96, 576), f32), S((192, 96), f32)),
        in_specs=[ANY] * 5,
        out_specs=(ANY,) * 4,
        scratch_shapes=[pltpu.SemaphoreType.DMA((5,))],
        compiler_params=pltpu.CompilerParams(vmem_limit_bytes=1 << 20),
        name="deliver",
    )(*arrays)


PACK = (1, 4, 2, 5, 7, 8, 0, 3, 6, 9)


def fast_shards(
    tokens, w_qkv, w_out, w_gate_up, w_down, norm_params, alibi_slope, lengths, placement, out_grad
):
    heads_n = lax.axis_size("head")
    blk_n = lax.axis_size("blk")
    head_idx = lax.axis_index("head")
    blk_idx = lax.axis_index("blk")
    tok_rows, width = tokens.shape
    per_dev = HEADS // heads_n
    group_rows = heads_n * tok_rows
    devs = heads_n * blk_n
    share = w_qkv.shape[0]
    bf16 = jnp.bfloat16

    held = [
        pltpu.with_memory_space_constraint(a, pltpu.MemorySpace.HBM)
        for a in (lengths, alibi_slope, tokens, w_qkv, w_out, norm_params.reshape(1, share), placement.reshape(devs, tok_rows))
    ]
    group_tokens, attn_w, q, kv, wo, norms, kcode, qcode = run_collect(held[0], *held[2:])
    wo = [wo] + [lax.ppermute(wo, "blk", [(i, i ^ (2 * r)) for i in range(blk_n)]) for r in (1, 2, 3)]
    mixed, lse = run_attend(held[0], held[1], q, kv, kcode, qcode)
    act, d_one, d_attn, d_heads, s_gate, s_down, up_sum, g_norm = run_middle(
        mixed, tokens, out_grad, norms, wo, w_gate_up, w_down.T
    )
    d_q, dkv, result, s_down = run_attend_back(
        held[0], held[1], q, kv, kcode, qcode, mixed, d_heads, lse, act, s_down
    )
    input_grad, s_qkv, s_out, s_norm, s_up = run_finish(
        dkv.reshape(blk_n, group_rows, 384), d_q.reshape(group_rows, 256),
        group_tokens.reshape(group_rows, width), attn_w.reshape(width, 640),
        d_attn, mixed.reshape(group_rows, 256), d_one, g_norm, up_sum,
    )
    input_grad, s_gu, s_qkv, s_out = run_deliver(input_grad, s_gate, s_up, s_qkv, s_out)
    return (
        result,
        input_grad,
        s_qkv,
        s_out,
        s_gu,
        s_down.T,
        s_norm[0, :share].reshape(share, 1),
    )


def solution(mesh):
    placed = (
        P(("blk", "head"), None),
        P("blk", "head"),
        P("head", "blk"),
        P(None, "blk", "head"),
        P("head", "blk"),
        P("blk", "head"),
        P(),
        P(),
        P(),
        P(("blk", "head"), None),
    )
    small = mesh.shape["blk"] == 8 and mesh.shape["head"] == 4
    return jax.shard_map(
        fast_shards if small else shards,
        mesh=mesh,
        in_specs=placed,
        out_specs=(
            P(("blk", "head"), None),
            P(("blk", "head"), None),
            P("blk", "head"),
            P("head", "blk"),
            P(None, "blk", "head"),
            P("head", "blk"),
            P("blk", "head"),
        ),
        check_vma=False,
    )
```

```python
import jax
import jax.numpy as jnp
from jax import lax
from jax.experimental import pallas as pl
from jax.experimental.pallas import tpu as pltpu
from jax.sharding import PartitionSpec as P

HEADS = 12
HEAD_DIM = 64


masked_score = -1e30


def layer_norm(residual, norm_gain, norm_shift):
    center = residual - jnp.mean(residual, axis=-1, keepdims=True)
    spread = jnp.mean(center * center, axis=-1, keepdims=True)
    return center * lax.rsqrt(spread + 1e-05) * norm_gain + norm_shift


def geglu(gate, upward):
    return jax.nn.gelu(gate, approximate=False) * upward


def dot_back(grad_rows, weight):
    return lax.dot_general(
        grad_rows, weight, (((1,), (1,)), ((), ())), preferred_element_type=jnp.float32
    )


def weight_grad(left, right):
    return lax.dot_general(
        left, right, (((0,), (0,)), ((), ())), preferred_element_type=jnp.float32
    )


def seq_of(positions, seq_ends):
    return jnp.sum((positions[:, None] >= seq_ends[None, :]).astype(jnp.int32), axis=1)


def prefix_sums(lengths):
    count = lengths.shape[0]
    upto = jnp.arange(count)[None, :] <= jnp.arange(count)[:, None]
    return jnp.sum(jnp.where(upto, lengths[None, :], 0), axis=1)


def biased_scores(queries, key_rows, q_pos, k_pos, q_seq, k_seq, slopes, qk_scale):
    scores = (
        jnp.einsum("qhd,khd->hqk", queries, key_rows, preferred_element_type=jnp.float32) * qk_scale
    )
    distance = jnp.abs(q_pos[:, None] - k_pos[None, :]).astype(jnp.float32)
    scores = scores - slopes[:, None, None] * distance[None]
    same_seq = (q_seq[:, None] == k_seq[None, :])[None]
    return (scores, same_seq)


def shards(
    tokens, w_qkv, w_out, w_gate_up, w_down, norm_params, alibi_slope, lengths, placement, out_grad
):
    heads_n = lax.axis_size("head")
    head_idx = lax.axis_index("head")
    blk_idx = lax.axis_index("blk")
    tok_rows = tokens.shape[0]
    per_dev = HEADS // heads_n
    group_rows = heads_n * tok_rows
    qk_scale = HEAD_DIM ** (-0.5)
    group_tokens, norm_cols = (
        lax.all_gather(tokens, "head", axis=0, tiled=True),
        lax.all_gather(norm_params, "head", axis=1, tiled=True),
    )
    f_qkv, f_out, f_gu, f_down, f_norm = (
        lax.all_gather(w_qkv, "blk", axis=0, tiled=True),
        lax.all_gather(w_out, "blk", axis=1, tiled=True),
        lax.all_gather(w_gate_up, "blk", axis=1, tiled=True),
        lax.all_gather(w_down, "blk", axis=1, tiled=True),
        lax.all_gather(norm_cols, "blk", axis=0, tiled=True),
    )
    grouped = jnp.dot(group_tokens, f_qkv, preferred_element_type=jnp.float32).astype(jnp.bfloat16)
    grouped = grouped.reshape(group_rows, per_dev, 3, HEAD_DIM)
    norms = f_norm.astype(jnp.float32)
    queries = grouped[:, :, 0]
    key_rows = grouped[:, :, 1]
    values = grouped[:, :, 2]
    seq_ends = prefix_sums(lengths)
    q_pos = lax.dynamic_slice_in_dim(placement, blk_idx * group_rows, group_rows)
    q_seq = seq_of(q_pos, seq_ends)
    slopes = lax.dynamic_slice_in_dim(alibi_slope, head_idx * per_dev, per_dev)

    def split_rows(shard_part):
        block_count = shard_part[0].shape[0] // group_rows
        pieces = tuple(
            (arr.reshape((block_count, group_rows) + arr.shape[1:]) for arr in shard_part)
        )
        starts = group_rows * jnp.arange(block_count, dtype=jnp.int32)
        return pieces + (starts,)

    start_state = (
        jnp.full((per_dev, group_rows), masked_score, jnp.float32),
        jnp.zeros((per_dev, group_rows), jnp.float32),
        jnp.zeros((group_rows, per_dev, HEAD_DIM), jnp.float32),
    )
    running = start_state

    def forward_per_block(state, block_in):
        k_blk, v_blk, k_first = block_in
        row_best, row_total, out_sum = state
        k_pos = lax.dynamic_slice_in_dim(placement, k_first, group_rows)
        scores, same_seq = biased_scores(
            queries, k_blk, q_pos, k_pos, q_seq, seq_of(k_pos, seq_ends), slopes, qk_scale
        )
        row_top = jnp.max(jnp.where(same_seq, scores, masked_score), axis=2)
        new_best = jnp.maximum(row_best, row_top)
        factor = jnp.exp(row_best - new_best)
        prob_tile = jnp.where(same_seq, jnp.exp(scores - new_best[:, :, None]), 0.0)
        row_total = row_total * factor + jnp.sum(prob_tile, axis=2)
        out_sum = out_sum * factor.T[:, :, None] + jnp.einsum(
            "hqk,khd->qhd",
            prob_tile.astype(jnp.bfloat16),
            v_blk,
            preferred_element_type=jnp.float32,
        )
        return ((new_best, row_total, out_sum), None)

    running, _ = lax.scan(
        forward_per_block,
        running,
        split_rows(
            (
                lax.all_gather(key_rows, "blk", axis=0, tiled=True),
                lax.all_gather(values, "blk", axis=0, tiled=True),
            )
        ),
    )
    row_best, row_total, out_sum = running
    attended = (out_sum / row_total.T[:, :, None]).astype(jnp.bfloat16)
    log_total = row_best + jnp.log(row_total)
    mixed = attended.reshape(group_rows, per_dev * HEAD_DIM)
    attn_out = lax.psum_scatter(
        jnp.dot(mixed, f_out, preferred_element_type=jnp.float32).astype(jnp.bfloat16),
        "head",
        scatter_dimension=0,
        tiled=True,
    ).astype(jnp.float32)
    resid_one = tokens.astype(jnp.float32) + attn_out
    hidden, norm_one_back = jax.vjp(layer_norm, resid_one, norms[:, 0], norms[:, 1])
    hidden_low = hidden.astype(jnp.bfloat16)
    ffn_rows = lax.all_gather(hidden_low, "head", axis=0, tiled=True)
    gate = jnp.dot(ffn_rows, f_gu[0], preferred_element_type=jnp.float32)
    upward = jnp.dot(ffn_rows, f_gu[1], preferred_element_type=jnp.float32)
    gated, geglu_back = jax.vjp(geglu, gate, upward)
    gated_low = gated.astype(jnp.bfloat16)
    branch_part = jnp.dot(gated_low, f_down, preferred_element_type=jnp.float32)
    branch = lax.psum_scatter(
        branch_part.astype(jnp.bfloat16), "head", scatter_dimension=0, tiled=True
    ).astype(jnp.float32)
    result, norm_two_back = jax.vjp(layer_norm, hidden + branch, norms[:, 2], norms[:, 3])
    d_two, d_gain_two, d_shift_two = norm_two_back(out_grad.astype(jnp.float32))
    d_branch = d_two.astype(jnp.bfloat16)
    branch_rows = lax.all_gather(d_branch, "head", axis=0, tiled=True)
    g_down = weight_grad(gated_low, branch_rows)
    d_gate, d_up = geglu_back(dot_back(branch_rows, f_down))
    d_gate_low = d_gate.astype(jnp.bfloat16)
    d_up_low = d_up.astype(jnp.bfloat16)
    g_gate_up = jnp.stack([weight_grad(ffn_rows, d_gate_low), weight_grad(ffn_rows, d_up_low)])
    hidden_part = dot_back(d_gate_low, f_gu[0]) + dot_back(d_up_low, f_gu[1])
    d_hidden = d_two + lax.psum_scatter(
        hidden_part.astype(jnp.bfloat16), "head", scatter_dimension=0, tiled=True
    ).astype(jnp.float32)
    d_one, d_gain_one, d_shift_one = norm_one_back(d_hidden)
    d_attn = d_one.astype(jnp.bfloat16)
    attn_rows = lax.all_gather(d_attn, "head", axis=0, tiled=True)
    g_out = weight_grad(mixed, attn_rows)
    d_heads = dot_back(attn_rows, f_out).astype(jnp.bfloat16).reshape(group_rows, per_dev, HEAD_DIM)
    delta = jnp.sum(d_heads.astype(jnp.float32) * attended.astype(jnp.float32), axis=2).T
    zero_grad = jnp.zeros((group_rows, per_dev, HEAD_DIM), jnp.float32)
    grad_q = zero_grad

    def query_per_block(running, block_in):
        k_blk, v_blk, k_first = block_in
        k_pos = lax.dynamic_slice_in_dim(placement, k_first, group_rows)
        scores, same_seq = biased_scores(
            queries, k_blk, q_pos, k_pos, q_seq, seq_of(k_pos, seq_ends), slopes, qk_scale
        )
        prob_tile = jnp.where(same_seq, jnp.exp(scores - log_total[:, :, None]), 0.0)
        d_prob = jnp.einsum("qhd,khd->hqk", d_heads, v_blk, preferred_element_type=jnp.float32)
        d_score = (prob_tile * (d_prob - delta[:, :, None])).astype(jnp.bfloat16)
        running = (
            running
            + jnp.einsum("hqk,khd->qhd", d_score, k_blk, preferred_element_type=jnp.float32)
            * qk_scale
        )
        return (running, None)

    grad_q, _ = lax.scan(
        query_per_block,
        grad_q,
        split_rows(
            (
                lax.all_gather(key_rows, "blk", axis=0, tiled=True),
                lax.all_gather(values, "blk", axis=0, tiled=True),
            )
        ),
    )
    stats_lse, stats_delta = (
        lax.all_gather(log_total, "blk", axis=1, tiled=True),
        lax.all_gather(delta, "blk", axis=1, tiled=True),
    )
    running = (zero_grad, zero_grad)

    def key_per_block(state, block_in):
        q_blk, do_blk, q_first = block_in
        grad_k, grad_v = state
        other_pos = lax.dynamic_slice_in_dim(placement, q_first, group_rows)
        lse_blk = lax.dynamic_slice_in_dim(stats_lse, q_first, group_rows, 1)
        delta_blk = lax.dynamic_slice_in_dim(stats_delta, q_first, group_rows, 1)
        scores, same_seq = biased_scores(
            q_blk, key_rows, other_pos, q_pos, seq_of(other_pos, seq_ends), q_seq, slopes, qk_scale
        )
        prob_tile = jnp.where(same_seq, jnp.exp(scores - lse_blk[:, :, None]), 0.0)
        grad_v = grad_v + jnp.einsum(
            "hqk,qhd->khd",
            prob_tile.astype(jnp.bfloat16),
            do_blk,
            preferred_element_type=jnp.float32,
        )
        d_prob = jnp.einsum("qhd,khd->hqk", do_blk, values, preferred_element_type=jnp.float32)
        d_score = (prob_tile * (d_prob - delta_blk[:, :, None])).astype(jnp.bfloat16)
        grad_k = (
            grad_k
            + jnp.einsum("hqk,qhd->khd", d_score, q_blk, preferred_element_type=jnp.float32)
            * qk_scale
        )
        return ((grad_k, grad_v), None)

    running, _ = lax.scan(
        key_per_block,
        running,
        split_rows(
            (
                lax.all_gather(queries, "blk", axis=0, tiled=True),
                lax.all_gather(d_heads, "blk", axis=0, tiled=True),
            )
        ),
    )
    grad_k, grad_v = running
    d_grouped = jnp.stack([grad_q, grad_k, grad_v], axis=2).astype(jnp.bfloat16)
    g_norm = jnp.stack([d_gain_one, d_shift_one, d_gain_two, d_shift_two], axis=1)
    d_qkv = d_grouped.reshape(group_rows, per_dev * 3 * HEAD_DIM)
    g_qkv = weight_grad(group_tokens, d_qkv)
    input_sum, norm_share = (
        lax.psum_scatter(
            dot_back(d_qkv, f_qkv).astype(jnp.bfloat16), "head", scatter_dimension=0, tiled=True
        ).astype(jnp.float32),
        lax.psum_scatter(
            g_norm.astype(jnp.bfloat16), "head", scatter_dimension=1, tiled=True
        ).astype(jnp.float32),
    )
    input_grad = d_one + input_sum
    s_qkv, s_out, s_gu, s_down, s_norm = (
        lax.psum_scatter(g_qkv, "blk", scatter_dimension=0, tiled=True),
        lax.psum_scatter(g_out, "blk", scatter_dimension=1, tiled=True),
        lax.psum_scatter(g_gate_up, "blk", scatter_dimension=1, tiled=True),
        lax.psum_scatter(g_down, "blk", scatter_dimension=1, tiled=True),
        lax.psum_scatter(norm_share, "blk", scatter_dimension=0, tiled=True),
    )
    return (result.astype(jnp.bfloat16), input_grad, s_qkv, s_out, s_gu, s_down, s_norm)


Q_SLOTS = 32
K_SLOTS = 16
SEQ_STEP = 65536.0
FAR = 32768.0
LANE_OF = (0, 64, 192)


def by_head(rows, lanes):
    lane = lax.broadcasted_iota(jnp.int32, rows.shape, 1)
    parts = [jnp.where((lane >= first) & (lane < first + HEAD_DIM), rows, 0.0) for first in lanes]
    return jnp.concatenate(parts, axis=0).astype(jnp.bfloat16)


def by_head_turned(rows, lanes):
    turned = rows.T
    lane = lax.broadcasted_iota(jnp.int32, turned.shape, 0)
    parts = [jnp.where((lane >= first) & (lane < first + HEAD_DIM), turned, 0.0) for first in lanes]
    return jnp.concatenate(parts, axis=1).astype(jnp.bfloat16)


def key_tiles(kv_ref, j):
    rows = kv_ref.shape[0] * K_SLOTS
    blk = kv_ref[:, pl.ds(pl.multiple_of(j * K_SLOTS, K_SLOTS), K_SLOTS), :]
    return blk.reshape(rows, blk.shape[2])


def key_span(len_ref, i, devs):
    first = i * (Q_SLOTS * devs)
    last = first + Q_SLOTS * devs - 1
    end, low, high = 0, 0, 0
    for k in range(8):
        start = end
        end = end + len_ref[k]
        low = jnp.where((first >= start) & (first < end), start, low)
        high = jnp.where((last >= start) & (last < end), end, high)
    step = K_SLOTS * devs
    return low // step, (high + step - 1) // step


def attend(len_any, slope_any, q_ref, kv_ref, kcode_ref, qcode_ref, out_ref, lse_ref, vt_ref, len_ref, slope_ref, few):
    z = lax.axis_index("head")
    scalars = [
        pltpu.make_async_copy(len_any, len_ref, few.at[0]),
        pltpu.make_async_copy(slope_any, slope_ref, few.at[1]),
    ]
    for c in scalars:
        c.start()
    devs, slots, _ = kv_ref.shape
    rows = devs * K_SLOTS
    q_rows = q_ref.shape[0] * Q_SLOTS

    def turn(j, _):
        kv = key_tiles(kv_ref, j)[:, 128:384]
        vt_ref[j] = kv.T
        return 0

    lax.fori_loop(0, slots // K_SLOTS, turn, 0)
    for c in scalars:
        c.wait()

    def chunk(i, _):
        first = pl.multiple_of(i * Q_SLOTS, Q_SLOTS)
        q = q_ref[:, pl.ds(first, Q_SLOTS), :].reshape(q_rows, 256).astype(jnp.float32)
        qbt = by_head_turned(q, (0, 64, 128))
        qcode = qcode_ref[i, 0:1, :]
        lo, hi = key_span(len_ref, i, devs)

        def block(j, state):
            kv = key_tiles(kv_ref, j)
            keys = jnp.concatenate([kv[:, 0:128], kv[:, 256:384]], axis=1)
            s_all = jnp.dot(keys, qbt, preferred_element_type=jnp.float32)
            dist = jnp.abs(key_tiles(kcode_ref, j) - qcode)
            keep = dist < FAR
            fresh, ps = [], []
            for h in range(3):
                best, total, acc = state[h]
                s = jnp.where(keep, s_all[:, 128 * h : 128 * h + 128] - slope_ref[3 * z + h] * dist, masked_score)
                top = jnp.maximum(best, jnp.max(s, axis=0, keepdims=True))
                factor = jnp.exp(best - top)
                p = jnp.exp(s - top)
                total = total * factor + jnp.sum(p, axis=0, keepdims=True)
                ps.append(p.astype(jnp.bfloat16))
                fresh.append((top, total, acc * factor))
            both = jnp.dot(vt_ref[j, 0:128, :], jnp.concatenate(ps[0:2], axis=1), preferred_element_type=jnp.float32)
            last = jnp.dot(vt_ref[j, 192:256, :], ps[2], preferred_element_type=jnp.float32)
            new = (both[0:64, 0:128], both[64:128, 128:256], last)
            fresh = [(top, total, acc + term) for (top, total, acc), term in zip(fresh, new)]
            return tuple(fresh)

        start = tuple(
            (
                jnp.full((1, q_rows), masked_score, jnp.float32),
                jnp.zeros((1, q_rows), jnp.float32),
                jnp.zeros((64, q_rows), jnp.float32),
            )
            for _ in range(3)
        )
        done = lax.fori_loop(lo, hi, block, start)
        outs = [acc / total for _, total, acc in done]
        full = jnp.concatenate([outs[0], outs[1], jnp.zeros((64, q_rows), jnp.float32), outs[2]], axis=0)
        out_ref[:, pl.ds(first, Q_SLOTS), :] = full.T.astype(jnp.bfloat16).reshape(-1, Q_SLOTS, 256)
        for h in range(3):
            lse_ref[i, h : h + 1, :] = done[h][0] + jnp.log(done[h][1])
        return 0

    lax.fori_loop(0, slots // Q_SLOTS, chunk, 0)


def attend_back(len_any, slope_any, q_ref, kv_ref, kcode_ref, qcode_ref, out_ref, do_ref, lse_ref, act_any,
                dq_ref, dkv_ref, act_out, kt_ref, sum_ref, sem, len_ref, slope_ref, few):
    z = lax.axis_index("head")
    scalars = [
        pltpu.make_async_copy(len_any, len_ref, few.at[0]),
        pltpu.make_async_copy(slope_any, slope_ref, few.at[1]),
    ]
    for c in scalars:
        c.start()
    devs, slots, _ = kv_ref.shape
    rows = devs * K_SLOTS
    q_rows = q_ref.shape[0] * Q_SLOTS
    scale = HEAD_DIM ** (-0.5)
    along = [
        pltpu.make_async_copy(act_any, act_out, sem.at[0]),
    ]
    for c in along:
        c.start()

    def turn(j, _):
        kv = key_tiles(kv_ref, j)
        keys = jnp.concatenate([kv[:, 0:128], kv[:, 256:384]], axis=1)
        kt_ref[j] = keys.T
        sum_ref[j] = jnp.zeros((rows, 384), jnp.float32)
        return 0

    lax.fori_loop(0, slots // K_SLOTS, turn, 0)
    for c in scalars:
        c.wait()

    def chunk(i, _):
        first = pl.multiple_of(i * Q_SLOTS, Q_SLOTS)
        q = q_ref[:, pl.ds(first, Q_SLOTS), :].reshape(q_rows, 256).astype(jnp.float32)
        qbd = by_head(q, (0, 64, 128))
        qbt = by_head_turned(q, (0, 64, 128))
        do = do_ref[:, pl.ds(first, Q_SLOTS), :].reshape(q_rows, 256).astype(jnp.float32)
        out = out_ref[:, pl.ds(first, Q_SLOTS), :].reshape(q_rows, 256).astype(jnp.float32)
        dobd = by_head(do, LANE_OF)
        dobt = by_head_turned(do, LANE_OF)
        prod = (do * out).T
        delta = [jnp.sum(prod[f : f + 64, :], axis=0, keepdims=True) for f in LANE_OF]
        qcode = qcode_ref[i, 0:1, :]
        lo, hi = key_span(len_ref, i, devs)

        def block(j, state):
            kv = key_tiles(kv_ref, j)
            keys = jnp.concatenate([kv[:, 0:128], kv[:, 256:384]], axis=1)
            vals = kv[:, 128:384]
            s_all = jnp.dot(keys, qbt, preferred_element_type=jnp.float32)
            dp_all = jnp.dot(vals, dobt, preferred_element_type=jnp.float32)
            dist = jnp.abs(key_tiles(kcode_ref, j) - qcode)
            keep = dist < FAR
            ps, dss, fresh = [], [], []
            for h in range(3):
                s = s_all[:, 128 * h : 128 * h + 128] - slope_ref[3 * z + h] * dist - lse_ref[i, h : h + 1, :]
                p = jnp.exp(jnp.where(keep, s, masked_score))
                ds = (p * (dp_all[:, 128 * h : 128 * h + 128] - delta[h])).astype(jnp.bfloat16)
                ps.append(p.astype(jnp.bfloat16))
                dss.append(ds)
            both = jnp.dot(kt_ref[j, 0:128, :], jnp.concatenate(dss[0:2], axis=1), preferred_element_type=jnp.float32)
            last = jnp.dot(kt_ref[j, 128:192, :], dss[2], preferred_element_type=jnp.float32)
            fresh = [state[0] + both[0:64, 0:128], state[1] + both[64:128, 128:256], state[2] + last]
            dv = jnp.dot(jnp.concatenate(ps, axis=1), dobd, preferred_element_type=jnp.float32)
            dk = jnp.dot(jnp.concatenate(dss, axis=1), qbd, preferred_element_type=jnp.float32)
            sum_ref[j, :, 0:128] += dk[:, 0:128]
            sum_ref[j, :, 128:256] += dv[:, 0:128]
            sum_ref[j, :, 256:384] += dk[:, 128:256] + dv[:, 128:256]
            return tuple(fresh)

        start = tuple(jnp.zeros((64, q_rows), jnp.float32) for _ in range(3))
        done = lax.fori_loop(lo, hi, block, start)
        full = jnp.concatenate(done + (jnp.zeros((64, q_rows), jnp.float32),), axis=0) * scale
        dq_ref[:, pl.ds(first, Q_SLOTS), :] = full.T.astype(jnp.bfloat16).reshape(-1, Q_SLOTS, 256)
        return 0

    lax.fori_loop(0, slots // Q_SLOTS, chunk, 0)

    def leave(j, _):
        dkv_ref[:, pl.ds(pl.multiple_of(j * K_SLOTS, K_SLOTS), K_SLOTS), :] = (
            sum_ref[j].astype(jnp.bfloat16).reshape(devs, K_SLOTS, 384)
        )
        return 0

    lax.fori_loop(0, slots // K_SLOTS, leave, 0)
    for c in along:
        c.wait()


VM = pl.BlockSpec(memory_space=pltpu.VMEM)
SM = pl.BlockSpec(memory_space=pltpu.SMEM)
ANY = pl.BlockSpec(memory_space=pl.ANY)
HBM = pl.BlockSpec(memory_space=pltpu.MemorySpace.HBM)


def run_attend(lengths, slopes, q, kv, kcode, qcode):
    heads_n, slots, _ = q.shape
    devs = kv.shape[0]
    return pl.pallas_call(
        attend,
        out_shape=(
            jax.ShapeDtypeStruct((heads_n, slots, 256), jnp.bfloat16),
            jax.ShapeDtypeStruct((slots // Q_SLOTS, 8, heads_n * Q_SLOTS), jnp.float32),
        ),
        in_specs=[HBM, HBM, VM, VM, VM, VM],
        out_specs=(VM, VM),
        scratch_shapes=[
            pltpu.VMEM((slots // K_SLOTS, 256, devs * K_SLOTS), jnp.bfloat16),
            pltpu.SMEM((8,), jnp.int32),
            pltpu.SMEM((HEADS,), jnp.float32),
            pltpu.SemaphoreType.DMA((2,)),
        ],
        compiler_params=pltpu.CompilerParams(vmem_limit_bytes=16 << 20),
        name="attend",
    )(lengths, slopes, q, kv, kcode, qcode)


def run_attend_back(lengths, slopes, q, kv, kcode, qcode, out, do, lse, act):
    heads_n, slots, _ = q.shape
    devs = kv.shape[0]
    return pl.pallas_call(
        attend_back,
        out_shape=(
            jax.ShapeDtypeStruct((heads_n, slots, 256), jnp.bfloat16),
            jax.ShapeDtypeStruct((devs, slots, 384), jnp.bfloat16),
            jax.ShapeDtypeStruct(act.shape, act.dtype),
        ),
        in_specs=[HBM, HBM, VM, VM, VM, VM, VM, VM, VM, ANY],
        out_specs=(VM, VM, ANY),
        scratch_shapes=[
            pltpu.VMEM((slots // K_SLOTS, 256, devs * K_SLOTS), jnp.bfloat16),
            pltpu.VMEM((slots // K_SLOTS, devs * K_SLOTS, 384), jnp.float32),
            pltpu.SemaphoreType.DMA((2,)),
            pltpu.SMEM((8,), jnp.int32),
            pltpu.SMEM((HEADS,), jnp.float32),
            pltpu.SemaphoreType.DMA((2,)),
        ],
        compiler_params=pltpu.CompilerParams(vmem_limit_bytes=26 << 20),
        name="attend_back",
    )(lengths, slopes, q, kv, kcode, qcode, out, do, lse, act)


MESH = pl.DeviceIdType.MESH


def dot_tn(left, right):
    return lax.dot_general(left, right, (((0,), (0,)), ((), ())), preferred_element_type=jnp.float32)


def dot_nt(left, right):
    return lax.dot_general(left, right, (((1,), (1,)), ((), ())), preferred_element_type=jnp.float32)


def greet(peers):
    barrier = pltpu.get_barrier_semaphore()
    for peer in peers:
        pl.semaphore_signal(barrier, inc=1, device_id=peer, device_id_type=MESH)
    pl.semaphore_wait(barrier, len(peers))


class Sender:
    def __init__(self, sems):
        self.sems = sems
        self.used = 0
        self.left = []

    def make(self, src, dst, peer, arrive=None):
        i = self.used
        self.used += 1
        assert i < self.sems.shape[1]
        copy = pltpu.make_async_remote_copy(
            src_ref=src, dst_ref=dst, send_sem=self.sems.at[0, i],
            recv_sem=self.sems.at[1, i] if arrive is None else arrive,
            device_id=peer, device_id_type=MESH,
        )
        copy.arrive = self.sems.at[1, i]
        return copy

    def start(self, copy, only=None):
        self.left.append((copy, only))
        if only is None:
            copy.start()
        else:
            pl.when(only)(copy.start)
        return copy

    def __call__(self, src, dst, peer, only=None, arrive=None):
        return self.start(self.make(src, dst, peer, arrive), only)

    def sent(self, copy):
        [(_, only)] = [item for item in self.left if item[0] is copy]
        self.left = [item for item in self.left if item[0] is not copy]
        if only is None:
            copy.wait_send()
        else:
            pl.when(only)(copy.wait_send)

    def finish(self):
        for copy, only in self.left:
            if only is None:
                copy.wait_send()
            else:
                pl.when(only)(copy.wait_send)


class Plane:
    def __init__(self, go, core, slot, me, near, flat, sib):
        self.go, self.core, self.slot, self.near, self.flat, self.sib = go, core, slot, near, flat, sib
        self.one = go(slot(me), slot(me), flat[1])
        self.two = go(slot(me), slot(me), flat[2])
        self.three = go.make(slot(me), slot(me), flat[3])
        self.handed = [self.hand(me)]

    def hand(self, n):
        return self.go(self.slot(n), self.slot(n), self.sib)

    def pass_on(self):
        for copy, r, turn in ((self.one, 1, 0), (self.two, 2, 1)):
            copy.wait_recv()
            block = self.slot(self.near[r])
            self.go(block, block, self.flat[3 - r], only=self.core == turn, arrive=self.three.arrive)
            self.handed.append(self.hand(self.near[r]))

    def last(self):
        self.three.wait_recv()
        self.handed.append(self.hand(self.near[3]))

    def whole(self):
        for copy in self.handed:
            copy.wait_recv()


class Spread:
    def __init__(self, go, mid, slot, z, line):
        self.go, self.mid, self.slot, self.z, self.line = go, mid, slot, z, line
        self.two = go(slot(z), slot(z), line[2])
        self.three = go.make(slot(z), slot(z), line[3])
        self.one = go.make(slot(z), slot(z), line[1])

    def rest(self):
        self.go.start(self.three, only=self.mid)
        self.go.start(self.one)

    def pass_on(self):
        self.two.wait_recv()
        far = self.slot(self.z ^ 2)
        self.go(far, far, self.line[1], only=self.mid, arrive=self.three.arrive)

    def wait(self):
        self.one.wait_recv()
        self.three.wait_recv()


def finish(
    dkv_ref, dq_ref, tok_ref, w_ref, datt_ref, mixed_ref, done_ref, gn_ref,
    dx_ref, sqkv_ref, sout_ref, snorm_ref,
    kv_sib, kv_sum, kv_in, g_one, g_two, g_sib, g_sum, g_in,
    part, part_in, att, dkvq, nz_in, nrow, np_in, relay, sems,
):
    b = lax.axis_index("blk")
    z = lax.axis_index("head")
    chip, core = b // 2, b % 2
    sib = (chip * 2 + 1 - core, z)
    flat = [((chip ^ r) * 2 + core, z) for r in (0, 1, 2, 3)]
    line = [(b, z ^ r) for r in (0, 1, 2, 3)]
    greet([sib] + flat[1:] + line[1:])
    f32, bf16 = jnp.float32, jnp.bfloat16
    go = Sender(sems)
    mid = (z == 1) | (z == 2)
    ends = (z == 0) | (z == 3)

    def member(r):
        return pl.ds(pl.multiple_of((z ^ r) * 128, 128), 128)

    kv_c = {
        (q, r): go(dkv_ref.at[(chip ^ r) * 2 + 1 - core, member(q)], kv_sib.at[q, r], sib)
        for q in (3, 2, 1, 0) for r in (3, 1, 2, 0)
    }
    att[z] = datt_ref[...]
    att_c = Spread(go, mid, lambda j: att.at[j], z, line)
    att_c.rest()
    nz_c = [go(gn_ref.at[pl.ds((z ^ r) * 8, 8)], nz_in.at[r - 1], line[r]) for r in (1, 2, 3)]
    kv_out = {}
    for q in (3, 2, 1, 0):
        for r in (3, 1, 2, 0):
            kv_c[q, r].wait_recv()
            both = dkv_ref[(chip ^ r) * 2 + core, member(q), :].astype(f32) + kv_sib[q, r].astype(f32)
            kv_sum[q, r] = both.astype(bf16)
            if r:
                kv_out[q, r] = go(kv_sum.at[q, r], kv_in.at[q, r - 1], flat[r])
    dkvq[:, 384:640] = dq_ref[...]

    @pl.when(ends)
    def _():
        relay[...] = jnp.zeros((128, 768), bf16)
        part_in[2] = jnp.zeros((128, 768), bf16)


    def send_half(part_i, grads):
        return [
            go(grads.at[pl.ds(pl.multiple_of(((chip ^ r) * 2 + 1 - core) * 96, 96), 96)], g_sib.at[part_i, r], sib)
            for r in (3, 1, 2, 0)
        ]

    def send_sum(part_i, grads, copies):
        out = []
        for k, r in enumerate((3, 1, 2, 0)):
            copies[k].wait_recv()
            mine = grads[pl.ds(pl.multiple_of(((chip ^ r) * 2 + core) * 96, 96), 96), :].astype(f32)
            g_sum[part_i, r] = (mine + g_sib[part_i, r].astype(f32)).astype(bf16)
            if r:
                out.append(go(g_sum.at[part_i, r], g_in.at[part_i, r - 1], flat[r]))
        return out

    def settle(part_i, copies):
        for c in copies:
            c.wait_recv()
        return (
            g_sum[part_i, 0].astype(f32) + g_in[part_i, 0].astype(f32)
            + g_in[part_i, 1].astype(f32) + g_in[part_i, 2].astype(f32)
        )

    att_c.pass_on()
    for c in nz_c:
        c.wait_recv()
    nrow[0] = gn_ref[pl.ds(z * 8, 8)] + nz_in[0] + nz_in[1] + nz_in[2]
    np_c = [go(nrow.at[0], np_in.at[r], flat[r]) for r in (1, 2, 3)]
    last = dot_tn(tok_ref[...], dq_ref[...])
    g_one[:, 0:128] = last[:, 0:128].astype(bf16)
    dx_c = []
    for q in (3, 2, 1, 0):
        for r in (1, 2, 3):
            kv_out[q, r].wait_recv()
        dkvq[member(q), 0:384] = (
            kv_sum[q, 0].astype(f32) + kv_in[q, 0].astype(f32) + kv_in[q, 1].astype(f32) + kv_in[q, 2].astype(f32)
        ).astype(bf16)
        term = dot_nt(dkvq[member(q), :], w_ref[...])
        if q == 3:
            part[2] = term.astype(bf16)
            passed = go(part.at[2], relay, line[1], only=ends)
            dx_three = go(part.at[2], part_in.at[2], line[3], only=mid)
        elif q == 2:
            far = term
        elif q == 1:
            part[0] = term.astype(bf16)
            dx_c.append(go(part.at[0], part_in.at[0], line[1]))
            pl.when(mid)(passed.wait_recv)
            part[1] = (far + relay[...].astype(f32)).astype(bf16)
            dx_c.append(go(part.at[1], part_in.at[1], line[2]))
        else:
            dx_ref[...] = done_ref[...] + term
    g_two[...] = dot_tn(tok_ref[...], dkvq[:, 0:384]).astype(bf16)
    two_c = send_half(1, g_two)
    att_c.one.wait_recv()
    att_c.three.wait_recv()
    outs = dot_tn(att[...].reshape(512, 768), mixed_ref[...])
    g_one[:, 128:256] = outs[:, 0:128].astype(bf16)
    g_one[:, 256:384] = (outs[:, 128:256] + last[:, 128:256]).astype(bf16)
    one_c = send_half(0, g_one)
    two_out = send_sum(1, g_two, two_c)
    one_out = send_sum(0, g_one, one_c)
    for c in np_c:
        c.wait_recv()
    nrow[1] = nrow[0] + np_in[1] + np_in[2] + np_in[3]
    half = go(nrow.at[1], np_in.at[0], sib)
    half.wait_recv()
    full = nrow[1] + np_in[0]
    snorm_ref[...] = pltpu.roll(full, lax.rem(768 - 96 * b, 768), 1)[0:1, 0:96]
    two = settle(1, two_out)
    one = settle(0, one_out)
    piece = [two[:, 64 * i : 64 * i + 64] for i in range(6)]
    piece += [one[:, 0:64], one[:, 64:128], one[:, 256:320]]
    for k, i in enumerate((6, 0, 2, 7, 1, 3, 8, 4, 5)):
        sqkv_ref[:, 64 * k : 64 * k + 64] = piece[i]
    turned = jnp.concatenate([one[:, 128:384], jnp.zeros((32, 256), f32)], axis=0).T
    sout_ref[0:128, :] = turned[0:128, 0:96]
    sout_ref[128:192, :] = turned[192:256, 0:96]
    for c in dx_c:
        c.wait_recv()
    pl.when(mid)(dx_three.wait_recv)
    dx_ref[...] += part_in[0].astype(f32) + part_in[1].astype(f32) + part_in[2].astype(f32)
    go.finish()


def run_finish(dkv, dq, toks, w, datt, mixed, done, gn):
    f32, bf16 = jnp.float32, jnp.bfloat16
    V = pltpu.VMEM
    return pl.pallas_call(
        finish,
        out_shape=(
            jax.ShapeDtypeStruct((128, 768), f32),
            jax.ShapeDtypeStruct((96, 576), f32),
            jax.ShapeDtypeStruct((192, 96), f32),
            jax.ShapeDtypeStruct((1, 96), f32),
        ),
        in_specs=[VM] * 8,
        out_specs=(VM,) * 4,
        scratch_shapes=[
            V((4, 4, 128, 384), bf16), V((4, 4, 128, 384), bf16), V((4, 3, 128, 384), bf16),
            V((768, 384), bf16), V((768, 384), bf16),
            V((2, 4, 96, 384), bf16), V((2, 4, 96, 384), bf16), V((2, 3, 96, 384), bf16),
            V((3, 128, 768), bf16), V((3, 128, 768), bf16), V((4, 128, 768), bf16), V((512, 640), bf16),
            V((3, 8, 768), f32), V((2, 8, 768), f32), V((4, 8, 768), f32), V((128, 768), bf16),
            pltpu.SemaphoreType.DMA((2, 72)),
        ],
        compiler_params=pltpu.CompilerParams(
            collective_id=5, has_side_effects=True, vmem_limit_bytes=28 << 20
        ),
        name="finish",
    )(dkv, dq, toks, w, datt, mixed, done, gn)


def collect(
    len_any, tok_any, wq_any, wout_any, nrm_any, pos_any,
    gt, wat, q_ref, kv, wout, norm_out, kcode, qcode,
    wa_ref, wo_ref, nr, code_ref, wq_ref, wout_ref, nrm_row, pos_ref, nrm_ref, len_ref, sems, lsem,
):
    b = lax.axis_index("blk")
    z = lax.axis_index("head")
    chip, core = b // 2, b % 2
    sib = (chip * 2 + 1 - core, z)
    near = [(chip ^ r) * 2 + core for r in (0, 1, 2, 3)]
    flat = [(n, z) for n in near]
    line = [(b, z ^ r) for r in (0, 1, 2, 3)]
    f32, bf16 = jnp.float32, jnp.bfloat16
    fetch = [
        pltpu.make_async_copy(wq_any, wq_ref, lsem.at[0]),
        pltpu.make_async_copy(wout_any, wout_ref, lsem.at[1]),
        pltpu.make_async_copy(nrm_any, nrm_row, lsem.at[2]),
        pltpu.make_async_copy(pos_any, pos_ref, lsem.at[3]),
        pltpu.make_async_copy(tok_any, gt.at[z], lsem.at[4]),
        pltpu.make_async_copy(len_any, len_ref, lsem.at[5]),
    ]
    for c in fetch:
        c.start()
    for c in fetch:
        c.wait()
    go = Sender(sems)
    mid = (z == 1) | (z == 2)
    ends = (z == 0) | (z == 3)

    wq = wq_ref[...].astype(f32)
    wo = wout_ref[...].astype(f32)
    wo = jnp.concatenate([wo[0:128], jnp.zeros((64, 96), f32), wo[128:192]], axis=0)
    wo = jnp.concatenate([wo, jnp.zeros((256, 32), f32)], axis=1).T[0:96]
    wo_ref[...] = wo.astype(bf16)
    piece = [wq[:, 64 * i : 64 * i + 64] for i in range(9)] + [wo[:, 192:256]]
    for k in range(5):
        tile = jnp.concatenate([piece[PACK[2 * k]], piece[PACK[2 * k + 1]]], axis=1)
        wa_ref[:, 128 * k : 128 * k + 128] = tile.astype(bf16)
    wat[b] = wa_ref[...]
    wout[z] = wo_ref[...]
    nrm_ref[...] = jnp.zeros((8, 128), f32)
    nrm_ref[0:1, 0:96] = nrm_row[...].astype(f32)
    nr[b, z] = nrm_ref[...]
    greet([sib] + flat[1:] + line[1:])
    tok_z = [Spread(go, mid, lambda j, h=h: gt.at[j, pl.ds(64 * h, 64)], z, line) for h in range(2)]
    wa_p = [go(wa_ref, wat.at[b], flat[r]) for r in (3, 1, 2)]
    wa_s = [go(wa_ref, wat.at[b], sib)]
    pos = pos_ref[...]
    seq = jnp.zeros(pos.shape, f32)
    end = 0
    for k in range(8):
        end = end + len_ref[k]
        seq = seq + jnp.where(pos >= end, 1.0, 0.0)
    code_ref[...] = pos.astype(f32) + SEQ_STEP * seq

    def spread_code(d, _):
        kcode[d] = jnp.broadcast_to(code_ref[pl.ds(d, 1), :], (128, 128)).T
        return 0

    lax.fori_loop(0, 32, spread_code, 0)
    own_code = [code_ref[pl.ds(b * 4 + j, 1), :] for j in range(4)]
    for i in range(4):
        qcode[i, 0:1, :] = jnp.concatenate([c[:, 32 * i : 32 * i + 32] for c in own_code], axis=1)
    go.sent(tok_z[0].two)
    tok_z[0].rest()
    tok_z[0].pass_on()
    go.sent(tok_z[1].two)
    tok_z[1].rest()
    wo_z = [go(wo_ref, wout.at[z], line[r]) for r in (3, 2, 1)]
    nr_z = [go(nrm_ref, nr.at[b, z], line[r]) for r in (3, 2, 1)]
    for k, r in enumerate((3, 1, 2)):
        wa_p[k].wait_recv()
        wa_s.append(go(wat.at[near[r]], wat.at[near[r]], sib))
    tok_z[1].pass_on()
    for c in wa_s:
        c.wait_recv()
    kv_p = []
    for r in (0, 2, 1, 3):
        for s in tok_z:
            if r in (1, 3):
                (s.one if r == 1 else s.three).wait_recv()
        j = z ^ r
        rows = jnp.dot(gt[j], wat[...].reshape(768, 640), preferred_element_type=f32)
        kv[b * 4 + j] = rows[:, 0:384].astype(bf16)
        if r == 3:
            kv_l = [go(kv.at[b * 4 + j], kv.at[b * 4 + j], flat[s]) for s in (3, 1, 2)]
            passed.append(go(kv.at[b * 4 + j], kv.at[b * 4 + j], sib))
        else:
            kv_p.append(Plane(go, core, lambda n, j=j: kv.at[n * 4 + j], b, near, flat, sib))
        q_ref[j] = rows[:, 384:640].astype(bf16) * bf16(HEAD_DIM ** (-0.5))
        if r:
            kv_p[{2: 0, 1: 1, 3: 2}[r]].pass_on()
        if r == 1:
            for c in wo_z + nr_z:
                c.wait_recv()
            nr_p = [go(nr.at[b], nr.at[b], flat[r]) for r in (3, 1, 2)]
            passed = [go(nr.at[b], nr.at[b], sib)]
    for k, r in enumerate((3, 1, 2)):
        nr_p[k].wait_recv()
        passed.append(go(nr.at[near[r]], nr.at[near[r]], sib))
    for p in kv_p:
        p.last()
    for k, s in enumerate((3, 1, 2)):
        kv_l[k].wait_recv()
        n = near[s] * 4 + (z ^ 3)
        passed.append(go(kv.at[n], kv.at[n], sib))
    for p in kv_p:
        p.whole()
    for c in passed:
        c.wait_recv()
    total = jnp.zeros((8, 768), f32)
    for n in range(8):
        rows = jnp.concatenate([nr[n, j, 0:1, :] for j in range(4)] + [jnp.zeros((4, 128), f32)], axis=0)
        total = total + pltpu.roll(jnp.concatenate([rows, jnp.zeros((8, 640), f32)], axis=1), 96 * n, 1)
    norm_out[...] = total
    go.finish()


def run_collect(lengths, tok, wq, wo, nrm, pos):
    f32, bf16 = jnp.float32, jnp.bfloat16
    S = jax.ShapeDtypeStruct
    V = pltpu.VMEM
    return pl.pallas_call(
        collect,
        out_shape=(
            S((4, 128, 768), bf16), S((8, 96, 640), bf16), S((4, 128, 256), bf16), S((32, 128, 384), bf16),
            S((4, 96, 256), bf16), S((8, 768), f32), S((32, 128, 128), f32), S((4, 8, 128), f32),
        ),
        in_specs=[HBM] * 6,
        out_specs=(VM,) * 8,
        scratch_shapes=[
            V((96, 640), bf16), V((96, 256), bf16), V((8, 4, 8, 128), f32), V((32, 128), f32),
            V((96, 576), bf16), V((192, 96), bf16), V((1, 96), bf16), V((32, 128), jnp.int32), V((8, 128), f32),
            pltpu.SMEM((8,), jnp.int32), pltpu.SemaphoreType.DMA((2, 80)), pltpu.SemaphoreType.DMA((6,)),
        ],
        compiler_params=pltpu.CompilerParams(
            collective_id=1, has_side_effects=True, vmem_limit_bytes=20 << 20
        ),
        name="collect",
    )(lengths, tok, wq, wo, nrm, pos)


def moments(rows):
    center = rows - jnp.mean(rows, axis=-1, keepdims=True)
    spread = lax.rsqrt(jnp.mean(center * center, axis=-1, keepdims=True) + 1e-05)
    return center * spread, spread


def norm_back(grad, gain, unit, spread):
    scaled = grad * gain
    return spread * (
        scaled - jnp.mean(scaled, axis=-1, keepdims=True) - unit * jnp.mean(scaled * unit, axis=-1, keepdims=True)
    )


def middle(
    mixed_ref, tok_any, og_any, norm_ref, wo_0, wo_1, wo_2, wo_3, gu_any, down_any,
    act_ref, done_ref, datt_ref, dheads, sum_0, sum_1, sum_2, sum_3, gn_ref,
    mix_in, wffn, rows_in, drow_in, gelu_a, gelu_b, gated, dgate, dup,
    part, part_in, part2, part2_in, gff, ffn_sib, hid, unit_one, held, held_two, head_out,
    wf_ref, tok_ref, og_ref, wout, part_relay, part2_relay, sems, lsem,
):
    b = lax.axis_index("blk")
    z = lax.axis_index("head")
    chip, core = b // 2, b % 2
    sib = (chip * 2 + 1 - core, z)
    near = [(chip ^ r) * 2 + core for r in (0, 1, 2, 3)]
    flat = [(n, z) for n in near]
    line = [(b, z ^ r) for r in (0, 1, 2, 3)]
    f32, bf16 = jnp.float32, jnp.bfloat16
    own = [
        pltpu.make_async_copy(gu_any, wf_ref.at[0:2], lsem.at[0]),
        pltpu.make_async_copy(down_any, wf_ref.at[2], lsem.at[1]),
        pltpu.make_async_copy(tok_any, tok_ref, lsem.at[2]),
        pltpu.make_async_copy(og_any, og_ref, lsem.at[3]),
    ]
    for c in own:
        c.start()
    greet([sib] + flat[1:] + line[1:])
    go = Sender(sems)
    mid = (z == 1) | (z == 2)
    ends = (z == 0) | (z == 3)

    HALF = 64

    @pl.when(ends)
    def _():
        for h in range(2):
            part_in[h, 2] = jnp.zeros((HALF, 768), bf16)
            part2_in[h, 2] = jnp.zeros((HALF, 768), bf16)

    def scatter(out, arrived, relay, terms, h):
        passed = go(out.at[h, z ^ 3], relay.at[h], line[1], only=ends)
        three = go(out.at[h, z ^ 3], arrived.at[h, 2], line[3], only=mid)
        one = go(out.at[h, z ^ 1], arrived.at[h, 0], line[1])
        two = go.make(out.at[h, z ^ 2], arrived.at[h, 1], line[2])
        go.start(two, only=ends)

        def later():
            @pl.when(mid)
            def _():
                passed.wait_recv()
                out[h, z ^ 2] = (terms[h, z ^ 2] + relay[h].astype(f32)).astype(bf16)

            go.left.append((two, mid))
            pl.when(mid)(two.start)

        return one, two, three, later

    def gathered(copies):
        copies[0].wait_recv()
        copies[1].wait_recv()
        pl.when(mid)(copies[2].wait_recv)

    wo_s = []
    for r, ref in enumerate((wo_0, wo_1, wo_2, wo_3)):
        wo_s.append(go(ref, wout.at[:, near[r]], sib))
        wout[:, near[r]] = ref[...]
    mix_c = []
    for h in range(2):
        rows = pl.ds(HALF * h, HALF)
        mix_c.append([go(mixed_ref.at[z ^ r, rows], mix_in.at[h, z], line[r]) for r in (3, 2, 1)])
    for c in own:
        c.wait()
    mine = pltpu.make_async_copy(wf_ref, wffn.at[:, b], lsem.at[0])
    mine.start()
    mine.wait()
    wf_p = [Plane(go, core, lambda n, t=t: wffn.at[t, n], b, near, flat, sib) for t in range(3)]

    for c in wo_s:
        c.wait_recv()

    def out_weight(j):
        return wout[j].reshape(768, 256)

    spreads = []
    row_c = []
    for h in range(2):
        rows = pl.ds(HALF * h, HALF)
        mix_in[h, z] = mixed_ref[z, rows, :]
        for c in mix_c[h]:
            c.wait_recv()
        attn = dot_nt(mix_in[h, 0], out_weight(0))
        for j in (1, 2, 3):
            attn = attn + dot_nt(mix_in[h, j], out_weight(j))
        unit, spread = moments(tok_ref[rows, :].astype(f32) + attn)
        hidden = unit * norm_ref[0:1, :] + norm_ref[1:2, :]
        unit_one[h] = unit
        spreads.append(spread)
        hid[h] = hidden
        rows_in[h, z] = hidden.astype(bf16)
        row_c.append(Spread(go, mid, lambda j, h=h: rows_in.at[h, j], z, line))
        if h == 1:
            row_c[0].rest()
        wf_p[h].pass_on()
    row_c[0].pass_on()
    row_c[1].rest()
    wf_p[2].pass_on()
    row_c[1].pass_on()
    for p in wf_p:
        p.last()
    wf_p[0].whole()
    wf_p[1].whole()

    def weight(t):
        return wffn[t].reshape(768, 768)

    part_c = []
    for h in range(2):
        row_c[h].wait()
        rows = rows_in[h].reshape(4 * HALF, 768)
        gate = jnp.dot(rows, weight(0), preferred_element_type=f32)
        up = jnp.dot(rows, weight(1), preferred_element_type=f32)
        half = 0.5 + 0.5 * lax.erf(gate * (0.5**0.5))
        value = gate * half
        low = (value * up).astype(bf16)
        gated[h] = low
        if h == 0:
            wf_p[2].whole()
        term = dot_nt(low, weight(2)).reshape(4, HALF, 768)
        held[h] = term
        part[h] = term.astype(bf16)
        if h == 1:
            part_c[0][3]()
        part_c.append(scatter(part, part_in, part_relay, held, h))
        slope = half + gate * jnp.exp(-0.5 * gate * gate) * 0.3989422804014327
        gelu_a[h] = slope * up
        gelu_b[h] = value
    part_c[1][3]()
    gains = []
    drow_c = []
    for h in range(2):
        rows = pl.ds(HALF * h, HALF)
        if h == 1:
            drow_c[0].pass_on()
        gathered(part_c[h])
        branch = held[h, z] + part_in[h, 0].astype(f32) + part_in[h, 1].astype(f32) + part_in[h, 2].astype(f32)
        unit_two, spread_two = moments(hid[h] + branch)
        grad = og_ref[rows, :].astype(f32)
        d_two = norm_back(grad, norm_ref[2:3, :], unit_two, spread_two)
        hid[h] = d_two
        drow_in[h, z] = d_two.astype(bf16)
        drow_c.append(Spread(go, mid, lambda j, h=h: drow_in.at[h, j], z, line))
        act_ref[rows, :] = (unit_two * norm_ref[2:3, :] + norm_ref[3:4, :]).astype(bf16)
        gains.append((jnp.sum(grad * unit_two, axis=0, keepdims=True), jnp.sum(grad, axis=0, keepdims=True)))
        drow_c[h].rest()
    gn_ref[...] = jnp.zeros((32, 768), f32)
    gn_ref[16:17, :] = gains[0][0] + gains[1][0]
    gn_ref[24:25, :] = gains[0][1] + gains[1][1]
    part2_c = []
    for h in range(2):
        if h == 1:
            drow_c[1].pass_on()
        drow_c[h].wait()
        d_gated = jnp.dot(drow_in[h].reshape(4 * HALF, 768), weight(2), preferred_element_type=f32)
        dg = (d_gated * gelu_a[h]).astype(bf16)
        du = (d_gated * gelu_b[h]).astype(bf16)
        dgate[h] = dg
        dup[h] = du
        term = (dot_nt(dg, weight(0)) + dot_nt(du, weight(1))).reshape(4, HALF, 768)
        held_two[h] = term
        part2[h] = term.astype(bf16)
        if h == 1:
            part2_c[0][3]()
        part2_c.append(scatter(part2, part2_in, part2_relay, held_two, h))
    part2_c[1][3]()
    sib_c = []
    acts = rows_in[...].reshape(512, 768)
    for t in (2, 0, 1):
        if t == 2:
            total = dot_tn(drow_in[...].reshape(512, 768), gated[...].reshape(512, 768))
        else:
            total = dot_tn(acts, (dgate, dup)[t][...].reshape(512, 768))
        gff[t] = total.astype(bf16).reshape(4, 2, 96, 768)
        sib_c.append(go(gff.at[t, :, 1 - core], ffn_sib.at[t], sib))
    gains = []
    head_c = []
    for h in range(2):
        rows = pl.ds(HALF * h, HALF)
        gathered(part2_c[h])
        d_hidden = (
            hid[h] + held_two[h, z]
            + part2_in[h, 0].astype(f32) + part2_in[h, 1].astype(f32) + part2_in[h, 2].astype(f32)
        )
        unit = unit_one[h]
        d_one = norm_back(d_hidden, norm_ref[0:1, :], unit, spreads[h])
        low_one = d_one.astype(bf16)
        for r in (3, 2, 1, 0):
            term = jnp.dot(low_one, out_weight(z ^ r), preferred_element_type=f32).astype(bf16)
            if r:
                head_out[h, r - 1] = term
                head_c.append(go(head_out.at[h, r - 1], dheads.at[z, rows], line[r]))
            else:
                dheads[z, rows, :] = term
        done_ref[rows, :] = d_one
        datt_ref[rows, :] = low_one
        gains.append((jnp.sum(d_hidden * unit, axis=0, keepdims=True), jnp.sum(d_hidden, axis=0, keepdims=True)))
    gn_ref[0:1, :] = gains[0][0] + gains[1][0]
    gn_ref[8:9, :] = gains[0][1] + gains[1][1]
    for k, t in enumerate((2, 0, 1)):
        sib_c[k].wait_recv()
        for r, ref in enumerate((sum_0, sum_1, sum_2, sum_3)):
            both = gff[t, chip ^ r, core].astype(f32) + ffn_sib[t, chip ^ r].astype(f32)
            ref[t] = both.astype(bf16)
    for c in head_c:
        c.wait_recv()
    go.finish()


def run_middle(mixed, tok, og, norms, wo, gu, down):
    f32, bf16 = jnp.float32, jnp.bfloat16
    S = jax.ShapeDtypeStruct
    V = pltpu.VMEM
    halves = (2, 256, 768)
    return pl.pallas_call(
        middle,
        out_shape=(
            S((128, 768), bf16), S((128, 768), f32), S((128, 768), bf16), S((4, 128, 256), bf16),
            *[S((3, 96, 768), bf16)] * 4, S((32, 768), f32),
        ),
        in_specs=[VM, HBM, HBM, VM, VM, VM, VM, VM, HBM, HBM],
        out_specs=(VM,) * 9,
        scratch_shapes=[
            V((2, 4, 64, 256), bf16), V((3, 8, 96, 768), bf16), V((2, 4, 64, 768), bf16), V((2, 4, 64, 768), bf16),
            V(halves, f32), V(halves, f32), V(halves, bf16), V(halves, bf16), V(halves, bf16),
            V((2, 4, 64, 768), bf16), V((2, 3, 64, 768), bf16), V((2, 4, 64, 768), bf16), V((2, 3, 64, 768), bf16),
            V((3, 4, 2, 96, 768), bf16), V((3, 4, 96, 768), bf16),
            V((2, 64, 768), f32), V((2, 64, 768), f32), V((2, 4, 64, 768), f32), V((2, 4, 64, 768), f32),
            V((2, 3, 64, 256), bf16),
            V((3, 96, 768), bf16), V((128, 768), bf16), V((128, 768), bf16), V((4, 8, 96, 256), bf16), V((2, 64, 768), bf16), V((2, 64, 768), bf16),
            pltpu.SemaphoreType.DMA((2, 108)), pltpu.SemaphoreType.DMA((4,)),
        ],
        compiler_params=pltpu.CompilerParams(
            collective_id=3, has_side_effects=True, vmem_limit_bytes=36 << 20
        ),
        name="middle",
    )(mixed, tok, og, norms, *wo, gu, down)


def deliver(*refs):
    dx, sqkv, sout, snorm, *sums = refs[:8]
    o_dx, o_qkv, o_out, o_norm, o_gu, o_down, sem = refs[8:]
    pairs = ((dx, o_dx), (sqkv, o_qkv), (sout, o_out), (snorm, o_norm))
    copies = [pltpu.make_async_copy(s, d, sem.at[i]) for i, (s, d) in enumerate(pairs)]
    for c in copies:
        c.start()
    for t in range(3):
        total = sum(s[t].astype(jnp.float32) for s in sums)
        if t < 2:
            o_gu[t] = total
        else:
            o_down[...] = total
    for c in copies:
        c.wait()


def run_deliver(*arrays):
    f32 = jnp.float32
    S = jax.ShapeDtypeStruct
    return pl.pallas_call(
        deliver,
        out_shape=(
            S((128, 768), f32), S((96, 576), f32), S((192, 96), f32), S((1, 96), f32),
            S((2, 96, 768), f32), S((96, 768), f32),
        ),
        in_specs=[ANY] * 4 + [VM] * 4,
        out_specs=(ANY,) * 4 + (VM,) * 2,
        scratch_shapes=[pltpu.SemaphoreType.DMA((4,))],
        compiler_params=pltpu.CompilerParams(vmem_limit_bytes=8 << 20),
        name="deliver",
    )(*arrays)


PACK = (1, 4, 2, 5, 7, 8, 0, 3, 6, 9)


def fast_shards(
    tokens, w_qkv, w_out, w_gate_up, w_down, norm_params, alibi_slope, lengths, placement, out_grad
):
    heads_n = lax.axis_size("head")
    blk_n = lax.axis_size("blk")
    head_idx = lax.axis_index("head")
    blk_idx = lax.axis_index("blk")
    tok_rows, width = tokens.shape
    per_dev = HEADS // heads_n
    group_rows = heads_n * tok_rows
    devs = heads_n * blk_n
    share = w_qkv.shape[0]
    bf16 = jnp.bfloat16

    held = [
        pltpu.with_memory_space_constraint(a, pltpu.MemorySpace.HBM)
        for a in (lengths, alibi_slope, tokens, w_qkv, w_out, norm_params.reshape(1, share), placement.reshape(devs, tok_rows))
    ]
    group_tokens, attn_w, q, kv, wo, norms, kcode, qcode = run_collect(held[0], *held[2:])
    wo = [wo] + [lax.ppermute(wo, "blk", [(i, i ^ (2 * r)) for i in range(blk_n)]) for r in (1, 2, 3)]
    mixed, lse = run_attend(held[0], held[1], q, kv, kcode, qcode)
    act, d_one, d_attn, d_heads, *sums, g_norm = run_middle(
        mixed, tokens, out_grad, norms, wo, w_gate_up, w_down.T
    )
    sums = [sums[0]] + [
        lax.ppermute(sums[r], "blk", [(i, i ^ (2 * r)) for i in range(blk_n)]) for r in (1, 2, 3)
    ]
    d_q, dkv, result = run_attend_back(
        held[0], held[1], q, kv, kcode, qcode, mixed, d_heads, lse, act
    )
    input_grad, s_qkv, s_out, s_norm = run_finish(
        dkv.reshape(blk_n, group_rows, 384), d_q.reshape(group_rows, 256),
        group_tokens.reshape(group_rows, width), attn_w.reshape(width, 640),
        d_attn, mixed.reshape(group_rows, 256), d_one, g_norm,
    )
    input_grad, s_qkv, s_out, s_norm, s_gu, s_down = run_deliver(input_grad, s_qkv, s_out, s_norm, *sums)
    return (
        result,
        input_grad,
        s_qkv,
        s_out,
        s_gu,
        s_down.T,
        s_norm.reshape(share, 1),
    )


def solution(mesh):
    placed = (
        P(("blk", "head"), None),
        P("blk", "head"),
        P("head", "blk"),
        P(None, "blk", "head"),
        P("head", "blk"),
        P("blk", "head"),
        P(),
        P(),
        P(),
        P(("blk", "head"), None),
    )
    small = mesh.shape["blk"] == 8 and mesh.shape["head"] == 4
    return jax.shard_map(
        fast_shards if small else shards,
        mesh=mesh,
        in_specs=placed,
        out_specs=(
            P(("blk", "head"), None),
            P(("blk", "head"), None),
            P("blk", "head"),
            P("head", "blk"),
            P(None, "blk", "head"),
            P("head", "blk"),
            P("blk", "head"),
        ),
        check_vma=False,
    )
```

```python
import jax
import jax.numpy as jnp
from jax import lax
from jax.experimental import pallas as pl
from jax.experimental.pallas import tpu as pltpu
from jax.sharding import PartitionSpec as P

HEADS = 12
HEAD_DIM = 64


masked_score = -1e30


def layer_norm(residual, norm_gain, norm_shift):
    center = residual - jnp.mean(residual, axis=-1, keepdims=True)
    spread = jnp.mean(center * center, axis=-1, keepdims=True)
    return center * lax.rsqrt(spread + 1e-05) * norm_gain + norm_shift


def geglu(gate, upward):
    return jax.nn.gelu(gate, approximate=False) * upward


def dot_back(grad_rows, weight):
    return lax.dot_general(
        grad_rows, weight, (((1,), (1,)), ((), ())), preferred_element_type=jnp.float32
    )


def weight_grad(left, right):
    return lax.dot_general(
        left, right, (((0,), (0,)), ((), ())), preferred_element_type=jnp.float32
    )


def seq_of(positions, seq_ends):
    return jnp.sum((positions[:, None] >= seq_ends[None, :]).astype(jnp.int32), axis=1)


def prefix_sums(lengths):
    count = lengths.shape[0]
    upto = jnp.arange(count)[None, :] <= jnp.arange(count)[:, None]
    return jnp.sum(jnp.where(upto, lengths[None, :], 0), axis=1)


def biased_scores(queries, key_rows, q_pos, k_pos, q_seq, k_seq, slopes, qk_scale):
    scores = (
        jnp.einsum("qhd,khd->hqk", queries, key_rows, preferred_element_type=jnp.float32) * qk_scale
    )
    distance = jnp.abs(q_pos[:, None] - k_pos[None, :]).astype(jnp.float32)
    scores = scores - slopes[:, None, None] * distance[None]
    same_seq = (q_seq[:, None] == k_seq[None, :])[None]
    return (scores, same_seq)


def shards(
    tokens, w_qkv, w_out, w_gate_up, w_down, norm_params, alibi_slope, lengths, placement, out_grad
):
    heads_n = lax.axis_size("head")
    head_idx = lax.axis_index("head")
    blk_idx = lax.axis_index("blk")
    tok_rows = tokens.shape[0]
    per_dev = HEADS // heads_n
    group_rows = heads_n * tok_rows
    qk_scale = HEAD_DIM ** (-0.5)
    group_tokens, norm_cols = (
        lax.all_gather(tokens, "head", axis=0, tiled=True),
        lax.all_gather(norm_params, "head", axis=1, tiled=True),
    )
    f_qkv, f_out, f_gu, f_down, f_norm = (
        lax.all_gather(w_qkv, "blk", axis=0, tiled=True),
        lax.all_gather(w_out, "blk", axis=1, tiled=True),
        lax.all_gather(w_gate_up, "blk", axis=1, tiled=True),
        lax.all_gather(w_down, "blk", axis=1, tiled=True),
        lax.all_gather(norm_cols, "blk", axis=0, tiled=True),
    )
    grouped = jnp.dot(group_tokens, f_qkv, preferred_element_type=jnp.float32).astype(jnp.bfloat16)
    grouped = grouped.reshape(group_rows, per_dev, 3, HEAD_DIM)
    norms = f_norm.astype(jnp.float32)
    queries = grouped[:, :, 0]
    key_rows = grouped[:, :, 1]
    values = grouped[:, :, 2]
    seq_ends = prefix_sums(lengths)
    q_pos = lax.dynamic_slice_in_dim(placement, blk_idx * group_rows, group_rows)
    q_seq = seq_of(q_pos, seq_ends)
    slopes = lax.dynamic_slice_in_dim(alibi_slope, head_idx * per_dev, per_dev)

    def split_rows(shard_part):
        block_count = shard_part[0].shape[0] // group_rows
        pieces = tuple(
            (arr.reshape((block_count, group_rows) + arr.shape[1:]) for arr in shard_part)
        )
        starts = group_rows * jnp.arange(block_count, dtype=jnp.int32)
        return pieces + (starts,)

    start_state = (
        jnp.full((per_dev, group_rows), masked_score, jnp.float32),
        jnp.zeros((per_dev, group_rows), jnp.float32),
        jnp.zeros((group_rows, per_dev, HEAD_DIM), jnp.float32),
    )
    running = start_state

    def forward_per_block(state, block_in):
        k_blk, v_blk, k_first = block_in
        row_best, row_total, out_sum = state
        k_pos = lax.dynamic_slice_in_dim(placement, k_first, group_rows)
        scores, same_seq = biased_scores(
            queries, k_blk, q_pos, k_pos, q_seq, seq_of(k_pos, seq_ends), slopes, qk_scale
        )
        row_top = jnp.max(jnp.where(same_seq, scores, masked_score), axis=2)
        new_best = jnp.maximum(row_best, row_top)
        factor = jnp.exp(row_best - new_best)
        prob_tile = jnp.where(same_seq, jnp.exp(scores - new_best[:, :, None]), 0.0)
        row_total = row_total * factor + jnp.sum(prob_tile, axis=2)
        out_sum = out_sum * factor.T[:, :, None] + jnp.einsum(
            "hqk,khd->qhd",
            prob_tile.astype(jnp.bfloat16),
            v_blk,
            preferred_element_type=jnp.float32,
        )
        return ((new_best, row_total, out_sum), None)

    running, _ = lax.scan(
        forward_per_block,
        running,
        split_rows(
            (
                lax.all_gather(key_rows, "blk", axis=0, tiled=True),
                lax.all_gather(values, "blk", axis=0, tiled=True),
            )
        ),
    )
    row_best, row_total, out_sum = running
    attended = (out_sum / row_total.T[:, :, None]).astype(jnp.bfloat16)
    log_total = row_best + jnp.log(row_total)
    mixed = attended.reshape(group_rows, per_dev * HEAD_DIM)
    attn_out = lax.psum_scatter(
        jnp.dot(mixed, f_out, preferred_element_type=jnp.float32).astype(jnp.bfloat16),
        "head",
        scatter_dimension=0,
        tiled=True,
    ).astype(jnp.float32)
    resid_one = tokens.astype(jnp.float32) + attn_out
    hidden, norm_one_back = jax.vjp(layer_norm, resid_one, norms[:, 0], norms[:, 1])
    hidden_low = hidden.astype(jnp.bfloat16)
    ffn_rows = lax.all_gather(hidden_low, "head", axis=0, tiled=True)
    gate = jnp.dot(ffn_rows, f_gu[0], preferred_element_type=jnp.float32)
    upward = jnp.dot(ffn_rows, f_gu[1], preferred_element_type=jnp.float32)
    gated, geglu_back = jax.vjp(geglu, gate, upward)
    gated_low = gated.astype(jnp.bfloat16)
    branch_part = jnp.dot(gated_low, f_down, preferred_element_type=jnp.float32)
    branch = lax.psum_scatter(
        branch_part.astype(jnp.bfloat16), "head", scatter_dimension=0, tiled=True
    ).astype(jnp.float32)
    result, norm_two_back = jax.vjp(layer_norm, hidden + branch, norms[:, 2], norms[:, 3])
    d_two, d_gain_two, d_shift_two = norm_two_back(out_grad.astype(jnp.float32))
    d_branch = d_two.astype(jnp.bfloat16)
    branch_rows = lax.all_gather(d_branch, "head", axis=0, tiled=True)
    g_down = weight_grad(gated_low, branch_rows)
    d_gate, d_up = geglu_back(dot_back(branch_rows, f_down))
    d_gate_low = d_gate.astype(jnp.bfloat16)
    d_up_low = d_up.astype(jnp.bfloat16)
    g_gate_up = jnp.stack([weight_grad(ffn_rows, d_gate_low), weight_grad(ffn_rows, d_up_low)])
    hidden_part = dot_back(d_gate_low, f_gu[0]) + dot_back(d_up_low, f_gu[1])
    d_hidden = d_two + lax.psum_scatter(
        hidden_part.astype(jnp.bfloat16), "head", scatter_dimension=0, tiled=True
    ).astype(jnp.float32)
    d_one, d_gain_one, d_shift_one = norm_one_back(d_hidden)
    d_attn = d_one.astype(jnp.bfloat16)
    attn_rows = lax.all_gather(d_attn, "head", axis=0, tiled=True)
    g_out = weight_grad(mixed, attn_rows)
    d_heads = dot_back(attn_rows, f_out).astype(jnp.bfloat16).reshape(group_rows, per_dev, HEAD_DIM)
    delta = jnp.sum(d_heads.astype(jnp.float32) * attended.astype(jnp.float32), axis=2).T
    zero_grad = jnp.zeros((group_rows, per_dev, HEAD_DIM), jnp.float32)
    grad_q = zero_grad

    def query_per_block(running, block_in):
        k_blk, v_blk, k_first = block_in
        k_pos = lax.dynamic_slice_in_dim(placement, k_first, group_rows)
        scores, same_seq = biased_scores(
            queries, k_blk, q_pos, k_pos, q_seq, seq_of(k_pos, seq_ends), slopes, qk_scale
        )
        prob_tile = jnp.where(same_seq, jnp.exp(scores - log_total[:, :, None]), 0.0)
        d_prob = jnp.einsum("qhd,khd->hqk", d_heads, v_blk, preferred_element_type=jnp.float32)
        d_score = (prob_tile * (d_prob - delta[:, :, None])).astype(jnp.bfloat16)
        running = (
            running
            + jnp.einsum("hqk,khd->qhd", d_score, k_blk, preferred_element_type=jnp.float32)
            * qk_scale
        )
        return (running, None)

    grad_q, _ = lax.scan(
        query_per_block,
        grad_q,
        split_rows(
            (
                lax.all_gather(key_rows, "blk", axis=0, tiled=True),
                lax.all_gather(values, "blk", axis=0, tiled=True),
            )
        ),
    )
    stats_lse, stats_delta = (
        lax.all_gather(log_total, "blk", axis=1, tiled=True),
        lax.all_gather(delta, "blk", axis=1, tiled=True),
    )
    running = (zero_grad, zero_grad)

    def key_per_block(state, block_in):
        q_blk, do_blk, q_first = block_in
        grad_k, grad_v = state
        other_pos = lax.dynamic_slice_in_dim(placement, q_first, group_rows)
        lse_blk = lax.dynamic_slice_in_dim(stats_lse, q_first, group_rows, 1)
        delta_blk = lax.dynamic_slice_in_dim(stats_delta, q_first, group_rows, 1)
        scores, same_seq = biased_scores(
            q_blk, key_rows, other_pos, q_pos, seq_of(other_pos, seq_ends), q_seq, slopes, qk_scale
        )
        prob_tile = jnp.where(same_seq, jnp.exp(scores - lse_blk[:, :, None]), 0.0)
        grad_v = grad_v + jnp.einsum(
            "hqk,qhd->khd",
            prob_tile.astype(jnp.bfloat16),
            do_blk,
            preferred_element_type=jnp.float32,
        )
        d_prob = jnp.einsum("qhd,khd->hqk", do_blk, values, preferred_element_type=jnp.float32)
        d_score = (prob_tile * (d_prob - delta_blk[:, :, None])).astype(jnp.bfloat16)
        grad_k = (
            grad_k
            + jnp.einsum("hqk,qhd->khd", d_score, q_blk, preferred_element_type=jnp.float32)
            * qk_scale
        )
        return ((grad_k, grad_v), None)

    running, _ = lax.scan(
        key_per_block,
        running,
        split_rows(
            (
                lax.all_gather(queries, "blk", axis=0, tiled=True),
                lax.all_gather(d_heads, "blk", axis=0, tiled=True),
            )
        ),
    )
    grad_k, grad_v = running
    d_grouped = jnp.stack([grad_q, grad_k, grad_v], axis=2).astype(jnp.bfloat16)
    g_norm = jnp.stack([d_gain_one, d_shift_one, d_gain_two, d_shift_two], axis=1)
    d_qkv = d_grouped.reshape(group_rows, per_dev * 3 * HEAD_DIM)
    g_qkv = weight_grad(group_tokens, d_qkv)
    input_sum, norm_share = (
        lax.psum_scatter(
            dot_back(d_qkv, f_qkv).astype(jnp.bfloat16), "head", scatter_dimension=0, tiled=True
        ).astype(jnp.float32),
        lax.psum_scatter(
            g_norm.astype(jnp.bfloat16), "head", scatter_dimension=1, tiled=True
        ).astype(jnp.float32),
    )
    input_grad = d_one + input_sum
    s_qkv, s_out, s_gu, s_down, s_norm = (
        lax.psum_scatter(g_qkv, "blk", scatter_dimension=0, tiled=True),
        lax.psum_scatter(g_out, "blk", scatter_dimension=1, tiled=True),
        lax.psum_scatter(g_gate_up, "blk", scatter_dimension=1, tiled=True),
        lax.psum_scatter(g_down, "blk", scatter_dimension=1, tiled=True),
        lax.psum_scatter(norm_share, "blk", scatter_dimension=0, tiled=True),
    )
    return (result.astype(jnp.bfloat16), input_grad, s_qkv, s_out, s_gu, s_down, s_norm)


Q_SLOTS = 32
K_SLOTS = 16
SEQ_STEP = 65536.0
FAR = 32768.0
LANE_OF = (0, 64, 192)


def by_head(rows, lanes):
    lane = lax.broadcasted_iota(jnp.int32, rows.shape, 1)
    parts = [jnp.where((lane >= first) & (lane < first + HEAD_DIM), rows, 0.0) for first in lanes]
    return jnp.concatenate(parts, axis=0).astype(jnp.bfloat16)


def by_head_turned(rows, lanes):
    turned = rows.T
    lane = lax.broadcasted_iota(jnp.int32, turned.shape, 0)
    parts = [jnp.where((lane >= first) & (lane < first + HEAD_DIM), turned, 0.0) for first in lanes]
    return jnp.concatenate(parts, axis=1).astype(jnp.bfloat16)


def key_tiles(kv_ref, j):
    rows = kv_ref.shape[0] * K_SLOTS
    blk = kv_ref[:, pl.ds(pl.multiple_of(j * K_SLOTS, K_SLOTS), K_SLOTS), :]
    return blk.reshape(rows, blk.shape[2])


def key_span(len_ref, i, devs):
    first = i * (Q_SLOTS * devs)
    last = first + Q_SLOTS * devs - 1
    end, low, high = 0, 0, 0
    for k in range(8):
        start = end
        end = end + len_ref[k]
        low = jnp.where((first >= start) & (first < end), start, low)
        high = jnp.where((last >= start) & (last < end), end, high)
    step = K_SLOTS * devs
    return low // step, (high + step - 1) // step


def attend(len_any, slope_any, q_ref, kv_ref, kcode_ref, qcode_ref, out_ref, lse_ref, vt_ref, len_ref, slope_ref, few):
    z = lax.axis_index("head")
    scalars = [
        pltpu.make_async_copy(len_any, len_ref, few.at[0]),
        pltpu.make_async_copy(slope_any, slope_ref, few.at[1]),
    ]
    for c in scalars:
        c.start()
    devs, slots, _ = kv_ref.shape
    rows = devs * K_SLOTS
    q_rows = q_ref.shape[0] * Q_SLOTS

    def turn(j, _):
        kv = key_tiles(kv_ref, j)[:, 128:384]
        vt_ref[j] = kv.T
        return 0

    lax.fori_loop(0, slots // K_SLOTS, turn, 0)
    for c in scalars:
        c.wait()

    def chunk(i, _):
        first = pl.multiple_of(i * Q_SLOTS, Q_SLOTS)
        q = q_ref[:, pl.ds(first, Q_SLOTS), :].reshape(q_rows, 256).astype(jnp.float32)
        qbt = by_head_turned(q, (0, 64, 128))
        qcode = qcode_ref[i, 0:1, :]
        lo, hi = key_span(len_ref, i, devs)

        def block(j, state):
            kv = key_tiles(kv_ref, j)
            keys = jnp.concatenate([kv[:, 0:128], kv[:, 256:384]], axis=1)
            s_all = jnp.dot(keys, qbt, preferred_element_type=jnp.float32)
            dist = jnp.abs(key_tiles(kcode_ref, j) - qcode)
            keep = dist < FAR
            fresh, ps = [], []
            for h in range(3):
                best, total, acc = state[h]
                s = jnp.where(keep, s_all[:, 128 * h : 128 * h + 128] - slope_ref[3 * z + h] * dist, masked_score)
                top = jnp.maximum(best, jnp.max(s, axis=0, keepdims=True))
                factor = jnp.exp(best - top)
                p = jnp.exp(s - top)
                total = total * factor + jnp.sum(p, axis=0, keepdims=True)
                ps.append(p.astype(jnp.bfloat16))
                fresh.append((top, total, acc * factor))
            both = jnp.dot(vt_ref[j, 0:128, :], jnp.concatenate(ps[0:2], axis=1), preferred_element_type=jnp.float32)
            last = jnp.dot(vt_ref[j, 192:256, :], ps[2], preferred_element_type=jnp.float32)
            new = (both[0:64, 0:128], both[64:128, 128:256], last)
            fresh = [(top, total, acc + term) for (top, total, acc), term in zip(fresh, new)]
            return tuple(fresh)

        start = tuple(
            (
                jnp.full((1, q_rows), masked_score, jnp.float32),
                jnp.zeros((1, q_rows), jnp.float32),
                jnp.zeros((64, q_rows), jnp.float32),
            )
            for _ in range(3)
        )
        done = lax.fori_loop(lo, hi, block, start)
        outs = [acc / total for _, total, acc in done]
        full = jnp.concatenate([outs[0], outs[1], jnp.zeros((64, q_rows), jnp.float32), outs[2]], axis=0)
        out_ref[:, pl.ds(first, Q_SLOTS), :] = full.T.astype(jnp.bfloat16).reshape(-1, Q_SLOTS, 256)
        for h in range(3):
            lse_ref[i, h : h + 1, :] = done[h][0] + jnp.log(done[h][1])
        return 0

    lax.fori_loop(0, slots // Q_SLOTS, chunk, 0)


def attend_back(len_any, slope_any, q_ref, kv_ref, kcode_ref, qcode_ref, out_ref, do_ref, lse_ref, act_any,
                dq_ref, dkv_ref, act_out, kt_ref, sum_ref, sem, len_ref, slope_ref, few):
    z = lax.axis_index("head")
    scalars = [
        pltpu.make_async_copy(len_any, len_ref, few.at[0]),
        pltpu.make_async_copy(slope_any, slope_ref, few.at[1]),
    ]
    for c in scalars:
        c.start()
    devs, slots, _ = kv_ref.shape
    rows = devs * K_SLOTS
    q_rows = q_ref.shape[0] * Q_SLOTS
    scale = HEAD_DIM ** (-0.5)
    along = [
        pltpu.make_async_copy(act_any, act_out, sem.at[0]),
    ]
    for c in along:
        c.start()

    def turn(j, _):
        kv = key_tiles(kv_ref, j)
        keys = jnp.concatenate([kv[:, 0:128], kv[:, 256:384]], axis=1)
        kt_ref[j] = keys.T
        sum_ref[j] = jnp.zeros((rows, 384), jnp.float32)
        return 0

    lax.fori_loop(0, slots // K_SLOTS, turn, 0)
    for c in scalars:
        c.wait()

    def chunk(i, _):
        first = pl.multiple_of(i * Q_SLOTS, Q_SLOTS)
        q = q_ref[:, pl.ds(first, Q_SLOTS), :].reshape(q_rows, 256).astype(jnp.float32)
        qbd = by_head(q, (0, 64, 128))
        qbt = by_head_turned(q, (0, 64, 128))
        do = do_ref[:, pl.ds(first, Q_SLOTS), :].reshape(q_rows, 256).astype(jnp.float32)
        out = out_ref[:, pl.ds(first, Q_SLOTS), :].reshape(q_rows, 256).astype(jnp.float32)
        dobd = by_head(do, LANE_OF)
        dobt = by_head_turned(do, LANE_OF)
        prod = (do * out).T
        delta = [jnp.sum(prod[f : f + 64, :], axis=0, keepdims=True) for f in LANE_OF]
        qcode = qcode_ref[i, 0:1, :]
        lo, hi = key_span(len_ref, i, devs)

        def block(j, state):
            kv = key_tiles(kv_ref, j)
            keys = jnp.concatenate([kv[:, 0:128], kv[:, 256:384]], axis=1)
            vals = kv[:, 128:384]
            s_all = jnp.dot(keys, qbt, preferred_element_type=jnp.float32)
            dp_all = jnp.dot(vals, dobt, preferred_element_type=jnp.float32)
            dist = jnp.abs(key_tiles(kcode_ref, j) - qcode)
            keep = dist < FAR
            ps, dss, fresh = [], [], []
            for h in range(3):
                s = s_all[:, 128 * h : 128 * h + 128] - slope_ref[3 * z + h] * dist - lse_ref[i, h : h + 1, :]
                p = jnp.exp(jnp.where(keep, s, masked_score))
                ds = (p * (dp_all[:, 128 * h : 128 * h + 128] - delta[h])).astype(jnp.bfloat16)
                ps.append(p.astype(jnp.bfloat16))
                dss.append(ds)
            both = jnp.dot(kt_ref[j, 0:128, :], jnp.concatenate(dss[0:2], axis=1), preferred_element_type=jnp.float32)
            last = jnp.dot(kt_ref[j, 128:192, :], dss[2], preferred_element_type=jnp.float32)
            fresh = [state[0] + both[0:64, 0:128], state[1] + both[64:128, 128:256], state[2] + last]
            dv = jnp.dot(jnp.concatenate(ps, axis=1), dobd, preferred_element_type=jnp.float32)
            dk = jnp.dot(jnp.concatenate(dss, axis=1), qbd, preferred_element_type=jnp.float32)
            sum_ref[j, :, 0:128] += dk[:, 0:128]
            sum_ref[j, :, 128:256] += dv[:, 0:128]
            sum_ref[j, :, 256:384] += dk[:, 128:256] + dv[:, 128:256]
            return tuple(fresh)

        start = tuple(jnp.zeros((64, q_rows), jnp.float32) for _ in range(3))
        done = lax.fori_loop(lo, hi, block, start)
        full = jnp.concatenate(done + (jnp.zeros((64, q_rows), jnp.float32),), axis=0) * scale
        dq_ref[:, pl.ds(first, Q_SLOTS), :] = full.T.astype(jnp.bfloat16).reshape(-1, Q_SLOTS, 256)
        return 0

    lax.fori_loop(0, slots // Q_SLOTS, chunk, 0)

    def leave(j, _):
        dkv_ref[:, pl.ds(pl.multiple_of(j * K_SLOTS, K_SLOTS), K_SLOTS), :] = (
            sum_ref[j].astype(jnp.bfloat16).reshape(devs, K_SLOTS, 384)
        )
        return 0

    lax.fori_loop(0, slots // K_SLOTS, leave, 0)
    for c in along:
        c.wait()


VM = pl.BlockSpec(memory_space=pltpu.VMEM)
SM = pl.BlockSpec(memory_space=pltpu.SMEM)
ANY = pl.BlockSpec(memory_space=pl.ANY)
HBM = pl.BlockSpec(memory_space=pltpu.MemorySpace.HBM)


def run_attend(lengths, slopes, q, kv, kcode, qcode):
    heads_n, slots, _ = q.shape
    devs = kv.shape[0]
    return pl.pallas_call(
        attend,
        out_shape=(
            jax.ShapeDtypeStruct((heads_n, slots, 256), jnp.bfloat16),
            jax.ShapeDtypeStruct((slots // Q_SLOTS, 8, heads_n * Q_SLOTS), jnp.float32),
        ),
        in_specs=[HBM, HBM, VM, VM, VM, VM],
        out_specs=(VM, VM),
        scratch_shapes=[
            pltpu.VMEM((slots // K_SLOTS, 256, devs * K_SLOTS), jnp.bfloat16),
            pltpu.SMEM((8,), jnp.int32),
            pltpu.SMEM((HEADS,), jnp.float32),
            pltpu.SemaphoreType.DMA((2,)),
        ],
        compiler_params=pltpu.CompilerParams(vmem_limit_bytes=16 << 20),
        name="attend",
    )(lengths, slopes, q, kv, kcode, qcode)


def run_attend_back(lengths, slopes, q, kv, kcode, qcode, out, do, lse, act):
    heads_n, slots, _ = q.shape
    devs = kv.shape[0]
    return pl.pallas_call(
        attend_back,
        out_shape=(
            jax.ShapeDtypeStruct((heads_n, slots, 256), jnp.bfloat16),
            jax.ShapeDtypeStruct((devs, slots, 384), jnp.bfloat16),
            jax.ShapeDtypeStruct(act.shape, act.dtype),
        ),
        in_specs=[HBM, HBM, VM, VM, VM, VM, VM, VM, VM, ANY],
        out_specs=(VM, VM, ANY),
        scratch_shapes=[
            pltpu.VMEM((slots // K_SLOTS, 256, devs * K_SLOTS), jnp.bfloat16),
            pltpu.VMEM((slots // K_SLOTS, devs * K_SLOTS, 384), jnp.float32),
            pltpu.SemaphoreType.DMA((2,)),
            pltpu.SMEM((8,), jnp.int32),
            pltpu.SMEM((HEADS,), jnp.float32),
            pltpu.SemaphoreType.DMA((2,)),
        ],
        compiler_params=pltpu.CompilerParams(vmem_limit_bytes=26 << 20),
        name="attend_back",
    )(lengths, slopes, q, kv, kcode, qcode, out, do, lse, act)


MESH = pl.DeviceIdType.MESH


def dot_tn(left, right):
    return lax.dot_general(left, right, (((0,), (0,)), ((), ())), preferred_element_type=jnp.float32)


def dot_nt(left, right):
    return lax.dot_general(left, right, (((1,), (1,)), ((), ())), preferred_element_type=jnp.float32)


def greet(peers):
    barrier = pltpu.get_barrier_semaphore()
    for peer in peers:
        pl.semaphore_signal(barrier, inc=1, device_id=peer, device_id_type=MESH)
    pl.semaphore_wait(barrier, len(peers))


class Sender:
    def __init__(self, sems):
        self.sems = sems
        self.used = 0
        self.left = []

    def make(self, src, dst, peer, arrive=None):
        i = self.used
        self.used += 1
        assert i < self.sems.shape[1]
        copy = pltpu.make_async_remote_copy(
            src_ref=src, dst_ref=dst, send_sem=self.sems.at[0, i],
            recv_sem=self.sems.at[1, i] if arrive is None else arrive,
            device_id=peer, device_id_type=MESH,
        )
        copy.arrive = self.sems.at[1, i]
        return copy

    def start(self, copy, only=None):
        self.left.append((copy, only))
        if only is None:
            copy.start()
        else:
            pl.when(only)(copy.start)
        return copy

    def __call__(self, src, dst, peer, only=None, arrive=None):
        return self.start(self.make(src, dst, peer, arrive), only)

    def sent(self, copy):
        [(_, only)] = [item for item in self.left if item[0] is copy]
        self.left = [item for item in self.left if item[0] is not copy]
        if only is None:
            copy.wait_send()
        else:
            pl.when(only)(copy.wait_send)

    def finish(self):
        for copy, only in self.left:
            if only is None:
                copy.wait_send()
            else:
                pl.when(only)(copy.wait_send)


class Plane:
    def __init__(self, go, core, slot, me, near, flat, sib):
        self.go, self.core, self.slot, self.near, self.flat, self.sib = go, core, slot, near, flat, sib
        self.one = go(slot(me), slot(me), flat[1])
        self.two = go(slot(me), slot(me), flat[2])
        self.three = go.make(slot(me), slot(me), flat[3])
        self.handed = [self.hand(me)]

    def hand(self, n):
        return self.go(self.slot(n), self.slot(n), self.sib)

    def pass_on(self):
        for copy, r, turn in ((self.one, 1, 0), (self.two, 2, 1)):
            copy.wait_recv()
            block = self.slot(self.near[r])
            self.go(block, block, self.flat[3 - r], only=self.core == turn, arrive=self.three.arrive)
            self.handed.append(self.hand(self.near[r]))

    def last(self):
        self.three.wait_recv()
        self.handed.append(self.hand(self.near[3]))

    def whole(self):
        for copy in self.handed:
            copy.wait_recv()


class Spread:
    def __init__(self, go, mid, slot, z, line):
        self.go, self.mid, self.slot, self.z, self.line = go, mid, slot, z, line
        self.two = go(slot(z), slot(z), line[2])
        self.three = go.make(slot(z), slot(z), line[3])
        self.one = go.make(slot(z), slot(z), line[1])

    def rest(self):
        self.go.start(self.three, only=self.mid)
        self.go.start(self.one)

    def pass_on(self):
        self.two.wait_recv()
        far = self.slot(self.z ^ 2)
        self.go(far, far, self.line[1], only=self.mid, arrive=self.three.arrive)

    def wait(self):
        self.one.wait_recv()
        self.three.wait_recv()


def finish(
    dkv_ref, dq_ref, tok_ref, w_ref, datt_ref, datt_two, mixed_ref, done_ref, gn_ref,
    dx_ref, sqkv_ref, sout_ref, snorm_ref,
    kv_sib, kv_sum, kv_in, g_one, g_two, g_sib, g_sum, g_in,
    part, part_in, att, dkvq, nz_in, nrow, np_in, relay, sems,
):
    b = lax.axis_index("blk")
    z = lax.axis_index("head")
    chip, core = b // 2, b % 2
    sib = (chip * 2 + 1 - core, z)
    flat = [((chip ^ r) * 2 + core, z) for r in (0, 1, 2, 3)]
    line = [(b, z ^ r) for r in (0, 1, 2, 3)]
    greet([sib] + flat[1:] + line[1:])
    f32, bf16 = jnp.float32, jnp.bfloat16
    go = Sender(sems)
    mid = (z == 1) | (z == 2)
    ends = (z == 0) | (z == 3)

    def member(r):
        return pl.ds(pl.multiple_of((z ^ r) * 128, 128), 128)

    kv_c = {
        (q, r): go(dkv_ref.at[(chip ^ r) * 2 + 1 - core, member(q)], kv_sib.at[q, r], sib)
        for q in (3, 2, 1, 0) for r in (3, 1, 2, 0)
    }
    att[z] = datt_ref[...]
    att[z ^ 2] = datt_two[...]
    att_three = go.make(att.at[z], att.at[z], line[3])
    go(att.at[z ^ 2], att.at[z ^ 2], line[1], only=mid, arrive=att_three.arrive)
    go.start(att_three, only=mid)
    att_one = go(att.at[z], att.at[z], line[1])
    nz_c = [go(gn_ref.at[pl.ds((z ^ r) * 8, 8)], nz_in.at[r - 1], line[r]) for r in (1, 2, 3)]
    side, other = 1 + core, 2 - core
    to_side = ((chip ^ side) * 2 + core, z)
    to_other = ((chip ^ other) * 2 + core, z)
    kv_plain, kv_pass, kv_both = {}, {}, {}
    for q in (3, 2, 1, 0):
        for r in (3, 1, 2, 0):
            kv_c[q, r].wait_recv()
            both = dkv_ref[(chip ^ r) * 2 + core, member(q), :].astype(f32) + kv_sib[q, r].astype(f32)
            kv_sum[q, r] = both.astype(bf16)
            if r == 3:
                kv_pass[q] = go(kv_sum.at[q, 3], kv_in.at[q, 2], to_side)
        kv_plain[q] = go(kv_sum.at[q, side], kv_in.at[q, 0], to_side)

    def add_passed(q):
        kv_pass[q].wait_recv()
        both = kv_sum[q, other].astype(f32) + kv_in[q, 2].astype(f32)
        kv_sum[q, other] = both.astype(bf16)
        kv_both[q] = go(kv_sum.at[q, other], kv_in.at[q, 1], to_other)

    add_passed(3)
    add_passed(2)
    dkvq[:, 384:640] = dq_ref[...]

    @pl.when(ends)
    def _():
        relay[...] = jnp.zeros((128, 768), bf16)
        part_in[2] = jnp.zeros((128, 768), bf16)


    def send_half(part_i, grads):
        return [
            go(grads.at[pl.ds(pl.multiple_of(((chip ^ r) * 2 + 1 - core) * 96, 96), 96)], g_sib.at[part_i, r], sib)
            for r in (3, 1, 2, 0)
        ]

    def send_sum(part_i, grads, copies):
        out = []
        for k, r in enumerate((3, 1, 2, 0)):
            copies[k].wait_recv()
            mine = grads[pl.ds(pl.multiple_of(((chip ^ r) * 2 + core) * 96, 96), 96), :].astype(f32)
            g_sum[part_i, r] = (mine + g_sib[part_i, r].astype(f32)).astype(bf16)
            if r:
                out.append(go(g_sum.at[part_i, r], g_in.at[part_i, r - 1], flat[r]))
        return out

    def settle(part_i, copies):
        for c in copies:
            c.wait_recv()
        return (
            g_sum[part_i, 0].astype(f32) + g_in[part_i, 0].astype(f32)
            + g_in[part_i, 1].astype(f32) + g_in[part_i, 2].astype(f32)
        )

    for c in nz_c:
        c.wait_recv()
    nrow[0] = gn_ref[pl.ds(z * 8, 8)] + nz_in[0] + nz_in[1] + nz_in[2]
    np_c = [go(nrow.at[0], np_in.at[r], flat[r]) for r in (1, 2, 3)]
    last = dot_tn(tok_ref[...], dq_ref[...])
    g_one[:, 0:128] = last[:, 0:128].astype(bf16)
    dx_c = []
    for q in (3, 2, 1, 0):
        if q == 1:
            att_one.wait_recv()
            att_three.wait_recv()
            outs = dot_tn(att[...].reshape(512, 768), mixed_ref[...])
            g_one[:, 128:256] = outs[:, 0:128].astype(bf16)
            g_one[:, 256:384] = (outs[:, 128:256] + last[:, 128:256]).astype(bf16)
            one_c = send_half(0, g_one)
        if q >= 2:
            add_passed(q - 2)
        kv_plain[q].wait_recv()
        kv_both[q].wait_recv()
        dkvq[member(q), 0:384] = (
            kv_sum[q, 0].astype(f32) + kv_in[q, 0].astype(f32) + kv_in[q, 1].astype(f32)
        ).astype(bf16)
        term = dot_nt(dkvq[member(q), :], w_ref[...])
        if q == 3:
            part[2] = term.astype(bf16)
            passed = go(part.at[2], relay, line[1], only=ends)
            dx_three = go(part.at[2], part_in.at[2], line[3], only=mid)
        elif q == 2:
            far = term
        elif q == 1:
            part[0] = term.astype(bf16)
            dx_c.append(go(part.at[0], part_in.at[0], line[1]))
            pl.when(mid)(passed.wait_recv)
            part[1] = (far + relay[...].astype(f32)).astype(bf16)
            dx_c.append(go(part.at[1], part_in.at[1], line[2]))
        else:
            dx_ref[...] = done_ref[...] + term
    one_out = send_sum(0, g_one, one_c)
    g_two[...] = dot_tn(tok_ref[...], dkvq[:, 0:384]).astype(bf16)
    two_c = send_half(1, g_two)
    two_out = send_sum(1, g_two, two_c)
    for c in np_c:
        c.wait_recv()
    nrow[1] = nrow[0] + np_in[1] + np_in[2] + np_in[3]
    half = go(nrow.at[1], np_in.at[0], sib)
    half.wait_recv()
    full = nrow[1] + np_in[0]
    snorm_ref[...] = pltpu.roll(full, lax.rem(768 - 96 * b, 768), 1)[0:1, 0:96]
    two = settle(1, two_out)
    one = settle(0, one_out)
    piece = [two[:, 64 * i : 64 * i + 64] for i in range(6)]
    piece += [one[:, 0:64], one[:, 64:128], one[:, 256:320]]
    for k, i in enumerate((6, 0, 2, 7, 1, 3, 8, 4, 5)):
        sqkv_ref[:, 64 * k : 64 * k + 64] = piece[i]
    turned = jnp.concatenate([one[:, 128:384], jnp.zeros((32, 256), f32)], axis=0).T
    sout_ref[0:128, :] = turned[0:128, 0:96]
    sout_ref[128:192, :] = turned[192:256, 0:96]
    for c in dx_c:
        c.wait_recv()
    pl.when(mid)(dx_three.wait_recv)
    dx_ref[...] += part_in[0].astype(f32) + part_in[1].astype(f32) + part_in[2].astype(f32)
    go.finish()


def run_finish(dkv, dq, toks, w, datt, datt_two, mixed, done, gn):
    f32, bf16 = jnp.float32, jnp.bfloat16
    V = pltpu.VMEM
    return pl.pallas_call(
        finish,
        out_shape=(
            jax.ShapeDtypeStruct((128, 768), f32),
            jax.ShapeDtypeStruct((96, 576), f32),
            jax.ShapeDtypeStruct((192, 96), f32),
            jax.ShapeDtypeStruct((1, 96), f32),
        ),
        in_specs=[VM] * 9,
        out_specs=(VM,) * 4,
        scratch_shapes=[
            V((4, 4, 128, 384), bf16), V((4, 4, 128, 384), bf16), V((4, 3, 128, 384), bf16),
            V((768, 384), bf16), V((768, 384), bf16),
            V((2, 4, 96, 384), bf16), V((2, 4, 96, 384), bf16), V((2, 3, 96, 384), bf16),
            V((3, 128, 768), bf16), V((3, 128, 768), bf16), V((4, 128, 768), bf16), V((512, 640), bf16),
            V((3, 8, 768), f32), V((2, 8, 768), f32), V((4, 8, 768), f32), V((128, 768), bf16),
            pltpu.SemaphoreType.DMA((2, 72)),
        ],
        compiler_params=pltpu.CompilerParams(
            collective_id=5, has_side_effects=True, vmem_limit_bytes=28 << 20
        ),
        name="finish",
    )(dkv, dq, toks, w, datt, datt_two, mixed, done, gn)


def collect(
    len_any, tok_any, wq_any, wout_any, nrm_any, pos_any,
    gt, wat, q_ref, kv, wout, norm_out, kcode, qcode,
    wa_ref, wo_ref, nr, code_ref, wq_ref, wout_ref, nrm_row, pos_ref, nrm_ref, len_ref, sems, lsem,
):
    b = lax.axis_index("blk")
    z = lax.axis_index("head")
    chip, core = b // 2, b % 2
    sib = (chip * 2 + 1 - core, z)
    near = [(chip ^ r) * 2 + core for r in (0, 1, 2, 3)]
    flat = [(n, z) for n in near]
    line = [(b, z ^ r) for r in (0, 1, 2, 3)]
    f32, bf16 = jnp.float32, jnp.bfloat16
    fetch = [
        pltpu.make_async_copy(wq_any, wq_ref, lsem.at[0]),
        pltpu.make_async_copy(wout_any, wout_ref, lsem.at[1]),
        pltpu.make_async_copy(nrm_any, nrm_row, lsem.at[2]),
        pltpu.make_async_copy(pos_any, pos_ref, lsem.at[3]),
        pltpu.make_async_copy(tok_any, gt.at[z], lsem.at[4]),
        pltpu.make_async_copy(len_any, len_ref, lsem.at[5]),
    ]
    for c in fetch:
        c.start()
    for c in fetch:
        c.wait()
    go = Sender(sems)
    mid = (z == 1) | (z == 2)
    ends = (z == 0) | (z == 3)

    wq = wq_ref[...].astype(f32)
    wo = wout_ref[...].astype(f32)
    wo = jnp.concatenate([wo[0:128], jnp.zeros((64, 96), f32), wo[128:192]], axis=0)
    wo = jnp.concatenate([wo, jnp.zeros((256, 32), f32)], axis=1).T[0:96]
    wo_ref[...] = wo.astype(bf16)
    piece = [wq[:, 64 * i : 64 * i + 64] for i in range(9)] + [wo[:, 192:256]]
    for k in range(5):
        tile = jnp.concatenate([piece[PACK[2 * k]], piece[PACK[2 * k + 1]]], axis=1)
        wa_ref[:, 128 * k : 128 * k + 128] = tile.astype(bf16)
    wat[b] = wa_ref[...]
    wout[z] = wo_ref[...]
    nrm_ref[...] = jnp.zeros((8, 128), f32)
    nrm_ref[0:1, 0:96] = nrm_row[...].astype(f32)
    nr[b, z] = nrm_ref[...]
    greet([sib] + flat[1:] + line[1:])
    tok_z = [Spread(go, mid, lambda j, h=h: gt.at[j, pl.ds(64 * h, 64)], z, line) for h in range(2)]
    wa_p = [go(wa_ref, wat.at[b], flat[r]) for r in (3, 1, 2)]
    wa_s = [go(wa_ref, wat.at[b], sib)]
    pos = pos_ref[...]
    seq = jnp.zeros(pos.shape, f32)
    end = 0
    for k in range(8):
        end = end + len_ref[k]
        seq = seq + jnp.where(pos >= end, 1.0, 0.0)
    code_ref[...] = pos.astype(f32) + SEQ_STEP * seq

    def spread_code(d, _):
        kcode[d] = jnp.broadcast_to(code_ref[pl.ds(d, 1), :], (128, 128)).T
        return 0

    lax.fori_loop(0, 32, spread_code, 0)
    own_code = [code_ref[pl.ds(b * 4 + j, 1), :] for j in range(4)]
    for i in range(4):
        qcode[i, 0:1, :] = jnp.concatenate([c[:, 32 * i : 32 * i + 32] for c in own_code], axis=1)
    go.sent(tok_z[0].two)
    tok_z[0].rest()
    tok_z[0].pass_on()
    go.sent(tok_z[1].two)
    tok_z[1].rest()
    wo_z = [go(wo_ref, wout.at[z], line[r]) for r in (3, 2, 1)]
    nr_z = [go(nrm_ref, nr.at[b, z], line[r]) for r in (3, 2, 1)]
    for k, r in enumerate((3, 1, 2)):
        wa_p[k].wait_recv()
        wa_s.append(go(wat.at[near[r]], wat.at[near[r]], sib))
    tok_z[1].pass_on()
    for c in wa_s:
        c.wait_recv()
    kv_p = []
    for r in (0, 2, 1, 3):
        for s in tok_z:
            if r in (1, 3):
                (s.one if r == 1 else s.three).wait_recv()
        j = z ^ r
        rows = jnp.dot(gt[j], wat[...].reshape(768, 640), preferred_element_type=f32)
        kv[b * 4 + j] = rows[:, 0:384].astype(bf16)
        if r == 3:
            kv_l = [go(kv.at[b * 4 + j], kv.at[b * 4 + j], flat[s]) for s in (3, 1, 2)]
            passed.append(go(kv.at[b * 4 + j], kv.at[b * 4 + j], sib))
        else:
            kv_p.append(Plane(go, core, lambda n, j=j: kv.at[n * 4 + j], b, near, flat, sib))
        q_ref[j] = rows[:, 384:640].astype(bf16) * bf16(HEAD_DIM ** (-0.5))
        if r:
            kv_p[{2: 0, 1: 1, 3: 2}[r]].pass_on()
        if r == 1:
            for c in wo_z + nr_z:
                c.wait_recv()
            nr_p = [go(nr.at[b], nr.at[b], flat[r]) for r in (3, 1, 2)]
            passed = [go(nr.at[b], nr.at[b], sib)]
    for k, r in enumerate((3, 1, 2)):
        nr_p[k].wait_recv()
        passed.append(go(nr.at[near[r]], nr.at[near[r]], sib))
    for p in kv_p:
        p.last()
    for k, s in enumerate((3, 1, 2)):
        kv_l[k].wait_recv()
        n = near[s] * 4 + (z ^ 3)
        passed.append(go(kv.at[n], kv.at[n], sib))
    for p in kv_p:
        p.whole()
    for c in passed:
        c.wait_recv()
    total = jnp.zeros((8, 768), f32)
    for n in range(8):
        rows = jnp.concatenate([nr[n, j, 0:1, :] for j in range(4)] + [jnp.zeros((4, 128), f32)], axis=0)
        total = total + pltpu.roll(jnp.concatenate([rows, jnp.zeros((8, 640), f32)], axis=1), 96 * n, 1)
    norm_out[...] = total
    go.finish()


def run_collect(lengths, tok, wq, wo, nrm, pos):
    f32, bf16 = jnp.float32, jnp.bfloat16
    S = jax.ShapeDtypeStruct
    V = pltpu.VMEM
    return pl.pallas_call(
        collect,
        out_shape=(
            S((4, 128, 768), bf16), S((8, 96, 640), bf16), S((4, 128, 256), bf16), S((32, 128, 384), bf16),
            S((4, 96, 256), bf16), S((8, 768), f32), S((32, 128, 128), f32), S((4, 8, 128), f32),
        ),
        in_specs=[HBM] * 6,
        out_specs=(VM,) * 8,
        scratch_shapes=[
            V((96, 640), bf16), V((96, 256), bf16), V((8, 4, 8, 128), f32), V((32, 128), f32),
            V((96, 576), bf16), V((192, 96), bf16), V((1, 96), bf16), V((32, 128), jnp.int32), V((8, 128), f32),
            pltpu.SMEM((8,), jnp.int32), pltpu.SemaphoreType.DMA((2, 80)), pltpu.SemaphoreType.DMA((6,)),
        ],
        compiler_params=pltpu.CompilerParams(
            collective_id=1, has_side_effects=True, vmem_limit_bytes=20 << 20
        ),
        name="collect",
    )(lengths, tok, wq, wo, nrm, pos)


def moments(rows):
    center = rows - jnp.mean(rows, axis=-1, keepdims=True)
    spread = lax.rsqrt(jnp.mean(center * center, axis=-1, keepdims=True) + 1e-05)
    return center * spread, spread


def norm_back(grad, gain, unit, spread):
    scaled = grad * gain
    return spread * (
        scaled - jnp.mean(scaled, axis=-1, keepdims=True) - unit * jnp.mean(scaled * unit, axis=-1, keepdims=True)
    )


def middle(
    mixed_ref, tok_any, og_any, norm_ref, wo_0, wo_1, wo_2, wo_3, gu_any, down_any,
    act_ref, done_ref, datt_ref, dheads, sum_0, sum_1, sum_2, sum_3, gn_ref,
    mix_in, wffn, rows_in, drow_in, gelu_a, gelu_b, gated, dgate, dup,
    part, part_in, part2, part2_in, gff, ffn_sib, hid, unit_one, held, held_two, head_out,
    wf_ref, tok_ref, og_ref, wout, part_relay, part2_relay, sems, lsem,
):
    b = lax.axis_index("blk")
    z = lax.axis_index("head")
    chip, core = b // 2, b % 2
    sib = (chip * 2 + 1 - core, z)
    near = [(chip ^ r) * 2 + core for r in (0, 1, 2, 3)]
    flat = [(n, z) for n in near]
    line = [(b, z ^ r) for r in (0, 1, 2, 3)]
    f32, bf16 = jnp.float32, jnp.bfloat16
    own = [
        pltpu.make_async_copy(gu_any, wf_ref.at[0:2], lsem.at[0]),
        pltpu.make_async_copy(down_any, wf_ref.at[2], lsem.at[1]),
        pltpu.make_async_copy(tok_any, tok_ref, lsem.at[2]),
        pltpu.make_async_copy(og_any, og_ref, lsem.at[3]),
    ]
    for c in own:
        c.start()
    greet([sib] + flat[1:] + line[1:])
    go = Sender(sems)
    mid = (z == 1) | (z == 2)
    ends = (z == 0) | (z == 3)

    HALF = 64

    @pl.when(ends)
    def _():
        for h in range(2):
            part_in[h, 2] = jnp.zeros((HALF, 768), bf16)
            part2_in[h, 2] = jnp.zeros((HALF, 768), bf16)

    def scatter(out, arrived, relay, terms, h):
        passed = go(out.at[h, z ^ 3], relay.at[h], line[1], only=ends)
        three = go(out.at[h, z ^ 3], arrived.at[h, 2], line[3], only=mid)
        one = go(out.at[h, z ^ 1], arrived.at[h, 0], line[1])
        two = go.make(out.at[h, z ^ 2], arrived.at[h, 1], line[2])
        go.start(two, only=ends)

        def later():
            @pl.when(mid)
            def _():
                passed.wait_recv()
                out[h, z ^ 2] = (terms[h, z ^ 2] + relay[h].astype(f32)).astype(bf16)

            go.left.append((two, mid))
            pl.when(mid)(two.start)

        return one, two, three, later

    def gathered(copies):
        copies[0].wait_recv()
        copies[1].wait_recv()
        pl.when(mid)(copies[2].wait_recv)

    wo_s = []
    for r, ref in enumerate((wo_0, wo_1, wo_2, wo_3)):
        wo_s.append(go(ref, wout.at[:, near[r]], sib))
        wout[:, near[r]] = ref[...]
    mix_c = []
    for h in range(2):
        rows = pl.ds(HALF * h, HALF)
        mix_c.append([go(mixed_ref.at[z ^ r, rows], mix_in.at[h, z], line[r]) for r in (3, 2, 1)])
    for c in own:
        c.wait()
    mine = pltpu.make_async_copy(wf_ref, wffn.at[:, b], lsem.at[0])
    mine.start()
    mine.wait()
    wf_p = [Plane(go, core, lambda n, t=t: wffn.at[t, n], b, near, flat, sib) for t in range(3)]

    for c in wo_s:
        c.wait_recv()

    def out_weight(j):
        return wout[j].reshape(768, 256)

    spreads = []
    row_c = []
    for h in range(2):
        rows = pl.ds(HALF * h, HALF)
        mix_in[h, z] = mixed_ref[z, rows, :]
        for c in mix_c[h]:
            c.wait_recv()
        attn = dot_nt(mix_in[h, 0], out_weight(0))
        for j in (1, 2, 3):
            attn = attn + dot_nt(mix_in[h, j], out_weight(j))
        unit, spread = moments(tok_ref[rows, :].astype(f32) + attn)
        hidden = unit * norm_ref[0:1, :] + norm_ref[1:2, :]
        unit_one[h] = unit
        spreads.append(spread)
        hid[h] = hidden
        rows_in[h, z] = hidden.astype(bf16)
        row_c.append(Spread(go, mid, lambda j, h=h: rows_in.at[h, j], z, line))
        if h == 1:
            row_c[0].rest()
        wf_p[h].pass_on()
    row_c[0].pass_on()
    row_c[1].rest()
    wf_p[2].pass_on()
    row_c[1].pass_on()
    for p in wf_p:
        p.last()
    wf_p[0].whole()
    wf_p[1].whole()

    def weight(t):
        return wffn[t].reshape(768, 768)

    part_c = []
    for h in range(2):
        row_c[h].wait()
        rows = rows_in[h].reshape(4 * HALF, 768)
        gate = jnp.dot(rows, weight(0), preferred_element_type=f32)
        up = jnp.dot(rows, weight(1), preferred_element_type=f32)
        half = 0.5 + 0.5 * lax.erf(gate * (0.5**0.5))
        value = gate * half
        low = (value * up).astype(bf16)
        gated[h] = low
        if h == 0:
            wf_p[2].whole()
        term = dot_nt(low, weight(2)).reshape(4, HALF, 768)
        held[h] = term
        part[h] = term.astype(bf16)
        if h == 1:
            part_c[0][3]()
        part_c.append(scatter(part, part_in, part_relay, held, h))
        slope = half + gate * jnp.exp(-0.5 * gate * gate) * 0.3989422804014327
        gelu_a[h] = slope * up
        gelu_b[h] = value
    part_c[1][3]()
    gains = []
    drow_c = []
    for h in range(2):
        rows = pl.ds(HALF * h, HALF)
        if h == 1:
            drow_c[0].pass_on()
        gathered(part_c[h])
        branch = held[h, z] + part_in[h, 0].astype(f32) + part_in[h, 1].astype(f32) + part_in[h, 2].astype(f32)
        unit_two, spread_two = moments(hid[h] + branch)
        grad = og_ref[rows, :].astype(f32)
        d_two = norm_back(grad, norm_ref[2:3, :], unit_two, spread_two)
        hid[h] = d_two
        drow_in[h, z] = d_two.astype(bf16)
        drow_c.append(Spread(go, mid, lambda j, h=h: drow_in.at[h, j], z, line))
        act_ref[rows, :] = (unit_two * norm_ref[2:3, :] + norm_ref[3:4, :]).astype(bf16)
        gains.append((jnp.sum(grad * unit_two, axis=0, keepdims=True), jnp.sum(grad, axis=0, keepdims=True)))
        drow_c[h].rest()
    gn_ref[...] = jnp.zeros((32, 768), f32)
    gn_ref[16:17, :] = gains[0][0] + gains[1][0]
    gn_ref[24:25, :] = gains[0][1] + gains[1][1]
    part2_c = []
    for h in range(2):
        if h == 1:
            drow_c[1].pass_on()
        drow_c[h].wait()
        d_gated = jnp.dot(drow_in[h].reshape(4 * HALF, 768), weight(2), preferred_element_type=f32)
        dg = (d_gated * gelu_a[h]).astype(bf16)
        du = (d_gated * gelu_b[h]).astype(bf16)
        dgate[h] = dg
        dup[h] = du
        term = (dot_nt(dg, weight(0)) + dot_nt(du, weight(1))).reshape(4, HALF, 768)
        held_two[h] = term
        part2[h] = term.astype(bf16)
        if h == 1:
            part2_c[0][3]()
        part2_c.append(scatter(part2, part2_in, part2_relay, held_two, h))
    part2_c[1][3]()
    sib_c = []
    acts = rows_in[...].reshape(512, 768)
    for t in (2, 0, 1):
        if t == 2:
            total = dot_tn(drow_in[...].reshape(512, 768), gated[...].reshape(512, 768))
        else:
            total = dot_tn(acts, (dgate, dup)[t][...].reshape(512, 768))
        gff[t] = total.astype(bf16).reshape(4, 2, 96, 768)
        sib_c.append(go(gff.at[t, :, 1 - core], ffn_sib.at[t], sib))
    gains = []
    head_c = []
    for h in range(2):
        rows = pl.ds(HALF * h, HALF)
        gathered(part2_c[h])
        d_hidden = (
            hid[h] + held_two[h, z]
            + part2_in[h, 0].astype(f32) + part2_in[h, 1].astype(f32) + part2_in[h, 2].astype(f32)
        )
        unit = unit_one[h]
        d_one = norm_back(d_hidden, norm_ref[0:1, :], unit, spreads[h])
        low_one = d_one.astype(bf16)
        for r in (3, 2, 1, 0):
            term = jnp.dot(low_one, out_weight(z ^ r), preferred_element_type=f32).astype(bf16)
            if r:
                head_out[h, r - 1] = term
                head_c.append(go(head_out.at[h, r - 1], dheads.at[z, rows], line[r]))
            else:
                dheads[z, rows, :] = term
        done_ref[rows, :] = d_one
        datt_ref[rows, :] = low_one
        gains.append((jnp.sum(d_hidden * unit, axis=0, keepdims=True), jnp.sum(d_hidden, axis=0, keepdims=True)))
    gn_ref[0:1, :] = gains[0][0] + gains[1][0]
    gn_ref[8:9, :] = gains[0][1] + gains[1][1]
    for k, t in enumerate((2, 0, 1)):
        sib_c[k].wait_recv()
        for r, ref in enumerate((sum_0, sum_1, sum_2, sum_3)):
            both = gff[t, chip ^ r, core].astype(f32) + ffn_sib[t, chip ^ r].astype(f32)
            ref[t] = both.astype(bf16)
    for c in head_c:
        c.wait_recv()
    go.finish()


def run_middle(mixed, tok, og, norms, wo, gu, down):
    f32, bf16 = jnp.float32, jnp.bfloat16
    S = jax.ShapeDtypeStruct
    V = pltpu.VMEM
    halves = (2, 256, 768)
    return pl.pallas_call(
        middle,
        out_shape=(
            S((128, 768), bf16), S((128, 768), f32), S((128, 768), bf16), S((4, 128, 256), bf16),
            *[S((3, 96, 768), bf16)] * 4, S((32, 768), f32),
        ),
        in_specs=[VM, HBM, HBM, VM, VM, VM, VM, VM, HBM, HBM],
        out_specs=(VM,) * 9,
        scratch_shapes=[
            V((2, 4, 64, 256), bf16), V((3, 8, 96, 768), bf16), V((2, 4, 64, 768), bf16), V((2, 4, 64, 768), bf16),
            V(halves, f32), V(halves, f32), V(halves, bf16), V(halves, bf16), V(halves, bf16),
            V((2, 4, 64, 768), bf16), V((2, 3, 64, 768), bf16), V((2, 4, 64, 768), bf16), V((2, 3, 64, 768), bf16),
            V((3, 4, 2, 96, 768), bf16), V((3, 4, 96, 768), bf16),
            V((2, 64, 768), f32), V((2, 64, 768), f32), V((2, 4, 64, 768), f32), V((2, 4, 64, 768), f32),
            V((2, 3, 64, 256), bf16),
            V((3, 96, 768), bf16), V((128, 768), bf16), V((128, 768), bf16), V((4, 8, 96, 256), bf16), V((2, 64, 768), bf16), V((2, 64, 768), bf16),
            pltpu.SemaphoreType.DMA((2, 108)), pltpu.SemaphoreType.DMA((4,)),
        ],
        compiler_params=pltpu.CompilerParams(
            collective_id=3, has_side_effects=True, vmem_limit_bytes=36 << 20
        ),
        name="middle",
    )(mixed, tok, og, norms, *wo, gu, down)


def deliver(*refs):
    dx, sqkv, sout, snorm, *sums = refs[:8]
    o_dx, o_qkv, o_out, o_norm, o_gu, o_down, sem = refs[8:]
    pairs = ((dx, o_dx), (sqkv, o_qkv), (sout, o_out), (snorm, o_norm))
    copies = [pltpu.make_async_copy(s, d, sem.at[i]) for i, (s, d) in enumerate(pairs)]
    for c in copies:
        c.start()
    for t in range(3):
        total = sum(s[t].astype(jnp.float32) for s in sums)
        if t < 2:
            o_gu[t] = total
        else:
            o_down[...] = total
    for c in copies:
        c.wait()


def run_deliver(*arrays):
    f32 = jnp.float32
    S = jax.ShapeDtypeStruct
    return pl.pallas_call(
        deliver,
        out_shape=(
            S((128, 768), f32), S((96, 576), f32), S((192, 96), f32), S((1, 96), f32),
            S((2, 96, 768), f32), S((96, 768), f32),
        ),
        in_specs=[ANY] * 4 + [VM] * 4,
        out_specs=(ANY,) * 4 + (VM,) * 2,
        scratch_shapes=[pltpu.SemaphoreType.DMA((4,))],
        compiler_params=pltpu.CompilerParams(vmem_limit_bytes=8 << 20),
        name="deliver",
    )(*arrays)


PACK = (1, 4, 2, 5, 7, 8, 0, 3, 6, 9)


def fast_shards(
    tokens, w_qkv, w_out, w_gate_up, w_down, norm_params, alibi_slope, lengths, placement, out_grad
):
    heads_n = lax.axis_size("head")
    blk_n = lax.axis_size("blk")
    head_idx = lax.axis_index("head")
    blk_idx = lax.axis_index("blk")
    tok_rows, width = tokens.shape
    per_dev = HEADS // heads_n
    group_rows = heads_n * tok_rows
    devs = heads_n * blk_n
    share = w_qkv.shape[0]
    bf16 = jnp.bfloat16

    held = [
        pltpu.with_memory_space_constraint(a, pltpu.MemorySpace.HBM)
        for a in (lengths, alibi_slope, tokens, w_qkv, w_out, norm_params.reshape(1, share), placement.reshape(devs, tok_rows))
    ]
    group_tokens, attn_w, q, kv, wo, norms, kcode, qcode = run_collect(held[0], *held[2:])
    wo = [wo] + [lax.ppermute(wo, "blk", [(i, i ^ (2 * r)) for i in range(blk_n)]) for r in (1, 2, 3)]
    mixed, lse = run_attend(held[0], held[1], q, kv, kcode, qcode)
    act, d_one, d_attn, d_heads, *sums, g_norm = run_middle(
        mixed, tokens, out_grad, norms, wo, w_gate_up, w_down.T
    )
    sums = [sums[0]] + [
        lax.ppermute(sums[r], "blk", [(i, i ^ (2 * r)) for i in range(blk_n)]) for r in (1, 2, 3)
    ]
    d_attn_two = lax.ppermute(d_attn, "head", [(i, i ^ 2) for i in range(heads_n)])
    d_q, dkv, result = run_attend_back(
        held[0], held[1], q, kv, kcode, qcode, mixed, d_heads, lse, act
    )
    input_grad, s_qkv, s_out, s_norm = run_finish(
        dkv.reshape(blk_n, group_rows, 384), d_q.reshape(group_rows, 256),
        group_tokens.reshape(group_rows, width), attn_w.reshape(width, 640),
        d_attn, d_attn_two, mixed.reshape(group_rows, 256), d_one, g_norm,
    )
    input_grad, s_qkv, s_out, s_norm, s_gu, s_down = run_deliver(input_grad, s_qkv, s_out, s_norm, *sums)
    return (
        result,
        input_grad,
        s_qkv,
        s_out,
        s_gu,
        s_down.T,
        s_norm.reshape(share, 1),
    )


def solution(mesh):
    placed = (
        P(("blk", "head"), None),
        P("blk", "head"),
        P("head", "blk"),
        P(None, "blk", "head"),
        P("head", "blk"),
        P("blk", "head"),
        P(),
        P(),
        P(),
        P(("blk", "head"), None),
    )
    small = mesh.shape["blk"] == 8 and mesh.shape["head"] == 4
    return jax.shard_map(
        fast_shards if small else shards,
        mesh=mesh,
        in_specs=placed,
        out_specs=(
            P(("blk", "head"), None),
            P(("blk", "head"), None),
            P("blk", "head"),
            P("head", "blk"),
            P(None, "blk", "head"),
            P("head", "blk"),
            P("blk", "head"),
        ),
        check_vma=False,
    )
```

```python
import jax
import jax.numpy as jnp
from jax import lax
from jax.experimental import pallas as pl
from jax.experimental.pallas import tpu as pltpu
from jax.sharding import PartitionSpec as P

HEADS = 12
HEAD_DIM = 64


masked_score = -1e30


def layer_norm(residual, norm_gain, norm_shift):
    center = residual - jnp.mean(residual, axis=-1, keepdims=True)
    spread = jnp.mean(center * center, axis=-1, keepdims=True)
    return center * lax.rsqrt(spread + 1e-05) * norm_gain + norm_shift


def geglu(gate, upward):
    return jax.nn.gelu(gate, approximate=False) * upward


def dot_back(grad_rows, weight):
    return lax.dot_general(
        grad_rows, weight, (((1,), (1,)), ((), ())), preferred_element_type=jnp.float32
    )


def weight_grad(left, right):
    return lax.dot_general(
        left, right, (((0,), (0,)), ((), ())), preferred_element_type=jnp.float32
    )


def seq_of(positions, seq_ends):
    return jnp.sum((positions[:, None] >= seq_ends[None, :]).astype(jnp.int32), axis=1)


def prefix_sums(lengths):
    count = lengths.shape[0]
    upto = jnp.arange(count)[None, :] <= jnp.arange(count)[:, None]
    return jnp.sum(jnp.where(upto, lengths[None, :], 0), axis=1)


def biased_scores(queries, key_rows, q_pos, k_pos, q_seq, k_seq, slopes, qk_scale):
    scores = (
        jnp.einsum("qhd,khd->hqk", queries, key_rows, preferred_element_type=jnp.float32) * qk_scale
    )
    distance = jnp.abs(q_pos[:, None] - k_pos[None, :]).astype(jnp.float32)
    scores = scores - slopes[:, None, None] * distance[None]
    same_seq = (q_seq[:, None] == k_seq[None, :])[None]
    return (scores, same_seq)


def shards(
    tokens, w_qkv, w_out, w_gate_up, w_down, norm_params, alibi_slope, lengths, placement, out_grad
):
    heads_n = lax.axis_size("head")
    head_idx = lax.axis_index("head")
    blk_idx = lax.axis_index("blk")
    tok_rows = tokens.shape[0]
    per_dev = HEADS // heads_n
    group_rows = heads_n * tok_rows
    qk_scale = HEAD_DIM ** (-0.5)
    group_tokens, norm_cols = (
        lax.all_gather(tokens, "head", axis=0, tiled=True),
        lax.all_gather(norm_params, "head", axis=1, tiled=True),
    )
    f_qkv, f_out, f_gu, f_down, f_norm = (
        lax.all_gather(w_qkv, "blk", axis=0, tiled=True),
        lax.all_gather(w_out, "blk", axis=1, tiled=True),
        lax.all_gather(w_gate_up, "blk", axis=1, tiled=True),
        lax.all_gather(w_down, "blk", axis=1, tiled=True),
        lax.all_gather(norm_cols, "blk", axis=0, tiled=True),
    )
    grouped = jnp.dot(group_tokens, f_qkv, preferred_element_type=jnp.float32).astype(jnp.bfloat16)
    grouped = grouped.reshape(group_rows, per_dev, 3, HEAD_DIM)
    norms = f_norm.astype(jnp.float32)
    queries = grouped[:, :, 0]
    key_rows = grouped[:, :, 1]
    values = grouped[:, :, 2]
    seq_ends = prefix_sums(lengths)
    q_pos = lax.dynamic_slice_in_dim(placement, blk_idx * group_rows, group_rows)
    q_seq = seq_of(q_pos, seq_ends)
    slopes = lax.dynamic_slice_in_dim(alibi_slope, head_idx * per_dev, per_dev)

    def split_rows(shard_part):
        block_count = shard_part[0].shape[0] // group_rows
        pieces = tuple(
            (arr.reshape((block_count, group_rows) + arr.shape[1:]) for arr in shard_part)
        )
        starts = group_rows * jnp.arange(block_count, dtype=jnp.int32)
        return pieces + (starts,)

    start_state = (
        jnp.full((per_dev, group_rows), masked_score, jnp.float32),
        jnp.zeros((per_dev, group_rows), jnp.float32),
        jnp.zeros((group_rows, per_dev, HEAD_DIM), jnp.float32),
    )
    running = start_state

    def forward_per_block(state, block_in):
        k_blk, v_blk, k_first = block_in
        row_best, row_total, out_sum = state
        k_pos = lax.dynamic_slice_in_dim(placement, k_first, group_rows)
        scores, same_seq = biased_scores(
            queries, k_blk, q_pos, k_pos, q_seq, seq_of(k_pos, seq_ends), slopes, qk_scale
        )
        row_top = jnp.max(jnp.where(same_seq, scores, masked_score), axis=2)
        new_best = jnp.maximum(row_best, row_top)
        factor = jnp.exp(row_best - new_best)
        prob_tile = jnp.where(same_seq, jnp.exp(scores - new_best[:, :, None]), 0.0)
        row_total = row_total * factor + jnp.sum(prob_tile, axis=2)
        out_sum = out_sum * factor.T[:, :, None] + jnp.einsum(
            "hqk,khd->qhd",
            prob_tile.astype(jnp.bfloat16),
            v_blk,
            preferred_element_type=jnp.float32,
        )
        return ((new_best, row_total, out_sum), None)

    running, _ = lax.scan(
        forward_per_block,
        running,
        split_rows(
            (
                lax.all_gather(key_rows, "blk", axis=0, tiled=True),
                lax.all_gather(values, "blk", axis=0, tiled=True),
            )
        ),
    )
    row_best, row_total, out_sum = running
    attended = (out_sum / row_total.T[:, :, None]).astype(jnp.bfloat16)
    log_total = row_best + jnp.log(row_total)
    mixed = attended.reshape(group_rows, per_dev * HEAD_DIM)
    attn_out = lax.psum_scatter(
        jnp.dot(mixed, f_out, preferred_element_type=jnp.float32).astype(jnp.bfloat16),
        "head",
        scatter_dimension=0,
        tiled=True,
    ).astype(jnp.float32)
    resid_one = tokens.astype(jnp.float32) + attn_out
    hidden, norm_one_back = jax.vjp(layer_norm, resid_one, norms[:, 0], norms[:, 1])
    hidden_low = hidden.astype(jnp.bfloat16)
    ffn_rows = lax.all_gather(hidden_low, "head", axis=0, tiled=True)
    gate = jnp.dot(ffn_rows, f_gu[0], preferred_element_type=jnp.float32)
    upward = jnp.dot(ffn_rows, f_gu[1], preferred_element_type=jnp.float32)
    gated, geglu_back = jax.vjp(geglu, gate, upward)
    gated_low = gated.astype(jnp.bfloat16)
    branch_part = jnp.dot(gated_low, f_down, preferred_element_type=jnp.float32)
    branch = lax.psum_scatter(
        branch_part.astype(jnp.bfloat16), "head", scatter_dimension=0, tiled=True
    ).astype(jnp.float32)
    result, norm_two_back = jax.vjp(layer_norm, hidden + branch, norms[:, 2], norms[:, 3])
    d_two, d_gain_two, d_shift_two = norm_two_back(out_grad.astype(jnp.float32))
    d_branch = d_two.astype(jnp.bfloat16)
    branch_rows = lax.all_gather(d_branch, "head", axis=0, tiled=True)
    g_down = weight_grad(gated_low, branch_rows)
    d_gate, d_up = geglu_back(dot_back(branch_rows, f_down))
    d_gate_low = d_gate.astype(jnp.bfloat16)
    d_up_low = d_up.astype(jnp.bfloat16)
    g_gate_up = jnp.stack([weight_grad(ffn_rows, d_gate_low), weight_grad(ffn_rows, d_up_low)])
    hidden_part = dot_back(d_gate_low, f_gu[0]) + dot_back(d_up_low, f_gu[1])
    d_hidden = d_two + lax.psum_scatter(
        hidden_part.astype(jnp.bfloat16), "head", scatter_dimension=0, tiled=True
    ).astype(jnp.float32)
    d_one, d_gain_one, d_shift_one = norm_one_back(d_hidden)
    d_attn = d_one.astype(jnp.bfloat16)
    attn_rows = lax.all_gather(d_attn, "head", axis=0, tiled=True)
    g_out = weight_grad(mixed, attn_rows)
    d_heads = dot_back(attn_rows, f_out).astype(jnp.bfloat16).reshape(group_rows, per_dev, HEAD_DIM)
    delta = jnp.sum(d_heads.astype(jnp.float32) * attended.astype(jnp.float32), axis=2).T
    zero_grad = jnp.zeros((group_rows, per_dev, HEAD_DIM), jnp.float32)
    grad_q = zero_grad

    def query_per_block(running, block_in):
        k_blk, v_blk, k_first = block_in
        k_pos = lax.dynamic_slice_in_dim(placement, k_first, group_rows)
        scores, same_seq = biased_scores(
            queries, k_blk, q_pos, k_pos, q_seq, seq_of(k_pos, seq_ends), slopes, qk_scale
        )
        prob_tile = jnp.where(same_seq, jnp.exp(scores - log_total[:, :, None]), 0.0)
        d_prob = jnp.einsum("qhd,khd->hqk", d_heads, v_blk, preferred_element_type=jnp.float32)
        d_score = (prob_tile * (d_prob - delta[:, :, None])).astype(jnp.bfloat16)
        running = (
            running
            + jnp.einsum("hqk,khd->qhd", d_score, k_blk, preferred_element_type=jnp.float32)
            * qk_scale
        )
        return (running, None)

    grad_q, _ = lax.scan(
        query_per_block,
        grad_q,
        split_rows(
            (
                lax.all_gather(key_rows, "blk", axis=0, tiled=True),
                lax.all_gather(values, "blk", axis=0, tiled=True),
            )
        ),
    )
    stats_lse, stats_delta = (
        lax.all_gather(log_total, "blk", axis=1, tiled=True),
        lax.all_gather(delta, "blk", axis=1, tiled=True),
    )
    running = (zero_grad, zero_grad)

    def key_per_block(state, block_in):
        q_blk, do_blk, q_first = block_in
        grad_k, grad_v = state
        other_pos = lax.dynamic_slice_in_dim(placement, q_first, group_rows)
        lse_blk = lax.dynamic_slice_in_dim(stats_lse, q_first, group_rows, 1)
        delta_blk = lax.dynamic_slice_in_dim(stats_delta, q_first, group_rows, 1)
        scores, same_seq = biased_scores(
            q_blk, key_rows, other_pos, q_pos, seq_of(other_pos, seq_ends), q_seq, slopes, qk_scale
        )
        prob_tile = jnp.where(same_seq, jnp.exp(scores - lse_blk[:, :, None]), 0.0)
        grad_v = grad_v + jnp.einsum(
            "hqk,qhd->khd",
            prob_tile.astype(jnp.bfloat16),
            do_blk,
            preferred_element_type=jnp.float32,
        )
        d_prob = jnp.einsum("qhd,khd->hqk", do_blk, values, preferred_element_type=jnp.float32)
        d_score = (prob_tile * (d_prob - delta_blk[:, :, None])).astype(jnp.bfloat16)
        grad_k = (
            grad_k
            + jnp.einsum("hqk,qhd->khd", d_score, q_blk, preferred_element_type=jnp.float32)
            * qk_scale
        )
        return ((grad_k, grad_v), None)

    running, _ = lax.scan(
        key_per_block,
        running,
        split_rows(
            (
                lax.all_gather(queries, "blk", axis=0, tiled=True),
                lax.all_gather(d_heads, "blk", axis=0, tiled=True),
            )
        ),
    )
    grad_k, grad_v = running
    d_grouped = jnp.stack([grad_q, grad_k, grad_v], axis=2).astype(jnp.bfloat16)
    g_norm = jnp.stack([d_gain_one, d_shift_one, d_gain_two, d_shift_two], axis=1)
    d_qkv = d_grouped.reshape(group_rows, per_dev * 3 * HEAD_DIM)
    g_qkv = weight_grad(group_tokens, d_qkv)
    input_sum, norm_share = (
        lax.psum_scatter(
            dot_back(d_qkv, f_qkv).astype(jnp.bfloat16), "head", scatter_dimension=0, tiled=True
        ).astype(jnp.float32),
        lax.psum_scatter(
            g_norm.astype(jnp.bfloat16), "head", scatter_dimension=1, tiled=True
        ).astype(jnp.float32),
    )
    input_grad = d_one + input_sum
    s_qkv, s_out, s_gu, s_down, s_norm = (
        lax.psum_scatter(g_qkv, "blk", scatter_dimension=0, tiled=True),
        lax.psum_scatter(g_out, "blk", scatter_dimension=1, tiled=True),
        lax.psum_scatter(g_gate_up, "blk", scatter_dimension=1, tiled=True),
        lax.psum_scatter(g_down, "blk", scatter_dimension=1, tiled=True),
        lax.psum_scatter(norm_share, "blk", scatter_dimension=0, tiled=True),
    )
    return (result.astype(jnp.bfloat16), input_grad, s_qkv, s_out, s_gu, s_down, s_norm)


Q_SLOTS = 32
K_SLOTS = 16
SEQ_STEP = 65536.0
FAR = 32768.0
LANE_OF = (0, 64, 192)


def by_head(rows, lanes):
    lane = lax.broadcasted_iota(jnp.int32, rows.shape, 1)
    parts = [jnp.where((lane >= first) & (lane < first + HEAD_DIM), rows, 0.0) for first in lanes]
    return jnp.concatenate(parts, axis=0).astype(jnp.bfloat16)


def by_head_turned(rows, lanes):
    turned = rows.T
    lane = lax.broadcasted_iota(jnp.int32, turned.shape, 0)
    parts = [jnp.where((lane >= first) & (lane < first + HEAD_DIM), turned, 0.0) for first in lanes]
    return jnp.concatenate(parts, axis=1).astype(jnp.bfloat16)


def key_tiles(kv_ref, j):
    rows = kv_ref.shape[0] * K_SLOTS
    blk = kv_ref[:, pl.ds(pl.multiple_of(j * K_SLOTS, K_SLOTS), K_SLOTS), :]
    return blk.reshape(rows, blk.shape[2])


def key_span(len_ref, i, devs):
    first = i * (Q_SLOTS * devs)
    last = first + Q_SLOTS * devs - 1
    end, low, high = 0, 0, 0
    for k in range(8):
        start = end
        end = end + len_ref[k]
        low = jnp.where((first >= start) & (first < end), start, low)
        high = jnp.where((last >= start) & (last < end), end, high)
    step = K_SLOTS * devs
    return low // step, (high + step - 1) // step


def attend(len_any, slope_any, q_ref, kv_ref, kcode_ref, qcode_ref, out_ref, lse_ref, vt_ref, len_ref, slope_ref, few):
    z = lax.axis_index("head")
    scalars = [
        pltpu.make_async_copy(len_any, len_ref, few.at[0]),
        pltpu.make_async_copy(slope_any, slope_ref, few.at[1]),
    ]
    for c in scalars:
        c.start()
    devs, slots, _ = kv_ref.shape
    rows = devs * K_SLOTS
    q_rows = q_ref.shape[0] * Q_SLOTS

    def turn(j, _):
        kv = key_tiles(kv_ref, j)[:, 128:384]
        vt_ref[j] = kv.T
        return 0

    lax.fori_loop(0, slots // K_SLOTS, turn, 0)
    for c in scalars:
        c.wait()

    def chunk(i, _):
        first = pl.multiple_of(i * Q_SLOTS, Q_SLOTS)
        q = q_ref[:, pl.ds(first, Q_SLOTS), :].reshape(q_rows, 256).astype(jnp.float32)
        qbt = by_head_turned(q, (0, 64, 128))
        qcode = qcode_ref[i, 0:1, :]
        lo, hi = key_span(len_ref, i, devs)

        def block(j, state):
            kv = key_tiles(kv_ref, j)
            keys = jnp.concatenate([kv[:, 0:128], kv[:, 256:384]], axis=1)
            s_all = jnp.dot(keys, qbt, preferred_element_type=jnp.float32)
            dist = jnp.abs(key_tiles(kcode_ref, j) - qcode)
            keep = dist < FAR
            fresh, ps = [], []
            for h in range(3):
                best, total, acc = state[h]
                s = jnp.where(keep, s_all[:, 128 * h : 128 * h + 128] - slope_ref[3 * z + h] * dist, masked_score)
                top = jnp.maximum(best, jnp.max(s, axis=0, keepdims=True))
                factor = jnp.exp(best - top)
                p = jnp.exp(s - top)
                total = total * factor + jnp.sum(p, axis=0, keepdims=True)
                ps.append(p.astype(jnp.bfloat16))
                fresh.append((top, total, acc * factor))
            both = jnp.dot(vt_ref[j, 0:128, :], jnp.concatenate(ps[0:2], axis=1), preferred_element_type=jnp.float32)
            last = jnp.dot(vt_ref[j, 192:256, :], ps[2], preferred_element_type=jnp.float32)
            new = (both[0:64, 0:128], both[64:128, 128:256], last)
            fresh = [(top, total, acc + term) for (top, total, acc), term in zip(fresh, new)]
            return tuple(fresh)

        start = tuple(
            (
                jnp.full((1, q_rows), masked_score, jnp.float32),
                jnp.zeros((1, q_rows), jnp.float32),
                jnp.zeros((64, q_rows), jnp.float32),
            )
            for _ in range(3)
        )
        done = lax.fori_loop(lo, hi, block, start)
        outs = [acc / total for _, total, acc in done]
        full = jnp.concatenate([outs[0], outs[1], jnp.zeros((64, q_rows), jnp.float32), outs[2]], axis=0)
        out_ref[:, pl.ds(first, Q_SLOTS), :] = full.T.astype(jnp.bfloat16).reshape(-1, Q_SLOTS, 256)
        for h in range(3):
            lse_ref[i, h : h + 1, :] = done[h][0] + jnp.log(done[h][1])
        return 0

    lax.fori_loop(0, slots // Q_SLOTS, chunk, 0)


def attend_back(len_any, slope_any, q_ref, kv_ref, kcode_ref, qcode_ref, out_ref, do_ref, lse_ref, act_any,
                dq_ref, dkv_ref, act_out, kt_ref, sum_ref, sem, len_ref, slope_ref, few):
    z = lax.axis_index("head")
    scalars = [
        pltpu.make_async_copy(len_any, len_ref, few.at[0]),
        pltpu.make_async_copy(slope_any, slope_ref, few.at[1]),
    ]
    for c in scalars:
        c.start()
    devs, slots, _ = kv_ref.shape
    rows = devs * K_SLOTS
    q_rows = q_ref.shape[0] * Q_SLOTS
    scale = HEAD_DIM ** (-0.5)
    along = [
        pltpu.make_async_copy(act_any, act_out, sem.at[0]),
    ]
    for c in along:
        c.start()

    def turn(j, _):
        kv = key_tiles(kv_ref, j)
        keys = jnp.concatenate([kv[:, 0:128], kv[:, 256:384]], axis=1)
        kt_ref[j] = keys.T
        sum_ref[j] = jnp.zeros((rows, 384), jnp.float32)
        return 0

    lax.fori_loop(0, slots // K_SLOTS, turn, 0)
    for c in scalars:
        c.wait()

    def chunk(i, _):
        first = pl.multiple_of(i * Q_SLOTS, Q_SLOTS)
        q = q_ref[:, pl.ds(first, Q_SLOTS), :].reshape(q_rows, 256).astype(jnp.float32)
        qbd = by_head(q, (0, 64, 128))
        qbt = by_head_turned(q, (0, 64, 128))
        do = do_ref[:, pl.ds(first, Q_SLOTS), :].reshape(q_rows, 256).astype(jnp.float32)
        out = out_ref[:, pl.ds(first, Q_SLOTS), :].reshape(q_rows, 256).astype(jnp.float32)
        dobd = by_head(do, LANE_OF)
        dobt = by_head_turned(do, LANE_OF)
        prod = (do * out).T
        delta = [jnp.sum(prod[f : f + 64, :], axis=0, keepdims=True) for f in LANE_OF]
        qcode = qcode_ref[i, 0:1, :]
        lo, hi = key_span(len_ref, i, devs)

        def block(j, state):
            kv = key_tiles(kv_ref, j)
            keys = jnp.concatenate([kv[:, 0:128], kv[:, 256:384]], axis=1)
            vals = kv[:, 128:384]
            s_all = jnp.dot(keys, qbt, preferred_element_type=jnp.float32)
            dp_all = jnp.dot(vals, dobt, preferred_element_type=jnp.float32)
            dist = jnp.abs(key_tiles(kcode_ref, j) - qcode)
            keep = dist < FAR
            ps, dss, fresh = [], [], []
            for h in range(3):
                s = s_all[:, 128 * h : 128 * h + 128] - slope_ref[3 * z + h] * dist - lse_ref[i, h : h + 1, :]
                p = jnp.exp(jnp.where(keep, s, masked_score))
                ds = (p * (dp_all[:, 128 * h : 128 * h + 128] - delta[h])).astype(jnp.bfloat16)
                ps.append(p.astype(jnp.bfloat16))
                dss.append(ds)
            both = jnp.dot(kt_ref[j, 0:128, :], jnp.concatenate(dss[0:2], axis=1), preferred_element_type=jnp.float32)
            last = jnp.dot(kt_ref[j, 128:192, :], dss[2], preferred_element_type=jnp.float32)
            fresh = [state[0] + both[0:64, 0:128], state[1] + both[64:128, 128:256], state[2] + last]
            dv = jnp.dot(jnp.concatenate(ps, axis=1), dobd, preferred_element_type=jnp.float32)
            dk = jnp.dot(jnp.concatenate(dss, axis=1), qbd, preferred_element_type=jnp.float32)
            sum_ref[j, :, 0:128] += dk[:, 0:128]
            sum_ref[j, :, 128:256] += dv[:, 0:128]
            sum_ref[j, :, 256:384] += dk[:, 128:256] + dv[:, 128:256]
            return tuple(fresh)

        start = tuple(jnp.zeros((64, q_rows), jnp.float32) for _ in range(3))
        done = lax.fori_loop(lo, hi, block, start)
        full = jnp.concatenate(done + (jnp.zeros((64, q_rows), jnp.float32),), axis=0) * scale
        dq_ref[:, pl.ds(first, Q_SLOTS), :] = full.T.astype(jnp.bfloat16).reshape(-1, Q_SLOTS, 256)
        return 0

    lax.fori_loop(0, slots // Q_SLOTS, chunk, 0)

    def leave(j, _):
        dkv_ref[:, pl.ds(pl.multiple_of(j * K_SLOTS, K_SLOTS), K_SLOTS), :] = (
            sum_ref[j].astype(jnp.bfloat16).reshape(devs, K_SLOTS, 384)
        )
        return 0

    lax.fori_loop(0, slots // K_SLOTS, leave, 0)
    for c in along:
        c.wait()


VM = pl.BlockSpec(memory_space=pltpu.VMEM)
SM = pl.BlockSpec(memory_space=pltpu.SMEM)
ANY = pl.BlockSpec(memory_space=pl.ANY)
HBM = pl.BlockSpec(memory_space=pltpu.MemorySpace.HBM)


def run_attend(lengths, slopes, q, kv, kcode, qcode):
    heads_n, slots, _ = q.shape
    devs = kv.shape[0]
    return pl.pallas_call(
        attend,
        out_shape=(
            jax.ShapeDtypeStruct((heads_n, slots, 256), jnp.bfloat16),
            jax.ShapeDtypeStruct((slots // Q_SLOTS, 8, heads_n * Q_SLOTS), jnp.float32),
        ),
        in_specs=[HBM, HBM, VM, VM, VM, VM],
        out_specs=(VM, VM),
        scratch_shapes=[
            pltpu.VMEM((slots // K_SLOTS, 256, devs * K_SLOTS), jnp.bfloat16),
            pltpu.SMEM((8,), jnp.int32),
            pltpu.SMEM((HEADS,), jnp.float32),
            pltpu.SemaphoreType.DMA((2,)),
        ],
        compiler_params=pltpu.CompilerParams(vmem_limit_bytes=16 << 20),
        name="attend",
    )(lengths, slopes, q, kv, kcode, qcode)


def run_attend_back(lengths, slopes, q, kv, kcode, qcode, out, do, lse, act):
    heads_n, slots, _ = q.shape
    devs = kv.shape[0]
    return pl.pallas_call(
        attend_back,
        out_shape=(
            jax.ShapeDtypeStruct((heads_n, slots, 256), jnp.bfloat16),
            jax.ShapeDtypeStruct((devs, slots, 384), jnp.bfloat16),
            jax.ShapeDtypeStruct(act.shape, act.dtype),
        ),
        in_specs=[HBM, HBM, VM, VM, VM, VM, VM, VM, VM, ANY],
        out_specs=(VM, VM, ANY),
        scratch_shapes=[
            pltpu.VMEM((slots // K_SLOTS, 256, devs * K_SLOTS), jnp.bfloat16),
            pltpu.VMEM((slots // K_SLOTS, devs * K_SLOTS, 384), jnp.float32),
            pltpu.SemaphoreType.DMA((2,)),
            pltpu.SMEM((8,), jnp.int32),
            pltpu.SMEM((HEADS,), jnp.float32),
            pltpu.SemaphoreType.DMA((2,)),
        ],
        compiler_params=pltpu.CompilerParams(vmem_limit_bytes=26 << 20),
        name="attend_back",
    )(lengths, slopes, q, kv, kcode, qcode, out, do, lse, act)


MESH = pl.DeviceIdType.MESH


def dot_tn(left, right):
    return lax.dot_general(left, right, (((0,), (0,)), ((), ())), preferred_element_type=jnp.float32)


def dot_nt(left, right):
    return lax.dot_general(left, right, (((1,), (1,)), ((), ())), preferred_element_type=jnp.float32)


def greet(peers):
    barrier = pltpu.get_barrier_semaphore()
    for peer in peers:
        pl.semaphore_signal(barrier, inc=1, device_id=peer, device_id_type=MESH)
    pl.semaphore_wait(barrier, len(peers))


class Sender:
    def __init__(self, sems):
        self.sems = sems
        self.used = 0
        self.left = []

    def make(self, src, dst, peer, arrive=None):
        i = self.used
        self.used += 1
        assert i < self.sems.shape[1]
        copy = pltpu.make_async_remote_copy(
            src_ref=src, dst_ref=dst, send_sem=self.sems.at[0, i],
            recv_sem=self.sems.at[1, i] if arrive is None else arrive,
            device_id=peer, device_id_type=MESH,
        )
        copy.arrive = self.sems.at[1, i]
        return copy

    def start(self, copy, only=None):
        self.left.append((copy, only))
        if only is None:
            copy.start()
        else:
            pl.when(only)(copy.start)
        return copy

    def __call__(self, src, dst, peer, only=None, arrive=None):
        return self.start(self.make(src, dst, peer, arrive), only)

    def sent(self, copy):
        [(_, only)] = [item for item in self.left if item[0] is copy]
        self.left = [item for item in self.left if item[0] is not copy]
        if only is None:
            copy.wait_send()
        else:
            pl.when(only)(copy.wait_send)

    def finish(self):
        for copy, only in self.left:
            if only is None:
                copy.wait_send()
            else:
                pl.when(only)(copy.wait_send)


class Plane:
    def __init__(self, go, core, slot, me, near, flat, sib):
        self.go, self.core, self.slot, self.near, self.flat, self.sib = go, core, slot, near, flat, sib
        self.one = go(slot(me), slot(me), flat[1])
        self.two = go(slot(me), slot(me), flat[2])
        self.three = go.make(slot(me), slot(me), flat[3])
        self.handed = [self.hand(me)]

    def hand(self, n):
        return self.go(self.slot(n), self.slot(n), self.sib)

    def pass_on(self):
        for copy, r, turn in ((self.one, 1, 0), (self.two, 2, 1)):
            copy.wait_recv()
            block = self.slot(self.near[r])
            self.go(block, block, self.flat[3 - r], only=self.core == turn, arrive=self.three.arrive)
            self.handed.append(self.hand(self.near[r]))

    def last(self):
        self.three.wait_recv()
        self.handed.append(self.hand(self.near[3]))

    def whole(self):
        for copy in self.handed:
            copy.wait_recv()


class Spread:
    def __init__(self, go, mid, slot, z, line):
        self.go, self.mid, self.slot, self.z, self.line = go, mid, slot, z, line
        self.two = go(slot(z), slot(z), line[2])
        self.three = go.make(slot(z), slot(z), line[3])
        self.one = go.make(slot(z), slot(z), line[1])

    def rest(self):
        self.go.start(self.three, only=self.mid)
        self.go.start(self.one)

    def pass_on(self):
        self.two.wait_recv()
        far = self.slot(self.z ^ 2)
        self.go(far, far, self.line[1], only=self.mid, arrive=self.three.arrive)

    def wait(self):
        self.one.wait_recv()
        self.three.wait_recv()


def finish(
    dkv_ref, dq_ref, tok_ref, w_ref, datt_ref, datt_two, mixed_ref, done_ref, gn_ref,
    dx_ref, sqkv_ref, sout_ref, snorm_ref,
    kv_sib, kv_sum, kv_in, g_one, g_two, g_sib, g_sum, g_in,
    part, part_in, att, dkvq, nz_in, nrow, np_in, relay, sems,
):
    b = lax.axis_index("blk")
    z = lax.axis_index("head")
    chip, core = b // 2, b % 2
    sib = (chip * 2 + 1 - core, z)
    flat = [((chip ^ r) * 2 + core, z) for r in (0, 1, 2, 3)]
    line = [(b, z ^ r) for r in (0, 1, 2, 3)]
    greet([sib] + flat[1:] + line[1:])
    f32, bf16 = jnp.float32, jnp.bfloat16
    go = Sender(sems)
    mid = (z == 1) | (z == 2)
    ends = (z == 0) | (z == 3)

    def member(r):
        return pl.ds(pl.multiple_of((z ^ r) * 128, 128), 128)

    kv_c = {
        (q, r): go(dkv_ref.at[(chip ^ r) * 2 + 1 - core, member(q)], kv_sib.at[q, r], sib)
        for q in (3, 2, 1, 0) for r in (3, 1, 2, 0)
    }
    att[z] = datt_ref[...]
    att[z ^ 2] = datt_two[...]
    att_three = go.make(att.at[z], att.at[z], line[3])
    go(att.at[z ^ 2], att.at[z ^ 2], line[1], only=mid, arrive=att_three.arrive)
    go.start(att_three, only=mid)
    att_one = go(att.at[z], att.at[z], line[1])
    nz_c = [go(gn_ref.at[pl.ds((z ^ r) * 8, 8)], nz_in.at[r - 1], line[r]) for r in (1, 2, 3)]
    side, other = 1 + core, 2 - core
    to_side = ((chip ^ side) * 2 + core, z)
    to_other = ((chip ^ other) * 2 + core, z)
    kv_plain, kv_pass, kv_both = {}, {}, {}
    for q in (3, 2, 1, 0):
        for r in (3, 1, 2, 0):
            kv_c[q, r].wait_recv()
            both = dkv_ref[(chip ^ r) * 2 + core, member(q), :].astype(f32) + kv_sib[q, r].astype(f32)
            kv_sum[q, r] = both.astype(bf16)
            if r == 3:
                kv_pass[q] = go(kv_sum.at[q, 3], kv_in.at[q, 2], to_side)
        kv_plain[q] = go(kv_sum.at[q, side], kv_in.at[q, 0], to_side)

    def add_passed(q):
        kv_pass[q].wait_recv()
        both = kv_sum[q, other].astype(f32) + kv_in[q, 2].astype(f32)
        kv_sum[q, other] = both.astype(bf16)
        kv_both[q] = go(kv_sum.at[q, other], kv_in.at[q, 1], to_other)

    add_passed(3)
    add_passed(2)
    dkvq[:, 384:640] = dq_ref[...]

    @pl.when(ends)
    def _():
        relay[...] = jnp.zeros((128, 768), bf16)
        part_in[2] = jnp.zeros((128, 768), bf16)


    def send_half(part_i, grads):
        return [
            go(grads.at[pl.ds(pl.multiple_of(((chip ^ r) * 2 + 1 - core) * 96, 96), 96)], g_sib.at[part_i, r], sib)
            for r in (3, 1, 2, 0)
        ]

    def send_sum(part_i, grads, copies):
        out = []
        for k, r in enumerate((3, 1, 2, 0)):
            copies[k].wait_recv()
            mine = grads[pl.ds(pl.multiple_of(((chip ^ r) * 2 + core) * 96, 96), 96), :].astype(f32)
            g_sum[part_i, r] = (mine + g_sib[part_i, r].astype(f32)).astype(bf16)
            if r:
                out.append(go(g_sum.at[part_i, r], g_in.at[part_i, r - 1], flat[r]))
        return out

    def settle(part_i, copies):
        for c in copies:
            c.wait_recv()
        return (
            g_sum[part_i, 0].astype(f32) + g_in[part_i, 0].astype(f32)
            + g_in[part_i, 1].astype(f32) + g_in[part_i, 2].astype(f32)
        )

    for c in nz_c:
        c.wait_recv()
    nrow[0] = gn_ref[pl.ds(z * 8, 8)] + nz_in[0] + nz_in[1] + nz_in[2]
    np_c = [go(nrow.at[0], np_in.at[r], flat[r]) for r in (1, 2, 3)]
    last = dot_tn(tok_ref[...], dq_ref[...])
    g_one[:, 0:128] = last[:, 0:128].astype(bf16)
    dx_c = []
    for q in (3, 2, 1, 0):
        if q == 1:
            att_one.wait_recv()
            att_three.wait_recv()
            outs = dot_tn(att[...].reshape(512, 768), mixed_ref[...])
            g_one[:, 128:256] = outs[:, 0:128].astype(bf16)
            g_one[:, 256:384] = (outs[:, 128:256] + last[:, 128:256]).astype(bf16)
            one_c = send_half(0, g_one)
        if q >= 2:
            add_passed(q - 2)
        kv_plain[q].wait_recv()
        kv_both[q].wait_recv()
        dkvq[member(q), 0:384] = (
            kv_sum[q, 0].astype(f32) + kv_in[q, 0].astype(f32) + kv_in[q, 1].astype(f32)
        ).astype(bf16)
        term = dot_nt(dkvq[member(q), :], w_ref[...])
        if q == 3:
            part[2] = term.astype(bf16)
            passed = go(part.at[2], relay, line[1], only=ends)
            dx_three = go(part.at[2], part_in.at[2], line[3], only=mid)
        elif q == 2:
            far = term
        elif q == 1:
            part[0] = term.astype(bf16)
            dx_c.append(go(part.at[0], part_in.at[0], line[1]))
            pl.when(mid)(passed.wait_recv)
            part[1] = (far + relay[...].astype(f32)).astype(bf16)
            dx_c.append(go(part.at[1], part_in.at[1], line[2]))
        else:
            dx_ref[...] = done_ref[...] + term
    one_out = send_sum(0, g_one, one_c)
    g_two[...] = dot_tn(tok_ref[...], dkvq[:, 0:384]).astype(bf16)
    two_c = send_half(1, g_two)
    two_out = send_sum(1, g_two, two_c)
    for c in np_c:
        c.wait_recv()
    nrow[1] = nrow[0] + np_in[1] + np_in[2] + np_in[3]
    half = go(nrow.at[1], np_in.at[0], sib)
    half.wait_recv()
    full = nrow[1] + np_in[0]
    snorm_ref[...] = pltpu.roll(full, lax.rem(768 - 96 * b, 768), 1)[0:1, 0:96]
    two = settle(1, two_out)
    one = settle(0, one_out)
    piece = [two[:, 64 * i : 64 * i + 64] for i in range(6)]
    piece += [one[:, 0:64], one[:, 64:128], one[:, 256:320]]
    for k, i in enumerate((6, 0, 2, 7, 1, 3, 8, 4, 5)):
        sqkv_ref[:, 64 * k : 64 * k + 64] = piece[i]
    turned = jnp.concatenate([one[:, 128:384], jnp.zeros((32, 256), f32)], axis=0).T
    sout_ref[0:128, :] = turned[0:128, 0:96]
    sout_ref[128:192, :] = turned[192:256, 0:96]
    for c in dx_c:
        c.wait_recv()
    pl.when(mid)(dx_three.wait_recv)
    dx_ref[...] += part_in[0].astype(f32) + part_in[1].astype(f32) + part_in[2].astype(f32)
    go.finish()


def run_finish(dkv, dq, toks, w, datt, datt_two, mixed, done, gn):
    f32, bf16 = jnp.float32, jnp.bfloat16
    V = pltpu.VMEM
    return pl.pallas_call(
        finish,
        out_shape=(
            jax.ShapeDtypeStruct((128, 768), f32),
            jax.ShapeDtypeStruct((96, 576), f32),
            jax.ShapeDtypeStruct((192, 96), f32),
            jax.ShapeDtypeStruct((1, 96), f32),
        ),
        in_specs=[VM] * 9,
        out_specs=(VM,) * 4,
        scratch_shapes=[
            V((4, 4, 128, 384), bf16), V((4, 4, 128, 384), bf16), V((4, 3, 128, 384), bf16),
            V((768, 384), bf16), V((768, 384), bf16),
            V((2, 4, 96, 384), bf16), V((2, 4, 96, 384), bf16), V((2, 3, 96, 384), bf16),
            V((3, 128, 768), bf16), V((3, 128, 768), bf16), V((4, 128, 768), bf16), V((512, 640), bf16),
            V((3, 8, 768), f32), V((2, 8, 768), f32), V((4, 8, 768), f32), V((128, 768), bf16),
            pltpu.SemaphoreType.DMA((2, 72)),
        ],
        compiler_params=pltpu.CompilerParams(
            collective_id=5, has_side_effects=True, vmem_limit_bytes=28 << 20
        ),
        name="finish",
    )(dkv, dq, toks, w, datt, datt_two, mixed, done, gn)


def collect(
    len_any, tok_any, wq_any, wout_any, nrm_any, pos_any,
    gt, wat, q_ref, kv, wout, norm_out, kcode, qcode,
    wa_ref, wo_ref, nr, code_ref, wq_ref, wout_ref, nrm_row, pos_ref, nrm_ref, len_ref, sems, lsem,
):
    b = lax.axis_index("blk")
    z = lax.axis_index("head")
    chip, core = b // 2, b % 2
    sib = (chip * 2 + 1 - core, z)
    near = [(chip ^ r) * 2 + core for r in (0, 1, 2, 3)]
    flat = [(n, z) for n in near]
    line = [(b, z ^ r) for r in (0, 1, 2, 3)]
    f32, bf16 = jnp.float32, jnp.bfloat16
    fetch = [
        pltpu.make_async_copy(wq_any, wq_ref, lsem.at[0]),
        pltpu.make_async_copy(wout_any, wout_ref, lsem.at[1]),
        pltpu.make_async_copy(nrm_any, nrm_row, lsem.at[2]),
        pltpu.make_async_copy(pos_any, pos_ref, lsem.at[3]),
        pltpu.make_async_copy(tok_any, gt.at[z], lsem.at[4]),
        pltpu.make_async_copy(len_any, len_ref, lsem.at[5]),
    ]
    for c in fetch:
        c.start()
    for c in fetch:
        c.wait()
    go = Sender(sems)
    mid = (z == 1) | (z == 2)
    ends = (z == 0) | (z == 3)

    wq = wq_ref[...].astype(f32)
    wo = wout_ref[...].astype(f32)
    wo = jnp.concatenate([wo[0:128], jnp.zeros((64, 96), f32), wo[128:192]], axis=0)
    wo = jnp.concatenate([wo, jnp.zeros((256, 32), f32)], axis=1).T[0:96]
    wo_ref[...] = wo.astype(bf16)
    piece = [wq[:, 64 * i : 64 * i + 64] for i in range(9)] + [wo[:, 192:256]]
    for k in range(5):
        tile = jnp.concatenate([piece[PACK[2 * k]], piece[PACK[2 * k + 1]]], axis=1)
        wa_ref[:, 128 * k : 128 * k + 128] = tile.astype(bf16)
    wat[b] = wa_ref[...]
    wout[z] = wo_ref[...]
    nrm_ref[...] = jnp.zeros((8, 128), f32)
    nrm_ref[0:1, 0:96] = nrm_row[...].astype(f32)
    nr[b, z] = nrm_ref[...]
    greet([sib] + flat[1:] + line[1:])
    tok_z = [Spread(go, mid, lambda j, h=h: gt.at[j, pl.ds(64 * h, 64)], z, line) for h in range(2)]
    wa_p = [go(wa_ref, wat.at[b], flat[r]) for r in (3, 1, 2)]
    wa_s = [go(wa_ref, wat.at[b], sib)]
    pos = pos_ref[...]
    seq = jnp.zeros(pos.shape, f32)
    end = 0
    for k in range(8):
        end = end + len_ref[k]
        seq = seq + jnp.where(pos >= end, 1.0, 0.0)
    code_ref[...] = pos.astype(f32) + SEQ_STEP * seq

    def spread_code(d, _):
        kcode[d] = jnp.broadcast_to(code_ref[pl.ds(d, 1), :], (128, 128)).T
        return 0

    lax.fori_loop(0, 32, spread_code, 0)
    own_code = [code_ref[pl.ds(b * 4 + j, 1), :] for j in range(4)]
    for i in range(4):
        qcode[i, 0:1, :] = jnp.concatenate([c[:, 32 * i : 32 * i + 32] for c in own_code], axis=1)
    go.sent(tok_z[0].two)
    tok_z[0].rest()
    tok_z[0].pass_on()
    go.sent(tok_z[1].two)
    tok_z[1].rest()
    wo_z = [go(wo_ref, wout.at[z], line[r]) for r in (3, 2, 1)]
    nr_z = [go(nrm_ref, nr.at[b, z], line[r]) for r in (3, 2, 1)]
    for k, r in enumerate((3, 1, 2)):
        wa_p[k].wait_recv()
        wa_s.append(go(wat.at[near[r]], wat.at[near[r]], sib))
    tok_z[1].pass_on()
    for c in wa_s:
        c.wait_recv()
    kv_p = []
    for r in (0, 2, 1, 3):
        for s in tok_z:
            if r in (1, 3):
                (s.one if r == 1 else s.three).wait_recv()
        j = z ^ r
        rows = jnp.dot(gt[j], wat[...].reshape(768, 640), preferred_element_type=f32)
        kv[b * 4 + j] = rows[:, 0:384].astype(bf16)
        if r == 3:
            kv_l = [go(kv.at[b * 4 + j], kv.at[b * 4 + j], flat[s]) for s in (3, 1, 2)]
            passed.append(go(kv.at[b * 4 + j], kv.at[b * 4 + j], sib))
        else:
            kv_p.append(Plane(go, core, lambda n, j=j: kv.at[n * 4 + j], b, near, flat, sib))
        q_ref[j] = rows[:, 384:640].astype(bf16) * bf16(HEAD_DIM ** (-0.5))
        if r:
            kv_p[{2: 0, 1: 1, 3: 2}[r]].pass_on()
        if r == 1:
            for c in wo_z + nr_z:
                c.wait_recv()
            nr_p = [go(nr.at[b], nr.at[b], flat[r]) for r in (3, 1, 2)]
            passed = [go(nr.at[b], nr.at[b], sib)]
    for k, r in enumerate((3, 1, 2)):
        nr_p[k].wait_recv()
        passed.append(go(nr.at[near[r]], nr.at[near[r]], sib))
    for p in kv_p:
        p.last()
    for k, s in enumerate((3, 1, 2)):
        kv_l[k].wait_recv()
        n = near[s] * 4 + (z ^ 3)
        passed.append(go(kv.at[n], kv.at[n], sib))
    for p in kv_p:
        p.whole()
    for c in passed:
        c.wait_recv()
    total = jnp.zeros((8, 768), f32)
    for n in range(8):
        rows = jnp.concatenate([nr[n, j, 0:1, :] for j in range(4)] + [jnp.zeros((4, 128), f32)], axis=0)
        total = total + pltpu.roll(jnp.concatenate([rows, jnp.zeros((8, 640), f32)], axis=1), 96 * n, 1)
    norm_out[...] = total
    go.finish()


def run_collect(lengths, tok, wq, wo, nrm, pos):
    f32, bf16 = jnp.float32, jnp.bfloat16
    S = jax.ShapeDtypeStruct
    V = pltpu.VMEM
    return pl.pallas_call(
        collect,
        out_shape=(
            S((4, 128, 768), bf16), S((8, 96, 640), bf16), S((4, 128, 256), bf16), S((32, 128, 384), bf16),
            S((4, 96, 256), bf16), S((8, 768), f32), S((32, 128, 128), f32), S((4, 8, 128), f32),
        ),
        in_specs=[HBM] * 6,
        out_specs=(VM,) * 8,
        scratch_shapes=[
            V((96, 640), bf16), V((96, 256), bf16), V((8, 4, 8, 128), f32), V((32, 128), f32),
            V((96, 576), bf16), V((192, 96), bf16), V((1, 96), bf16), V((32, 128), jnp.int32), V((8, 128), f32),
            pltpu.SMEM((8,), jnp.int32), pltpu.SemaphoreType.DMA((2, 80)), pltpu.SemaphoreType.DMA((6,)),
        ],
        compiler_params=pltpu.CompilerParams(
            collective_id=1, has_side_effects=True, vmem_limit_bytes=20 << 20
        ),
        name="collect",
    )(lengths, tok, wq, wo, nrm, pos)


def moments(rows):
    center = rows - jnp.mean(rows, axis=-1, keepdims=True)
    spread = lax.rsqrt(jnp.mean(center * center, axis=-1, keepdims=True) + 1e-05)
    return center * spread, spread


def norm_back(grad, gain, unit, spread):
    scaled = grad * gain
    return spread * (
        scaled - jnp.mean(scaled, axis=-1, keepdims=True) - unit * jnp.mean(scaled * unit, axis=-1, keepdims=True)
    )


def middle(
    mixed_ref, tok_any, og_any, norm_ref, wo_0, wo_1, wo_2, wo_3, gu_any, down_any,
    act_ref, done_ref, datt_ref, dheads, sum_0, sum_1, sum_2, sum_3, gn_ref,
    mix_in, wffn, rows_in, drow_in, gelu_a, gelu_b, gated, dgate, dup,
    part, part_in, part2, part2_in, gff, ffn_sib, hid, unit_one, held, held_two, head_out,
    tok_ref, og_ref, wout, part_relay, part2_relay, sems, lsem,
):
    b = lax.axis_index("blk")
    z = lax.axis_index("head")
    chip, core = b // 2, b % 2
    sib = (chip * 2 + 1 - core, z)
    near = [(chip ^ r) * 2 + core for r in (0, 1, 2, 3)]
    flat = [(n, z) for n in near]
    line = [(b, z ^ r) for r in (0, 1, 2, 3)]
    f32, bf16 = jnp.float32, jnp.bfloat16
    own = [
        pltpu.make_async_copy(gu_any, wffn.at[0:2, b], lsem.at[0]),
        pltpu.make_async_copy(down_any, wffn.at[2, b], lsem.at[1]),
        pltpu.make_async_copy(tok_any, tok_ref, lsem.at[2]),
        pltpu.make_async_copy(og_any, og_ref, lsem.at[3]),
    ]
    for c in own:
        c.start()
    greet([sib] + flat[1:] + line[1:])
    go = Sender(sems)
    mid = (z == 1) | (z == 2)
    ends = (z == 0) | (z == 3)

    HALF = 64

    @pl.when(ends)
    def _():
        for h in range(2):
            part_in[h, 2] = jnp.zeros((HALF, 768), bf16)
            part2_in[h, 2] = jnp.zeros((HALF, 768), bf16)

    def scatter(out, arrived, relay, terms, h):
        passed = go(out.at[h, z ^ 3], relay.at[h], line[1], only=ends)
        three = go(out.at[h, z ^ 3], arrived.at[h, 2], line[3], only=mid)
        one = go(out.at[h, z ^ 1], arrived.at[h, 0], line[1])
        two = go.make(out.at[h, z ^ 2], arrived.at[h, 1], line[2])
        go.start(two, only=ends)

        def later():
            @pl.when(mid)
            def _():
                passed.wait_recv()
                out[h, z ^ 2] = (terms[h, z ^ 2] + relay[h].astype(f32)).astype(bf16)

            go.left.append((two, mid))
            pl.when(mid)(two.start)

        return one, two, three, later

    def gathered(copies):
        copies[0].wait_recv()
        copies[1].wait_recv()
        pl.when(mid)(copies[2].wait_recv)

    wo_s = []
    for r, ref in enumerate((wo_0, wo_1, wo_2, wo_3)):
        wo_s.append(go(ref, wout.at[:, near[r]], sib))
        wout[:, near[r]] = ref[...]
    mix_c = []
    for h in range(2):
        rows = pl.ds(HALF * h, HALF)
        mix_c.append([go(mixed_ref.at[z ^ r, rows], mix_in.at[h, z], line[r]) for r in (3, 2, 1)])

    for c in own:
        c.wait()
    wf_p = [Plane(go, core, lambda n, t=t: wffn.at[t, n], b, near, flat, sib) for t in range(3)]
    for c in wo_s:
        c.wait_recv()

    def out_weight(j):
        return wout[j].reshape(768, 256)

    spreads = []
    row_c = []
    for h in range(2):
        rows = pl.ds(HALF * h, HALF)
        mix_in[h, z] = mixed_ref[z, rows, :]
        for c in mix_c[h]:
            c.wait_recv()
        attn = dot_nt(mix_in[h, 0], out_weight(0))
        for j in (1, 2, 3):
            attn = attn + dot_nt(mix_in[h, j], out_weight(j))
        unit, spread = moments(tok_ref[rows, :].astype(f32) + attn)
        hidden = unit * norm_ref[0:1, :] + norm_ref[1:2, :]
        unit_one[h] = unit
        spreads.append(spread)
        hid[h] = hidden
        rows_in[h, z] = hidden.astype(bf16)
        row_c.append(Spread(go, mid, lambda j, h=h: rows_in.at[h, j], z, line))
        if h == 1:
            row_c[0].rest()
        wf_p[h].pass_on()
    row_c[0].pass_on()
    row_c[1].rest()
    wf_p[2].pass_on()
    row_c[1].pass_on()
    for p in wf_p:
        p.last()
    wf_p[0].whole()
    wf_p[1].whole()

    def weight(t):
        return wffn[t].reshape(768, 768)

    part_c = []
    for h in range(2):
        row_c[h].wait()
        rows = rows_in[h].reshape(4 * HALF, 768)
        gate = jnp.dot(rows, weight(0), preferred_element_type=f32)
        up = jnp.dot(rows, weight(1), preferred_element_type=f32)
        half = 0.5 + 0.5 * lax.erf(gate * (0.5**0.5))
        value = gate * half
        low = (value * up).astype(bf16)
        gated[h] = low
        if h == 0:
            wf_p[2].whole()
        term = dot_nt(low, weight(2)).reshape(4, HALF, 768)
        held[h] = term
        part[h] = term.astype(bf16)
        if h == 1:
            part_c[0][3]()
        part_c.append(scatter(part, part_in, part_relay, held, h))
        slope = half + gate * jnp.exp(-0.5 * gate * gate) * 0.3989422804014327
        gelu_a[h] = slope * up
        gelu_b[h] = value
    part_c[1][3]()
    gains = []
    drow_c = []
    for h in range(2):
        rows = pl.ds(HALF * h, HALF)
        if h == 1:
            drow_c[0].pass_on()
        gathered(part_c[h])
        branch = held[h, z] + part_in[h, 0].astype(f32) + part_in[h, 1].astype(f32) + part_in[h, 2].astype(f32)
        unit_two, spread_two = moments(hid[h] + branch)
        grad = og_ref[rows, :].astype(f32)
        d_two = norm_back(grad, norm_ref[2:3, :], unit_two, spread_two)
        hid[h] = d_two
        drow_in[h, z] = d_two.astype(bf16)
        drow_c.append(Spread(go, mid, lambda j, h=h: drow_in.at[h, j], z, line))
        act_ref[rows, :] = (unit_two * norm_ref[2:3, :] + norm_ref[3:4, :]).astype(bf16)
        gains.append((jnp.sum(grad * unit_two, axis=0, keepdims=True), jnp.sum(grad, axis=0, keepdims=True)))
        drow_c[h].rest()
    gn_ref[...] = jnp.zeros((32, 768), f32)
    gn_ref[16:17, :] = gains[0][0] + gains[1][0]
    gn_ref[24:25, :] = gains[0][1] + gains[1][1]
    part2_c = []
    for h in range(2):
        if h == 1:
            drow_c[1].pass_on()
        drow_c[h].wait()
        d_gated = jnp.dot(drow_in[h].reshape(4 * HALF, 768), weight(2), preferred_element_type=f32)
        dg = (d_gated * gelu_a[h]).astype(bf16)
        du = (d_gated * gelu_b[h]).astype(bf16)
        dgate[h] = dg
        dup[h] = du
        term = (dot_nt(dg, weight(0)) + dot_nt(du, weight(1))).reshape(4, HALF, 768)
        held_two[h] = term
        part2[h] = term.astype(bf16)
        if h == 1:
            part2_c[0][3]()
        part2_c.append(scatter(part2, part2_in, part2_relay, held_two, h))
    part2_c[1][3]()
    sib_c = []
    acts = rows_in[...].reshape(512, 768)
    for t in (2, 0, 1):
        if t == 2:
            total = dot_tn(drow_in[...].reshape(512, 768), gated[...].reshape(512, 768))
        else:
            total = dot_tn(acts, (dgate, dup)[t][...].reshape(512, 768))
        gff[t] = total.astype(bf16).reshape(4, 2, 96, 768)
        sib_c.append(go(gff.at[t, :, 1 - core], ffn_sib.at[t], sib))
    gains = []
    head_c = []
    for h in range(2):
        rows = pl.ds(HALF * h, HALF)
        gathered(part2_c[h])
        d_hidden = (
            hid[h] + held_two[h, z]
            + part2_in[h, 0].astype(f32) + part2_in[h, 1].astype(f32) + part2_in[h, 2].astype(f32)
        )
        unit = unit_one[h]
        d_one = norm_back(d_hidden, norm_ref[0:1, :], unit, spreads[h])
        low_one = d_one.astype(bf16)
        for r in (3, 2, 1, 0):
            term = jnp.dot(low_one, out_weight(z ^ r), preferred_element_type=f32).astype(bf16)
            if r:
                head_out[h, r - 1] = term
                head_c.append(go(head_out.at[h, r - 1], dheads.at[z, rows], line[r]))
            else:
                dheads[z, rows, :] = term
        done_ref[rows, :] = d_one
        datt_ref[rows, :] = low_one
        gains.append((jnp.sum(d_hidden * unit, axis=0, keepdims=True), jnp.sum(d_hidden, axis=0, keepdims=True)))
    gn_ref[0:1, :] = gains[0][0] + gains[1][0]
    gn_ref[8:9, :] = gains[0][1] + gains[1][1]
    for k, t in enumerate((2, 0, 1)):
        sib_c[k].wait_recv()
        for r, ref in enumerate((sum_0, sum_1, sum_2, sum_3)):
            both = gff[t, chip ^ r, core].astype(f32) + ffn_sib[t, chip ^ r].astype(f32)
            ref[t] = both.astype(bf16)
    for c in head_c:
        c.wait_recv()
    go.finish()


def run_middle(mixed, tok, og, norms, wo, gu, down):
    f32, bf16 = jnp.float32, jnp.bfloat16
    S = jax.ShapeDtypeStruct
    V = pltpu.VMEM
    halves = (2, 256, 768)
    return pl.pallas_call(
        middle,
        out_shape=(
            S((128, 768), bf16), S((128, 768), f32), S((128, 768), bf16), S((4, 128, 256), bf16),
            *[S((3, 96, 768), bf16)] * 4, S((32, 768), f32),
        ),
        in_specs=[VM, HBM, HBM, VM, VM, VM, VM, VM, HBM, HBM],
        out_specs=(VM,) * 9,
        scratch_shapes=[
            V((2, 4, 64, 256), bf16), V((3, 8, 96, 768), bf16), V((2, 4, 64, 768), bf16), V((2, 4, 64, 768), bf16),
            V(halves, f32), V(halves, f32), V(halves, bf16), V(halves, bf16), V(halves, bf16),
            V((2, 4, 64, 768), bf16), V((2, 3, 64, 768), bf16), V((2, 4, 64, 768), bf16), V((2, 3, 64, 768), bf16),
            V((3, 4, 2, 96, 768), bf16), V((3, 4, 96, 768), bf16),
            V((2, 64, 768), f32), V((2, 64, 768), f32), V((2, 4, 64, 768), f32), V((2, 4, 64, 768), f32),
            V((2, 3, 64, 256), bf16),
            V((128, 768), bf16), V((128, 768), bf16), V((4, 8, 96, 256), bf16), V((2, 64, 768), bf16), V((2, 64, 768), bf16),
            pltpu.SemaphoreType.DMA((2, 108)), pltpu.SemaphoreType.DMA((4,)),
        ],
        compiler_params=pltpu.CompilerParams(
            collective_id=3, has_side_effects=True, vmem_limit_bytes=36 << 20
        ),
        name="middle",
    )(mixed, tok, og, norms, *wo, gu, down)


def deliver(*refs):
    dx, sqkv, sout, snorm, *sums = refs[:8]
    o_dx, o_qkv, o_out, o_norm, o_gu, o_down, sem = refs[8:]
    pairs = ((dx, o_dx), (sqkv, o_qkv), (sout, o_out), (snorm, o_norm))
    copies = [pltpu.make_async_copy(s, d, sem.at[i]) for i, (s, d) in enumerate(pairs)]
    for c in copies:
        c.start()
    for t in range(3):
        total = sum(s[t].astype(jnp.float32) for s in sums)
        if t < 2:
            o_gu[t] = total
        else:
            o_down[...] = total
    for c in copies:
        c.wait()


def run_deliver(*arrays):
    f32 = jnp.float32
    S = jax.ShapeDtypeStruct
    return pl.pallas_call(
        deliver,
        out_shape=(
            S((128, 768), f32), S((96, 576), f32), S((192, 96), f32), S((1, 96), f32),
            S((2, 96, 768), f32), S((96, 768), f32),
        ),
        in_specs=[ANY] * 4 + [VM] * 4,
        out_specs=(ANY,) * 4 + (VM,) * 2,
        scratch_shapes=[pltpu.SemaphoreType.DMA((4,))],
        compiler_params=pltpu.CompilerParams(vmem_limit_bytes=8 << 20),
        name="deliver",
    )(*arrays)


PACK = (1, 4, 2, 5, 7, 8, 0, 3, 6, 9)


def fast_shards(
    tokens, w_qkv, w_out, w_gate_up, w_down, norm_params, alibi_slope, lengths, placement, out_grad
):
    heads_n = lax.axis_size("head")
    blk_n = lax.axis_size("blk")
    head_idx = lax.axis_index("head")
    blk_idx = lax.axis_index("blk")
    tok_rows, width = tokens.shape
    per_dev = HEADS // heads_n
    group_rows = heads_n * tok_rows
    devs = heads_n * blk_n
    share = w_qkv.shape[0]
    bf16 = jnp.bfloat16

    held = [
        pltpu.with_memory_space_constraint(a, pltpu.MemorySpace.HBM)
        for a in (lengths, alibi_slope, tokens, w_qkv, w_out, norm_params.reshape(1, share), placement.reshape(devs, tok_rows))
    ]
    group_tokens, attn_w, q, kv, wo, norms, kcode, qcode = run_collect(held[0], *held[2:])
    wo = [wo] + [lax.ppermute(wo, "blk", [(i, i ^ (2 * r)) for i in range(blk_n)]) for r in (1, 2, 3)]
    mixed, lse = run_attend(held[0], held[1], q, kv, kcode, qcode)
    act, d_one, d_attn, d_heads, *sums, g_norm = run_middle(
        mixed, tokens, out_grad, norms, wo, w_gate_up, w_down.T
    )
    sums = [sums[0]] + [
        lax.ppermute(sums[r], "blk", [(i, i ^ (2 * r)) for i in range(blk_n)]) for r in (1, 2, 3)
    ]
    d_attn_two = lax.ppermute(d_attn, "head", [(i, i ^ 2) for i in range(heads_n)])
    d_q, dkv, result = run_attend_back(
        held[0], held[1], q, kv, kcode, qcode, mixed, d_heads, lse, act
    )
    input_grad, s_qkv, s_out, s_norm = run_finish(
        dkv.reshape(blk_n, group_rows, 384), d_q.reshape(group_rows, 256),
        group_tokens.reshape(group_rows, width), attn_w.reshape(width, 640),
        d_attn, d_attn_two, mixed.reshape(group_rows, 256), d_one, g_norm,
    )
    input_grad, s_qkv, s_out, s_norm, s_gu, s_down = run_deliver(input_grad, s_qkv, s_out, s_norm, *sums)
    return (
        result,
        input_grad,
        s_qkv,
        s_out,
        s_gu,
        s_down.T,
        s_norm.reshape(share, 1),
    )


def solution(mesh):
    placed = (
        P(("blk", "head"), None),
        P("blk", "head"),
        P("head", "blk"),
        P(None, "blk", "head"),
        P("head", "blk"),
        P("blk", "head"),
        P(),
        P(),
        P(),
        P(("blk", "head"), None),
    )
    small = mesh.shape["blk"] == 8 and mesh.shape["head"] == 4
    return jax.shard_map(
        fast_shards if small else shards,
        mesh=mesh,
        in_specs=placed,
        out_specs=(
            P(("blk", "head"), None),
            P(("blk", "head"), None),
            P("blk", "head"),
            P("head", "blk"),
            P(None, "blk", "head"),
            P("head", "blk"),
            P("blk", "head"),
        ),
        check_vma=False,
    )
```

```python
import jax
import jax.numpy as jnp
from jax import lax
from jax.experimental import pallas as pl
from jax.experimental.pallas import tpu as pltpu
from jax.sharding import PartitionSpec as P

HEADS = 12
HEAD_DIM = 64


masked_score = -1e30


def layer_norm(residual, norm_gain, norm_shift):
    center = residual - jnp.mean(residual, axis=-1, keepdims=True)
    spread = jnp.mean(center * center, axis=-1, keepdims=True)
    return center * lax.rsqrt(spread + 1e-05) * norm_gain + norm_shift


def geglu(gate, upward):
    return jax.nn.gelu(gate, approximate=False) * upward


def dot_back(grad_rows, weight):
    return lax.dot_general(
        grad_rows, weight, (((1,), (1,)), ((), ())), preferred_element_type=jnp.float32
    )


def weight_grad(left, right):
    return lax.dot_general(
        left, right, (((0,), (0,)), ((), ())), preferred_element_type=jnp.float32
    )


def seq_of(positions, seq_ends):
    return jnp.sum((positions[:, None] >= seq_ends[None, :]).astype(jnp.int32), axis=1)


def prefix_sums(lengths):
    count = lengths.shape[0]
    upto = jnp.arange(count)[None, :] <= jnp.arange(count)[:, None]
    return jnp.sum(jnp.where(upto, lengths[None, :], 0), axis=1)


def biased_scores(queries, key_rows, q_pos, k_pos, q_seq, k_seq, slopes, qk_scale):
    scores = (
        jnp.einsum("qhd,khd->hqk", queries, key_rows, preferred_element_type=jnp.float32) * qk_scale
    )
    distance = jnp.abs(q_pos[:, None] - k_pos[None, :]).astype(jnp.float32)
    scores = scores - slopes[:, None, None] * distance[None]
    same_seq = (q_seq[:, None] == k_seq[None, :])[None]
    return (scores, same_seq)


def shards(
    tokens, w_qkv, w_out, w_gate_up, w_down, norm_params, alibi_slope, lengths, placement, out_grad
):
    heads_n = lax.axis_size("head")
    head_idx = lax.axis_index("head")
    blk_idx = lax.axis_index("blk")
    tok_rows = tokens.shape[0]
    per_dev = HEADS // heads_n
    group_rows = heads_n * tok_rows
    qk_scale = HEAD_DIM ** (-0.5)
    group_tokens, norm_cols = (
        lax.all_gather(tokens, "head", axis=0, tiled=True),
        lax.all_gather(norm_params, "head", axis=1, tiled=True),
    )
    f_qkv, f_out, f_gu, f_down, f_norm = (
        lax.all_gather(w_qkv, "blk", axis=0, tiled=True),
        lax.all_gather(w_out, "blk", axis=1, tiled=True),
        lax.all_gather(w_gate_up, "blk", axis=1, tiled=True),
        lax.all_gather(w_down, "blk", axis=1, tiled=True),
        lax.all_gather(norm_cols, "blk", axis=0, tiled=True),
    )
    grouped = jnp.dot(group_tokens, f_qkv, preferred_element_type=jnp.float32).astype(jnp.bfloat16)
    grouped = grouped.reshape(group_rows, per_dev, 3, HEAD_DIM)
    norms = f_norm.astype(jnp.float32)
    queries = grouped[:, :, 0]
    key_rows = grouped[:, :, 1]
    values = grouped[:, :, 2]
    seq_ends = prefix_sums(lengths)
    q_pos = lax.dynamic_slice_in_dim(placement, blk_idx * group_rows, group_rows)
    q_seq = seq_of(q_pos, seq_ends)
    slopes = lax.dynamic_slice_in_dim(alibi_slope, head_idx * per_dev, per_dev)

    def split_rows(shard_part):
        block_count = shard_part[0].shape[0] // group_rows
        pieces = tuple(
            (arr.reshape((block_count, group_rows) + arr.shape[1:]) for arr in shard_part)
        )
        starts = group_rows * jnp.arange(block_count, dtype=jnp.int32)
        return pieces + (starts,)

    start_state = (
        jnp.full((per_dev, group_rows), masked_score, jnp.float32),
        jnp.zeros((per_dev, group_rows), jnp.float32),
        jnp.zeros((group_rows, per_dev, HEAD_DIM), jnp.float32),
    )
    running = start_state

    def forward_per_block(state, block_in):
        k_blk, v_blk, k_first = block_in
        row_best, row_total, out_sum = state
        k_pos = lax.dynamic_slice_in_dim(placement, k_first, group_rows)
        scores, same_seq = biased_scores(
            queries, k_blk, q_pos, k_pos, q_seq, seq_of(k_pos, seq_ends), slopes, qk_scale
        )
        row_top = jnp.max(jnp.where(same_seq, scores, masked_score), axis=2)
        new_best = jnp.maximum(row_best, row_top)
        factor = jnp.exp(row_best - new_best)
        prob_tile = jnp.where(same_seq, jnp.exp(scores - new_best[:, :, None]), 0.0)
        row_total = row_total * factor + jnp.sum(prob_tile, axis=2)
        out_sum = out_sum * factor.T[:, :, None] + jnp.einsum(
            "hqk,khd->qhd",
            prob_tile.astype(jnp.bfloat16),
            v_blk,
            preferred_element_type=jnp.float32,
        )
        return ((new_best, row_total, out_sum), None)

    running, _ = lax.scan(
        forward_per_block,
        running,
        split_rows(
            (
                lax.all_gather(key_rows, "blk", axis=0, tiled=True),
                lax.all_gather(values, "blk", axis=0, tiled=True),
            )
        ),
    )
    row_best, row_total, out_sum = running
    attended = (out_sum / row_total.T[:, :, None]).astype(jnp.bfloat16)
    log_total = row_best + jnp.log(row_total)
    mixed = attended.reshape(group_rows, per_dev * HEAD_DIM)
    attn_out = lax.psum_scatter(
        jnp.dot(mixed, f_out, preferred_element_type=jnp.float32).astype(jnp.bfloat16),
        "head",
        scatter_dimension=0,
        tiled=True,
    ).astype(jnp.float32)
    resid_one = tokens.astype(jnp.float32) + attn_out
    hidden, norm_one_back = jax.vjp(layer_norm, resid_one, norms[:, 0], norms[:, 1])
    hidden_low = hidden.astype(jnp.bfloat16)
    ffn_rows = lax.all_gather(hidden_low, "head", axis=0, tiled=True)
    gate = jnp.dot(ffn_rows, f_gu[0], preferred_element_type=jnp.float32)
    upward = jnp.dot(ffn_rows, f_gu[1], preferred_element_type=jnp.float32)
    gated, geglu_back = jax.vjp(geglu, gate, upward)
    gated_low = gated.astype(jnp.bfloat16)
    branch_part = jnp.dot(gated_low, f_down, preferred_element_type=jnp.float32)
    branch = lax.psum_scatter(
        branch_part.astype(jnp.bfloat16), "head", scatter_dimension=0, tiled=True
    ).astype(jnp.float32)
    result, norm_two_back = jax.vjp(layer_norm, hidden + branch, norms[:, 2], norms[:, 3])
    d_two, d_gain_two, d_shift_two = norm_two_back(out_grad.astype(jnp.float32))
    d_branch = d_two.astype(jnp.bfloat16)
    branch_rows = lax.all_gather(d_branch, "head", axis=0, tiled=True)
    g_down = weight_grad(gated_low, branch_rows)
    d_gate, d_up = geglu_back(dot_back(branch_rows, f_down))
    d_gate_low = d_gate.astype(jnp.bfloat16)
    d_up_low = d_up.astype(jnp.bfloat16)
    g_gate_up = jnp.stack([weight_grad(ffn_rows, d_gate_low), weight_grad(ffn_rows, d_up_low)])
    hidden_part = dot_back(d_gate_low, f_gu[0]) + dot_back(d_up_low, f_gu[1])
    d_hidden = d_two + lax.psum_scatter(
        hidden_part.astype(jnp.bfloat16), "head", scatter_dimension=0, tiled=True
    ).astype(jnp.float32)
    d_one, d_gain_one, d_shift_one = norm_one_back(d_hidden)
    d_attn = d_one.astype(jnp.bfloat16)
    attn_rows = lax.all_gather(d_attn, "head", axis=0, tiled=True)
    g_out = weight_grad(mixed, attn_rows)
    d_heads = dot_back(attn_rows, f_out).astype(jnp.bfloat16).reshape(group_rows, per_dev, HEAD_DIM)
    delta = jnp.sum(d_heads.astype(jnp.float32) * attended.astype(jnp.float32), axis=2).T
    zero_grad = jnp.zeros((group_rows, per_dev, HEAD_DIM), jnp.float32)
    grad_q = zero_grad

    def query_per_block(running, block_in):
        k_blk, v_blk, k_first = block_in
        k_pos = lax.dynamic_slice_in_dim(placement, k_first, group_rows)
        scores, same_seq = biased_scores(
            queries, k_blk, q_pos, k_pos, q_seq, seq_of(k_pos, seq_ends), slopes, qk_scale
        )
        prob_tile = jnp.where(same_seq, jnp.exp(scores - log_total[:, :, None]), 0.0)
        d_prob = jnp.einsum("qhd,khd->hqk", d_heads, v_blk, preferred_element_type=jnp.float32)
        d_score = (prob_tile * (d_prob - delta[:, :, None])).astype(jnp.bfloat16)
        running = (
            running
            + jnp.einsum("hqk,khd->qhd", d_score, k_blk, preferred_element_type=jnp.float32)
            * qk_scale
        )
        return (running, None)

    grad_q, _ = lax.scan(
        query_per_block,
        grad_q,
        split_rows(
            (
                lax.all_gather(key_rows, "blk", axis=0, tiled=True),
                lax.all_gather(values, "blk", axis=0, tiled=True),
            )
        ),
    )
    stats_lse, stats_delta = (
        lax.all_gather(log_total, "blk", axis=1, tiled=True),
        lax.all_gather(delta, "blk", axis=1, tiled=True),
    )
    running = (zero_grad, zero_grad)

    def key_per_block(state, block_in):
        q_blk, do_blk, q_first = block_in
        grad_k, grad_v = state
        other_pos = lax.dynamic_slice_in_dim(placement, q_first, group_rows)
        lse_blk = lax.dynamic_slice_in_dim(stats_lse, q_first, group_rows, 1)
        delta_blk = lax.dynamic_slice_in_dim(stats_delta, q_first, group_rows, 1)
        scores, same_seq = biased_scores(
            q_blk, key_rows, other_pos, q_pos, seq_of(other_pos, seq_ends), q_seq, slopes, qk_scale
        )
        prob_tile = jnp.where(same_seq, jnp.exp(scores - lse_blk[:, :, None]), 0.0)
        grad_v = grad_v + jnp.einsum(
            "hqk,qhd->khd",
            prob_tile.astype(jnp.bfloat16),
            do_blk,
            preferred_element_type=jnp.float32,
        )
        d_prob = jnp.einsum("qhd,khd->hqk", do_blk, values, preferred_element_type=jnp.float32)
        d_score = (prob_tile * (d_prob - delta_blk[:, :, None])).astype(jnp.bfloat16)
        grad_k = (
            grad_k
            + jnp.einsum("hqk,qhd->khd", d_score, q_blk, preferred_element_type=jnp.float32)
            * qk_scale
        )
        return ((grad_k, grad_v), None)

    running, _ = lax.scan(
        key_per_block,
        running,
        split_rows(
            (
                lax.all_gather(queries, "blk", axis=0, tiled=True),
                lax.all_gather(d_heads, "blk", axis=0, tiled=True),
            )
        ),
    )
    grad_k, grad_v = running
    d_grouped = jnp.stack([grad_q, grad_k, grad_v], axis=2).astype(jnp.bfloat16)
    g_norm = jnp.stack([d_gain_one, d_shift_one, d_gain_two, d_shift_two], axis=1)
    d_qkv = d_grouped.reshape(group_rows, per_dev * 3 * HEAD_DIM)
    g_qkv = weight_grad(group_tokens, d_qkv)
    input_sum, norm_share = (
        lax.psum_scatter(
            dot_back(d_qkv, f_qkv).astype(jnp.bfloat16), "head", scatter_dimension=0, tiled=True
        ).astype(jnp.float32),
        lax.psum_scatter(
            g_norm.astype(jnp.bfloat16), "head", scatter_dimension=1, tiled=True
        ).astype(jnp.float32),
    )
    input_grad = d_one + input_sum
    s_qkv, s_out, s_gu, s_down, s_norm = (
        lax.psum_scatter(g_qkv, "blk", scatter_dimension=0, tiled=True),
        lax.psum_scatter(g_out, "blk", scatter_dimension=1, tiled=True),
        lax.psum_scatter(g_gate_up, "blk", scatter_dimension=1, tiled=True),
        lax.psum_scatter(g_down, "blk", scatter_dimension=1, tiled=True),
        lax.psum_scatter(norm_share, "blk", scatter_dimension=0, tiled=True),
    )
    return (result.astype(jnp.bfloat16), input_grad, s_qkv, s_out, s_gu, s_down, s_norm)


Q_SLOTS = 32
K_SLOTS = 16
SEQ_STEP = 65536.0
FAR = 32768.0
LANE_OF = (0, 64, 192)


def by_head(rows, lanes):
    lane = lax.broadcasted_iota(jnp.int32, rows.shape, 1)
    parts = [jnp.where((lane >= first) & (lane < first + HEAD_DIM), rows, 0.0) for first in lanes]
    return jnp.concatenate(parts, axis=0).astype(jnp.bfloat16)


def by_head_turned(rows, lanes):
    turned = rows.T
    lane = lax.broadcasted_iota(jnp.int32, turned.shape, 0)
    parts = [jnp.where((lane >= first) & (lane < first + HEAD_DIM), turned, 0.0) for first in lanes]
    return jnp.concatenate(parts, axis=1).astype(jnp.bfloat16)


def key_tiles(kv_ref, j):
    rows = kv_ref.shape[0] * K_SLOTS
    blk = kv_ref[:, pl.ds(pl.multiple_of(j * K_SLOTS, K_SLOTS), K_SLOTS), :]
    return blk.reshape(rows, blk.shape[2])


def key_span(len_ref, i, devs):
    first = i * (Q_SLOTS * devs)
    last = first + Q_SLOTS * devs - 1
    end, low, high = 0, 0, 0
    for k in range(8):
        start = end
        end = end + len_ref[k]
        low = jnp.where((first >= start) & (first < end), start, low)
        high = jnp.where((last >= start) & (last < end), end, high)
    step = K_SLOTS * devs
    return low // step, (high + step - 1) // step


def attend(len_any, slope_any, q_ref, kv_ref, kcode_ref, qcode_ref, out_ref, lse_ref, vt_ref, len_ref, slope_ref, few):
    z = lax.axis_index("head")
    scalars = [
        pltpu.make_async_copy(len_any, len_ref, few.at[0]),
        pltpu.make_async_copy(slope_any, slope_ref, few.at[1]),
    ]
    for c in scalars:
        c.start()
    devs, slots, _ = kv_ref.shape
    rows = devs * K_SLOTS
    q_rows = q_ref.shape[0] * Q_SLOTS

    def turn(j, _):
        kv = key_tiles(kv_ref, j)[:, 128:384]
        vt_ref[j] = kv.T
        return 0

    lax.fori_loop(0, slots // K_SLOTS, turn, 0)
    for c in scalars:
        c.wait()

    def chunk(i, _):
        first = pl.multiple_of(i * Q_SLOTS, Q_SLOTS)
        q = q_ref[:, pl.ds(first, Q_SLOTS), :].reshape(q_rows, 256).astype(jnp.float32)
        qbt = by_head_turned(q, (0, 64, 128))
        qcode = qcode_ref[i, 0:1, :]
        lo, hi = key_span(len_ref, i, devs)

        def block(j, state):
            kv = key_tiles(kv_ref, j)
            keys = jnp.concatenate([kv[:, 0:128], kv[:, 256:384]], axis=1)
            s_all = jnp.dot(keys, qbt, preferred_element_type=jnp.float32)
            dist = jnp.abs(key_tiles(kcode_ref, j) - qcode)
            keep = dist < FAR
            fresh, ps = [], []
            for h in range(3):
                best, total, acc = state[h]
                s = jnp.where(keep, s_all[:, 128 * h : 128 * h + 128] - slope_ref[3 * z + h] * dist, masked_score)
                top = jnp.maximum(best, jnp.max(s, axis=0, keepdims=True))
                factor = jnp.exp(best - top)
                p = jnp.exp(s - top)
                total = total * factor + jnp.sum(p, axis=0, keepdims=True)
                ps.append(p.astype(jnp.bfloat16))
                fresh.append((top, total, acc * factor))
            both = jnp.dot(vt_ref[j, 0:128, :], jnp.concatenate(ps[0:2], axis=1), preferred_element_type=jnp.float32)
            last = jnp.dot(vt_ref[j, 192:256, :], ps[2], preferred_element_type=jnp.float32)
            new = (both[0:64, 0:128], both[64:128, 128:256], last)
            fresh = [(top, total, acc + term) for (top, total, acc), term in zip(fresh, new)]
            return tuple(fresh)

        start = tuple(
            (
                jnp.full((1, q_rows), masked_score, jnp.float32),
                jnp.zeros((1, q_rows), jnp.float32),
                jnp.zeros((64, q_rows), jnp.float32),
            )
            for _ in range(3)
        )
        done = lax.fori_loop(lo, hi, block, start)
        outs = [acc / total for _, total, acc in done]
        full = jnp.concatenate([outs[0], outs[1], jnp.zeros((64, q_rows), jnp.float32), outs[2]], axis=0)
        out_ref[:, pl.ds(first, Q_SLOTS), :] = full.T.astype(jnp.bfloat16).reshape(-1, Q_SLOTS, 256)
        for h in range(3):
            lse_ref[i, h : h + 1, :] = done[h][0] + jnp.log(done[h][1])
        return 0

    lax.fori_loop(0, slots // Q_SLOTS, chunk, 0)


def attend_back(len_any, slope_any, q_ref, kv_ref, kcode_ref, qcode_ref, out_ref, do_ref, lse_ref, act_any,
                dq_ref, dkv_ref, act_out, kt_ref, sum_ref, sem, len_ref, slope_ref, few):
    z = lax.axis_index("head")
    scalars = [
        pltpu.make_async_copy(len_any, len_ref, few.at[0]),
        pltpu.make_async_copy(slope_any, slope_ref, few.at[1]),
    ]
    for c in scalars:
        c.start()
    devs, slots, _ = kv_ref.shape
    rows = devs * K_SLOTS
    q_rows = q_ref.shape[0] * Q_SLOTS
    scale = HEAD_DIM ** (-0.5)
    along = [
        pltpu.make_async_copy(act_any, act_out, sem.at[0]),
    ]
    for c in along:
        c.start()

    def turn(j, _):
        kv = key_tiles(kv_ref, j)
        keys = jnp.concatenate([kv[:, 0:128], kv[:, 256:384]], axis=1)
        kt_ref[j] = keys.T
        sum_ref[j] = jnp.zeros((rows, 384), jnp.float32)
        return 0

    lax.fori_loop(0, slots // K_SLOTS, turn, 0)
    for c in scalars:
        c.wait()

    def chunk(i, _):
        first = pl.multiple_of(i * Q_SLOTS, Q_SLOTS)
        q = q_ref[:, pl.ds(first, Q_SLOTS), :].reshape(q_rows, 256).astype(jnp.float32)
        qbd = by_head(q, (0, 64, 128))
        qbt = by_head_turned(q, (0, 64, 128))
        do = do_ref[:, pl.ds(first, Q_SLOTS), :].reshape(q_rows, 256).astype(jnp.float32)
        out = out_ref[:, pl.ds(first, Q_SLOTS), :].reshape(q_rows, 256).astype(jnp.float32)
        dobd = by_head(do, LANE_OF)
        dobt = by_head_turned(do, LANE_OF)
        prod = (do * out).T
        delta = [jnp.sum(prod[f : f + 64, :], axis=0, keepdims=True) for f in LANE_OF]
        qcode = qcode_ref[i, 0:1, :]
        lo, hi = key_span(len_ref, i, devs)

        def block(j, state):
            kv = key_tiles(kv_ref, j)
            keys = jnp.concatenate([kv[:, 0:128], kv[:, 256:384]], axis=1)
            vals = kv[:, 128:384]
            s_all = jnp.dot(keys, qbt, preferred_element_type=jnp.float32)
            dp_all = jnp.dot(vals, dobt, preferred_element_type=jnp.float32)
            dist = jnp.abs(key_tiles(kcode_ref, j) - qcode)
            keep = dist < FAR
            ps, dss, fresh = [], [], []
            for h in range(3):
                s = s_all[:, 128 * h : 128 * h + 128] - slope_ref[3 * z + h] * dist - lse_ref[i, h : h + 1, :]
                p = jnp.exp(jnp.where(keep, s, masked_score))
                ds = (p * (dp_all[:, 128 * h : 128 * h + 128] - delta[h])).astype(jnp.bfloat16)
                ps.append(p.astype(jnp.bfloat16))
                dss.append(ds)
            both = jnp.dot(kt_ref[j, 0:128, :], jnp.concatenate(dss[0:2], axis=1), preferred_element_type=jnp.float32)
            last = jnp.dot(kt_ref[j, 128:192, :], dss[2], preferred_element_type=jnp.float32)
            fresh = [state[0] + both[0:64, 0:128], state[1] + both[64:128, 128:256], state[2] + last]
            dv = jnp.dot(jnp.concatenate(ps, axis=1), dobd, preferred_element_type=jnp.float32)
            dk = jnp.dot(jnp.concatenate(dss, axis=1), qbd, preferred_element_type=jnp.float32)
            sum_ref[j, :, 0:128] += dk[:, 0:128]
            sum_ref[j, :, 128:256] += dv[:, 0:128]
            sum_ref[j, :, 256:384] += dk[:, 128:256] + dv[:, 128:256]
            return tuple(fresh)

        start = tuple(jnp.zeros((64, q_rows), jnp.float32) for _ in range(3))
        done = lax.fori_loop(lo, hi, block, start)
        full = jnp.concatenate(done + (jnp.zeros((64, q_rows), jnp.float32),), axis=0) * scale
        dq_ref[:, pl.ds(first, Q_SLOTS), :] = full.T.astype(jnp.bfloat16).reshape(-1, Q_SLOTS, 256)
        return 0

    lax.fori_loop(0, slots // Q_SLOTS, chunk, 0)

    def leave(j, _):
        dkv_ref[:, pl.ds(pl.multiple_of(j * K_SLOTS, K_SLOTS), K_SLOTS), :] = (
            sum_ref[j].astype(jnp.bfloat16).reshape(devs, K_SLOTS, 384)
        )
        return 0

    lax.fori_loop(0, slots // K_SLOTS, leave, 0)
    for c in along:
        c.wait()


VM = pl.BlockSpec(memory_space=pltpu.VMEM)
SM = pl.BlockSpec(memory_space=pltpu.SMEM)
ANY = pl.BlockSpec(memory_space=pl.ANY)
HBM = pl.BlockSpec(memory_space=pltpu.MemorySpace.HBM)


def run_attend(lengths, slopes, q, kv, kcode, qcode):
    heads_n, slots, _ = q.shape
    devs = kv.shape[0]
    return pl.pallas_call(
        attend,
        out_shape=(
            jax.ShapeDtypeStruct((heads_n, slots, 256), jnp.bfloat16),
            jax.ShapeDtypeStruct((slots // Q_SLOTS, 8, heads_n * Q_SLOTS), jnp.float32),
        ),
        in_specs=[HBM, HBM, VM, VM, VM, VM],
        out_specs=(VM, VM),
        scratch_shapes=[
            pltpu.VMEM((slots // K_SLOTS, 256, devs * K_SLOTS), jnp.bfloat16),
            pltpu.SMEM((8,), jnp.int32),
            pltpu.SMEM((HEADS,), jnp.float32),
            pltpu.SemaphoreType.DMA((2,)),
        ],
        compiler_params=pltpu.CompilerParams(vmem_limit_bytes=16 << 20),
        name="attend",
    )(lengths, slopes, q, kv, kcode, qcode)


def run_attend_back(lengths, slopes, q, kv, kcode, qcode, out, do, lse, act):
    heads_n, slots, _ = q.shape
    devs = kv.shape[0]
    return pl.pallas_call(
        attend_back,
        out_shape=(
            jax.ShapeDtypeStruct((heads_n, slots, 256), jnp.bfloat16),
            jax.ShapeDtypeStruct((devs, slots, 384), jnp.bfloat16),
            jax.ShapeDtypeStruct(act.shape, act.dtype),
        ),
        in_specs=[HBM, HBM, VM, VM, VM, VM, VM, VM, VM, ANY],
        out_specs=(VM, VM, ANY),
        scratch_shapes=[
            pltpu.VMEM((slots // K_SLOTS, 256, devs * K_SLOTS), jnp.bfloat16),
            pltpu.VMEM((slots // K_SLOTS, devs * K_SLOTS, 384), jnp.float32),
            pltpu.SemaphoreType.DMA((2,)),
            pltpu.SMEM((8,), jnp.int32),
            pltpu.SMEM((HEADS,), jnp.float32),
            pltpu.SemaphoreType.DMA((2,)),
        ],
        compiler_params=pltpu.CompilerParams(vmem_limit_bytes=26 << 20),
        name="attend_back",
    )(lengths, slopes, q, kv, kcode, qcode, out, do, lse, act)


MESH = pl.DeviceIdType.MESH


def dot_tn(left, right):
    return lax.dot_general(left, right, (((0,), (0,)), ((), ())), preferred_element_type=jnp.float32)


def dot_nt(left, right):
    return lax.dot_general(left, right, (((1,), (1,)), ((), ())), preferred_element_type=jnp.float32)


def greet(peers):
    barrier = pltpu.get_barrier_semaphore()
    for peer in peers:
        pl.semaphore_signal(barrier, inc=1, device_id=peer, device_id_type=MESH)
    pl.semaphore_wait(barrier, len(peers))


class Sender:
    def __init__(self, sems):
        self.sems = sems
        self.used = 0
        self.left = []

    def make(self, src, dst, peer, arrive=None):
        i = self.used
        self.used += 1
        assert i < self.sems.shape[1]
        copy = pltpu.make_async_remote_copy(
            src_ref=src, dst_ref=dst, send_sem=self.sems.at[0, i],
            recv_sem=self.sems.at[1, i] if arrive is None else arrive,
            device_id=peer, device_id_type=MESH,
        )
        copy.arrive = self.sems.at[1, i]
        return copy

    def start(self, copy, only=None):
        self.left.append((copy, only))
        if only is None:
            copy.start()
        else:
            pl.when(only)(copy.start)
        return copy

    def __call__(self, src, dst, peer, only=None, arrive=None):
        return self.start(self.make(src, dst, peer, arrive), only)

    def sent(self, copy):
        [(_, only)] = [item for item in self.left if item[0] is copy]
        self.left = [item for item in self.left if item[0] is not copy]
        if only is None:
            copy.wait_send()
        else:
            pl.when(only)(copy.wait_send)

    def finish(self):
        for copy, only in self.left:
            if only is None:
                copy.wait_send()
            else:
                pl.when(only)(copy.wait_send)


class Plane:
    def __init__(self, go, core, slot, me, near, flat, sib):
        self.go, self.core, self.slot, self.near, self.flat, self.sib = go, core, slot, near, flat, sib
        self.one = go(slot(me), slot(me), flat[1])
        self.two = go(slot(me), slot(me), flat[2])
        self.three = go.make(slot(me), slot(me), flat[3])
        self.handed = [self.hand(me)]

    def hand(self, n):
        return self.go(self.slot(n), self.slot(n), self.sib)

    def pass_on(self):
        for copy, r, turn in ((self.one, 1, 0), (self.two, 2, 1)):
            copy.wait_recv()
            block = self.slot(self.near[r])
            self.go(block, block, self.flat[3 - r], only=self.core == turn, arrive=self.three.arrive)
            self.handed.append(self.hand(self.near[r]))

    def last(self):
        self.three.wait_recv()
        self.handed.append(self.hand(self.near[3]))

    def whole(self):
        for copy in self.handed:
            copy.wait_recv()


class Spread:
    def __init__(self, go, mid, slot, z, line):
        self.go, self.mid, self.slot, self.z, self.line = go, mid, slot, z, line
        self.two = go(slot(z), slot(z), line[2])
        self.three = go.make(slot(z), slot(z), line[3])
        self.one = go.make(slot(z), slot(z), line[1])

    def rest(self):
        self.go.start(self.three, only=self.mid)
        self.go.start(self.one)

    def pass_on(self):
        self.two.wait_recv()
        far = self.slot(self.z ^ 2)
        self.go(far, far, self.line[1], only=self.mid, arrive=self.three.arrive)

    def wait(self):
        self.one.wait_recv()
        self.three.wait_recv()


def finish(
    dkv_ref, dq_ref, tok_ref, w_ref, datt_ref, datt_two, mixed_ref, done_ref, gn_ref,
    dx_ref, sqkv_ref, sout_ref, snorm_ref,
    kv_sib, kv_sum, kv_in, g_one, g_two, g_sib, g_sum, g_in,
    part, part_in, att, dkvq, nz_in, nrow, np_in, relay, sems,
):
    b = lax.axis_index("blk")
    z = lax.axis_index("head")
    chip, core = b // 2, b % 2
    sib = (chip * 2 + 1 - core, z)
    flat = [((chip ^ r) * 2 + core, z) for r in (0, 1, 2, 3)]
    line = [(b, z ^ r) for r in (0, 1, 2, 3)]
    greet([sib] + flat[1:] + line[1:])
    f32, bf16 = jnp.float32, jnp.bfloat16
    go = Sender(sems)
    mid = (z == 1) | (z == 2)
    ends = (z == 0) | (z == 3)

    def member(r):
        return pl.ds(pl.multiple_of((z ^ r) * 128, 128), 128)

    kv_c = {
        (q, r): go(dkv_ref.at[(chip ^ r) * 2 + 1 - core, member(q)], kv_sib.at[q, r], sib)
        for q in (3, 2, 1, 0) for r in (3, 1, 2, 0)
    }
    att[z] = datt_ref[...]
    att[z ^ 2] = datt_two[...]
    att_three = go.make(att.at[z], att.at[z], line[3])
    go(att.at[z ^ 2], att.at[z ^ 2], line[1], only=mid, arrive=att_three.arrive)
    go.start(att_three, only=mid)
    att_one = go(att.at[z], att.at[z], line[1])
    nz_c = [go(gn_ref.at[pl.ds((z ^ r) * 8, 8)], nz_in.at[r - 1], line[r]) for r in (1, 2, 3)]
    side, other = 1 + core, 2 - core
    to_side = ((chip ^ side) * 2 + core, z)
    to_other = ((chip ^ other) * 2 + core, z)
    kv_plain, kv_pass, kv_both = {}, {}, {}
    for q in (3, 2, 1, 0):
        for r in (3, 1, 2, 0):
            kv_c[q, r].wait_recv()
            both = dkv_ref[(chip ^ r) * 2 + core, member(q), :].astype(f32) + kv_sib[q, r].astype(f32)
            kv_sum[q, r] = both.astype(bf16)
            if r == 3:
                kv_pass[q] = go(kv_sum.at[q, 3], kv_in.at[q, 2], to_side)
        kv_plain[q] = go(kv_sum.at[q, side], kv_in.at[q, 0], to_side)

    def add_passed(q):
        kv_pass[q].wait_recv()
        both = kv_sum[q, other].astype(f32) + kv_in[q, 2].astype(f32)
        kv_sum[q, other] = both.astype(bf16)
        kv_both[q] = go(kv_sum.at[q, other], kv_in.at[q, 1], to_other)

    add_passed(3)
    add_passed(2)
    dkvq[:, 384:640] = dq_ref[...]

    @pl.when(ends)
    def _():
        relay[...] = jnp.zeros((128, 768), bf16)
        part_in[2] = jnp.zeros((128, 768), bf16)


    def send_half(part_i, grads):
        return [
            go(grads.at[pl.ds(pl.multiple_of(((chip ^ r) * 2 + 1 - core) * 96, 96), 96)], g_sib.at[part_i, r], sib)
            for r in (3, 1, 2, 0)
        ]

    def send_sum(part_i, grads, copies):
        out = []
        for k, r in enumerate((3, 1, 2, 0)):
            copies[k].wait_recv()
            mine = grads[pl.ds(pl.multiple_of(((chip ^ r) * 2 + core) * 96, 96), 96), :].astype(f32)
            g_sum[part_i, r] = (mine + g_sib[part_i, r].astype(f32)).astype(bf16)
            if r:
                out.append(go(g_sum.at[part_i, r], g_in.at[part_i, r - 1], flat[r]))
        return out

    def settle(part_i, copies):
        for c in copies:
            c.wait_recv()
        return (
            g_sum[part_i, 0].astype(f32) + g_in[part_i, 0].astype(f32)
            + g_in[part_i, 1].astype(f32) + g_in[part_i, 2].astype(f32)
        )

    for c in nz_c:
        c.wait_recv()
    nrow[0] = gn_ref[pl.ds(z * 8, 8)] + nz_in[0] + nz_in[1] + nz_in[2]
    np_c = [go(nrow.at[0], np_in.at[r], flat[r]) for r in (1, 2, 3)]
    last = dot_tn(tok_ref[...], dq_ref[...])
    g_one[:, 0:128] = last[:, 0:128].astype(bf16)
    dx_c = []
    for q in (3, 2, 1, 0):
        if q == 1:
            att_one.wait_recv()
            att_three.wait_recv()
            outs = dot_tn(att[...].reshape(512, 768), mixed_ref[...])
            g_one[:, 128:256] = outs[:, 0:128].astype(bf16)
            g_one[:, 256:384] = (outs[:, 128:256] + last[:, 128:256]).astype(bf16)
            one_c = send_half(0, g_one)
        if q >= 2:
            add_passed(q - 2)
        kv_plain[q].wait_recv()
        kv_both[q].wait_recv()
        dkvq[member(q), 0:384] = (
            kv_sum[q, 0].astype(f32) + kv_in[q, 0].astype(f32) + kv_in[q, 1].astype(f32)
        ).astype(bf16)
        term = dot_nt(dkvq[member(q), :], w_ref[...])
        if q == 3:
            part[2] = term.astype(bf16)
            passed = go(part.at[2], relay, line[1], only=ends)
            dx_three = go(part.at[2], part_in.at[2], line[3], only=mid)
        elif q == 2:
            far = term
        elif q == 1:
            part[0] = term.astype(bf16)
            dx_c.append(go(part.at[0], part_in.at[0], line[1]))
            pl.when(mid)(passed.wait_recv)
            part[1] = (far + relay[...].astype(f32)).astype(bf16)
            dx_c.append(go(part.at[1], part_in.at[1], line[2]))
        else:
            dx_ref[...] = done_ref[...] + term
    one_out = send_sum(0, g_one, one_c)
    g_two[...] = dot_tn(tok_ref[...], dkvq[:, 0:384]).astype(bf16)
    two_c = send_half(1, g_two)
    two_out = send_sum(1, g_two, two_c)
    for c in np_c:
        c.wait_recv()
    nrow[1] = nrow[0] + np_in[1] + np_in[2] + np_in[3]
    half = go(nrow.at[1], np_in.at[0], sib)
    half.wait_recv()
    full = nrow[1] + np_in[0]
    snorm_ref[...] = pltpu.roll(full, lax.rem(768 - 96 * b, 768), 1)[0:1, 0:96]
    two = settle(1, two_out)
    one = settle(0, one_out)
    piece = [two[:, 64 * i : 64 * i + 64] for i in range(6)]
    piece += [one[:, 0:64], one[:, 64:128], one[:, 256:320]]
    for k, i in enumerate((6, 0, 2, 7, 1, 3, 8, 4, 5)):
        sqkv_ref[:, 64 * k : 64 * k + 64] = piece[i]
    turned = jnp.concatenate([one[:, 128:384], jnp.zeros((32, 256), f32)], axis=0).T
    sout_ref[0:128, :] = turned[0:128, 0:96]
    sout_ref[128:192, :] = turned[192:256, 0:96]
    for c in dx_c:
        c.wait_recv()
    pl.when(mid)(dx_three.wait_recv)
    dx_ref[...] += part_in[0].astype(f32) + part_in[1].astype(f32) + part_in[2].astype(f32)
    go.finish()


def run_finish(dkv, dq, toks, w, datt, datt_two, mixed, done, gn):
    f32, bf16 = jnp.float32, jnp.bfloat16
    V = pltpu.VMEM
    return pl.pallas_call(
        finish,
        out_shape=(
            jax.ShapeDtypeStruct((128, 768), f32),
            jax.ShapeDtypeStruct((96, 576), f32),
            jax.ShapeDtypeStruct((192, 96), f32),
            jax.ShapeDtypeStruct((1, 96), f32),
        ),
        in_specs=[VM] * 9,
        out_specs=(VM,) * 4,
        scratch_shapes=[
            V((4, 4, 128, 384), bf16), V((4, 4, 128, 384), bf16), V((4, 3, 128, 384), bf16),
            V((768, 384), bf16), V((768, 384), bf16),
            V((2, 4, 96, 384), bf16), V((2, 4, 96, 384), bf16), V((2, 3, 96, 384), bf16),
            V((3, 128, 768), bf16), V((3, 128, 768), bf16), V((4, 128, 768), bf16), V((512, 640), bf16),
            V((3, 8, 768), f32), V((2, 8, 768), f32), V((4, 8, 768), f32), V((128, 768), bf16),
            pltpu.SemaphoreType.DMA((2, 72)),
        ],
        compiler_params=pltpu.CompilerParams(
            collective_id=5, has_side_effects=True, vmem_limit_bytes=28 << 20
        ),
        name="finish",
    )(dkv, dq, toks, w, datt, datt_two, mixed, done, gn)


def collect(
    len_any, tok_any, wq_any, wout_any, nrm_any, pos_any,
    gt, wat, q_ref, kv, wout, norm_out, kcode, qcode,
    wa_ref, wo_ref, nr, code_ref, wq_ref, wout_ref, nrm_row, pos_ref, nrm_ref, len_ref, sems, lsem,
):
    b = lax.axis_index("blk")
    z = lax.axis_index("head")
    chip, core = b // 2, b % 2
    sib = (chip * 2 + 1 - core, z)
    near = [(chip ^ r) * 2 + core for r in (0, 1, 2, 3)]
    flat = [(n, z) for n in near]
    line = [(b, z ^ r) for r in (0, 1, 2, 3)]
    f32, bf16 = jnp.float32, jnp.bfloat16
    fetch = [
        pltpu.make_async_copy(wq_any, wq_ref, lsem.at[0]),
        pltpu.make_async_copy(wout_any, wout_ref, lsem.at[1]),
        pltpu.make_async_copy(nrm_any, nrm_row, lsem.at[2]),
        pltpu.make_async_copy(pos_any, pos_ref, lsem.at[3]),
        pltpu.make_async_copy(tok_any, gt.at[z], lsem.at[4]),
        pltpu.make_async_copy(len_any, len_ref, lsem.at[5]),
    ]
    for c in fetch:
        c.start()
    for c in fetch:
        c.wait()
    go = Sender(sems)
    mid = (z == 1) | (z == 2)
    ends = (z == 0) | (z == 3)

    wq = wq_ref[...].astype(f32)
    wo = wout_ref[...].astype(f32)
    wo = jnp.concatenate([wo[0:128], jnp.zeros((64, 96), f32), wo[128:192]], axis=0)
    wo = jnp.concatenate([wo, jnp.zeros((256, 32), f32)], axis=1).T[0:96]
    wo_ref[...] = wo.astype(bf16)
    piece = [wq[:, 64 * i : 64 * i + 64] for i in range(9)] + [wo[:, 192:256]]
    for k in range(5):
        tile = jnp.concatenate([piece[PACK[2 * k]], piece[PACK[2 * k + 1]]], axis=1)
        wa_ref[:, 128 * k : 128 * k + 128] = tile.astype(bf16)
    wat[b] = wa_ref[...]
    wout[z] = wo_ref[...]
    nrm_ref[...] = jnp.zeros((8, 128), f32)
    nrm_ref[0:1, 0:96] = nrm_row[...].astype(f32)
    nr[b, z] = nrm_ref[...]
    greet([sib] + flat[1:] + line[1:])
    tok_z = [Spread(go, mid, lambda j, h=h: gt.at[j, pl.ds(64 * h, 64)], z, line) for h in range(2)]
    wa_p = [go(wa_ref, wat.at[b], flat[r]) for r in (3, 1, 2)]
    wa_s = [go(wa_ref, wat.at[b], sib)]
    pos = pos_ref[...]
    seq = jnp.zeros(pos.shape, f32)
    end = 0
    for k in range(8):
        end = end + len_ref[k]
        seq = seq + jnp.where(pos >= end, 1.0, 0.0)
    code_ref[...] = pos.astype(f32) + SEQ_STEP * seq

    def spread_code(d, _):
        kcode[d] = jnp.broadcast_to(code_ref[pl.ds(d, 1), :], (128, 128)).T
        return 0

    lax.fori_loop(0, 32, spread_code, 0)
    own_code = [code_ref[pl.ds(b * 4 + j, 1), :] for j in range(4)]
    for i in range(4):
        qcode[i, 0:1, :] = jnp.concatenate([c[:, 32 * i : 32 * i + 32] for c in own_code], axis=1)
    go.sent(tok_z[0].two)
    tok_z[0].rest()
    tok_z[0].pass_on()
    go.sent(tok_z[1].two)
    tok_z[1].rest()
    wo_z = [go(wo_ref, wout.at[z], line[r]) for r in (3, 2, 1)]
    nr_z = [go(nrm_ref, nr.at[b, z], line[r]) for r in (3, 2, 1)]
    for k, r in enumerate((3, 1, 2)):
        wa_p[k].wait_recv()
        wa_s.append(go(wat.at[near[r]], wat.at[near[r]], sib))
    tok_z[1].pass_on()
    for c in wa_s:
        c.wait_recv()
    kv_p = []
    for r in (0, 2, 1, 3):
        for s in tok_z:
            if r in (1, 3):
                (s.one if r == 1 else s.three).wait_recv()
        j = z ^ r
        rows = jnp.dot(gt[j], wat[...].reshape(768, 640), preferred_element_type=f32)
        kv[b * 4 + j] = rows[:, 0:384].astype(bf16)
        if r == 3:
            kv_l = [go(kv.at[b * 4 + j], kv.at[b * 4 + j], flat[s]) for s in (3, 1, 2)]
            passed.append(go(kv.at[b * 4 + j], kv.at[b * 4 + j], sib))
        else:
            kv_p.append(Plane(go, core, lambda n, j=j: kv.at[n * 4 + j], b, near, flat, sib))
        q_ref[j] = rows[:, 384:640].astype(bf16) * bf16(HEAD_DIM ** (-0.5))
        if r:
            kv_p[{2: 0, 1: 1, 3: 2}[r]].pass_on()
        if r == 1:
            for c in wo_z + nr_z:
                c.wait_recv()
            nr_p = [go(nr.at[b], nr.at[b], flat[r]) for r in (3, 1, 2)]
            passed = [go(nr.at[b], nr.at[b], sib)]
    for k, r in enumerate((3, 1, 2)):
        nr_p[k].wait_recv()
        passed.append(go(nr.at[near[r]], nr.at[near[r]], sib))
    for p in kv_p:
        p.last()
    for k, s in enumerate((3, 1, 2)):
        kv_l[k].wait_recv()
        n = near[s] * 4 + (z ^ 3)
        passed.append(go(kv.at[n], kv.at[n], sib))
    for p in kv_p:
        p.whole()
    for c in passed:
        c.wait_recv()
    total = jnp.zeros((8, 768), f32)
    for n in range(8):
        rows = jnp.concatenate([nr[n, j, 0:1, :] for j in range(4)] + [jnp.zeros((4, 128), f32)], axis=0)
        total = total + pltpu.roll(jnp.concatenate([rows, jnp.zeros((8, 640), f32)], axis=1), 96 * n, 1)
    norm_out[...] = total
    go.finish()


def run_collect(lengths, tok, wq, wo, nrm, pos):
    f32, bf16 = jnp.float32, jnp.bfloat16
    S = jax.ShapeDtypeStruct
    V = pltpu.VMEM
    return pl.pallas_call(
        collect,
        out_shape=(
            S((4, 128, 768), bf16), S((8, 96, 640), bf16), S((4, 128, 256), bf16), S((32, 128, 384), bf16),
            S((4, 96, 256), bf16), S((8, 768), f32), S((32, 128, 128), f32), S((4, 8, 128), f32),
        ),
        in_specs=[HBM] * 6,
        out_specs=(VM,) * 8,
        scratch_shapes=[
            V((96, 640), bf16), V((96, 256), bf16), V((8, 4, 8, 128), f32), V((32, 128), f32),
            V((96, 576), bf16), V((192, 96), bf16), V((1, 96), bf16), V((32, 128), jnp.int32), V((8, 128), f32),
            pltpu.SMEM((8,), jnp.int32), pltpu.SemaphoreType.DMA((2, 80)), pltpu.SemaphoreType.DMA((6,)),
        ],
        compiler_params=pltpu.CompilerParams(
            collective_id=1, has_side_effects=True, vmem_limit_bytes=20 << 20
        ),
        name="collect",
    )(lengths, tok, wq, wo, nrm, pos)


def moments(rows):
    center = rows - jnp.mean(rows, axis=-1, keepdims=True)
    spread = lax.rsqrt(jnp.mean(center * center, axis=-1, keepdims=True) + 1e-05)
    return center * spread, spread


def norm_back(grad, gain, unit, spread):
    scaled = grad * gain
    return spread * (
        scaled - jnp.mean(scaled, axis=-1, keepdims=True) - unit * jnp.mean(scaled * unit, axis=-1, keepdims=True)
    )


def middle(
    mixed_ref, tok_any, og_any, norm_ref, wo_0, wo_1, wo_2, gu_any, down_any,
    act_ref, done_ref, datt_ref, dheads, sum_0, sum_1, sum_2, sum_3, gn_ref,
    mix_in, wffn, rows_in, drow_in, gelu_a, gelu_b, gated, dgate, dup,
    part, part_in, part2, part2_in, gff, ffn_sib, hid, unit_one, held, held_two, head_out,
    tok_ref, og_ref, wout, part_relay, part2_relay, sems, lsem,
):
    b = lax.axis_index("blk")
    z = lax.axis_index("head")
    chip, core = b // 2, b % 2
    sib = (chip * 2 + 1 - core, z)
    near = [(chip ^ r) * 2 + core for r in (0, 1, 2, 3)]
    flat = [(n, z) for n in near]
    line = [(b, z ^ r) for r in (0, 1, 2, 3)]
    f32, bf16 = jnp.float32, jnp.bfloat16
    own = [
        pltpu.make_async_copy(gu_any, wffn.at[0:2, b], lsem.at[0]),
        pltpu.make_async_copy(down_any, wffn.at[2, b], lsem.at[1]),
        pltpu.make_async_copy(tok_any, tok_ref, lsem.at[2]),
        pltpu.make_async_copy(og_any, og_ref, lsem.at[3]),
    ]
    for c in own:
        c.start()
    greet([sib] + flat[1:] + line[1:])
    go = Sender(sems)
    mid = (z == 1) | (z == 2)
    ends = (z == 0) | (z == 3)

    HALF = 64

    @pl.when(ends)
    def _():
        for h in range(2):
            part_in[h, 2] = jnp.zeros((HALF, 768), bf16)
            part2_in[h, 2] = jnp.zeros((HALF, 768), bf16)

    def scatter(out, arrived, relay, terms, h):
        passed = go(out.at[h, z ^ 3], relay.at[h], line[1], only=ends)
        three = go(out.at[h, z ^ 3], arrived.at[h, 2], line[3], only=mid)
        one = go(out.at[h, z ^ 1], arrived.at[h, 0], line[1])
        two = go.make(out.at[h, z ^ 2], arrived.at[h, 1], line[2])
        go.start(two, only=ends)

        def later():
            @pl.when(mid)
            def _():
                passed.wait_recv()
                out[h, z ^ 2] = (terms[h, z ^ 2] + relay[h].astype(f32)).astype(bf16)

            go.left.append((two, mid))
            pl.when(mid)(two.start)

        return one, two, three, later

    def gathered(copies):
        copies[0].wait_recv()
        copies[1].wait_recv()
        pl.when(mid)(copies[2].wait_recv)

    wo_three = go.make(wout.at[:, b], wout.at[:, b], flat[3])
    go(wo_1, wout.at[:, near[1]], flat[2], only=core == 0, arrive=wo_three.arrive)
    go(wo_2, wout.at[:, near[2]], flat[1], only=core == 1, arrive=wo_three.arrive)
    wo_s = []
    for r, ref in enumerate((wo_0, wo_1, wo_2)):
        wo_s.append(go(ref, wout.at[:, near[r]], sib))
        wout[:, near[r]] = ref[...]
    mix_c = []
    for h in range(2):
        rows = pl.ds(HALF * h, HALF)
        mix_c.append([go(mixed_ref.at[z ^ r, rows], mix_in.at[h, z], line[r]) for r in (3, 2, 1)])

    for c in own:
        c.wait()
    wf_p = [Plane(go, core, lambda n, t=t: wffn.at[t, n], b, near, flat, sib) for t in range(3)]
    wo_three.wait_recv()
    wo_s.append(go(wout.at[:, near[3]], wout.at[:, near[3]], sib))
    for c in wo_s:
        c.wait_recv()

    def out_weight(j):
        return wout[j].reshape(768, 256)

    spreads = []
    row_c = []
    for h in range(2):
        rows = pl.ds(HALF * h, HALF)
        mix_in[h, z] = mixed_ref[z, rows, :]
        for c in mix_c[h]:
            c.wait_recv()
        attn = dot_nt(mix_in[h, 0], out_weight(0))
        for j in (1, 2, 3):
            attn = attn + dot_nt(mix_in[h, j], out_weight(j))
        unit, spread = moments(tok_ref[rows, :].astype(f32) + attn)
        hidden = unit * norm_ref[0:1, :] + norm_ref[1:2, :]
        unit_one[h] = unit
        spreads.append(spread)
        hid[h] = hidden
        rows_in[h, z] = hidden.astype(bf16)
        row_c.append(Spread(go, mid, lambda j, h=h: rows_in.at[h, j], z, line))
        if h == 1:
            row_c[0].rest()
        wf_p[h].pass_on()
    row_c[0].pass_on()
    row_c[1].rest()
    wf_p[2].pass_on()
    row_c[1].pass_on()
    for p in wf_p:
        p.last()
    wf_p[0].whole()
    wf_p[1].whole()

    def weight(t):
        return wffn[t].reshape(768, 768)

    part_c = []
    for h in range(2):
        row_c[h].wait()
        rows = rows_in[h].reshape(4 * HALF, 768)
        gate = jnp.dot(rows, weight(0), preferred_element_type=f32)
        up = jnp.dot(rows, weight(1), preferred_element_type=f32)
        half = 0.5 + 0.5 * lax.erf(gate * (0.5**0.5))
        value = gate * half
        low = (value * up).astype(bf16)
        gated[h] = low
        if h == 0:
            wf_p[2].whole()
        term = dot_nt(low, weight(2)).reshape(4, HALF, 768)
        held[h] = term
        part[h] = term.astype(bf16)
        if h == 1:
            part_c[0][3]()
        part_c.append(scatter(part, part_in, part_relay, held, h))
        slope = half + gate * jnp.exp(-0.5 * gate * gate) * 0.3989422804014327
        gelu_a[h] = slope * up
        gelu_b[h] = value
    part_c[1][3]()
    gains = []
    drow_c = []
    for h in range(2):
        rows = pl.ds(HALF * h, HALF)
        if h == 1:
            drow_c[0].pass_on()
        gathered(part_c[h])
        branch = held[h, z] + part_in[h, 0].astype(f32) + part_in[h, 1].astype(f32) + part_in[h, 2].astype(f32)
        unit_two, spread_two = moments(hid[h] + branch)
        grad = og_ref[rows, :].astype(f32)
        d_two = norm_back(grad, norm_ref[2:3, :], unit_two, spread_two)
        hid[h] = d_two
        drow_in[h, z] = d_two.astype(bf16)
        drow_c.append(Spread(go, mid, lambda j, h=h: drow_in.at[h, j], z, line))
        act_ref[rows, :] = (unit_two * norm_ref[2:3, :] + norm_ref[3:4, :]).astype(bf16)
        gains.append((jnp.sum(grad * unit_two, axis=0, keepdims=True), jnp.sum(grad, axis=0, keepdims=True)))
        drow_c[h].rest()
    gn_ref[...] = jnp.zeros((32, 768), f32)
    gn_ref[16:17, :] = gains[0][0] + gains[1][0]
    gn_ref[24:25, :] = gains[0][1] + gains[1][1]
    part2_c = []
    for h in range(2):
        if h == 1:
            drow_c[1].pass_on()
        drow_c[h].wait()
        d_gated = jnp.dot(drow_in[h].reshape(4 * HALF, 768), weight(2), preferred_element_type=f32)
        dg = (d_gated * gelu_a[h]).astype(bf16)
        du = (d_gated * gelu_b[h]).astype(bf16)
        dgate[h] = dg
        dup[h] = du
        term = (dot_nt(dg, weight(0)) + dot_nt(du, weight(1))).reshape(4, HALF, 768)
        held_two[h] = term
        part2[h] = term.astype(bf16)
        if h == 1:
            part2_c[0][3]()
        part2_c.append(scatter(part2, part2_in, part2_relay, held_two, h))
    part2_c[1][3]()
    sib_c = []
    acts = rows_in[...].reshape(512, 768)
    for t in (2, 0, 1):
        if t == 2:
            total = dot_tn(drow_in[...].reshape(512, 768), gated[...].reshape(512, 768))
        else:
            total = dot_tn(acts, (dgate, dup)[t][...].reshape(512, 768))
        gff[t] = total.astype(bf16).reshape(4, 2, 96, 768)
        sib_c.append(go(gff.at[t, :, 1 - core], ffn_sib.at[t], sib))
    gains = []
    head_c = []
    for h in range(2):
        rows = pl.ds(HALF * h, HALF)
        gathered(part2_c[h])
        d_hidden = (
            hid[h] + held_two[h, z]
            + part2_in[h, 0].astype(f32) + part2_in[h, 1].astype(f32) + part2_in[h, 2].astype(f32)
        )
        unit = unit_one[h]
        d_one = norm_back(d_hidden, norm_ref[0:1, :], unit, spreads[h])
        low_one = d_one.astype(bf16)
        for r in (3, 2, 1, 0):
            term = jnp.dot(low_one, out_weight(z ^ r), preferred_element_type=f32).astype(bf16)
            if r:
                head_out[h, r - 1] = term
                head_c.append(go(head_out.at[h, r - 1], dheads.at[z, rows], line[r]))
            else:
                dheads[z, rows, :] = term
        done_ref[rows, :] = d_one
        datt_ref[rows, :] = low_one
        gains.append((jnp.sum(d_hidden * unit, axis=0, keepdims=True), jnp.sum(d_hidden, axis=0, keepdims=True)))
    gn_ref[0:1, :] = gains[0][0] + gains[1][0]
    gn_ref[8:9, :] = gains[0][1] + gains[1][1]
    for k, t in enumerate((2, 0, 1)):
        sib_c[k].wait_recv()
        for r, ref in enumerate((sum_0, sum_1, sum_2, sum_3)):
            both = gff[t, chip ^ r, core].astype(f32) + ffn_sib[t, chip ^ r].astype(f32)
            ref[t] = both.astype(bf16)
    for c in head_c:
        c.wait_recv()
    go.finish()


def run_middle(mixed, tok, og, norms, wo, gu, down):
    f32, bf16 = jnp.float32, jnp.bfloat16
    S = jax.ShapeDtypeStruct
    V = pltpu.VMEM
    halves = (2, 256, 768)
    return pl.pallas_call(
        middle,
        out_shape=(
            S((128, 768), bf16), S((128, 768), f32), S((128, 768), bf16), S((4, 128, 256), bf16),
            *[S((3, 96, 768), bf16)] * 4, S((32, 768), f32),
        ),
        in_specs=[VM, HBM, HBM, VM, VM, VM, VM, HBM, HBM],
        out_specs=(VM,) * 9,
        scratch_shapes=[
            V((2, 4, 64, 256), bf16), V((3, 8, 96, 768), bf16), V((2, 4, 64, 768), bf16), V((2, 4, 64, 768), bf16),
            V(halves, f32), V(halves, f32), V(halves, bf16), V(halves, bf16), V(halves, bf16),
            V((2, 4, 64, 768), bf16), V((2, 3, 64, 768), bf16), V((2, 4, 64, 768), bf16), V((2, 3, 64, 768), bf16),
            V((3, 4, 2, 96, 768), bf16), V((3, 4, 96, 768), bf16),
            V((2, 64, 768), f32), V((2, 64, 768), f32), V((2, 4, 64, 768), f32), V((2, 4, 64, 768), f32),
            V((2, 3, 64, 256), bf16),
            V((128, 768), bf16), V((128, 768), bf16), V((4, 8, 96, 256), bf16), V((2, 64, 768), bf16), V((2, 64, 768), bf16),
            pltpu.SemaphoreType.DMA((2, 108)), pltpu.SemaphoreType.DMA((4,)),
        ],
        compiler_params=pltpu.CompilerParams(
            collective_id=3, has_side_effects=True, vmem_limit_bytes=36 << 20
        ),
        name="middle",
    )(mixed, tok, og, norms, *wo, gu, down)


def deliver(*refs):
    dx, sqkv, sout, snorm, *sums = refs[:8]
    o_dx, o_qkv, o_out, o_norm, o_gu, o_down, sem = refs[8:]
    pairs = ((dx, o_dx), (sqkv, o_qkv), (sout, o_out), (snorm, o_norm))
    copies = [pltpu.make_async_copy(s, d, sem.at[i]) for i, (s, d) in enumerate(pairs)]
    for c in copies:
        c.start()
    for t in range(3):
        total = sum(s[t].astype(jnp.float32) for s in sums)
        if t < 2:
            o_gu[t] = total
        else:
            o_down[...] = total
    for c in copies:
        c.wait()


def run_deliver(*arrays):
    f32 = jnp.float32
    S = jax.ShapeDtypeStruct
    return pl.pallas_call(
        deliver,
        out_shape=(
            S((128, 768), f32), S((96, 576), f32), S((192, 96), f32), S((1, 96), f32),
            S((2, 96, 768), f32), S((96, 768), f32),
        ),
        in_specs=[ANY] * 4 + [VM] * 4,
        out_specs=(ANY,) * 4 + (VM,) * 2,
        scratch_shapes=[pltpu.SemaphoreType.DMA((4,))],
        compiler_params=pltpu.CompilerParams(vmem_limit_bytes=8 << 20),
        name="deliver",
    )(*arrays)


PACK = (1, 4, 2, 5, 7, 8, 0, 3, 6, 9)


def fast_shards(
    tokens, w_qkv, w_out, w_gate_up, w_down, norm_params, alibi_slope, lengths, placement, out_grad
):
    heads_n = lax.axis_size("head")
    blk_n = lax.axis_size("blk")
    head_idx = lax.axis_index("head")
    blk_idx = lax.axis_index("blk")
    tok_rows, width = tokens.shape
    per_dev = HEADS // heads_n
    group_rows = heads_n * tok_rows
    devs = heads_n * blk_n
    share = w_qkv.shape[0]
    bf16 = jnp.bfloat16

    held = [
        pltpu.with_memory_space_constraint(a, pltpu.MemorySpace.HBM)
        for a in (lengths, alibi_slope, tokens, w_qkv, w_out, norm_params.reshape(1, share), placement.reshape(devs, tok_rows))
    ]
    group_tokens, attn_w, q, kv, wo, norms, kcode, qcode = run_collect(held[0], *held[2:])
    wo = [wo] + [lax.ppermute(wo, "blk", [(i, i ^ (2 * r)) for i in range(blk_n)]) for r in (1, 2)]
    mixed, lse = run_attend(held[0], held[1], q, kv, kcode, qcode)
    act, d_one, d_attn, d_heads, *sums, g_norm = run_middle(
        mixed, tokens, out_grad, norms, wo, w_gate_up, w_down.T
    )
    sums = [sums[0]] + [
        lax.ppermute(sums[r], "blk", [(i, i ^ (2 * r)) for i in range(blk_n)]) for r in (1, 2, 3)
    ]
    d_attn_two = lax.ppermute(d_attn, "head", [(i, i ^ 2) for i in range(heads_n)])
    d_q, dkv, result = run_attend_back(
        held[0], held[1], q, kv, kcode, qcode, mixed, d_heads, lse, act
    )
    input_grad, s_qkv, s_out, s_norm = run_finish(
        dkv.reshape(blk_n, group_rows, 384), d_q.reshape(group_rows, 256),
        group_tokens.reshape(group_rows, width), attn_w.reshape(width, 640),
        d_attn, d_attn_two, mixed.reshape(group_rows, 256), d_one, g_norm,
    )
    input_grad, s_qkv, s_out, s_norm, s_gu, s_down = run_deliver(input_grad, s_qkv, s_out, s_norm, *sums)
    return (
        result,
        input_grad,
        s_qkv,
        s_out,
        s_gu,
        s_down.T,
        s_norm.reshape(share, 1),
    )


def solution(mesh):
    placed = (
        P(("blk", "head"), None),
        P("blk", "head"),
        P("head", "blk"),
        P(None, "blk", "head"),
        P("head", "blk"),
        P("blk", "head"),
        P(),
        P(),
        P(),
        P(("blk", "head"), None),
    )
    small = mesh.shape["blk"] == 8 and mesh.shape["head"] == 4
    return jax.shard_map(
        fast_shards if small else shards,
        mesh=mesh,
        in_specs=placed,
        out_specs=(
            P(("blk", "head"), None),
            P(("blk", "head"), None),
            P("blk", "head"),
            P("head", "blk"),
            P(None, "blk", "head"),
            P("head", "blk"),
            P("blk", "head"),
        ),
        check_vma=False,
    )
```
